128 devices in a mesh: seq: 4 (over z), fsdp: 32 (over y, x, core).
Axes of the slice: x: 4, y: 4, z: 4, core: 2. Of those that a mesh axis runs over, the one named last changes fastest.
Arguments:
- tokens_in: bfloat16 [32, 512, 1536], P('fsdp', 'seq'), may hold values from -6 to 6
- cotangent: bfloat16 [32, 512, 1536], P('fsdp', 'seq'), may hold values from -6 to 6
- routes: int32 [2, 32, 512, 4], P(None, 'fsdp', 'seq'), may hold values from 0 to 7, all different within a row
- order: int32 [2, 32, 512, 4], P(None, 'fsdp', 'seq'), may hold values from 0 to 511, as said below
- segment_ids: int32 [32, 256], P('fsdp'), may hold values from 0 to 3, never falling along the last dimension, each value on 1 to 128 neighbouring positions
- gain_attn: bfloat16 [2, 1536], P(None, ('seq', 'fsdp')), may hold values from 0.5 to 1.5
- w_query: bfloat16 [2, 1536, 1536], P(None, ('seq', 'fsdp')), may hold values from -0.15625 to 0.15625
- w_key: bfloat16 [2, 1536, 256], P(None, ('seq', 'fsdp')), may hold values from -0.15625 to 0.15625
- w_value: bfloat16 [2, 1536, 256], P(None, ('seq', 'fsdp')), may hold values from -0.15625 to 0.15625
- w_out: bfloat16 [2, 1536, 1536], P(None, ('seq', 'fsdp')), may hold values from -0.625 to 0.625
- gain_ffn: bfloat16 [2, 1536], P(None, ('seq', 'fsdp')), may hold values from 0.5 to 1.5
- w_router: bfloat16 [2, 1536, 8], P(None, ('seq', 'fsdp')), may hold values from -0.078125 to 0.078125
- w_gate: bfloat16 [2, 8, 1536, 768], P(None, 'seq', 'fsdp'), may hold values from -0.15625 to 0.15625
- w_up: bfloat16 [2, 8, 1536, 768], P(None, 'seq', 'fsdp'), may hold values from -0.15625 to 0.15625
- w_down: bfloat16 [2, 8, 768, 1536], P(None, 'seq', 'fsdp'), may hold values from -0.4375 to 0.4375
Outputs:
- result: bfloat16 [32, 512, 1536], P('fsdp', 'seq')
- grad_tokens: float32 [32, 512, 1536], P('fsdp', 'seq')
- grad_gain_attn: float32 [2, 1536], P(None, ('seq', 'fsdp'))
- grad_w_query: float32 [2, 1536, 1536], P(None, ('seq', 'fsdp'))
- grad_w_key: float32 [2, 1536, 256], P(None, ('seq', 'fsdp'))
- grad_w_value: float32 [2, 1536, 256], P(None, ('seq', 'fsdp'))
- grad_w_out: float32 [2, 1536, 1536], P(None, ('seq', 'fsdp'))
- grad_gain_ffn: float32 [2, 1536], P(None, ('seq', 'fsdp'))
- grad_w_router: float32 [2, 1536, 8], P(None, ('seq', 'fsdp'))
- grad_w_gate: float32 [2, 8, 1536, 768], P(None, 'seq', 'fsdp')
- grad_w_up: float32 [2, 8, 1536, 768], P(None, 'seq', 'fsdp')
- grad_w_down: float32 [2, 8, 768, 1536], P(None, 'seq', 'fsdp')
The draws below stay inside these ranges and needn't reach their ends.
Inputs may be any that keep to these rules, and one draw needn't show every extreme that they name: `routes`: each token names 4 different experts in each layer. `order`: in each layer, the 512 entries of an aligned block of 128 tokens hold each of 0 to 511 once. `segment_ids`: in each row the numbers never fall, each of 0 to 3 stands on 1 to 128 places, one on exactly 128.
All inputs are finite; a program needn't handle non-finite values.
Results may differ from the reference program's by a relative error of at most 0.028.
Values may be sent and summed in bfloat16 or wider, within the bound.
No kernel may reach another device: no remote copies, remote signals or barrier semaphores. Data moves between devices by JAX's collectives and lax.ppermute only.
A program may use at most 320 MiB of HBM per device.

```python
import math
from functools import partial
import jax
import jax.numpy as jnp
import numpy as np
from jax import lax

D = 1536
HEADS = 12
KVHEADS = 2
HD = 128
FF = 768
TOPK = 4
LAYERS = 2
NCONT = 4
TOK_DEV = 128
EXPERTS = 8
GROUPS = 32
GROUP_TOK = 512
TOKENS = 16384
PROMPT = 256
CONT_TOK = 256
CONT_MOST = 128
CAP = 72
N_SEQ = 4


def shuffle_block(block_key):
    return jax.random.permutation(block_key, TOK_DEV * TOPK)


def draw_order(key, part):
    key = jax.random.fold_in(key, 7)
    block_count = LAYERS * GROUPS * (GROUP_TOK // TOK_DEV)
    block_keys = jax.random.split(key, block_count)
    ranks = jax.vmap(shuffle_block)(block_keys)
    return ranks.reshape(LAYERS, GROUPS, GROUP_TOK, TOPK).astype(jnp.int32)


def level_of(own_key, extent, pieces, low, largest):
    factor_of = 1.0
    for dim, blocks in pieces:
        draws = jax.random.uniform(jax.random.fold_in(jax.random.fold_in(own_key, 6), dim), (blocks,), jnp.float32, low / len(pieces), largest / len(pieces))
        factor_of = factor_of * jnp.repeat(jnp.exp(draws), extent[dim] // blocks).reshape((-1,) + (1,) * (len(extent) - 1 - dim))
    return factor_of


def distinct(own_key, rows, count, top, lift):
    order = jax.random.permutation(jax.random.fold_in(own_key, 1), count)
    pull = order
    for power in range(3):
        pull = pull * pull // count
    pull = pull * lift // count
    tickets = jax.random.randint(jax.random.fold_in(own_key, 2), (rows, count), 0, 4096) + pull
    fixed_rows = jax.random.permutation(jax.random.fold_in(own_key, 3), rows)[jnp.arange(count) % rows]
    tickets = jnp.where(jnp.arange(rows)[:, None] == fixed_rows[None, :], 1 << 14, tickets)
    priority = tickets * count + jnp.arange(count)
    return lax.top_k(priority.astype(jnp.int32), top)[1].astype(jnp.int32)


def length_profile(amount, total, reach, lean):
    portions = [(1 << 20) // math.isqrt(rank ** lean) + 1 for rank in range(2, amount + 1)]
    spare, holding = total - reach - (amount - 1), [1] * (amount - 1)
    while spare > 0:
        free = [i for i in range(amount - 1) if holding[i] < reach]
        whole, budget = sum([portions[i] for i in free]), spare
        for i in free:
            extra = min(reach - holding[i], max(1, budget * portions[i] // whole), spare)
            holding[i] = holding[i] + extra
            spare = spare - extra
    return np.array([reach] + holding)


def uneven(rng, number_of, total, bound, lean):
    if number_of == 2:
        one = jax.random.randint(rng, (), max(1, total - bound), min(bound, total - 1) + 1)
        return jnp.stack([one, total - one])
    tallies = jnp.asarray(length_profile(number_of, total, bound, lean), jnp.int32)
    pairs = (number_of - 1) // 2
    donor, sink = tallies[1:1 + 2 * pairs:2], tallies[2:2 + 2 * pairs:2]
    margin = jnp.minimum(donor - 1, bound - sink)
    shifted = jax.random.randint(jax.random.fold_in(rng, 1), (pairs,), 0, 1 << 20) % (margin + 1)
    tallies = tallies.at[1:1 + 2 * pairs:2].set(donor - shifted).at[2:2 + 2 * pairs:2].set(sink + shifted)
    return tallies[jax.random.permutation(jax.random.fold_in(rng, 2), number_of)]


def centred(key, extent, deviation, reach, cuts=(), held_as=jnp.bfloat16):
    level = level_of(key, extent, cuts, -0.22, 0.18) if cuts else 1.0
    array = jax.random.normal(key, extent, jnp.float32) * deviation * level
    return jnp.minimum(jnp.maximum(array, -reach), reach).astype(held_as)


def setup_inputs(seed: int = 0) -> dict:
    splits = jax.random.split(jax.random.key(seed), 16)
    tokens_in = centred(splits[0], (GROUPS, GROUP_TOK, D), 1.0, 6.0, ((0, 32), (1, 4)))
    cotangent = centred(splits[1], (GROUPS, GROUP_TOK, D), 1.0, 6.0, ((0, 32), (1, 4)))
    routes = distinct(splits[2], LAYERS * GROUPS * GROUP_TOK, EXPERTS, TOPK, 4096).reshape((LAYERS, GROUPS, GROUP_TOK, TOPK))
    order = draw_order(jax.random.fold_in(splits[15], 71), 0)
    segment_ids = jax.vmap(lambda own: jnp.searchsorted(jnp.cumsum(uneven(own, NCONT, CONT_TOK, CONT_MOST, 1)), jnp.arange(CONT_TOK), side="right"))(jax.random.split(splits[4], GROUPS)).reshape((GROUPS, CONT_TOK)).astype(jnp.int32)
    gain_attn = jnp.clip(1.0 + 0.1 * jax.random.normal(splits[5], (LAYERS, D), jnp.float32), 0.5, 1.5).astype(jnp.bfloat16)
    w_query = centred(splits[6], (LAYERS, D, HEADS * HD), D ** -0.5, 0.15625, ((1, 128),))
    w_key = centred(splits[7], (LAYERS, D, KVHEADS * HD), D ** -0.5, 0.15625, ((1, 128),))
    w_value = centred(splits[8], (LAYERS, D, KVHEADS * HD), D ** -0.5, 0.15625, ((1, 128),))
    w_out = centred(splits[9], (LAYERS, HEADS * HD, D), (D // 16) ** -0.5, 0.625, ((1, 128),))
    gain_ffn = jnp.clip(1.0 + 0.1 * jax.random.normal(splits[10], (LAYERS, D), jnp.float32), 0.5, 1.5).astype(jnp.bfloat16)
    w_router = centred(splits[11], (LAYERS, D, EXPERTS), 0.0128, 0.078125, ((1, 128),))
    w_gate = centred(splits[12], (LAYERS, EXPERTS, D, FF), D ** -0.5, 0.15625, ((1, 4), (2, 32)))
    w_up = centred(splits[13], (LAYERS, EXPERTS, D, FF), D ** -0.5, 0.15625, ((1, 4), (2, 32)))
    w_down = centred(splits[14], (LAYERS, EXPERTS, FF, D), (FF // 4) ** -0.5, 0.4375, ((1, 4), (2, 32)))
    return {"tokens_in": tokens_in, "cotangent": cotangent, "routes": routes, "order": order, "segment_ids": segment_ids, "gain_attn": gain_attn, "w_query": w_query, "w_key": w_key, "w_value": w_value, "w_out": w_out, "gain_ffn": gain_ffn, "w_router": w_router, "w_gate": w_gate, "w_up": w_up, "w_down": w_down}


@jax.custom_vjp
def low(v):
    return lax.optimization_barrier(v.astype(jnp.bfloat16)).astype(jnp.float32)

@jax.custom_vjp
def low_back(v):
    return v

def low_keep(v):
    return (low(v), None)

def low_pass(kept, grad):
    return (grad,)

def back_keep(v):
    return (v, None)

def back_low(kept, grad):
    return (low(grad),)
low.defvjp(low_keep, low_pass)
low_back.defvjp(back_keep, back_low)
norm_eps = 1e-06
rope_base = 10000.0
masked_value = -1e+30

def product(left, right):
    return jnp.dot(left, right, precision=lax.Precision.HIGHEST, preferred_element_type=jnp.float32)

def rms_scale(values, gain):
    inverse = lax.rsqrt(lax.optimization_barrier(jnp.mean(values * values, axis=-1, keepdims=True)) + norm_eps)
    return values * inverse * gain

def rotary(values, cosines, sines):
    half_width = values.shape[-1] // 2
    first_half = values[..., :half_width]
    second = values[..., half_width:]
    return jnp.concatenate([first_half * cosines - second * sines, second * cosines + first_half * sines], axis=-1)

def group_tables(segment_row):
    onehot = (segment_row[:, None] == jnp.arange(NCONT, dtype=jnp.int32)[None, :]).astype(jnp.int32)
    counts = lax.optimization_barrier(jnp.sum(onehot, axis=0)).astype(jnp.int32)
    starts = (jnp.cumsum(counts) - counts).astype(jnp.int32)
    seg_begin = lax.optimization_barrier(jnp.sum(onehot * starts[None, :], axis=1)).astype(jnp.int32)
    within = jnp.arange(CONT_TOK, dtype=jnp.int32) - seg_begin
    positions = jnp.concatenate([jnp.arange(PROMPT, dtype=jnp.int32), PROMPT + within])
    labels = jnp.concatenate([jnp.full((PROMPT,), -1, jnp.int32), segment_row.astype(jnp.int32)])
    frequency = rope_base ** (-(jnp.arange(HD // 2, dtype=jnp.float32) * 2.0 / HD))
    angles = positions.astype(jnp.float32)[:, None] * frequency[None, :]
    return (jnp.cos(angles), jnp.sin(angles), labels)

def block_slots(expert_row, order_row):
    same_expert = expert_row[:, None] == expert_row[None, :]
    earlier = order_row[None, :] < order_row[:, None]
    return lax.optimization_barrier(jnp.sum(jnp.logical_and(same_expert, earlier).astype(jnp.int32), axis=1)).astype(jnp.int32)

def attend_group(arguments):
    queries, key_rows, value_rows, labels = arguments
    repeat = HEADS // KVHEADS
    keys_all = jnp.repeat(key_rows, repeat, axis=1)
    values_all = jnp.repeat(value_rows, repeat, axis=1)
    scores = low_back(jnp.einsum('qhd,khd->hqk', queries, keys_all, precision=lax.Precision.HIGHEST) * HD ** (-0.5))
    query_pos = jnp.arange(GROUP_TOK, dtype=jnp.int32)[:, None]
    key_pos = jnp.arange(GROUP_TOK, dtype=jnp.int32)[None, :]
    allowed = jnp.logical_and(key_pos <= query_pos, jnp.logical_or(key_pos < PROMPT, labels[None, :] == labels[:, None]))
    scores = jnp.where(allowed[None], scores, masked_value)
    probabilities = low(jax.nn.softmax(scores, axis=-1))
    return jnp.einsum('hqk,khd->qhd', probabilities, values_all, precision=lax.Precision.HIGHEST)

def expert_block(arguments, w_gate, w_up, w_down):
    normed_rows, gate_rows, expert_rows, slot_rows = arguments
    pair_expert = expert_rows.reshape(-1)
    pair_slot = slot_rows.reshape(-1)
    total_slots = EXPERTS * CAP
    target = jnp.where(pair_slot < CAP, pair_expert * CAP + pair_slot, total_slots).astype(jnp.int32)
    pair_token = (jnp.arange(TOK_DEV * TOPK, dtype=jnp.int32) // TOPK).astype(jnp.int32)
    slot_token = jnp.zeros((total_slots + 1,), jnp.int32).at[target].set(pair_token)[:total_slots]
    slot_filled = jnp.zeros((total_slots + 1,), jnp.float32).at[target].set(1.0)[:total_slots]
    sent_rows = low_back(normed_rows[slot_token]) * slot_filled[:, None]
    buffer = sent_rows.reshape(EXPERTS, CAP, D)
    gate_val = low_back(jnp.einsum('ecd,edf->ecf', buffer, w_gate, precision=lax.Precision.HIGHEST))
    up_val = low_back(jnp.einsum('ecd,edf->ecf', buffer, w_up, precision=lax.Precision.HIGHEST))
    inner_act = low(jax.nn.gelu(gate_val, approximate=True) * up_val)
    expert_out = low(low_back(jnp.einsum('ecf,efd->ecd', inner_act, w_down, precision=lax.Precision.HIGHEST)))
    flat_out = jnp.concatenate([expert_out.reshape(total_slots, D), jnp.zeros((1, D), jnp.float32)], axis=0)
    pair_out = flat_out[target].reshape(TOK_DEV, TOPK, D)
    return lax.optimization_barrier(jnp.sum(gate_rows[:, :, None] * pair_out, axis=1))

def layer_forward(hidden, weights, cosines, sines, labels, expert_ids, slot_table):
    gain_attn, w_query, w_key, w_value, w_out, gain_ffn, w_router, w_gate, w_up, w_down = weights
    flat_rows = hidden.reshape(TOKENS, D)
    normed = low(rms_scale(flat_rows, gain_attn))
    query_raw = low_back(product(normed, w_query))
    key_raw = low_back(product(normed, w_key))
    value_raw = low_back(product(normed, w_value))
    queries = low(rotary(query_raw.reshape(GROUPS, GROUP_TOK, HEADS, HD), cosines, sines))
    key_rows = low(rotary(key_raw.reshape(GROUPS, GROUP_TOK, KVHEADS, HD), cosines, sines))
    value_rows = low(value_raw.reshape(GROUPS, GROUP_TOK, KVHEADS, HD))
    attended = lax.map(jax.checkpoint(attend_group), (queries, key_rows, value_rows, labels))
    attended = low(low_back(attended)).reshape(TOKENS, HEADS * HD)
    middle = flat_rows + low_back(product(attended, w_out))
    normed_ffn = low(rms_scale(middle, gain_ffn))
    logits = low_back(product(normed_ffn, w_router))
    chosen = jnp.take_along_axis(logits, expert_ids, axis=1)
    gate_weights = jax.nn.softmax(chosen, axis=-1)
    block_count = GROUPS * N_SEQ
    expert_step = jax.checkpoint(partial(expert_block, w_gate=w_gate, w_up=w_up, w_down=w_down))
    mixture = lax.map(expert_step, (normed_ffn.reshape(block_count, TOK_DEV, D), gate_weights.reshape(block_count, TOK_DEV, TOPK), expert_ids.reshape(block_count, TOK_DEV, TOPK), slot_table.reshape(block_count, TOK_DEV, TOPK)))
    return (middle + mixture.reshape(TOKENS, D)).reshape(GROUPS, GROUP_TOK, D)

def reference(tokens_in, cotangent, routes, order, segment_ids, gain_attn, w_query, w_key, w_value, w_out, gain_ffn, w_router, w_gate, w_up, w_down):
    cos_table, sin_table, labels = jax.vmap(group_tables)(segment_ids)
    cosines = cos_table[:, :, None, :]
    sines = sin_table[:, :, None, :]
    block_count = GROUPS * N_SEQ
    expert_ids = routes.reshape(LAYERS, TOKENS, TOPK).astype(jnp.int32)
    slot_table = jax.vmap(block_slots)(routes.reshape(LAYERS * block_count, TOK_DEV * TOPK), order.reshape(LAYERS * block_count, TOK_DEV * TOPK)).reshape(LAYERS, TOKENS, TOPK)
    weights = (gain_attn.astype(jnp.float32), w_query.astype(jnp.float32), w_key.astype(jnp.float32), w_value.astype(jnp.float32), w_out.astype(jnp.float32), gain_ffn.astype(jnp.float32), w_router.astype(jnp.float32), w_gate.astype(jnp.float32), w_up.astype(jnp.float32), w_down.astype(jnp.float32))
    inputs = tokens_in.astype(jnp.float32)

    def whole(inputs_arg, weights_arg):
        hidden = inputs_arg
        for layer_index in range(LAYERS):
            layer_weights = tuple((member[layer_index] for member in weights_arg))
            hidden = layer_forward(hidden, layer_weights, cosines, sines, labels, expert_ids[layer_index], slot_table[layer_index])
        return hidden
    final, pullback = jax.vjp(whole, inputs, weights)
    grad_inputs, grad_weights = pullback(cotangent.astype(jnp.float32))
    return (final.astype(jnp.bfloat16), grad_inputs, grad_weights[0], grad_weights[1], grad_weights[2], grad_weights[3], grad_weights[4], grad_weights[5], grad_weights[6], grad_weights[7], grad_weights[8], grad_weights[9])
```

```python
import functools

import jax
import jax.numpy as jnp
import numpy as np
from jax import lax
from jax.experimental import pallas as pl
from jax.experimental.pallas import tpu as pltpu
from jax.sharding import PartitionSpec as P

HEADS = 12
KVHEADS = 2
HD = 128
TOPK = 4
LAYERS = 2
NCONT = 4

norm_eps = 1e-06
rope_base = 10000.0
masked_value = -1e30

bf16 = jnp.bfloat16
f32 = jnp.float32
MIB = 1024 * 1024


def group_tables(segment_row, prompt_len):
    cont_len = segment_row.shape[0]
    onehot = (segment_row[:, None] == jnp.arange(NCONT, dtype=jnp.int32)[None, :]).astype(jnp.int32)
    counts = jnp.sum(onehot, axis=0)
    starts = jnp.cumsum(counts) - counts
    seg_begin = jnp.sum(onehot * starts[None, :], axis=1)
    within = jnp.arange(cont_len, dtype=jnp.int32) - seg_begin
    positions = jnp.concatenate([jnp.arange(prompt_len, dtype=jnp.int32), prompt_len + within])
    labels = jnp.concatenate([jnp.full((prompt_len,), -1, jnp.int32), segment_row])
    frequency = rope_base ** (-(jnp.arange(HD // 2, dtype=jnp.float32) * 2.0 / HD))
    angles = positions.astype(jnp.float32)[:, None] * frequency[None, :]
    return (jnp.cos(angles), jnp.sin(angles), labels)


def slot_table(expert_rows, order_rows, expert_count, capacity):
    pair_expert = expert_rows.reshape(-1)
    pair_order = order_rows.reshape(-1)
    same_expert = pair_expert[:, None] == pair_expert[None, :]
    earlier = pair_order[None, :] < pair_order[:, None]
    pair_slot = jnp.sum(jnp.logical_and(same_expert, earlier).astype(jnp.int32), axis=1)
    target = jnp.where(
        pair_slot < capacity, pair_expert * capacity + pair_slot, expert_count * capacity
    )
    return target.reshape(expert_rows.shape).T


def nn(left, right):
    return lax.dot_general(left, right, (((1,), (0,)), ((), ())), preferred_element_type=f32)


def nt(left, right):
    return lax.dot_general(left, right, (((1,), (1,)), ((), ())), preferred_element_type=f32)


def tn(left, right):
    return lax.dot_general(left, right, (((0,), (0,)), ((), ())), preferred_element_type=f32)


def split(value):
    high = value.astype(bf16)
    return high, (value - high.astype(f32)).astype(bf16)


def run(kernel, outs, *args, limit=48, flops=0, grid=None, in_specs=None, out_specs=None):
    moved = sum(int(np.prod(a.shape)) * a.dtype.itemsize for a in args)
    moved += sum(int(np.prod(o.shape)) * o.dtype.itemsize for o in outs)
    extra = {}
    if grid is not None:
        extra["grid"] = grid
    if in_specs is not None:
        extra["in_specs"] = in_specs
    if out_specs is not None:
        extra["out_specs"] = out_specs
    return pl.pallas_call(
        kernel,
        out_shape=list(outs),
        compiler_params=pltpu.CompilerParams(vmem_limit_bytes=limit * MIB),
        cost_estimate=pl.CostEstimate(flops=flops, bytes_accessed=moved, transcendentals=0),
        **extra,
    )(*args)


def shape(dims, dtype):
    return jax.ShapeDtypeStruct(dims, dtype)


def normalize(value, gain):
    inverse = lax.rsqrt(jnp.mean(value * value, axis=-1, keepdims=True) + norm_eps)
    return value * inverse * gain


def normalize_back(value, gain, grad):
    inverse = lax.rsqrt(jnp.mean(value * value, axis=-1, keepdims=True) + norm_eps)
    unit = value * inverse
    grad_gain = jnp.sum(grad * unit, axis=0, keepdims=True)
    scaled = grad * gain
    grad_value = inverse * (scaled - unit * jnp.mean(scaled * unit, axis=-1, keepdims=True))
    return grad_value, grad_gain


def turn(block, cosines, sines):
    return block * cosines + pltpu.roll(block, HD // 2, 1) * sines


def smooth_parts(value):
    root = np.float32(np.sqrt(2.0 / np.pi))
    square = value * value
    high = jnp.tanh(root * (value + 0.044715 * value * square))
    half = 0.5 * (1.0 + high)
    slope = half + 0.5 * value * (1.0 - high * high) * root * (1.0 + 3 * 0.044715 * square)
    return value * half, slope


def choose(target_t, slots):
    place = lax.broadcasted_iota(jnp.int32, (slots, target_t.shape[1]), 0)
    total = jnp.zeros(place.shape, f32)
    for k in range(TOPK):
        total = total + jnp.where(place == target_t[k : k + 1], 1.0, 0.0)
    return total


def choose_weighted(target_t, gates_t, slots):
    place = lax.broadcasted_iota(jnp.int32, (slots, target_t.shape[1]), 0)
    total = jnp.zeros(place.shape, f32)
    for k in range(TOPK):
        total = total + jnp.where(place == target_t[k : k + 1], gates_t[k : k + 1], 0.0)
    return total


def attention_input(hidden, small, spread, weight, cosines, sines, send_ref, normed_ref):
    expert_count = 8
    gain = small[expert_count : expert_count + 1].astype(f32)
    normed = normalize(hidden, gain).astype(bf16)
    normed = nn(normed, spread).astype(bf16)
    normed_ref[...] = normed
    raw = nn(normed, weight)
    seq_count = send_ref.shape[0]
    local = HEADS // seq_count
    for s in range(seq_count):
        pick = s * KVHEADS // seq_count
        for j in range(local):
            at = (s * local + j) * HD
            send_ref[s, :, j * HD : (j + 1) * HD] = turn(
                raw[:, at : at + HD], cosines, sines
            ).astype(bf16)
        at = (HEADS + pick) * HD
        send_ref[s, :, local * HD : (local + 1) * HD] = turn(
            raw[:, at : at + HD], cosines, sines
        ).astype(bf16)
        at = (HEADS + KVHEADS + pick) * HD
        send_ref[s, :, (local + 1) * HD :] = raw[:, at : at + HD].astype(bf16)


def first_input_kernel(tokens, small, spread, weight, cosines, sines, send_ref, normed_ref):
    hidden = tokens[...].astype(f32)
    qkv = weight[:, : (HEADS + 2 * KVHEADS) * HD]
    attention_input(
        hidden, small[...], spread[...], qkv, cosines[...], sines[...], send_ref, normed_ref
    )


def next_input_kernel(
    middle, combined, gates_t, target_t, small, spread, weight, cosines, sines,
    send_ref, normed_ref, hidden_ref,
):
    hidden = middle[...] + mix(combined[...], gates_t[...], target_t[...])
    hidden_ref[...] = hidden
    qkv = weight[:, : (HEADS + 2 * KVHEADS) * HD]
    attention_input(
        hidden, small[...], spread[...], qkv, cosines[...], sines[...], send_ref, normed_ref
    )


def mix(combined, gates_t, target_t):
    high, low = split(choose_weighted(target_t, gates_t, combined.shape[0]))
    return tn(high, combined) + tn(low, combined)


def result_kernel(middle, combined, gates_t, target_t, result_ref):
    mixture = mix(combined[...], gates_t[...], target_t[...])
    result_ref[...] = (middle[...] + mixture).astype(bf16)


def attention_kernel(heads_ref, bias_ref, out_ref):
    seq_count, tokens, columns = heads_ref.shape
    group = seq_count * tokens
    heads = heads_ref[...].reshape(group, columns)
    local = columns // HD - 2
    prompt = group // 2
    key = heads[:, local * HD : (local + 1) * HD]
    value = heads[:, (local + 1) * HD :]
    scale = HD ** (-0.5)
    for j in range(local):
        query = heads[:, j * HD : (j + 1) * HD]
        for rows, seen in ((slice(0, prompt), prompt), (slice(prompt, group), group)):
            scores = nt(query[rows], key[:seen]) * scale + bias_ref[rows, :seen]
            peak = jnp.max(scores, axis=-1, keepdims=True)
            weights = jnp.exp(scores - peak)
            weights = weights / jnp.sum(weights, axis=-1, keepdims=True)
            part = nn(weights.astype(bf16), value[:seen]).astype(bf16)
            first = rows.start // tokens
            out_ref[first : first + prompt // tokens, :, j * HD : (j + 1) * HD] = part.reshape(
                prompt // tokens, tokens, HD
            )


def after_attention_kernel(
    back, hidden, small, spread, out_w, routes_t, target_t,
    middle_ref, normed_ref, gates_ref, send_ref,
):
    expert_count = 8
    seq_count, tokens, part = back.shape
    width = seq_count * part
    attended = jnp.zeros((tokens, width), f32)
    for s in range(seq_count):
        attended = attended + nn(back[s], spread[s * part : (s + 1) * part])
    attended = attended.astype(bf16)
    rows = out_w.shape[1] // 2
    half = out_w.shape[2]
    for side in range(2):
        weight = out_w[:, side * rows : (side + 1) * rows].reshape(width, half)
        cols = slice(side * half, (side + 1) * half)
        middle_ref[:, cols] = hidden[:, cols].astype(f32) + nn(attended, weight)
    middle = middle_ref[...]
    gain = small[expert_count + 1 : expert_count + 2].astype(f32)
    normed = normalize(middle, gain).astype(bf16)
    normed_ref[...] = normed
    logits = nt(small[...], normed)
    chosen = []
    for k in range(TOPK):
        route = routes_t[k : k + 1]
        value = jnp.zeros((1, tokens), f32)
        for e in range(expert_count):
            value = value + jnp.where(route == e, logits[e : e + 1], 0.0)
        chosen.append(value)
    peak = functools.reduce(jnp.maximum, chosen)
    powers = [jnp.exp(value - peak) for value in chosen]
    total = functools.reduce(jnp.add, powers)
    for k in range(TOPK):
        gates_ref[k : k + 1] = powers[k] / total
    gates_ref[TOPK:] = jnp.zeros((gates_ref.shape[0] - TOPK, tokens), f32)
    send_ref[...] = nn(choose(target_t[...], send_ref.shape[0]).astype(bf16), normed).astype(bf16)


def flat_rows(block):
    sources, capacity, width = block.shape
    return block.astype(f32).reshape(sources * capacity, width).astype(bf16)


def down_parts(block):
    shards, rows, half = block.shape
    wide = block.astype(f32)
    left = wide[:, : rows // 2].reshape(shards * rows // 2, half).astype(bf16)
    right = wide[:, rows // 2 :].reshape(shards * rows // 2, half).astype(bf16)
    return left, right


def expert_kernel(rows_ref, weights_ref, out_ref, gate_ref, up_ref):
    shards, rows, half = weights_ref.shape
    rows = rows // 3
    width = shards * rows
    tokens = flat_rows(rows_ref[:, 0])
    gate_val = nn(tokens, weights_ref[:, :rows].reshape(width, half))
    up_val = nn(tokens, weights_ref[:, rows : 2 * rows].reshape(width, half))
    gate_ref[0] = gate_val
    up_ref[0] = up_val
    activated, slope = smooth_parts(gate_val)
    inner = (activated * up_val).astype(bf16)
    left, right = down_parts(weights_ref[:, 2 * rows :])
    sources, capacity = rows_ref.shape[0], rows_ref.shape[2]
    out_ref[:, 0, :, :half] = nn(inner, left).reshape(sources, capacity, half).astype(bf16)
    out_ref[:, 0, :, half:] = nn(inner, right).reshape(sources, capacity, half).astype(bf16)


def slot_grad_kernel(grad, combined, gates_t, routes_t, target_t, send_ref, logits_ref):
    tokens = grad.shape[0]
    slots = combined.shape[0]
    high, low = split(grad[...])
    weights_high, weights_low = split(choose_weighted(target_t[...], gates_t[...], slots))
    send = nn(weights_high, high) + (nn(weights_high, low) + nn(weights_low, high))
    send_ref[...] = send.astype(bf16)
    products = nt(combined[...], high) + nt(combined[...], low)
    place = lax.broadcasted_iota(jnp.int32, (slots, tokens), 0)
    grad_gates = [
        jnp.sum(jnp.where(place == target_t[k : k + 1], products, 0.0), axis=0, keepdims=True)
        for k in range(TOPK)
    ]
    gates = [gates_t[k : k + 1] for k in range(TOPK)]
    center = functools.reduce(jnp.add, [a * b for a, b in zip(gates, grad_gates)])
    label = lax.broadcasted_iota(jnp.int32, logits_ref.shape, 0)
    total = jnp.zeros(logits_ref.shape, f32)
    for k in range(TOPK):
        choice = gates[k] * (grad_gates[k] - center)
        total = total + jnp.where(label == routes_t[k : k + 1], choice, 0.0)
    logits_ref[...] = total.astype(bf16)


def expert_back_kernel(
    grad_ref, weights_ref, gate_ref, up_ref, out_ref, gate_grad_ref, up_grad_ref, inner_ref
):
    shards, rows, half = weights_ref.shape
    rows = rows // 3
    width = shards * rows
    sources, capacity = grad_ref.shape[0], grad_ref.shape[2]
    grad = flat_rows(grad_ref[:, 0])
    left, right = down_parts(weights_ref[:, 2 * rows :])
    grad_inner = nt(grad[:, :half], left) + nt(grad[:, half:], right)
    up_val = up_ref[0]
    activated, slope = smooth_parts(gate_ref[0])
    inner_ref[0] = (activated * up_val).astype(bf16)
    grad_gate = (grad_inner * up_val * slope).astype(bf16)
    grad_up = (grad_inner * activated).astype(bf16)
    gate_grad_ref[0] = grad_gate
    up_grad_ref[0] = grad_up
    total = nt(grad_gate, weights_ref[:, :rows].reshape(width, half))
    total = total + nt(grad_up, weights_ref[:, rows : 2 * rows].reshape(width, half))
    out_ref[:, 0] = total.reshape(sources, capacity, width).astype(bf16)


def expert_weight_kernel(
    rows_ref, grad_ref, gate_grad_ref, up_grad_ref, inner_ref, *rest, experts
):
    pack_ref = rest[-1]
    shards, rows, half = pack_ref.shape
    rows = rows // 3

    @pl.when(pl.program_id(0) < experts)
    def _():
        tokens = flat_rows(rows_ref[:, 0])
        grad = flat_rows(grad_ref[:, 0])
        pack_ref[:, :rows] = tn(tokens, gate_grad_ref[0]).astype(bf16).reshape(shards, rows, half)
        pack_ref[:, rows : 2 * rows] = (
            tn(tokens, up_grad_ref[0]).astype(bf16).reshape(shards, rows, half)
        )
        left = tn(inner_ref[0], grad[:, :half]).reshape(shards, rows // 2, half)
        right = tn(inner_ref[0], grad[:, half:]).reshape(shards, rows // 2, half)
        pack_ref[:, 2 * rows :] = jnp.concatenate([left, right], axis=1).astype(bf16)

    if len(rest) > 1:
        qkv_ref, out_ref = rest[:2]
        cut = qkv_ref.shape[1]

        @pl.when(pl.program_id(0) == experts)
        def _():
            pack_ref[:, :cut] = qkv_ref[...]
            pack_ref[:, cut : cut + out_ref.shape[1]] = out_ref[...]


def after_experts_kernel(
    grad, sent, middle, normed, logits_grad, target_t, small, spread, out_w,
    grad_ref, branch_ref, send_ref, small_ref,
):
    expert_count = 8
    seq_count, tokens, part = send_ref.shape
    width = seq_count * part
    chosen = choose(target_t[...], sent.shape[0]).astype(bf16)
    grad_normed = tn(chosen, sent[...]) + tn(logits_grad[...], small[...])
    router = nn(logits_grad[...], normed[...])
    gain = small[expert_count + 1 : expert_count + 2].astype(f32)
    grad_value, grad_gain = normalize_back(middle[...], gain, grad_normed)
    label = lax.broadcasted_iota(jnp.int32, small_ref.shape, 0)
    small_ref[...] = jnp.where(label == expert_count + 1, grad_gain, router)
    grad_middle = grad[...] + grad_value
    grad_ref[...] = grad_middle
    branch = grad_middle.astype(bf16)
    branch_ref[...] = branch
    rows = out_w.shape[1] // 2
    half = out_w.shape[2]
    parts = [
        nt(branch[:, :half], out_w[:, :rows].reshape(width, half)),
        nt(branch[:, half:], out_w[:, rows:].reshape(width, half)),
    ]
    attended = (parts[0] + parts[1]).astype(bf16)
    for s in range(seq_count):
        send_ref[s] = nt(attended, spread[s * part : (s + 1) * part]).astype(bf16)


def attention_back_kernel(heads_ref, grad_ref, bias_ref, cosines, sines, out_ref):
    seq_count, tokens, columns = heads_ref.shape
    group = seq_count * tokens
    heads = heads_ref[...].reshape(group, columns)
    grads = grad_ref[...].reshape(group, grad_ref.shape[2])
    local = columns // HD - 2
    prompt = group // 2
    key = heads[:, local * HD : (local + 1) * HD]
    value = heads[:, (local + 1) * HD :]
    scale = HD ** (-0.5)

    def keep(at, block):
        out_ref[:, :, at * HD : (at + 1) * HD] = block.astype(bf16).reshape(seq_count, tokens, HD)

    def unturn(block):
        return block * cosines[...] - pltpu.roll(block, HD // 2, 1) * sines[...]

    grad_key = [jnp.zeros((prompt, HD), f32), jnp.zeros((prompt, HD), f32)]
    grad_value = [jnp.zeros((prompt, HD), f32), jnp.zeros((prompt, HD), f32)]
    for j in range(local):
        query = heads[:, j * HD : (j + 1) * HD]
        grad = grads[:, j * HD : (j + 1) * HD]
        grad_query = []
        for rows, seen in ((slice(0, prompt), prompt), (slice(prompt, group), group)):
            scores = nt(query[rows], key[:seen]) * scale + bias_ref[rows, :seen]
            peak = jnp.max(scores, axis=-1, keepdims=True)
            weights = jnp.exp(scores - peak)
            weights = weights / jnp.sum(weights, axis=-1, keepdims=True)
            grad_weights = nt(grad[rows], value[:seen])
            center = jnp.sum(weights * grad_weights, axis=-1, keepdims=True)
            grad_scores = (weights * (grad_weights - center)).astype(bf16)
            low = weights.astype(bf16)
            grad_query.append(nn(grad_scores, key[:seen]) * scale)
            for side in range(seen // prompt):
                cols = slice(side * prompt, (side + 1) * prompt)
                grad_key[side] = grad_key[side] + tn(grad_scores[:, cols], query[rows])
                grad_value[side] = grad_value[side] + tn(low[:, cols], grad[rows])
        keep(j, unturn(jnp.concatenate(grad_query, axis=0)))
    keep(local, unturn(jnp.concatenate(grad_key, axis=0) * scale))
    keep(local + 1, jnp.concatenate(grad_value, axis=0))


def before_attention_kernel(
    grad_middle, sent, hidden, small, spread, weight, small_grad, out_ref, small_ref
):
    expert_count = 8
    seq_count, tokens, columns = sent.shape
    local = columns // HD - 2
    share = seq_count // KVHEADS
    blocks = [sent[s, :, : local * HD] for s in range(seq_count)]
    for at in (local, local + 1):
        for c in range(KVHEADS):
            total = jnp.zeros((tokens, HD), f32)
            for s in range(c * share, (c + 1) * share):
                total = total + sent[s, :, at * HD : (at + 1) * HD].astype(f32)
            blocks.append(total.astype(bf16))
    raw = jnp.concatenate(blocks, axis=1)
    high, low = split(nt(raw, weight[:, : raw.shape[1]]))
    grad_normed = nt(high, spread[...]) + nt(low, spread[...])
    gain = small[expert_count : expert_count + 1].astype(f32)
    grad_value, grad_gain = normalize_back(hidden[...].astype(f32), gain, grad_normed)
    out_ref[...] = grad_middle[...] + grad_value
    label = lax.broadcasted_iota(jnp.int32, small_ref.shape, 0)
    small_ref[...] = jnp.where(label == expert_count, grad_gain, small_grad[...])


def qkv_weight_kernel(place, own, one, two, three, grads, small, spread, out_ref):
    me = place[0]
    seq_count, tokens, columns = grads.shape
    shards, rows, wide = out_ref.shape
    inputs = jnp.concatenate([own[...], one[...], two[...], three[...]], axis=0)
    grad = jnp.concatenate([grads[lax.rem(me + k, seq_count)] for k in range(seq_count)], axis=0)
    total = tn(inputs, grad)
    out_ref[:, :, :columns] = total.astype(bf16).reshape(shards, rows, columns)
    extra = small[...].astype(bf16)
    extra = jnp.concatenate([extra, jnp.zeros((HD - extra.shape[0], extra.shape[1]), bf16)], axis=0)
    extra = nn(extra, spread[...]).T
    out_ref[:, :, columns:] = extra.astype(bf16).reshape(shards, rows, wide - columns)


def out_weight_kernel(place, own, one, two, three, attended, out_ref):
    me = place[0]
    seq_count, tokens, part = attended.shape
    shards, rows, half = out_ref.shape
    rows = rows // 2
    valid = part // shards
    branch = jnp.concatenate([own[...], one[...], two[...], three[...]], axis=0)
    heads = jnp.concatenate([attended[lax.rem(me + k, seq_count)] for k in range(seq_count)], axis=0)
    place_in = lax.broadcasted_iota(jnp.int32, (part, shards * rows), 0)
    place_out = lax.broadcasted_iota(jnp.int32, (part, shards * rows), 1)
    source = place_out // rows * valid + place_out % rows
    same = jnp.logical_and(place_in == source, place_out % rows < valid)
    heads = nn(heads, jnp.where(same, 1.0, 0.0).astype(bf16)).astype(bf16)
    for side in range(2):
        total = tn(heads, branch[:, side * half : (side + 1) * half])
        out_ref[:, side * rows : (side + 1) * rows] = total.astype(bf16).reshape(shards, rows, half)


def gather_seq(block):
    return lax.all_gather(block, "seq", axis=0, tiled=False)


def swap_seq(block):
    return lax.all_to_all(block, "seq", split_axis=0, concat_axis=0, tiled=True)


def around_seq(block):
    count = lax.axis_size("seq")
    others = [
        lax.ppermute(block, "seq", [((i + k) % count, i) for i in range(count)])
        for k in range(1, count)
    ]
    return [block] + others


def halves(block):
    cut = block.shape[-1] // 2
    return jnp.concatenate([block[..., :cut], block[..., cut:]], axis=-2)


def per_device(
    tokens_in,
    cotangent,
    routes,
    order,
    segment_ids,
    gain_attn,
    w_query,
    w_key,
    w_value,
    w_out,
    gain_ffn,
    w_router,
    w_gate,
    w_up,
    w_down,
):
    tok_count = tokens_in.shape[1]
    width = tokens_in.shape[2]
    seq_count = lax.axis_size("seq")
    shard_count = lax.axis_size("fsdp")
    seq_index = lax.axis_index("seq")
    place = jnp.full((1,), seq_index, jnp.int32)
    group_tok = seq_count * tok_count
    prompt_len = group_tok - segment_ids.shape[1]
    local_experts = w_gate.shape[1]
    expert_count = local_experts * seq_count
    capacity = 9 * tok_count * TOPK // (8 * expert_count)
    total_slots = expert_count * capacity
    head_local = HEADS // seq_count
    local_width = head_local * HD
    dense_rows = w_query.shape[1]
    shard_rows = dense_rows * seq_count
    gate_rows = w_gate.shape[2]
    down_rows = w_down.shape[2]
    expert_rows = 2 * gate_rows + 2 * down_rows
    qkv_width = (HEADS + 2 * KVHEADS) * HD
    half_width = width // 2
    inner_width = w_gate.shape[3]
    slot_rows = seq_count * capacity

    cos_half, sin_half, labels = group_tables(segment_ids[0], prompt_len)
    cos_all = jnp.concatenate([cos_half, cos_half], axis=1)
    sin_all = jnp.concatenate([-sin_half, sin_half], axis=1)
    cos_own = lax.dynamic_slice_in_dim(cos_all, seq_index * tok_count, tok_count, 0)
    sin_own = lax.dynamic_slice_in_dim(sin_all, seq_index * tok_count, tok_count, 0)
    key_pos = jnp.arange(group_tok, dtype=jnp.int32)
    allowed = jnp.logical_and(
        key_pos[None, :] <= key_pos[:, None],
        jnp.logical_or(key_pos[None, :] < prompt_len, labels[None, :] == labels[:, None]),
    )
    bias = jnp.where(allowed, 0.0, masked_value)

    column = jnp.arange(width, dtype=jnp.int32)
    natural = (
        column % shard_rows // dense_rows * (width // seq_count)
        + column // shard_rows * dense_rows
        + column % dense_rows
    )
    spread = (column[:, None] == natural[None, :]).astype(bf16)

    def fetch(layer):
        extras = jnp.concatenate(
            [
                w_router[layer],
                gain_attn[layer][:, None],
                gain_ffn[layer][:, None],
                jnp.zeros((dense_rows, HD - 2 - expert_count), bf16),
            ],
            axis=1,
        )
        dense = jnp.concatenate(
            [w_query[layer], w_key[layer], w_value[layer], extras, w_out[layer]], axis=1
        )
        dense = gather_seq(dense).reshape(shard_rows, dense.shape[1])
        qkv = lax.all_gather(dense[:, : qkv_width + HD], "fsdp", axis=0, tiled=True)
        pack = [
            part
            for e in range(local_experts)
            for part in (w_gate[layer, e], w_up[layer, e], halves(w_down[layer, e]))
        ]
        pack = jnp.concatenate(pack + [halves(dense[:, qkv_width + HD :])], axis=0)
        pack = lax.all_gather(pack, "fsdp", axis=0, tiled=False)
        small = lax.dot_general(
            qkv[:, qkv_width : qkv_width + 16],
            spread,
            (((0,), (1,)), ((), ())),
            preferred_element_type=f32,
        ).astype(bf16)
        return qkv, pack, small

    whole = pl.BlockSpec(memory_space=pltpu.VMEM)
    slots_spec = pl.BlockSpec(
        (seq_count, 1, capacity, width), lambda e: (0, jnp.minimum(e, local_experts - 1), 0, 0)
    )
    weights_spec = pl.BlockSpec(
        (shard_count, expert_rows, half_width), lambda e: (0, jnp.minimum(e, local_experts - 1), 0)
    )
    inner_spec = pl.BlockSpec(
        (1, slot_rows, inner_width), lambda e: (jnp.minimum(e, local_experts - 1), 0, 0)
    )
    out_block = 2 * shard_rows
    out_at = local_experts * expert_rows // out_block
    out_w_spec = pl.BlockSpec((shard_count, out_block, half_width), lambda i: (0, out_at, 0))

    def fixed(array):
        return pl.BlockSpec(array.shape, lambda i: (0,) * array.ndim)

    def once(kernel, outs, *args, weight=None, **kw):
        specs = [out_w_spec if n == weight else fixed(a) for n, a in enumerate(args)]
        return run(
            kernel, outs, *args, grid=(1,), in_specs=specs, out_specs=[fixed(o) for o in outs], **kw
        )

    slots_shape = shape((seq_count, local_experts, capacity, width), bf16)
    inner_shape = (local_experts, slot_rows, inner_width)
    expert_flops = 6 * total_slots * width * inner_width
    dense_flops = 2 * tok_count * width * width
    records = []
    hidden = tokens_in[0]
    for layer in range(LAYERS):
        qkv_w, pack, small = fetch(layer)
        routes_t = routes[layer, 0].T
        target_t = slot_table(routes[layer, 0], order[layer, 0], expert_count, capacity)
        send_shape = shape((seq_count, tok_count, local_width + 2 * HD), bf16)
        normed_shape = shape((tok_count, width), bf16)
        if layer == 0:
            send, normed_p = once(
                first_input_kernel, [send_shape, normed_shape],
                hidden, small, spread, qkv_w, cos_own, sin_own, flops=3 * dense_flops,
            )
        else:
            send, normed_p, hidden = once(
                next_input_kernel, [send_shape, normed_shape, shape((tok_count, width), f32)],
                middle, combined, gates_t, above_target, small, spread, qkv_w, cos_own, sin_own,
                flops=4 * dense_flops,
            )
        heads = swap_seq(send)
        normed_all = around_seq(normed_p)
        (attended,) = once(
            attention_kernel, [shape((seq_count, tok_count, local_width), bf16)], heads, bias,
            flops=4 * head_local * group_tok * group_tok * HD,
        )
        back = swap_seq(attended)
        middle, normed_ffn, gates_t, send_rows = once(
            after_attention_kernel,
            [
                shape((tok_count, width), f32),
                shape((tok_count, width), bf16),
                shape((2 * TOPK, tok_count), f32),
                shape((total_slots, width), bf16),
            ],
            back, hidden, small, spread, pack, routes_t, target_t, weight=4, flops=3 * dense_flops,
        )
        received = swap_seq(send_rows.reshape(slots_shape.shape))
        expert_out, gate_val, up_val = run(
            expert_kernel,
            [slots_shape, shape(inner_shape, f32), shape(inner_shape, f32)],
            received, pack,
            grid=(local_experts,),
            in_specs=[slots_spec, weights_spec],
            out_specs=[slots_spec, inner_spec, inner_spec],
            flops=expert_flops,
        )
        combined = swap_seq(expert_out).reshape(total_slots, width)
        above_target = target_t
        records.append(
            (
                (qkv_w, pack, small, routes_t, target_t),
                (hidden, normed_all, heads, attended),
                (middle, normed_ffn, gates_t, combined),
                (received, gate_val, up_val),
            )
        )
    (result,) = once(
        result_kernel, [shape((tok_count, width), bf16)], middle, combined, gates_t, target_t,
        flops=dense_flops,
    )

    def scatter(block):
        return lax.psum_scatter(block, "fsdp", scatter_dimension=0, tiled=False)

    def expert_unpack(block):
        block = block[: local_experts * expert_rows].astype(f32)
        block = block.reshape(local_experts, expert_rows, half_width)
        down = block[:, 2 * gate_rows :].reshape(local_experts, 2, down_rows, half_width)
        return (
            block[:, :gate_rows],
            block[:, gate_rows : 2 * gate_rows],
            down.transpose(0, 2, 1, 3).reshape(local_experts, down_rows, width),
        )

    def qkv_unpack(block):
        part = swap_seq(block.reshape(seq_count, dense_rows, local_width + 3 * HD)).astype(f32)
        query = part[:, :, :local_width].transpose(1, 0, 2).reshape(dense_rows, HEADS * HD)

        def pairs(block):
            block = block.reshape(KVHEADS, seq_count // KVHEADS, dense_rows, HD)
            return jnp.sum(block, axis=1).transpose(1, 0, 2).reshape(dense_rows, KVHEADS * HD)

        key = pairs(part[:, :, local_width : local_width + HD])
        value = pairs(part[:, :, local_width + HD : local_width + 2 * HD])
        extra = jnp.sum(part[:, :, local_width + 2 * HD :], axis=0)
        router = extra[:, :expert_count]
        return query, key, value, extra[:, expert_count], extra[:, expert_count + 1], router

    out_rows = 16

    def out_unpack(block):
        block = block.astype(f32)
        return jnp.concatenate(
            [block[:dense_rows], block[out_rows : out_rows + dense_rows]], axis=1
        )

    grad_hidden = cotangent[0].astype(f32)
    grads = [None] * LAYERS
    waiting = None
    for layer in range(LAYERS - 1, -1, -1):
        weights, attn_saved, mid_saved, expert_saved = records[layer]
        qkv_w, pack, small, routes_t, target_t = weights
        below, normed_all, heads, attended = attn_saved
        middle, normed_ffn, gates_t, combined = mid_saved
        received, gate_val, up_val = expert_saved
        grad_slots, logits_grad = once(
            slot_grad_kernel,
            [shape((total_slots, width), bf16), shape((2 * expert_count, tok_count), bf16)],
            grad_hidden, combined, gates_t, routes_t, target_t, flops=3 * dense_flops,
        )
        grad_expert = swap_seq(grad_slots.reshape(slots_shape.shape))
        grad_rows, gate_grad, up_grad, inner = run(
            expert_back_kernel,
            [slots_shape] + [shape(inner_shape, bf16)] * 3,
            grad_expert, pack, gate_val, up_val,
            grid=(local_experts,),
            in_specs=[slots_spec, weights_spec, inner_spec, inner_spec],
            out_specs=[slots_spec] + [inner_spec] * 3,
            flops=expert_flops,
        )
        sent = swap_seq(grad_rows)
        extra = () if layer == LAYERS - 1 else waiting
        extra_rows = sum(a.shape[1] for a in extra)
        (packed,) = run(
            functools.partial(expert_weight_kernel, experts=local_experts),
            [shape((shard_count, local_experts * expert_rows + extra_rows, half_width), bf16)],
            received, grad_expert, gate_grad, up_grad, inner, *extra,
            grid=(local_experts + (1 if extra else 0),),
            in_specs=[slots_spec, slots_spec] + [inner_spec] * 3 + [fixed(a) for a in extra],
            out_specs=[
                pl.BlockSpec((shard_count, expert_rows, half_width), lambda e: (0, e, 0))
            ],
            flops=expert_flops,
        )
        sent, packed = lax.optimization_barrier((sent, packed))
        summed = scatter(packed)
        if extra:
            above_block = summed[local_experts * expert_rows :]
        grad_middle, branch, send, small_grad = once(
            after_experts_kernel,
            [
                shape((tok_count, width), f32),
                shape((tok_count, width), bf16),
                shape((seq_count, tok_count, local_width), bf16),
                shape((2 * expert_count, width), f32),
            ],
            grad_hidden, sent.reshape(total_slots, width), middle, normed_ffn, logits_grad,
            target_t, small, spread, pack, weight=8, flops=4 * dense_flops,
        )
        grad_heads = swap_seq(send)
        branch_all = around_seq(branch)
        (grad_own,) = once(
            attention_back_kernel,
            [shape((seq_count, tok_count, local_width + 2 * HD), bf16)],
            heads, grad_heads, bias, cos_all, sin_all,
            flops=10 * head_local * group_tok * group_tok * HD,
        )
        sent = swap_seq(grad_own)
        (out_block_grad,) = run(
            out_weight_kernel,
            [shape((shard_count, 2 * out_rows, half_width), bf16)],
            place, *branch_all, attended,
            in_specs=[pl.BlockSpec(memory_space=pltpu.SMEM)] + [whole] * 5,
            out_specs=[whole],
            flops=dense_flops,
        )
        grad_hidden, small_grad = once(
            before_attention_kernel,
            [shape((tok_count, width), f32), shape((2 * expert_count, width), f32)],
            grad_middle, sent, below, small, spread, qkv_w, small_grad, flops=4 * dense_flops,
        )
        (qkv_block_grad,) = run(
            qkv_weight_kernel,
            [shape((shard_count, shard_rows, half_width), bf16)],
            place, *normed_all, grad_own, small_grad, spread,
            in_specs=[pl.BlockSpec(memory_space=pltpu.SMEM)] + [whole] * 7,
            out_specs=[whole],
            flops=2 * dense_flops,
        )
        expert_grads = expert_unpack(summed)
        if layer > 0:
            waiting = (qkv_block_grad, out_block_grad)
        else:

            def shard_sum(block):
                block = lax.all_to_all(block, "fsdp", split_axis=0, concat_axis=0, tiled=True)
                return jnp.sum(block.astype(f32), axis=0)

            own_out = out_unpack(shard_sum(out_block_grad))
            own_qkv = qkv_unpack(shard_sum(qkv_block_grad))
            above_qkv = qkv_unpack(above_block[:shard_rows])
            above_out = out_unpack(above_block[shard_rows:])
        grads[layer] = expert_grads

    def both(first, second):
        return jnp.stack([first, second])

    return (
        result[None],
        grad_hidden[None],
        both(own_qkv[3], above_qkv[3]),
        both(own_qkv[0], above_qkv[0]),
        both(own_qkv[1], above_qkv[1]),
        both(own_qkv[2], above_qkv[2]),
        both(own_out, above_out),
        both(own_qkv[4], above_qkv[4]),
        both(own_qkv[5], above_qkv[5]),
        both(grads[0][0], grads[1][0]),
        both(grads[0][1], grads[1][1]),
        both(grads[0][2], grads[1][2]),
    )


def solution(mesh):
    in_specs = (
        P("fsdp", "seq", None),
        P("fsdp", "seq", None),
        P(None, "fsdp", "seq", None),
        P(None, "fsdp", "seq", None),
        P("fsdp", None),
        P(None, ("seq", "fsdp")),
        P(None, ("seq", "fsdp"), None),
        P(None, ("seq", "fsdp"), None),
        P(None, ("seq", "fsdp"), None),
        P(None, ("seq", "fsdp"), None),
        P(None, ("seq", "fsdp")),
        P(None, ("seq", "fsdp"), None),
        P(None, "seq", "fsdp", None),
        P(None, "seq", "fsdp", None),
        P(None, "seq", "fsdp", None),
    )
    out_specs = (
        P("fsdp", "seq", None),
        P("fsdp", "seq", None),
        P(None, ("seq", "fsdp")),
        P(None, ("seq", "fsdp"), None),
        P(None, ("seq", "fsdp"), None),
        P(None, ("seq", "fsdp"), None),
        P(None, ("seq", "fsdp"), None),
        P(None, ("seq", "fsdp")),
        P(None, ("seq", "fsdp"), None),
        P(None, "seq", "fsdp", None),
        P(None, "seq", "fsdp", None),
        P(None, "seq", "fsdp", None),
    )
    return jax.shard_map(
        per_device, mesh=mesh, in_specs=in_specs, out_specs=out_specs, check_vma=False
    )
```

```python
import functools

import jax
import jax.numpy as jnp
import numpy as np
from jax import lax
from jax.experimental import pallas as pl
from jax.experimental.pallas import tpu as pltpu
from jax.sharding import PartitionSpec as P

HEADS = 12
KVHEADS = 2
HD = 128
TOPK = 4
LAYERS = 2
NCONT = 4

norm_eps = 1e-06
rope_base = 10000.0
masked_value = -1e30

bf16 = jnp.bfloat16
f32 = jnp.float32
VMEM_BYTES = 64 * 1024 * 1024 - 256 * 1024


def group_tables(segment_row, prompt_len):
    cont_len = segment_row.shape[0]
    onehot = (segment_row[:, None] == jnp.arange(NCONT, dtype=jnp.int32)[None, :]).astype(jnp.int32)
    counts = jnp.sum(onehot, axis=0)
    starts = jnp.cumsum(counts) - counts
    seg_begin = jnp.sum(onehot * starts[None, :], axis=1)
    within = jnp.arange(cont_len, dtype=jnp.int32) - seg_begin
    positions = jnp.concatenate([jnp.arange(prompt_len, dtype=jnp.int32), prompt_len + within])
    labels = jnp.concatenate([jnp.full((prompt_len,), -1, jnp.int32), segment_row])
    frequency = rope_base ** (-(jnp.arange(HD // 2, dtype=jnp.float32) * 2.0 / HD))
    angles = positions.astype(jnp.float32)[:, None] * frequency[None, :]
    return (jnp.cos(angles), jnp.sin(angles), labels)


def slot_table(expert_rows, order_rows, expert_count, capacity):
    pair_expert = expert_rows.reshape(-1)
    pair_order = order_rows.reshape(-1)
    same_expert = pair_expert[:, None] == pair_expert[None, :]
    earlier = pair_order[None, :] < pair_order[:, None]
    pair_slot = jnp.sum(jnp.logical_and(same_expert, earlier).astype(jnp.int32), axis=1)
    target = jnp.where(
        pair_slot < capacity, pair_expert * capacity + pair_slot, expert_count * capacity
    )
    return target.reshape(expert_rows.shape).T


def nn(left, right):
    return lax.dot_general(left, right, (((1,), (0,)), ((), ())), preferred_element_type=f32)


def nt(left, right):
    return lax.dot_general(left, right, (((1,), (1,)), ((), ())), preferred_element_type=f32)


def tn(left, right):
    return lax.dot_general(left, right, (((0,), (0,)), ((), ())), preferred_element_type=f32)


def split(value):
    high = value.astype(bf16)
    return high, (value - high.astype(f32)).astype(bf16)


class Late:
    def __init__(self, ref, copy):
        self.ref, self.copy, self.shape = ref, copy, ref.shape
        copy.start()

    def wait(self):
        if self.copy is not None:
            self.copy.wait()
            self.copy = None

    def __getitem__(self, index):
        self.wait()
        return self.ref[index]


class Out:
    def __init__(self, ref, copies):
        self.ref, self.copies, self.shape = ref, copies, ref.shape
        self.sent = [False] * len(copies)

    def send(self, piece=None):
        for n in range(len(self.copies)) if piece is None else (piece,):
            if not self.sent[n]:
                self.copies[n].start()
                self.sent[n] = True

    def __getitem__(self, index):
        return self.ref[index]

    def __setitem__(self, index, value):
        self.ref[index] = value


def cost(args, outs, flops):
    moved = sum(int(np.prod(a.shape)) * a.dtype.itemsize for a in (*args, *outs))
    return pl.CostEstimate(flops=flops, bytes_accessed=moved, transcendentals=0)


def once(kernel, outs, *args, scalar=False, cut=None, pieces=None, flops=0):
    cut, pieces = cut or {}, pieces or {}
    hbm = pl.BlockSpec(memory_space=pltpu.HBM)
    late = [n for n in range(len(args)) if not (scalar and n == 0)]
    specs = [hbm] * len(args)
    if scalar:
        specs[0] = pl.BlockSpec(memory_space=pltpu.SMEM)
    scratch = []
    for n in late:
        dims = list(args[n].shape)
        for dim, start, size in cut.get(n, ()):
            dims[dim] = size
        scratch.append(pltpu.VMEM(tuple(dims), args[n].dtype))
    scratch += [pltpu.VMEM(o.shape, o.dtype) for o in outs]
    parts = [pieces.get(n, (0, 1)) for n in range(len(outs))]
    scratch.append(pltpu.SemaphoreType.DMA((len(late) + sum(count for _, count in parts),)))

    def body(*refs):
        ins = list(refs[: len(args)])
        out_refs = refs[len(args) : len(args) + len(outs)]
        rooms = refs[len(args) + len(outs) : -1]
        sems = refs[-1]
        for i, n in enumerate(late):
            source = ins[n]
            for dim, start, size in cut.get(n, ()):
                if callable(start):
                    start = pl.multiple_of(start(ins[0][0]), 16 if dim == 1 else HD)
                source = source.at[(slice(None),) * dim + (pl.ds(start, size),)]
            ins[n] = Late(rooms[i], pltpu.make_async_copy(source, rooms[i], sems.at[i]))
        results = []
        used = len(late)
        for i, out in enumerate(out_refs):
            room = rooms[len(late) + i]
            dim, count = parts[i]
            size = room.shape[dim] // count
            copies = []
            for n in range(count):
                at = (slice(None),) * dim + (pl.ds(n * size, size),)
                copies.append(pltpu.make_async_copy(room.at[at], out.at[at], sems.at[used]))
                used += 1
            results.append(Out(room, copies))
        kernel(*ins, *results)
        for result in results:
            result.send()
        for n in late:
            ins[n].wait()
        for result in results:
            for copy in result.copies:
                copy.wait()

    return pl.pallas_call(
        body,
        out_shape=list(outs),
        in_specs=specs,
        out_specs=[hbm] * len(outs),
        scratch_shapes=scratch,
        compiler_params=pltpu.CompilerParams(vmem_limit_bytes=VMEM_BYTES),
        cost_estimate=cost(args, outs, flops),
    )(*args)


def shape(dims, dtype):
    return jax.ShapeDtypeStruct(dims, dtype)


def normalize(value, gain):
    inverse = lax.rsqrt(jnp.mean(value * value, axis=-1, keepdims=True) + norm_eps)
    return value * inverse * gain


def normalize_back(value, gain, grad):
    inverse = lax.rsqrt(jnp.mean(value * value, axis=-1, keepdims=True) + norm_eps)
    unit = value * inverse
    grad_gain = jnp.sum(grad * unit, axis=0, keepdims=True)
    scaled = grad * gain
    grad_value = inverse * (scaled - unit * jnp.mean(scaled * unit, axis=-1, keepdims=True))
    return grad_value, grad_gain


def to_gathered(parts, order):
    count = len(parts)
    share = parts[0].shape[1] // count
    done = []
    for j in range(count):
        piece = jnp.concatenate([part[:, j * share : (j + 1) * share] for part in parts], axis=1)
        done.append(nn(piece, order))
    return jnp.concatenate(done, axis=1)


def to_natural(value, order):
    count = value.shape[1] // order.shape[0]
    size = order.shape[0]
    share = size // count
    done = [nt(value[:, j * size : (j + 1) * size], order) for j in range(count)]
    return [
        jnp.concatenate([part[:, s * share : (s + 1) * share] for part in done], axis=1)
        for s in range(count)
    ]


def column_blocks(value, count):
    size = value.shape[1] // count
    return [value[:, s * size : (s + 1) * size] for s in range(count)]


def turn(block, cosines, sines):
    return block * cosines + pltpu.roll(block, HD // 2, 1) * sines


def smooth_parts(value):
    root = np.float32(np.sqrt(2.0 / np.pi))
    square = value * value
    high = jnp.tanh(root * (value + 0.044715 * value * square))
    half = 0.5 * (1.0 + high)
    slope = half + 0.5 * value * (1.0 - high * high) * root * (1.0 + 3 * 0.044715 * square)
    return value * half, slope


def choose(target_t, slots):
    place = lax.broadcasted_iota(jnp.int32, (slots, target_t.shape[1]), 0)
    total = jnp.zeros(place.shape, f32)
    for k in range(TOPK):
        total = total + jnp.where(place == target_t[k : k + 1], 1.0, 0.0)
    return total


def choose_weighted(target_t, gates_t, slots):
    place = lax.broadcasted_iota(jnp.int32, (slots, target_t.shape[1]), 0)
    total = jnp.zeros(place.shape, f32)
    for k in range(TOPK):
        total = total + jnp.where(place == target_t[k : k + 1], gates_t[k : k + 1], 0.0)
    return total


def input_kernel(
    middle, combined, gates_t, target_t, small, spread, normed_ref, hidden_ref
):
    expert_count = 8
    hidden = middle[...] + mix(combined[...], gates_t[...], target_t[...])
    hidden_ref[...] = hidden
    hidden_ref.send()
    gain = small[expert_count : expert_count + 1].astype(f32)
    normed = normalize(hidden, gain).astype(bf16)
    count = normed.shape[1] // spread.shape[0]
    normed_ref[...] = to_gathered(column_blocks(normed, count), spread[...]).astype(bf16)


def mix(combined, gates_t, target_t):
    high, low = split(choose_weighted(target_t, gates_t, combined.shape[0]))
    tokens = high.shape[1]
    both = tn(jnp.concatenate([high, low], axis=1), combined)
    return both[:tokens] + both[tokens:]


def result_kernel(middle, combined, gates_t, target_t, result_ref):
    mixture = mix(combined[...], gates_t[...], target_t[...])
    result_ref[...] = (middle[...] + mixture).astype(bf16)


def attend(rows, weight, cosines, sines, bias_ref, heads_ref, out_ref):
    seq_count, tokens, columns = heads_ref.shape
    group = seq_count * tokens
    local = columns // HD - 2
    prompt = group // 2
    raw = nn(rows, weight)
    heads = []
    for j in range(local + 2):
        block = raw[:, j * HD : (j + 1) * HD]
        if j <= local:
            block = turn(block, cosines, sines)
        heads.append(block.astype(bf16))
        heads_ref[:, :, j * HD : (j + 1) * HD] = heads[j].reshape(seq_count, tokens, HD)
    heads_ref.send()
    key, value = heads[local], heads[local + 1]
    scale = HD ** (-0.5)
    for j in range(local):
        query = heads[j]
        for rows, seen in ((slice(0, prompt), prompt), (slice(prompt, group), group)):
            scores = nt(query[rows], key[:seen]) * scale + bias_ref[rows, :seen]
            peak = jnp.max(scores, axis=-1, keepdims=True)
            weights = jnp.exp(scores - peak)
            weights = weights / jnp.sum(weights, axis=-1, keepdims=True)
            part = nn(weights.astype(bf16), value[:seen]).astype(bf16)
            first = rows.start // tokens
            out_ref[first : first + prompt // tokens, :, j * HD : (j + 1) * HD] = part.reshape(
                prompt // tokens, tokens, HD
            )


def first_attention_kernel(
    place, own, one, two, three, weight, spread, cosines, sines, bias_ref,
    heads_ref, out_ref, normed_ref, small_ref,
):
    expert_count = 8
    me = place[0]
    seq_count, tokens, width = normed_ref.shape
    columns = heads_ref.shape[2]
    count = small_ref.shape[1]
    extras = weight[:, columns:].astype(f32).T.astype(bf16)
    extras = jnp.concatenate([extras[:count], extras[HD : HD + count]], axis=0)
    small = jnp.concatenate(to_natural(extras, spread[...]), axis=1)
    small_ref[0] = small[:count].astype(bf16)
    small_ref[1] = small[count:].astype(bf16)
    small_ref.send()
    gain = small[expert_count : expert_count + 1]
    for k, block in enumerate((own, one, two, three)):
        normed = normalize(block[...].astype(f32), gain).astype(bf16)
        normed = to_gathered(column_blocks(normed, seq_count), spread[...]).astype(bf16)
        normed_ref[lax.rem(me + k, seq_count)] = normed
    normed_ref.send()
    rows = normed_ref[...].reshape(seq_count * tokens, width)
    attend(rows, weight[:, :columns], cosines[...], sines[...], bias_ref, heads_ref, out_ref)


def next_attention_kernel(
    place, own, one, two, three, query_w, key_w, value_w, cosines, sines, bias_ref,
    heads_ref, out_ref, normed_ref,
):
    me = place[0]
    seq_count, tokens, width = normed_ref.shape
    weight = [w[...].reshape(width, w.shape[2]) for w in (query_w, key_w, value_w)]
    weight = jnp.concatenate(weight, axis=1)
    for k, block in enumerate((own, one, two, three)):
        normed_ref[lax.rem(me + k, seq_count)] = block[...]
    normed_ref.send()
    rows = normed_ref[...].reshape(seq_count * tokens, width)
    attend(rows, weight, cosines[...], sines[...], bias_ref, heads_ref, out_ref)


def after_attention_kernel(
    back, spread, hidden, small, out_w, routes_t, target_t,
    middle_ref, normed_ref, gates_ref, send_ref,
):
    expert_count = 8
    seq_count, tokens, part = back.shape
    width = seq_count * part
    attended = to_gathered([back[s] for s in range(seq_count)], spread[...]).astype(bf16)
    rows = out_w.shape[1] // 2
    half = out_w.shape[2]
    for side in range(2):
        weight = out_w[:, side * rows : (side + 1) * rows].reshape(width, half)
        cols = slice(side * half, (side + 1) * half)
        middle_ref[:, cols] = hidden[:, cols].astype(f32) + nn(attended, weight)
    middle_ref.send()
    middle = middle_ref[...]
    gain = small[expert_count + 1 : expert_count + 2].astype(f32)
    normed = normalize(middle, gain).astype(bf16)
    normed_ref[...] = normed
    normed_ref.send()
    send_ref[...] = nn(choose(target_t[...], send_ref.shape[0]).astype(bf16), normed).astype(bf16)
    send_ref.send()
    logits = nt(small[...], normed)
    chosen = []
    for k in range(TOPK):
        route = routes_t[k : k + 1]
        value = jnp.zeros((1, tokens), f32)
        for e in range(expert_count):
            value = value + jnp.where(route == e, logits[e : e + 1], 0.0)
        chosen.append(value)
    peak = functools.reduce(jnp.maximum, chosen)
    powers = [jnp.exp(value - peak) for value in chosen]
    total = functools.reduce(jnp.add, powers)
    for k in range(TOPK):
        gates_ref[k : k + 1] = powers[k] / total
    gates_ref[TOPK:] = jnp.zeros((gates_ref.shape[0] - TOPK, tokens), f32)


def flat_rows(block):
    sources, capacity, width = block.shape
    return block.astype(f32).reshape(sources * capacity, width).astype(bf16)


def down_parts(block):
    shards, rows, half = block.shape
    wide = block.astype(f32)
    left = wide[:, : rows // 2].reshape(shards * rows // 2, half).astype(bf16)
    right = wide[:, rows // 2 :].reshape(shards * rows // 2, half).astype(bf16)
    return left, right


def expert_kernel(rows_ref, *rest):
    experts = rows_ref.shape[1]
    weights = rest[: 3 * experts]
    out_ref, gate_ref, up_ref = rest[3 * experts :]
    sources, capacity = rows_ref.shape[0], rows_ref.shape[2]
    for e in range(experts):
        gate_w, up_w, down_w = weights[3 * e : 3 * e + 3]
        shards, rows, half = gate_w.shape
        tokens = flat_rows(rows_ref[:, e])
        gate_val = nn(tokens, gate_w[...].reshape(shards * rows, half))
        gate_ref[e] = gate_val.astype(bf16)
        gate_ref.send(e)
        up_val = nn(tokens, up_w[...].reshape(shards * rows, half))
        up_ref[e] = up_val.astype(bf16)
        up_ref.send(e)
        activated, slope = smooth_parts(gate_val)
        inner = (activated * up_val).astype(bf16)
        for side, part in enumerate(down_parts(down_w[...])):
            block = nn(inner, part).reshape(sources, capacity, half).astype(bf16)
            out_ref[:, e, :, side * half : (side + 1) * half] = block
        out_ref.send(e)


def slot_grad_kernel(grad, combined, gates_t, routes_t, target_t, send_ref, logits_ref):
    tokens = grad.shape[0]
    slots = combined.shape[0]
    high, low = split(grad[...])
    weights_high, weights_low = split(choose_weighted(target_t[...], gates_t[...], slots))
    weights = jnp.concatenate([weights_high, weights_low, weights_high], axis=1)
    send = nn(weights, jnp.concatenate([high, high, low], axis=0))
    send_ref[...] = send.astype(bf16)
    send_ref.send()
    products = nt(combined[...], jnp.concatenate([high, low], axis=0))
    products = products[:, :tokens] + products[:, tokens:]
    place = lax.broadcasted_iota(jnp.int32, (slots, tokens), 0)
    grad_gates = [
        jnp.sum(jnp.where(place == target_t[k : k + 1], products, 0.0), axis=0, keepdims=True)
        for k in range(TOPK)
    ]
    gates = [gates_t[k : k + 1] for k in range(TOPK)]
    center = functools.reduce(jnp.add, [a * b for a, b in zip(gates, grad_gates)])
    label = lax.broadcasted_iota(jnp.int32, logits_ref.shape, 0)
    total = jnp.zeros(logits_ref.shape, f32)
    for k in range(TOPK):
        choice = gates[k] * (grad_gates[k] - center)
        total = total + jnp.where(label == routes_t[k : k + 1], choice, 0.0)
    logits_ref[...] = total.astype(bf16)


def expert_back_kernel(grad_ref, down_first, gate_ref, up_ref, *rest):
    experts = grad_ref.shape[1]
    weights = (down_first,) + rest[: 3 * experts - 1]
    out_ref, gate_grad_ref, up_grad_ref, inner_ref = rest[3 * experts - 1 :]
    sources, capacity = grad_ref.shape[0], grad_ref.shape[2]
    for e in range(experts):
        down_w, gate_w, up_w = weights[3 * e : 3 * e + 3]
        shards, rows, half = gate_w.shape
        grad = flat_rows(grad_ref[:, e])
        left, right = down_parts(down_w[...])
        grad_inner = nt(grad[:, :half], left) + nt(grad[:, half:], right)
        up_val = up_ref[e].astype(f32)
        activated, slope = smooth_parts(gate_ref[e].astype(f32))
        inner_ref[e] = (activated * up_val).astype(bf16)
        inner_ref.send(e)
        gate_grad_ref[e] = (grad_inner * up_val * slope).astype(bf16)
        gate_grad_ref.send(e)
        up_grad_ref[e] = (grad_inner * activated).astype(bf16)
        up_grad_ref.send(e)
        parts = 4
        some, size = shards // parts, shards * rows // parts
        for c in range(parts):
            at = slice(c * some, (c + 1) * some)
            total = nt(gate_grad_ref[e], gate_w[at].reshape(size, half))
            total = total + nt(up_grad_ref[e], up_w[at].reshape(size, half))
            total = total.reshape(sources, capacity, size).astype(bf16)
            out_ref[:, e, :, c * size : (c + 1) * size] = total
        out_ref.send(e)


def expert_weight_kernel(rows_ref, grad_ref, gate_grad_ref, up_grad_ref, inner_ref, *rest):
    pack_ref = rest[-1]
    experts = rows_ref.shape[1]
    shards, rows, half = pack_ref.shape
    width = rows_ref.shape[3]
    rows = width // shards
    at = 0

    def send(start, count):
        for piece in range(start // 16, (start + count) // 16):
            pack_ref.send(piece)

    for e in range(experts):
        tokens = flat_rows(rows_ref[:, e])
        grad = flat_rows(grad_ref[:, e])
        grads = jnp.concatenate([gate_grad_ref[e], up_grad_ref[e]], axis=1)
        both = tn(tokens, grads).astype(bf16)
        pack_ref[:, at : at + rows] = both[:, :half].reshape(shards, rows, half)
        pack_ref[:, at + rows : at + 2 * rows] = both[:, half:].reshape(shards, rows, half)
        send(at, 2 * rows)
        down = tn(inner_ref[e], grad)
        left = down[:, :half].reshape(shards, rows // 2, half)
        right = down[:, half:].reshape(shards, rows // 2, half)
        down = jnp.concatenate([left, right], axis=1).astype(bf16)
        pack_ref[:, at + 2 * rows : at + 3 * rows] = down
        send(at + 2 * rows, rows)
        at += 3 * rows
    for extra in rest[:-1]:
        pack_ref[:, at : at + extra.shape[1]] = extra[...]
        at += extra.shape[1]


def after_experts_kernel(
    grad, sent, middle, normed, logits_grad, target_t, small, out_w, spread,
    grad_ref, branch_ref, send_ref, small_ref,
):
    expert_count = 8
    seq_count, tokens, part = send_ref.shape
    width = seq_count * part
    chosen = choose(target_t[...], sent.shape[0]).astype(bf16)
    grad_normed = tn(chosen, sent[...]) + tn(logits_grad[...], small[...])
    router = nn(logits_grad[...], normed[...])
    gain = small[expert_count + 1 : expert_count + 2].astype(f32)
    grad_value, grad_gain = normalize_back(middle[...], gain, grad_normed)
    label = lax.broadcasted_iota(jnp.int32, small_ref.shape, 0)
    small_ref[...] = jnp.where(label == expert_count + 1, grad_gain, router)
    grad_middle = grad[...] + grad_value
    grad_ref[...] = grad_middle
    grad_ref.send()
    branch = grad_middle.astype(bf16)
    branch_ref[...] = branch
    branch_ref.send()
    rows = out_w.shape[1] // 2
    half = out_w.shape[2]
    parts = [
        nt(branch[:, :half], out_w[:, :rows].reshape(width, half)),
        nt(branch[:, half:], out_w[:, rows:].reshape(width, half)),
    ]
    attended = (parts[0] + parts[1]).astype(bf16)
    for s, block in enumerate(to_natural(attended, spread[...])):
        send_ref[s] = block.astype(bf16)


def attention_back_kernel(heads_ref, grad_ref, bias_ref, cosines, sines, out_ref):
    seq_count, tokens, columns = heads_ref.shape
    group = seq_count * tokens
    heads = heads_ref[...].reshape(group, columns)
    grads = grad_ref[...].reshape(group, grad_ref.shape[2])
    local = columns // HD - 2
    prompt = group // 2
    key = heads[:, local * HD : (local + 1) * HD]
    value = heads[:, (local + 1) * HD :]
    scale = HD ** (-0.5)

    def keep(at, block):
        out_ref[:, :, at * HD : (at + 1) * HD] = block.astype(bf16).reshape(seq_count, tokens, HD)

    cosines, sines = cosines[...], sines[...]

    def unturn(block):
        return block * cosines - pltpu.roll(block, HD // 2, 1) * sines

    grad_key = [jnp.zeros((prompt, HD), f32), jnp.zeros((prompt, HD), f32)]
    grad_value = [jnp.zeros((prompt, HD), f32), jnp.zeros((prompt, HD), f32)]
    for j in range(local):
        query = heads[:, j * HD : (j + 1) * HD]
        grad = grads[:, j * HD : (j + 1) * HD]
        grad_query = []
        for rows, seen in ((slice(0, prompt), prompt), (slice(prompt, group), group)):
            scores = nt(query[rows], key[:seen]) * scale + bias_ref[rows, :seen]
            peak = jnp.max(scores, axis=-1, keepdims=True)
            weights = jnp.exp(scores - peak)
            weights = weights / jnp.sum(weights, axis=-1, keepdims=True)
            grad_weights = nt(grad[rows], value[:seen])
            center = jnp.sum(weights * grad_weights, axis=-1, keepdims=True)
            grad_scores = (weights * (grad_weights - center)).astype(bf16)
            low = weights.astype(bf16)
            grad_query.append(nn(grad_scores, key[:seen]) * scale)
            for side in range(seen // prompt):
                cols = slice(side * prompt, (side + 1) * prompt)
                grad_key[side] = grad_key[side] + tn(grad_scores[:, cols], query[rows])
                grad_value[side] = grad_value[side] + tn(low[:, cols], grad[rows])
        keep(j, unturn(jnp.concatenate(grad_query, axis=0)))
    keep(local, unturn(jnp.concatenate(grad_key, axis=0) * scale))
    keep(local + 1, jnp.concatenate(grad_value, axis=0))


def before_attention_kernel(
    sent, left_w, right_w, kv_w, spread, small, hidden, grad_middle, out_ref, gain_ref
):
    expert_count = 8
    seq_count, tokens, columns = sent.shape
    local = columns // HD - 2
    share = seq_count // KVHEADS
    blocks = [sent[s, :, : local * HD] for s in range(seq_count)]
    for at in (local, local + 1):
        for c in range(KVHEADS):
            total = jnp.zeros((tokens, HD), f32)
            for s in range(c * share, (c + 1) * share):
                total = total + sent[s, :, at * HD : (at + 1) * HD].astype(f32)
            blocks.append(total.astype(bf16))
    raw = jnp.concatenate(blocks, axis=1)
    at, total = 0, 0.0
    for part in (left_w, right_w, kv_w):
        shards, rows, columns = part.shape
        weight = part[...].reshape(shards * rows, columns)
        total = total + nt(raw[:, at : at + columns], weight)
        at += columns
    high, low = split(total)
    both = to_natural(jnp.concatenate([high, low], axis=0), spread[...])
    both = jnp.concatenate(both, axis=1)
    grad_normed = both[:tokens] + both[tokens:]
    gain = small[expert_count : expert_count + 1].astype(f32)
    grad_value, grad_gain = normalize_back(hidden[...].astype(f32), gain, grad_normed)
    out_ref[...] = grad_middle[...] + grad_value
    out_ref.send()
    shards = gain_ref.shape[0]
    width = grad_gain.shape[1]
    share = width // seq_count
    part = share // shards
    shard = lax.broadcasted_iota(jnp.int32, (shards, width), 0)
    at = lax.broadcasted_iota(jnp.int32, (shards, width), 1)
    kept = jnp.where(at % share // part == shard, grad_gain, 0.0).astype(bf16)
    source = lax.broadcasted_iota(jnp.int32, (width, HD), 0)
    wanted = lax.broadcasted_iota(jnp.int32, (width, HD), 1)
    place = source // share * part + source % part
    gain_ref[...] = nn(kept, jnp.where(place == wanted, 1.0, 0.0).astype(bf16))


def qkv_weight_kernel(normed, grads, small, spread, out_ref):
    seq_count, tokens, columns = grads.shape
    shards, rows, wide = out_ref.shape
    inputs = normed[...].reshape(seq_count * tokens, normed.shape[2])
    total = tn(inputs, grads[...].reshape(seq_count * tokens, columns))
    out_ref[:, :, :columns] = total.astype(bf16).reshape(shards, rows, columns)
    extra = column_blocks(small[...].astype(bf16), seq_count)
    extra = to_gathered(extra, spread[...])
    extra = jnp.concatenate([extra, jnp.zeros((HD - extra.shape[0], extra.shape[1]), f32)], axis=0).T
    out_ref[:, :, columns:] = extra.astype(bf16).reshape(shards, rows, wide - columns)


def out_weight_kernel(place, own, one, two, three, attended, gain, out_ref):
    me = place[0]
    seq_count, tokens, part = attended.shape
    shards, rows, half = out_ref.shape
    rows = rows // 2
    valid = part // shards
    branch = jnp.concatenate([own[...], one[...], two[...], three[...]], axis=0)
    heads = jnp.concatenate([attended[lax.rem(me + k, seq_count)] for k in range(seq_count)], axis=0)
    place_in = lax.broadcasted_iota(jnp.int32, (part, shards * rows), 0)
    place_out = lax.broadcasted_iota(jnp.int32, (part, shards * rows), 1)
    source = place_out // rows * valid + place_out % rows
    same = jnp.logical_and(place_in == source, place_out % rows < valid)
    heads = nn(heads, jnp.where(same, 1.0, 0.0).astype(bf16)).astype(bf16)
    wide = jnp.concatenate([gain[...], jnp.zeros((shards, half - HD), f32)], axis=1)
    row = lax.broadcasted_iota(jnp.int32, (shards, rows, half), 1)
    for side in range(2):
        total = tn(heads, branch[:, side * half : (side + 1) * half]).reshape(shards, rows, half)
        if side == 0:
            total = jnp.where(row == valid, wide[:, None, :], total)
        out_ref[:, side * rows : (side + 1) * rows] = total.astype(bf16)


def expert_grads_kernel(*refs):
    sums, (gate_ref, up_ref, down_ref) = refs[:LAYERS], refs[LAYERS:]
    rows = gate_ref.shape[2]
    half = gate_ref.shape[3]
    for layer in range(LAYERS):
        block = sums[layer][...].astype(f32)
        for e in range(gate_ref.shape[1]):
            at = 3 * rows * e
            gate_ref[layer, e] = block[at : at + rows]
            up_ref[layer, e] = block[at + rows : at + 2 * rows]
            at += 2 * rows
            down_ref[layer, e, :, :half] = block[at : at + rows // 2]
            down_ref[layer, e, :, half:] = block[at + rows // 2 : at + rows]


def dense_grads_kernel(*refs):
    blocks, outs = refs[:LAYERS], refs[LAYERS : 2 * LAYERS]
    query_ref, key_ref, value_ref, out_ref, small_ref = refs[2 * LAYERS :]
    seq_count, rows, columns = blocks[0].shape
    local = columns - 3 * HD
    share = seq_count // KVHEADS
    for layer in range(LAYERS):
        parts = [blocks[layer][s].astype(f32) for s in range(seq_count)]
        for s in range(seq_count):
            query_ref[:, layer, s * local : (s + 1) * local] = parts[s][:, :local]
        for c in range(KVHEADS):
            total = functools.reduce(jnp.add, parts[c * share : (c + 1) * share])
            key_ref[:, layer, c * HD : (c + 1) * HD] = total[:, local : local + HD]
            value_ref[:, layer, c * HD : (c + 1) * HD] = total[:, local + HD : local + 2 * HD]
        total = functools.reduce(jnp.add, parts)
        small_ref[layer] = total[:, local + 2 * HD :]
        block = outs[layer][...].astype(f32)
        half = block.shape[1]
        out_ref[:, layer, :half] = block[:rows]
        out_ref[:, layer, half:] = block[block.shape[0] // 2 :][:rows]


def swap_seq(block):
    return lax.all_to_all(block, "seq", split_axis=0, concat_axis=0, tiled=True)


def around_seq(block):
    count = lax.axis_size("seq")
    others = [
        lax.ppermute(block, "seq", [((i + k) % count, i) for i in range(count)])
        for k in range(1, count)
    ]
    return [block] + others


def halves(block):
    cut = block.shape[-1] // 2
    return jnp.concatenate([block[..., :cut], block[..., cut:]], axis=-2)


def per_device(
    tokens_in,
    cotangent,
    routes,
    order,
    segment_ids,
    gain_attn,
    w_query,
    w_key,
    w_value,
    w_out,
    gain_ffn,
    w_router,
    w_gate,
    w_up,
    w_down,
):
    tok_count = tokens_in.shape[1]
    width = tokens_in.shape[2]
    seq_count = lax.axis_size("seq")
    shard_count = lax.axis_size("fsdp")
    seq_index = lax.axis_index("seq")
    place = jnp.full((1,), seq_index, jnp.int32)
    group_tok = seq_count * tok_count
    prompt_len = group_tok - segment_ids.shape[1]
    local_experts = w_gate.shape[1]
    expert_count = local_experts * seq_count
    capacity = 9 * tok_count * TOPK // (8 * expert_count)
    total_slots = expert_count * capacity
    head_local = HEADS // seq_count
    local_width = head_local * HD
    dense_rows = w_query.shape[1]
    shard_rows = dense_rows * seq_count
    gate_rows = w_gate.shape[2]
    down_rows = w_down.shape[2]
    expert_rows = 2 * gate_rows + 2 * down_rows
    qkv_width = (HEADS + 2 * KVHEADS) * HD
    half_width = width // 2
    inner_width = w_gate.shape[3]
    slot_rows = seq_count * capacity

    cos_half, sin_half, labels = group_tables(segment_ids[0], prompt_len)
    cos_all = jnp.concatenate([cos_half, cos_half], axis=1)
    sin_all = jnp.concatenate([-sin_half, sin_half], axis=1)
    cos_own = lax.dynamic_slice_in_dim(cos_all, seq_index * tok_count, tok_count, 0)
    sin_own = lax.dynamic_slice_in_dim(sin_all, seq_index * tok_count, tok_count, 0)
    key_pos = jnp.arange(group_tok, dtype=jnp.int32)
    allowed = jnp.logical_and(
        key_pos[None, :] <= key_pos[:, None],
        jnp.logical_or(key_pos[None, :] < prompt_len, labels[None, :] == labels[:, None]),
    )
    bias = jnp.where(allowed, 0.0, masked_value)

    column = jnp.arange(width // seq_count, dtype=jnp.int32)
    natural = (
        column % shard_rows // dense_rows * (width // seq_count // seq_count)
        + column // shard_rows * dense_rows
        + column % dense_rows
    )
    spread = (column[:, None] == natural[None, :]).astype(bf16)

    def small_rows_of(layer):
        return jnp.concatenate(
            [
                w_router[layer],
                gain_attn[layer][:, None],
                gain_ffn[layer][:, None],
                jnp.zeros((dense_rows, HD - 2 - expert_count), bf16),
            ],
            axis=1,
        )

    def dense_rows_of(layer):
        return jnp.concatenate(
            [w_query[layer], w_key[layer], w_value[layer], small_rows_of(layer), w_out[layer]],
            axis=1,
        )

    def spread_seq(dense):
        dense = swap_seq(jnp.broadcast_to(dense[None], (seq_count,) + dense.shape))
        return dense.reshape(shard_rows, dense.shape[2])

    def own_columns(weight):
        pick = seq_index * KVHEADS // seq_count
        starts = (seq_index * local_width, (HEADS + pick) * HD, (HEADS + KVHEADS + pick) * HD)
        parts = [
            lax.dynamic_slice_in_dim(weight, start, size, 1)
            for start, size in zip(starts, (local_width, HD, HD))
        ]
        return jnp.concatenate(parts + [weight[:, qkv_width : qkv_width + HD]], axis=1)

    def expert_part(layer):
        return [
            part
            for e in range(local_experts)
            for part in (w_gate[layer, e], w_up[layer, e], halves(w_down[layer, e]))
        ]

    def out_part(dense):
        return [halves(dense[:, qkv_width + HD :])]

    def qkv_part(dense):
        wide = jnp.concatenate(
            [dense[:, : qkv_width + HD], jnp.zeros((shard_rows, HD), bf16)], axis=1
        )
        return [wide[:, at : at + half_width] for at in range(0, wide.shape[1], half_width)]

    def fetch(parts):
        return lax.all_gather(jnp.concatenate(parts, axis=0), "fsdp", axis=0, tiled=False)

    core = lax.rem(lax.axis_index("fsdp"), 2)
    chips = [[i + c for i in range(0, shard_count, 2)] for c in range(2)]

    def swap_chips(block):
        return lax.all_to_all(
            block, "fsdp", split_axis=0, concat_axis=0, tiled=True, axis_index_groups=chips
        )

    def swap_cores(block):
        return lax.ppermute(block, "fsdp", [(i, i ^ 1) for i in range(shard_count)])

    def both_cores(block):
        other = swap_cores(block)
        first = jnp.where(core == 0, block, other)
        second = jnp.where(core == 0, other, block)
        return jnp.stack([first, second], axis=1).reshape((shard_count,) + block.shape[1:])

    def to_chips(block):
        return swap_chips(jnp.broadcast_to(block[None], (shard_count // 2,) + block.shape))

    weight_parts = [
        (e * expert_rows + k * gate_rows, gate_rows) for e in range(local_experts) for k in range(3)
    ]
    back_parts = [weight_parts[3 * e + k] for e in range(local_experts) for k in (2, 0, 1)]
    out_cut = ((1, local_experts * expert_rows, 2 * shard_rows),)

    slots_shape = shape((seq_count, local_experts, capacity, width), bf16)
    inner_shape = (local_experts, slot_rows, inner_width)
    expert_flops = 6 * total_slots * width * inner_width
    dense_flops = 2 * tok_count * width * width
    records = []
    hidden = tokens_in[0]
    dense = spread_seq(jnp.concatenate([dense_rows_of(0), small_rows_of(1)], axis=1))
    columns = jnp.concatenate([own_columns(dense), dense[:, -HD:]], axis=1)
    dense = dense[:, :-HD]
    columns, hidden = lax.optimization_barrier((columns, hidden))
    token_blocks = around_seq(hidden)
    packs = [fetch(expert_part(0) + out_part(dense)), None]
    columns = to_chips(columns)
    targets = [
        slot_table(routes[layer, 0], order[layer, 0], expert_count, capacity)
        for layer in range(LAYERS)
    ]
    routes_ts = [routes[layer, 0].T for layer in range(LAYERS)]
    early = (token_blocks, targets, routes_ts, cos_all, sin_all, bias, spread)
    columns, early, next_rows = lax.optimization_barrier((columns, early, dense_rows_of(1)))
    token_blocks, targets, routes_ts, cos_all, sin_all, bias, spread = early
    first_columns = both_cores(columns).reshape(width, columns.shape[2])
    next_dense = spread_seq(next_rows)
    qkv_at = local_experts * expert_rows + 2 * shard_rows
    qkv_ws = [None, None]
    blocks = half_width // local_width

    def query_row(me):
        return qkv_at + me // blocks * shard_rows

    def query_column(me):
        return me % blocks * local_width

    def key_column(me):
        return me * KVHEADS // seq_count * HD

    def value_column(me):
        return KVHEADS * HD + me * KVHEADS // seq_count * HD

    kv_rows = (1, qkv_at + 2 * shard_rows, shard_rows)
    own_cuts = {
        5: ((1, query_row, shard_rows), (2, query_column, local_width)),
        6: (kv_rows, (2, key_column, HD)),
        7: (kv_rows, (2, value_column, HD)),
    }
    heads_shape = shape((seq_count, tok_count, local_width + 2 * HD), bf16)
    attended_shape = shape((seq_count, tok_count, local_width), bf16)
    normed_shape = shape((seq_count, tok_count, width), bf16)
    small_shape = shape((LAYERS, 2 * expert_count, width), bf16)
    attention_flops = 4 * head_local * group_tok * group_tok * HD + 2 * dense_flops
    for layer in range(LAYERS):
        pack, routes_t, target_t = packs[layer], routes_ts[layer], targets[layer]
        if layer == 0:
            heads, attended, normed_all, smalls = once(
                first_attention_kernel,
                [heads_shape, attended_shape, normed_shape, small_shape],
                place, *token_blocks, first_columns, spread, cos_all, sin_all, bias,
                scalar=True, flops=attention_flops + 4 * dense_flops,
            )
            small = smalls[layer]
        else:
            small = smalls[layer]
            normed_p, hidden = once(
                input_kernel,
                [shape((tok_count, width), bf16), shape((tok_count, width), f32)],
                middle, combined, gates_t, above_target, small, spread, flops=2 * dense_flops,
            )
            heads, attended, normed_all = once(
                next_attention_kernel,
                [heads_shape, attended_shape, normed_shape],
                place, *around_seq(normed_p), pack, pack, pack, cos_all, sin_all, bias,
                scalar=True, cut=own_cuts, flops=attention_flops,
            )
        back = swap_seq(attended)
        if layer == 0:
            next_parts = expert_part(1) + out_part(next_dense) + qkv_part(next_dense)
            next_parts = jnp.concatenate(next_parts, axis=0)
            pack, next_parts, back = lax.optimization_barrier((pack, next_parts, back))
            packs = [pack, fetch([next_parts])]
            qkv_ws[1] = (packs[1], qkv_at)
        else:
            first_parts = jnp.concatenate(qkv_part(dense), axis=0)
            first_parts, back = lax.optimization_barrier((first_parts, back))
            qkv_ws[0] = (fetch([first_parts]), 0)
        middle, normed_ffn, gates_t, send_rows = once(
            after_attention_kernel,
            [
                shape((tok_count, width), f32),
                shape((tok_count, width), bf16),
                shape((2 * TOPK, tok_count), f32),
                shape((total_slots, width), bf16),
            ],
            back, spread, hidden, small, pack, routes_t, target_t,
            cut={4: out_cut}, flops=3 * dense_flops,
        )
        received = swap_seq(send_rows.reshape(slots_shape.shape))
        expert_out, gate_val, up_val = once(
            expert_kernel,
            [slots_shape, shape(inner_shape, bf16), shape(inner_shape, bf16)],
            received, *[pack] * len(weight_parts),
            cut={n + 1: ((1, *part),) for n, part in enumerate(weight_parts)},
            pieces={0: (1, local_experts), 1: (0, local_experts), 2: (0, local_experts)},
            flops=expert_flops,
        )
        combined = swap_seq(expert_out).reshape(total_slots, width)
        above_target = target_t
        records.append(
            (
                (pack, small, routes_t, target_t),
                (hidden, normed_all, heads, attended),
                (middle, normed_ffn, gates_t, combined),
                (received, gate_val, up_val),
            )
        )
    (result,) = once(
        result_kernel, [shape((tok_count, width), bf16)], middle, combined, gates_t, target_t,
        flops=dense_flops,
    )

    def scatter(block):
        return lax.psum_scatter(block, "fsdp", scatter_dimension=0, tiled=False)

    def spread_qkv(block, out_block):
        gain = out_block[dense_rows, :shard_rows]
        label = jnp.arange(local_width + 3 * HD)[None, :]
        block = jnp.where(label == local_width + 2 * HD + expert_count, gain[:, None], block)
        return swap_seq(block.reshape(seq_count, dense_rows, local_width + 3 * HD))

    out_rows = 16

    grad_hidden = cotangent[0].astype(f32)
    sums = [None] * LAYERS
    waiting = None
    for layer in range(LAYERS - 1, -1, -1):
        weights, attn_saved, mid_saved, expert_saved = records[layer]
        pack, small, routes_t, target_t = weights
        qkv_w, row = qkv_ws[layer]
        below, normed_all, heads, attended = attn_saved
        middle, normed_ffn, gates_t, combined = mid_saved
        received, gate_val, up_val = expert_saved
        grad_slots, logits_grad = once(
            slot_grad_kernel,
            [shape((total_slots, width), bf16), shape((2 * expert_count, tok_count), bf16)],
            grad_hidden, combined, gates_t, routes_t, target_t, flops=3 * dense_flops,
        )
        grad_expert = swap_seq(grad_slots.reshape(slots_shape.shape))
        if waiting is None:
            tied = lax.optimization_barrier((grad_expert, qkv_ws[0][0], result))
            grad_expert, result = tied[0], tied[2]
            qkv_ws[0] = (tied[1], 0)
        else:
            grad_expert, waiting = lax.optimization_barrier((grad_expert, waiting))
        grad_rows, gate_grad, up_grad, inner = once(
            expert_back_kernel,
            [slots_shape] + [shape(inner_shape, bf16)] * 3,
            grad_expert, pack, gate_val, up_val, *[pack] * (len(back_parts) - 1),
            cut={n + 3 if n else 1: ((1, *part),) for n, part in enumerate(back_parts)},
            pieces={0: (1, local_experts), 1: (0, local_experts), 2: (0, local_experts), 3: (0, local_experts)},
            flops=expert_flops,
        )
        sent = swap_seq(grad_rows)
        extra = () if layer == LAYERS - 1 else waiting
        extra_rows = sum(a.shape[1] for a in extra)
        (packed,) = once(
            expert_weight_kernel,
            [shape((shard_count, local_experts * expert_rows + extra_rows, half_width), bf16)],
            received, grad_expert, gate_grad, up_grad, inner, *extra,
            pieces={0: (1, (local_experts * expert_rows + extra_rows) // 16)}, flops=expert_flops,
        )
        sent, packed = lax.optimization_barrier((sent, packed))
        if layer < LAYERS - 1:
            packed, sums[layer + 1] = lax.optimization_barrier((packed, sums[layer + 1]))
        summed = scatter(packed)
        grad_middle, branch, send, small_grad = once(
            after_experts_kernel,
            [
                shape((tok_count, width), f32),
                shape((tok_count, width), bf16),
                shape((seq_count, tok_count, local_width), bf16),
                shape((2 * expert_count, width), f32),
            ],
            grad_hidden, sent.reshape(total_slots, width), middle, normed_ffn, logits_grad,
            target_t, small, pack, spread,
            cut={7: out_cut}, flops=4 * dense_flops,
        )
        grad_heads = swap_seq(send)
        grad_heads, branch = lax.optimization_barrier((grad_heads, branch))
        branch_all = around_seq(branch)
        (grad_own,) = once(
            attention_back_kernel,
            [shape((seq_count, tok_count, local_width + 2 * HD), bf16)],
            heads, grad_heads, bias, cos_all, sin_all,
            flops=10 * head_local * group_tok * group_tok * HD,
        )
        (qkv_block_grad,) = once(
            qkv_weight_kernel,
            [shape((shard_count, shard_rows, half_width), bf16)],
            normed_all, grad_own, small_grad, spread, flops=2 * dense_flops,
        )
        sent, qkv_block_grad = lax.optimization_barrier((swap_seq(grad_own), qkv_block_grad))
        grad_hidden, gain_grad = once(
            before_attention_kernel,
            [shape((tok_count, width), f32), shape((shard_count, HD), f32)],
            sent, qkv_w, qkv_w, qkv_w, spread, small, below, grad_middle,
            cut={
                1: ((1, row, shard_rows),),
                2: ((1, row + shard_rows, shard_rows),),
                3: ((1, row + 2 * shard_rows, shard_rows), (2, 0, 2 * KVHEADS * HD)),
            },
            flops=4 * dense_flops,
        )
        grad_hidden, branch_all = lax.optimization_barrier((grad_hidden, branch_all))
        (out_block_grad,) = once(
            out_weight_kernel,
            [shape((shard_count, 2 * out_rows, half_width), bf16)],
            place, *branch_all, attended, gain_grad, scalar=True, flops=dense_flops,
        )
        sums[layer] = summed
        if layer > 0:
            waiting = (qkv_block_grad, out_block_grad)

    def shard_sum(block):
        block = block.reshape((shard_count // 2, 2) + block.shape[1:])
        own = lax.dynamic_index_in_dim(block, core, 1, False)
        other = swap_cores(lax.dynamic_index_in_dim(block, 1 - core, 1, False))
        block = (own.astype(f32) + other.astype(f32)).astype(bf16)
        return jnp.sum(swap_chips(block).astype(f32), axis=0)

    qkv_sum = shard_sum(qkv_block_grad)
    out_sum = shard_sum(out_block_grad)
    above = sums[0][local_experts * expert_rows :]
    above_out = above[shard_rows:]
    own_rows = spread_qkv(qkv_sum, out_sum)
    above_rows = spread_qkv(above[:shard_rows], above_out)
    gate_grads, up_grads, down_grads = once(
        expert_grads_kernel,
        [
            shape((LAYERS,) + w_gate.shape[1:], f32),
            shape((LAYERS,) + w_up.shape[1:], f32),
            shape((LAYERS,) + w_down.shape[1:], f32),
        ],
        *sums,
        cut={0: ((0, 0, local_experts * expert_rows),)},
    )
    query_grads, key_grads, value_grads, out_grads, small_grads = once(
        dense_grads_kernel,
        [
            shape((dense_rows, LAYERS, HEADS * HD), f32),
            shape((dense_rows, LAYERS, KVHEADS * HD), f32),
            shape((dense_rows, LAYERS, KVHEADS * HD), f32),
            shape((dense_rows, LAYERS, width), f32),
            shape((LAYERS, dense_rows, HD), f32),
        ],
        own_rows, above_rows, out_sum, above_out,
    )
    return (
        result[None],
        grad_hidden[None],
        small_grads[:, :, expert_count],
        query_grads.transpose(1, 0, 2),
        key_grads.transpose(1, 0, 2),
        value_grads.transpose(1, 0, 2),
        out_grads.transpose(1, 0, 2),
        small_grads[:, :, expert_count + 1],
        small_grads[:, :, :expert_count],
        gate_grads,
        up_grads,
        down_grads,
    )


def solution(mesh):
    in_specs = (
        P("fsdp", "seq", None),
        P("fsdp", "seq", None),
        P(None, "fsdp", "seq", None),
        P(None, "fsdp", "seq", None),
        P("fsdp", None),
        P(None, ("seq", "fsdp")),
        P(None, ("seq", "fsdp"), None),
        P(None, ("seq", "fsdp"), None),
        P(None, ("seq", "fsdp"), None),
        P(None, ("seq", "fsdp"), None),
        P(None, ("seq", "fsdp")),
        P(None, ("seq", "fsdp"), None),
        P(None, "seq", "fsdp", None),
        P(None, "seq", "fsdp", None),
        P(None, "seq", "fsdp", None),
    )
    out_specs = (
        P("fsdp", "seq", None),
        P("fsdp", "seq", None),
        P(None, ("seq", "fsdp")),
        P(None, ("seq", "fsdp"), None),
        P(None, ("seq", "fsdp"), None),
        P(None, ("seq", "fsdp"), None),
        P(None, ("seq", "fsdp"), None),
        P(None, ("seq", "fsdp")),
        P(None, ("seq", "fsdp"), None),
        P(None, "seq", "fsdp", None),
        P(None, "seq", "fsdp", None),
        P(None, "seq", "fsdp", None),
    )
    return jax.shard_map(
        per_device, mesh=mesh, in_specs=in_specs, out_specs=out_specs, check_vma=False
    )
```

```python
import functools

import jax
import jax.numpy as jnp
import numpy as np
from jax import lax
from jax.experimental import pallas as pl
from jax.experimental.pallas import tpu as pltpu
from jax.sharding import PartitionSpec as P

HEADS = 12
KVHEADS = 2
HD = 128
TOPK = 4
LAYERS = 2
NCONT = 4

norm_eps = 1e-06
rope_base = 10000.0
masked_value = -1e30

bf16 = jnp.bfloat16
f32 = jnp.float32
VMEM_BYTES = 64 * 1024 * 1024 - 256 * 1024


def group_tables(segment_row, prompt_len):
    cont_len = segment_row.shape[0]
    onehot = (segment_row[:, None] == jnp.arange(NCONT, dtype=jnp.int32)[None, :]).astype(jnp.int32)
    counts = jnp.sum(onehot, axis=0)
    starts = jnp.cumsum(counts) - counts
    seg_begin = jnp.sum(onehot * starts[None, :], axis=1)
    within = jnp.arange(cont_len, dtype=jnp.int32) - seg_begin
    positions = jnp.concatenate([jnp.arange(prompt_len, dtype=jnp.int32), prompt_len + within])
    labels = jnp.concatenate([jnp.full((prompt_len,), -1, jnp.int32), segment_row])
    frequency = rope_base ** (-(jnp.arange(HD // 2, dtype=jnp.float32) * 2.0 / HD))
    angles = positions.astype(jnp.float32)[:, None] * frequency[None, :]
    return (jnp.cos(angles), jnp.sin(angles), labels)


def slot_table(routes_t, order_t, expert_count, capacity):
    pair_expert = routes_t.reshape(-1)
    pair_order = order_t.reshape(-1)
    same_expert = pair_expert[:, None] == pair_expert[None, :]
    earlier = pair_order[None, :] < pair_order[:, None]
    pair_slot = jnp.sum(jnp.logical_and(same_expert, earlier).astype(jnp.int32), axis=1)
    target = jnp.where(
        pair_slot < capacity, pair_expert * capacity + pair_slot, expert_count * capacity
    )
    return target.reshape(routes_t.shape)


def nn(left, right):
    return lax.dot_general(left, right, (((1,), (0,)), ((), ())), preferred_element_type=f32)


def nt(left, right):
    return lax.dot_general(left, right, (((1,), (1,)), ((), ())), preferred_element_type=f32)


def tn(left, right):
    return lax.dot_general(left, right, (((0,), (0,)), ((), ())), preferred_element_type=f32)


def split(value):
    high = value.astype(bf16)
    return high, (value - high.astype(f32)).astype(bf16)


class Late:
    def __init__(self, ref, copy):
        self.ref, self.copy, self.shape = ref, copy, ref.shape
        copy.start()

    def wait(self):
        if self.copy is not None:
            self.copy.wait()
            self.copy = None

    def __getitem__(self, index):
        self.wait()
        return self.ref[index]


class Out:
    def __init__(self, ref, copies):
        self.ref, self.copies, self.shape = ref, copies, ref.shape
        self.sent = [False] * len(copies)

    def send(self, piece=None):
        for n in range(len(self.copies)) if piece is None else (piece,):
            if not self.sent[n]:
                self.copies[n].start()
                self.sent[n] = True

    def __getitem__(self, index):
        return self.ref[index]

    def __setitem__(self, index, value):
        self.ref[index] = value


def cost(args, outs, flops):
    moved = sum(int(np.prod(a.shape)) * a.dtype.itemsize for a in (*args, *outs))
    return pl.CostEstimate(flops=flops, bytes_accessed=moved, transcendentals=0)


def once(kernel, outs, *args, scalar=False, cut=None, pieces=None, flops=0):
    cut, pieces = cut or {}, pieces or {}
    hbm = pl.BlockSpec(memory_space=pltpu.HBM)
    late = [n for n in range(len(args)) if not (scalar and n == 0)]
    specs = [hbm] * len(args)
    if scalar:
        specs[0] = pl.BlockSpec(memory_space=pltpu.SMEM)
    scratch = []
    for n in late:
        dims = list(args[n].shape)
        for dim, start, size in cut.get(n, ()):
            dims[dim] = size
        scratch.append(pltpu.VMEM(tuple(dims), args[n].dtype))
    scratch += [pltpu.VMEM(o.shape, o.dtype) for o in outs]
    parts = [pieces.get(n, (0, 1)) for n in range(len(outs))]
    scratch.append(pltpu.SemaphoreType.DMA((len(late) + sum(count for _, count in parts),)))

    def body(*refs):
        ins = list(refs[: len(args)])
        out_refs = refs[len(args) : len(args) + len(outs)]
        rooms = refs[len(args) + len(outs) : -1]
        sems = refs[-1]
        for i, n in enumerate(late):
            source = ins[n]
            for dim, start, size in cut.get(n, ()):
                if callable(start):
                    start = pl.multiple_of(start(ins[0][0]), 16 if dim == 1 else HD)
                source = source.at[(slice(None),) * dim + (pl.ds(start, size),)]
            ins[n] = Late(rooms[i], pltpu.make_async_copy(source, rooms[i], sems.at[i]))
        results = []
        used = len(late)
        for i, out in enumerate(out_refs):
            room = rooms[len(late) + i]
            dim, count = parts[i]
            size = room.shape[dim] // count
            copies = []
            for n in range(count):
                at = (slice(None),) * dim + (pl.ds(n * size, size),)
                copies.append(pltpu.make_async_copy(room.at[at], out.at[at], sems.at[used]))
                used += 1
            results.append(Out(room, copies))
        kernel(*ins, *results)
        for result in results:
            result.send()
        for n in late:
            ins[n].wait()
        for result in results:
            for copy in result.copies:
                copy.wait()

    return pl.pallas_call(
        body,
        out_shape=list(outs),
        in_specs=specs,
        out_specs=[hbm] * len(outs),
        scratch_shapes=scratch,
        compiler_params=pltpu.CompilerParams(vmem_limit_bytes=VMEM_BYTES),
        cost_estimate=cost(args, outs, flops),
    )(*args)


def shape(dims, dtype):
    return jax.ShapeDtypeStruct(dims, dtype)


def normalize(value, gain):
    inverse = lax.rsqrt(jnp.mean(value * value, axis=-1, keepdims=True) + norm_eps)
    return value * inverse * gain


def normalize_back(value, gain, grad):
    inverse = lax.rsqrt(jnp.mean(value * value, axis=-1, keepdims=True) + norm_eps)
    unit = value * inverse
    grad_gain = jnp.sum(grad * unit, axis=0, keepdims=True)
    scaled = grad * gain
    grad_value = inverse * (scaled - unit * jnp.mean(scaled * unit, axis=-1, keepdims=True))
    return grad_value, grad_gain


def to_gathered(parts, order):
    count = len(parts)
    share = parts[0].shape[1] // count
    done = []
    for j in range(count):
        piece = jnp.concatenate([part[:, j * share : (j + 1) * share] for part in parts], axis=1)
        done.append(nn(piece, order))
    return jnp.concatenate(done, axis=1)


def to_natural(value, order):
    count = value.shape[1] // order.shape[0]
    size = order.shape[0]
    share = size // count
    done = [nt(value[:, j * size : (j + 1) * size], order) for j in range(count)]
    return [
        jnp.concatenate([part[:, s * share : (s + 1) * share] for part in done], axis=1)
        for s in range(count)
    ]


def column_blocks(value, count):
    size = value.shape[1] // count
    return [value[:, s * size : (s + 1) * size] for s in range(count)]


def turn(block, cosines, sines):
    return block * cosines + pltpu.roll(block, HD // 2, 1) * sines


def smooth_parts(value):
    root = np.float32(np.sqrt(2.0 / np.pi))
    square = value * value
    high = jnp.tanh(root * (value + 0.044715 * value * square))
    half = 0.5 * (1.0 + high)
    slope = half + 0.5 * value * (1.0 - high * high) * root * (1.0 + 3 * 0.044715 * square)
    return value * half, slope


def choose(target_t, slots):
    place = lax.broadcasted_iota(jnp.int32, (slots, target_t.shape[1]), 0)
    total = jnp.zeros(place.shape, f32)
    for k in range(TOPK):
        total = total + jnp.where(place == target_t[k : k + 1], 1.0, 0.0)
    return total


def choose_weighted(target_t, gates_t, slots):
    place = lax.broadcasted_iota(jnp.int32, (slots, target_t.shape[1]), 0)
    total = jnp.zeros(place.shape, f32)
    for k in range(TOPK):
        total = total + jnp.where(place == target_t[k : k + 1], gates_t[k : k + 1], 0.0)
    return total


def input_kernel(
    middle, combined, gates_t, target_t, small, spread, normed_ref, hidden_ref
):
    expert_count = 8
    hidden = middle[...] + mix(combined[...], gates_t[...], target_t[...])
    hidden_ref[...] = hidden
    hidden_ref.send()
    gain = small[expert_count : expert_count + 1].astype(f32)
    normed = normalize(hidden, gain).astype(bf16)
    count = normed.shape[1] // spread.shape[0]
    normed_ref[...] = to_gathered(column_blocks(normed, count), spread[...]).astype(bf16)


def mix(combined, gates_t, target_t):
    high, low = split(choose_weighted(target_t, gates_t, combined.shape[0]))
    tokens = high.shape[1]
    both = tn(jnp.concatenate([high, low], axis=1), combined)
    return both[:tokens] + both[tokens:]


def result_kernel(middle, combined, gates_t, target_t, result_ref):
    mixture = mix(combined[...], gates_t[...], target_t[...])
    result_ref[...] = (middle[...] + mixture).astype(bf16)


def attend(rows, weight, cosines, sines, bias_ref, heads_ref, out_ref):
    seq_count, tokens, columns = heads_ref.shape
    group = seq_count * tokens
    local = columns // HD - 2
    prompt = group // 2
    raw = nn(rows, weight)
    heads = []
    for j in range(local + 2):
        block = raw[:, j * HD : (j + 1) * HD]
        if j <= local:
            block = turn(block, cosines, sines)
        heads.append(block.astype(bf16))
        heads_ref[:, :, j * HD : (j + 1) * HD] = heads[j].reshape(seq_count, tokens, HD)
    heads_ref.send()
    key, value = heads[local], heads[local + 1]
    scale = HD ** (-0.5)
    for j in range(local):
        query = heads[j]
        for rows, seen in ((slice(0, prompt), prompt), (slice(prompt, group), group)):
            scores = nt(query[rows], key[:seen]) * scale + bias_ref[rows, :seen]
            peak = jnp.max(scores, axis=-1, keepdims=True)
            weights = jnp.exp(scores - peak)
            weights = weights / jnp.sum(weights, axis=-1, keepdims=True)
            part = nn(weights.astype(bf16), value[:seen]).astype(bf16)
            first = rows.start // tokens
            out_ref[first : first + prompt // tokens, :, j * HD : (j + 1) * HD] = part.reshape(
                prompt // tokens, tokens, HD
            )


def first_attention_kernel(
    place, own, one, two, three, weight, spread, cosines, sines, bias_ref,
    heads_ref, out_ref, normed_ref, small_ref,
):
    expert_count = 8
    me = place[0]
    seq_count, tokens, width = normed_ref.shape
    columns = heads_ref.shape[2]
    count = small_ref.shape[1]
    extras = weight[:, columns:].astype(f32).T.astype(bf16)
    extras = jnp.concatenate([extras[:count], extras[HD : HD + count]], axis=0)
    small = jnp.concatenate(to_natural(extras, spread[...]), axis=1)
    small_ref[0] = small[:count].astype(bf16)
    small_ref[1] = small[count:].astype(bf16)
    small_ref.send()
    gain = small[expert_count : expert_count + 1]
    for k, block in enumerate((own, one, two, three)):
        normed = normalize(block[...].astype(f32), gain).astype(bf16)
        normed = to_gathered(column_blocks(normed, seq_count), spread[...]).astype(bf16)
        normed_ref[lax.rem(me + k, seq_count)] = normed
    normed_ref.send()
    rows = normed_ref[...].reshape(seq_count * tokens, width)
    attend(rows, weight[:, :columns], cosines[...], sines[...], bias_ref, heads_ref, out_ref)


def next_attention_kernel(
    place, own, one, two, three, weight, cosines, sines, bias_ref, heads_ref, out_ref, normed_ref
):
    me = place[0]
    seq_count, tokens, width = normed_ref.shape
    weight = weight[...].reshape(width, weight.shape[2])[:, : heads_ref.shape[2]]
    for k, block in enumerate((own, one, two, three)):
        normed_ref[lax.rem(me + k, seq_count)] = block[...]
    normed_ref.send()
    rows = normed_ref[...].reshape(seq_count * tokens, width)
    attend(rows, weight, cosines[...], sines[...], bias_ref, heads_ref, out_ref)


def gates_of(logits, routes_t, rows):
    expert_count = 8
    tokens = logits.shape[1]
    chosen = []
    for k in range(TOPK):
        route = routes_t[k : k + 1]
        value = jnp.zeros((1, tokens), f32)
        for e in range(expert_count):
            value = value + jnp.where(route == e, logits[e : e + 1], 0.0)
        chosen.append(value)
    peak = functools.reduce(jnp.maximum, chosen)
    powers = [jnp.exp(value - peak) for value in chosen]
    total = functools.reduce(jnp.add, powers)
    gates = [power / total for power in powers]
    return jnp.concatenate(gates + [jnp.zeros((rows - TOPK, tokens), f32)], axis=0)


def after_attention_kernel(
    back, spread, hidden, small, out_w, routes_t, middle_ref, normed_ref, gates_ref
):
    expert_count = 8
    seq_count, tokens, part = back.shape
    width = seq_count * part
    attended = to_gathered([back[s] for s in range(seq_count)], spread[...]).astype(bf16)
    rows = out_w.shape[1] // 2
    half = out_w.shape[2]
    for side in range(2):
        weight = out_w[:, side * rows : (side + 1) * rows].reshape(width, half)
        cols = slice(side * half, (side + 1) * half)
        middle_ref[:, cols] = hidden[:, cols].astype(f32) + nn(attended, weight)
    middle_ref.send()
    middle = middle_ref[...]
    gain = small[expert_count + 1 : expert_count + 2].astype(f32)
    normed = normalize(middle, gain).astype(bf16)
    normed_ref[...] = normed
    normed_ref.send()
    gates_ref[...] = gates_of(nt(small[...], normed), routes_t[...], gates_ref.shape[0])


def down_parts(block):
    shards, rows, half = block.shape
    wide = block.astype(f32)
    left = wide[:, : rows // 2].reshape(shards * rows // 2, half).astype(bf16)
    right = wide[:, rows // 2 :].reshape(shards * rows // 2, half).astype(bf16)
    return left, right


def expert_kernel(place, own, one, two, three, targets, routes, small, *rest):
    me = place[0]
    blocks = (own, one, two, three)
    out_ref, rows_ref, gate_ref, up_ref, gates_ref = rest[-5:]
    weights = rest[:-5]
    sources, experts, capacity, width = out_ref.shape
    half = width // 2
    for e in range(experts):
        gate_w, up_w, down_w = weights[3 * e : 3 * e + 3]
        first = (me * experts + e) * capacity
        parts = []
        for k, block in enumerate(blocks):
            hot = choose(targets[lax.rem(me + k, sources)] - first, capacity)
            parts.append(nn(hot.astype(bf16), block[...]))
        tokens = jnp.concatenate(parts, axis=0).astype(bf16)
        rows_ref[e] = tokens
        rows_ref.send(e)
        gate_val = nn(tokens, gate_w[...].reshape(width, half))
        gate_ref[e] = gate_val.astype(bf16)
        gate_ref.send(e)
        up_val = nn(tokens, up_w[...].reshape(width, half))
        up_ref[e] = up_val.astype(bf16)
        up_ref.send(e)
        activated, slope = smooth_parts(gate_val)
        inner = (activated * up_val).astype(bf16)
        for side, part in enumerate(down_parts(down_w[...])):
            done = nn(inner, part).astype(bf16)
            for k in range(sources):
                out_ref[lax.rem(me + k, sources), e, :, side * half : (side + 1) * half] = done[
                    k * capacity : (k + 1) * capacity
                ]
        out_ref.send(e)
    for k, block in enumerate(blocks):
        logits = nt(small[...], block[...])
        gates_ref[k] = gates_of(logits, routes[lax.rem(me + k, sources)], gates_ref.shape[1])


def logits_grad_kernel(grad, combined, gates_t, routes_t, target_t, logits_ref):
    tokens = grad.shape[0]
    slots = combined.shape[0]
    high, low = split(grad[...])
    products = nt(combined[...], jnp.concatenate([high, low], axis=0))
    products = products[:, :tokens] + products[:, tokens:]
    place = lax.broadcasted_iota(jnp.int32, (slots, tokens), 0)
    grad_gates = [
        jnp.sum(jnp.where(place == target_t[k : k + 1], products, 0.0), axis=0, keepdims=True)
        for k in range(TOPK)
    ]
    gates = [gates_t[k : k + 1] for k in range(TOPK)]
    center = functools.reduce(jnp.add, [a * b for a, b in zip(gates, grad_gates)])
    label = lax.broadcasted_iota(jnp.int32, logits_ref.shape, 0)
    total = jnp.zeros(logits_ref.shape, f32)
    for k in range(TOPK):
        choice = gates[k] * (grad_gates[k] - center)
        total = total + jnp.where(label == routes_t[k : k + 1], choice, 0.0)
    logits_ref[...] = total.astype(bf16)


def expert_back_kernel(
    place, own, one, two, three, targets, gates, down_first, gate_ref, up_ref, *rest
):
    me = place[0]
    blocks = (own, one, two, three)
    out_ref, rows_ref, gate_grad_ref, up_grad_ref, inner_ref = rest[-5:]
    weights = (down_first,) + rest[:-5]
    sources, experts, capacity, width = out_ref.shape
    half = width // 2
    for e in range(experts):
        down_w, gate_w, up_w = weights[3 * e : 3 * e + 3]
        shards, rows, _ = gate_w.shape
        first = (me * experts + e) * capacity
        parts = []
        for k, block in enumerate(blocks):
            target = targets[lax.rem(me + k, sources)] - first
            hot = jnp.concatenate(split(choose_weighted(target, gates[k], capacity)), axis=1)
            twice = jnp.concatenate([block[...], block[...]], axis=0)
            parts.append(nn(hot, twice))
        grad = jnp.concatenate(parts, axis=0).astype(bf16)
        rows_ref[e] = grad
        rows_ref.send(e)
        left, right = down_parts(down_w[...])
        grad_inner = nt(grad[:, :half], left) + nt(grad[:, half:], right)
        up_val = up_ref[e].astype(f32)
        activated, slope = smooth_parts(gate_ref[e].astype(f32))
        inner_ref[e] = (activated * up_val).astype(bf16)
        inner_ref.send(e)
        gate_grad_ref[e] = (grad_inner * up_val * slope).astype(bf16)
        gate_grad_ref.send(e)
        up_grad_ref[e] = (grad_inner * activated).astype(bf16)
        up_grad_ref.send(e)
        parts = 4
        some, size = shards // parts, shards * rows // parts
        for c in range(parts):
            at = slice(c * some, (c + 1) * some)
            total = nt(gate_grad_ref[e], gate_w[at].reshape(size, half))
            total = total + nt(up_grad_ref[e], up_w[at].reshape(size, half))
            total = total.astype(bf16)
            for k in range(sources):
                out_ref[lax.rem(me + k, sources), e, :, c * size : (c + 1) * size] = total[
                    k * capacity : (k + 1) * capacity
                ]
        out_ref.send(e)


def expert_weight_kernel(rows_ref, grad_ref, gate_grad_ref, up_grad_ref, inner_ref, *rest):
    pack_ref = rest[-1]
    experts, _, width = rows_ref.shape
    shards, _, half = pack_ref.shape
    rows = width // shards
    at = 0

    def send(start, count):
        for piece in range(start // 16, (start + count) // 16):
            pack_ref.send(piece)

    for e in range(experts):
        grads = jnp.concatenate([gate_grad_ref[e], up_grad_ref[e]], axis=1)
        both = tn(rows_ref[e], grads).astype(bf16)
        pack_ref[:, at : at + rows] = both[:, :half].reshape(shards, rows, half)
        pack_ref[:, at + rows : at + 2 * rows] = both[:, half:].reshape(shards, rows, half)
        send(at, 2 * rows)
        down = tn(inner_ref[e], grad_ref[e])
        left = down[:, :half].reshape(shards, rows // 2, half)
        right = down[:, half:].reshape(shards, rows // 2, half)
        down = jnp.concatenate([left, right], axis=1).astype(bf16)
        pack_ref[:, at + 2 * rows : at + 3 * rows] = down
        send(at + 2 * rows, rows)
        at += 3 * rows
    for extra in rest[:-1]:
        pack_ref[:, at : at + extra.shape[1]] = extra[...]
        at += extra.shape[1]


def after_experts_kernel(
    grad, sent, middle, normed, logits_grad, target_t, small, out_w, spread,
    grad_ref, branch_ref, send_ref, small_ref,
):
    expert_count = 8
    seq_count, tokens, part = send_ref.shape
    width = seq_count * part
    chosen = choose(target_t[...], sent.shape[0]).astype(bf16)
    grad_normed = tn(chosen, sent[...]) + tn(logits_grad[...], small[...])
    router = nn(logits_grad[...], normed[...])
    gain = small[expert_count + 1 : expert_count + 2].astype(f32)
    grad_value, grad_gain = normalize_back(middle[...], gain, grad_normed)
    label = lax.broadcasted_iota(jnp.int32, small_ref.shape, 0)
    small_ref[...] = jnp.where(label == expert_count + 1, grad_gain, router)
    grad_middle = grad[...] + grad_value
    grad_ref[...] = grad_middle
    grad_ref.send()
    branch = grad_middle.astype(bf16)
    branch_ref[...] = branch
    branch_ref.send()
    rows = out_w.shape[1] // 2
    half = out_w.shape[2]
    parts = [
        nt(branch[:, :half], out_w[:, :rows].reshape(width, half)),
        nt(branch[:, half:], out_w[:, rows:].reshape(width, half)),
    ]
    attended = (parts[0] + parts[1]).astype(bf16)
    for s, block in enumerate(to_natural(attended, spread[...])):
        send_ref[s] = block.astype(bf16)


def attention_back_kernel(heads_ref, grad_ref, bias_ref, cosines, sines, out_ref):
    seq_count, tokens, columns = heads_ref.shape
    group = seq_count * tokens
    heads = heads_ref[...].reshape(group, columns)
    grads = grad_ref[...].reshape(group, grad_ref.shape[2])
    local = columns // HD - 2
    prompt = group // 2
    key = heads[:, local * HD : (local + 1) * HD]
    value = heads[:, (local + 1) * HD :]
    scale = HD ** (-0.5)

    def keep(at, block):
        out_ref[:, :, at * HD : (at + 1) * HD] = block.astype(bf16).reshape(seq_count, tokens, HD)

    cosines, sines = cosines[...], sines[...]

    def unturn(block):
        return block * cosines - pltpu.roll(block, HD // 2, 1) * sines

    grad_key = [jnp.zeros((prompt, HD), f32), jnp.zeros((prompt, HD), f32)]
    grad_value = [jnp.zeros((prompt, HD), f32), jnp.zeros((prompt, HD), f32)]
    for j in range(local):
        query = heads[:, j * HD : (j + 1) * HD]
        grad = grads[:, j * HD : (j + 1) * HD]
        grad_query = []
        for rows, seen in ((slice(0, prompt), prompt), (slice(prompt, group), group)):
            scores = nt(query[rows], key[:seen]) * scale + bias_ref[rows, :seen]
            peak = jnp.max(scores, axis=-1, keepdims=True)
            weights = jnp.exp(scores - peak)
            weights = weights / jnp.sum(weights, axis=-1, keepdims=True)
            grad_weights = nt(grad[rows], value[:seen])
            center = jnp.sum(weights * grad_weights, axis=-1, keepdims=True)
            grad_scores = (weights * (grad_weights - center)).astype(bf16)
            low = weights.astype(bf16)
            grad_query.append(nn(grad_scores, key[:seen]) * scale)
            for side in range(seen // prompt):
                cols = slice(side * prompt, (side + 1) * prompt)
                grad_key[side] = grad_key[side] + tn(grad_scores[:, cols], query[rows])
                grad_value[side] = grad_value[side] + tn(low[:, cols], grad[rows])
        keep(j, unturn(jnp.concatenate(grad_query, axis=0)))
    keep(local, unturn(jnp.concatenate(grad_key, axis=0) * scale))
    keep(local + 1, jnp.concatenate(grad_value, axis=0))


def before_attention_kernel(
    sent, left_w, right_w, kv_w, spread, small, hidden, grad_middle, out_ref, low_ref, gain_ref
):
    expert_count = 8
    seq_count, tokens, columns = sent.shape
    local = columns // HD - 2
    share = seq_count // KVHEADS
    blocks = [sent[s, :, : local * HD] for s in range(seq_count)]
    for at in (local, local + 1):
        for c in range(KVHEADS):
            total = jnp.zeros((tokens, HD), f32)
            for s in range(c * share, (c + 1) * share):
                total = total + sent[s, :, at * HD : (at + 1) * HD].astype(f32)
            blocks.append(total.astype(bf16))
    raw = jnp.concatenate(blocks, axis=1)
    at, total = 0, 0.0
    for part in (left_w, right_w, kv_w):
        shards, rows, columns = part.shape
        weight = part[...].reshape(shards * rows, columns)
        total = total + nt(raw[:, at : at + columns], weight)
        at += columns
    high, low = split(total)
    both = to_natural(jnp.concatenate([high, low], axis=0), spread[...])
    both = jnp.concatenate(both, axis=1)
    grad_normed = both[:tokens] + both[tokens:]
    gain = small[expert_count : expert_count + 1].astype(f32)
    grad_value, grad_gain = normalize_back(hidden[...].astype(f32), gain, grad_normed)
    total = grad_middle[...] + grad_value
    low_ref[...] = total.astype(bf16)
    low_ref.send()
    out_ref[...] = total
    out_ref.send()
    shards = gain_ref.shape[0]
    width = grad_gain.shape[1]
    share = width // seq_count
    part = share // shards
    shard = lax.broadcasted_iota(jnp.int32, (shards, width), 0)
    at = lax.broadcasted_iota(jnp.int32, (shards, width), 1)
    kept = jnp.where(at % share // part == shard, grad_gain, 0.0).astype(bf16)
    source = lax.broadcasted_iota(jnp.int32, (width, HD), 0)
    wanted = lax.broadcasted_iota(jnp.int32, (width, HD), 1)
    place = source // share * part + source % part
    gain_ref[...] = nn(kept, jnp.where(place == wanted, 1.0, 0.0).astype(bf16))


def qkv_weight_kernel(normed, grads, small, spread, out_ref):
    seq_count, tokens, columns = grads.shape
    shards, rows, wide = out_ref.shape
    inputs = normed[...].reshape(seq_count * tokens, normed.shape[2])
    total = tn(inputs, grads[...].reshape(seq_count * tokens, columns))
    out_ref[:, :, :columns] = total.astype(bf16).reshape(shards, rows, columns)
    extra = column_blocks(small[...].astype(bf16), seq_count)
    extra = to_gathered(extra, spread[...])
    extra = jnp.concatenate([extra, jnp.zeros((HD - extra.shape[0], extra.shape[1]), f32)], axis=0).T
    out_ref[:, :, columns:] = extra.astype(bf16).reshape(shards, rows, wide - columns)


def out_weight_kernel(place, own, one, two, three, *rest):
    out_ref = rest[-1]
    me = place[0]
    shards, rows, half = out_ref.shape
    rows = rows // (2 * LAYERS)
    for layer in range(LAYERS):
        attended, gain = rest[layer], rest[LAYERS + layer]
        seq_count, tokens, part = attended.shape
        valid = part // shards
        branch = jnp.concatenate([block[layer] for block in (own, one, two, three)], axis=0)
        heads = jnp.concatenate(
            [attended[lax.rem(me + k, seq_count)] for k in range(seq_count)], axis=0
        )
        place_in = lax.broadcasted_iota(jnp.int32, (part, shards * rows), 0)
        place_out = lax.broadcasted_iota(jnp.int32, (part, shards * rows), 1)
        source = place_out // rows * valid + place_out % rows
        same = jnp.logical_and(place_in == source, place_out % rows < valid)
        heads = nn(heads, jnp.where(same, 1.0, 0.0).astype(bf16)).astype(bf16)
        wide = jnp.concatenate([gain[...], jnp.zeros((shards, half - HD), f32)], axis=1)
        row = lax.broadcasted_iota(jnp.int32, (shards, rows, half), 1)
        for side in range(2):
            total = tn(heads, branch[:, side * half : (side + 1) * half])
            total = total.reshape(shards, rows, half)
            if side == 0:
                total = jnp.where(row == valid, wide[:, None, :], total)
            at = (2 * layer + side) * rows
            out_ref[:, at : at + rows] = total.astype(bf16)


def expert_grads_kernel(*refs):
    sums, (gate_ref, up_ref, down_ref) = refs[:LAYERS], refs[LAYERS:]
    rows = gate_ref.shape[2]
    half = gate_ref.shape[3]
    for layer in range(LAYERS):
        block = sums[layer][...].astype(f32)
        for e in range(gate_ref.shape[1]):
            at = 3 * rows * e
            gate_ref[layer, e] = block[at : at + rows]
            up_ref[layer, e] = block[at + rows : at + 2 * rows]
            at += 2 * rows
            down_ref[layer, e, :, :half] = block[at : at + rows // 2]
            down_ref[layer, e, :, half:] = block[at + rows // 2 : at + rows]


def dense_grads_kernel(*refs):
    blocks, outs = refs[:LAYERS], refs[LAYERS : 2 * LAYERS]
    query_ref, key_ref, value_ref, out_ref, small_ref = refs[2 * LAYERS :]
    seq_count, rows, columns = blocks[0].shape
    local = columns - 3 * HD
    share = seq_count // KVHEADS
    for layer in range(LAYERS):
        parts = [blocks[layer][s].astype(f32) for s in range(seq_count)]
        for s in range(seq_count):
            query_ref[:, layer, s * local : (s + 1) * local] = parts[s][:, :local]
        for c in range(KVHEADS):
            total = functools.reduce(jnp.add, parts[c * share : (c + 1) * share])
            key_ref[:, layer, c * HD : (c + 1) * HD] = total[:, local : local + HD]
            value_ref[:, layer, c * HD : (c + 1) * HD] = total[:, local + HD : local + 2 * HD]
        total = functools.reduce(jnp.add, parts)
        small_ref[layer] = total[:, local + 2 * HD :]
        block = outs[layer][...].astype(f32)
        half = block.shape[1]
        out_ref[:, layer, :half] = block[:rows]
        out_ref[:, layer, half:] = block[block.shape[0] // 2 :][:rows]


def swap_seq(block):
    return lax.all_to_all(block, "seq", split_axis=0, concat_axis=0, tiled=True)


def around_seq(block):
    count = lax.axis_size("seq")
    others = [
        lax.ppermute(block, "seq", [((i + k) % count, i) for i in range(count)])
        for k in range(1, count)
    ]
    return [block] + others


def halves(block):
    cut = block.shape[-1] // 2
    return jnp.concatenate([block[..., :cut], block[..., cut:]], axis=-2)


def per_device(
    tokens_in,
    cotangent,
    routes,
    order,
    segment_ids,
    gain_attn,
    w_query,
    w_key,
    w_value,
    w_out,
    gain_ffn,
    w_router,
    w_gate,
    w_up,
    w_down,
):
    tok_count = tokens_in.shape[1]
    width = tokens_in.shape[2]
    seq_count = lax.axis_size("seq")
    shard_count = lax.axis_size("fsdp")
    seq_index = lax.axis_index("seq")
    place = jnp.full((1,), seq_index, jnp.int32)
    group_tok = seq_count * tok_count
    prompt_len = group_tok - segment_ids.shape[1]
    local_experts = w_gate.shape[1]
    expert_count = local_experts * seq_count
    capacity = 9 * tok_count * TOPK // (8 * expert_count)
    total_slots = expert_count * capacity
    head_local = HEADS // seq_count
    local_width = head_local * HD
    dense_rows = w_query.shape[1]
    shard_rows = dense_rows * seq_count
    gate_rows = w_gate.shape[2]
    down_rows = w_down.shape[2]
    expert_rows = 2 * gate_rows + 2 * down_rows
    qkv_width = (HEADS + 2 * KVHEADS) * HD
    half_width = width // 2
    inner_width = w_gate.shape[3]
    slot_rows = seq_count * capacity

    cos_half, sin_half, labels = group_tables(segment_ids[0], prompt_len)
    cos_all = jnp.concatenate([cos_half, cos_half], axis=1)
    sin_all = jnp.concatenate([-sin_half, sin_half], axis=1)
    cos_own = lax.dynamic_slice_in_dim(cos_all, seq_index * tok_count, tok_count, 0)
    sin_own = lax.dynamic_slice_in_dim(sin_all, seq_index * tok_count, tok_count, 0)
    key_pos = jnp.arange(group_tok, dtype=jnp.int32)
    allowed = jnp.logical_and(
        key_pos[None, :] <= key_pos[:, None],
        jnp.logical_or(key_pos[None, :] < prompt_len, labels[None, :] == labels[:, None]),
    )
    bias = jnp.where(allowed, 0.0, masked_value)

    column = jnp.arange(width // seq_count, dtype=jnp.int32)
    natural = (
        column % shard_rows // dense_rows * (width // seq_count // seq_count)
        + column // shard_rows * dense_rows
        + column % dense_rows
    )
    spread = (column[:, None] == natural[None, :]).astype(bf16)

    def small_rows_of(layer):
        return jnp.concatenate(
            [
                w_router[layer],
                gain_attn[layer][:, None],
                gain_ffn[layer][:, None],
                jnp.zeros((dense_rows, HD - 2 - expert_count), bf16),
            ],
            axis=1,
        )

    def dense_rows_of(layer):
        return jnp.concatenate(
            [w_query[layer], w_key[layer], w_value[layer], small_rows_of(layer), w_out[layer]],
            axis=1,
        )

    def spread_seq(dense):
        dense = swap_seq(jnp.broadcast_to(dense[None], (seq_count,) + dense.shape))
        return dense.reshape(shard_rows, dense.shape[2])

    def own_columns(weight):
        pick = seq_index * KVHEADS // seq_count
        starts = (seq_index * local_width, (HEADS + pick) * HD, (HEADS + KVHEADS + pick) * HD)
        parts = [
            lax.dynamic_slice_in_dim(weight, start, size, 1)
            for start, size in zip(starts, (local_width, HD, HD))
        ]
        return jnp.concatenate(parts + [weight[:, qkv_width : qkv_width + HD]], axis=1)

    def expert_part(layer):
        return [
            part
            for e in range(local_experts)
            for part in (w_gate[layer, e], w_up[layer, e], halves(w_down[layer, e]))
        ]

    def out_part(dense):
        return [halves(dense[:, qkv_width + HD :])]

    def qkv_part(dense):
        wide = jnp.concatenate(
            [dense[:, : qkv_width + HD], jnp.zeros((shard_rows, HD), bf16)], axis=1
        )
        return [wide[:, at : at + half_width] for at in range(0, wide.shape[1], half_width)]

    def fetch(parts):
        return lax.all_gather(jnp.concatenate(parts, axis=0), "fsdp", axis=0, tiled=False)

    core = lax.rem(lax.axis_index("fsdp"), 2)
    chips = [[i + c for i in range(0, shard_count, 2)] for c in range(2)]

    def swap_chips(block):
        return lax.all_to_all(
            block, "fsdp", split_axis=0, concat_axis=0, tiled=True, axis_index_groups=chips
        )

    def swap_cores(block):
        return lax.ppermute(block, "fsdp", [(i, i ^ 1) for i in range(shard_count)])

    def both_cores(block):
        other = swap_cores(block)
        first = jnp.where(core == 0, block, other)
        second = jnp.where(core == 0, other, block)
        return jnp.stack([first, second], axis=1).reshape((shard_count,) + block.shape[1:])

    def to_chips(block):
        return swap_chips(jnp.broadcast_to(block[None], (shard_count // 2,) + block.shape))

    weight_parts = [
        (e * expert_rows + k * gate_rows, gate_rows) for e in range(local_experts) for k in range(3)
    ]
    back_parts = [weight_parts[3 * e + k] for e in range(local_experts) for k in (2, 0, 1)]
    out_cut = ((1, local_experts * expert_rows, 2 * shard_rows),)

    slots_shape = shape((seq_count, local_experts, capacity, width), bf16)
    inner_shape = (local_experts, slot_rows, inner_width)
    expert_flops = 6 * total_slots * width * inner_width
    dense_flops = 2 * tok_count * width * width
    records = []
    hidden = tokens_in[0]
    dense = spread_seq(jnp.concatenate([dense_rows_of(0), small_rows_of(1)], axis=1))
    columns = jnp.concatenate([own_columns(dense), dense[:, -HD:]], axis=1)
    dense = dense[:, :-HD]
    columns, hidden = lax.optimization_barrier((columns, hidden))
    token_blocks = around_seq(hidden)
    packs = [fetch(expert_part(0) + out_part(dense)), None]
    columns = to_chips(columns)
    pairs = jnp.concatenate(
        [array[layer, 0].T for array in (routes, order) for layer in range(LAYERS)], axis=0
    )
    pairs = swap_seq(jnp.broadcast_to(pairs[None], (seq_count,) + pairs.shape))
    pairs = pairs.reshape(seq_count, 2, LAYERS, TOPK, tok_count)
    slots_of = functools.partial(slot_table, expert_count=expert_count, capacity=capacity)
    all_routes = [pairs[:, 0, layer] for layer in range(LAYERS)]
    all_targets = [
        jax.vmap(slots_of)(pairs[:, 0, layer], pairs[:, 1, layer]) for layer in range(LAYERS)
    ]
    early = (token_blocks, all_targets, all_routes, cos_all, sin_all, bias, spread)
    columns, early, next_rows = lax.optimization_barrier((columns, early, dense_rows_of(1)))
    token_blocks, all_targets, all_routes, cos_all, sin_all, bias, spread = early
    targets = [lax.dynamic_index_in_dim(t, seq_index, 0, False) for t in all_targets]
    routes_ts = [lax.dynamic_index_in_dim(t, seq_index, 0, False) for t in all_routes]
    first_columns = both_cores(columns).reshape(width, columns.shape[2])
    next_dense = spread_seq(next_rows)
    own_at = local_experts * expert_rows + 2 * shard_rows
    grad_blocks = around_seq(cotangent[0])

    heads_shape = shape((seq_count, tok_count, local_width + 2 * HD), bf16)
    attended_shape = shape((seq_count, tok_count, local_width), bf16)
    normed_shape = shape((seq_count, tok_count, width), bf16)
    small_shape = shape((LAYERS, 2 * expert_count, width), bf16)
    attention_flops = 4 * head_local * group_tok * group_tok * HD + 2 * dense_flops
    for layer in range(LAYERS):
        pack, routes_t, target_t = packs[layer], routes_ts[layer], targets[layer]
        if layer == 0:
            heads, attended, normed_all, smalls = once(
                first_attention_kernel,
                [heads_shape, attended_shape, normed_shape, small_shape],
                place, *token_blocks, first_columns, spread, cos_all, sin_all, bias,
                scalar=True, flops=attention_flops + 4 * dense_flops,
            )
            small = smalls[layer]
        else:
            small = smalls[layer]
            normed_p, hidden = once(
                input_kernel,
                [shape((tok_count, width), bf16), shape((tok_count, width), f32)],
                middle, combined, gates_t, above_target, small, spread, flops=2 * dense_flops,
            )
            heads, attended, normed_all = once(
                next_attention_kernel,
                [heads_shape, attended_shape, normed_shape],
                place, *around_seq(normed_p), pack, cos_all, sin_all, bias,
                scalar=True, cut={5: ((1, own_at, shard_rows),)}, flops=attention_flops,
            )
        back = swap_seq(attended)
        if layer == 0:
            next_parts = expert_part(1) + out_part(next_dense) + [own_columns(next_dense)]
            next_parts = jnp.concatenate(next_parts, axis=0)
            tied = lax.optimization_barrier((pack, next_parts, back, grad_blocks))
            pack, next_parts, back, grad_blocks = tied
            packs = [pack, fetch([next_parts])]
        else:
            qkv_parts = jnp.concatenate(qkv_part(dense) + qkv_part(next_dense), axis=0)
            qkv_parts, back = lax.optimization_barrier((qkv_parts, back))
            qkv_w = fetch([qkv_parts])
        middle, normed_ffn, gates_t = once(
            after_attention_kernel,
            [
                shape((tok_count, width), f32),
                shape((tok_count, width), bf16),
                shape((2 * TOPK, tok_count), f32),
            ],
            back, spread, hidden, small, pack, routes_t,
            cut={4: out_cut}, flops=3 * dense_flops,
        )
        expert_out, received, gate_val, up_val, all_gates = once(
            expert_kernel,
            [
                slots_shape,
                shape((local_experts, slot_rows, width), bf16),
                shape(inner_shape, bf16),
                shape(inner_shape, bf16),
                shape((seq_count, 2 * TOPK, tok_count), f32),
            ],
            place, *around_seq(normed_ffn), all_targets[layer], all_routes[layer], small,
            *[pack] * len(weight_parts),
            scalar=True,
            cut={n + 8: ((1, *part),) for n, part in enumerate(weight_parts)},
            pieces={n: (1 if n == 0 else 0, local_experts) for n in range(4)},
            flops=expert_flops,
        )
        combined = swap_seq(expert_out).reshape(total_slots, width)
        above_target = target_t
        records.append(
            (
                (pack, small, routes_t, target_t),
                (hidden, normed_all, heads, attended),
                (middle, normed_ffn, gates_t, combined),
                (received, gate_val, up_val, all_gates),
            )
        )
    (result,) = once(
        result_kernel, [shape((tok_count, width), bf16)], middle, combined, gates_t, target_t,
        flops=dense_flops,
    )

    def scatter(block):
        return lax.psum_scatter(block, "fsdp", scatter_dimension=0, tiled=False)

    def spread_qkv(block, out_block):
        gain = out_block[dense_rows, :shard_rows]
        label = jnp.arange(local_width + 3 * HD)[None, :]
        block = jnp.where(label == local_width + 2 * HD + expert_count, gain[:, None], block)
        return swap_seq(block.reshape(seq_count, dense_rows, local_width + 3 * HD))

    out_rows = 16

    grad_hidden = cotangent[0].astype(f32)
    sums, gains = [None] * LAYERS, [None] * LAYERS
    branches, attendeds = [None] * LAYERS, [None] * LAYERS
    waiting = None
    for layer in range(LAYERS - 1, -1, -1):
        weights, attn_saved, mid_saved, expert_saved = records[layer]
        pack, small, routes_t, target_t = weights
        row = layer * 3 * shard_rows
        below, normed_all, heads, attended = attn_saved
        middle, normed_ffn, gates_t, combined = mid_saved
        received, gate_val, up_val, all_gates = expert_saved
        if waiting is None:
            tied = lax.optimization_barrier((grad_blocks, qkv_w, result, combined))
            grad_blocks, qkv_w, result, combined = tied
        else:
            grad_blocks, waiting = lax.optimization_barrier((grad_blocks, waiting))
        grad_rows, grad_expert, gate_grad, up_grad, inner = once(
            expert_back_kernel,
            [slots_shape, shape((local_experts, slot_rows, width), bf16)]
            + [shape(inner_shape, bf16)] * 3,
            place, *grad_blocks, all_targets[layer], all_gates, pack, gate_val, up_val,
            *[pack] * (len(back_parts) - 1),
            scalar=True,
            cut={n + 9 if n else 7: ((1, *part),) for n, part in enumerate(back_parts)},
            pieces={n: (1 if n == 0 else 0, local_experts) for n in range(5)},
            flops=expert_flops,
        )
        (logits_grad,) = once(
            logits_grad_kernel,
            [shape((2 * expert_count, tok_count), bf16)],
            grad_hidden, combined, gates_t, routes_t, target_t, flops=3 * dense_flops,
        )
        sent = swap_seq(grad_rows)
        extra = () if layer == LAYERS - 1 else waiting
        extra_rows = sum(a.shape[1] for a in extra)
        (packed,) = once(
            expert_weight_kernel,
            [shape((shard_count, local_experts * expert_rows + extra_rows, half_width), bf16)],
            received, grad_expert, gate_grad, up_grad, inner, *extra,
            pieces={0: (1, (local_experts * expert_rows + extra_rows) // 16)}, flops=expert_flops,
        )
        sent, packed, logits_grad = lax.optimization_barrier((sent, packed, logits_grad))
        if layer < LAYERS - 1:
            packed, sums[layer + 1] = lax.optimization_barrier((packed, sums[layer + 1]))
        summed = scatter(packed)
        grad_middle, branch, send, small_grad = once(
            after_experts_kernel,
            [
                shape((tok_count, width), f32),
                shape((tok_count, width), bf16),
                shape((seq_count, tok_count, local_width), bf16),
                shape((2 * expert_count, width), f32),
            ],
            grad_hidden, sent.reshape(total_slots, width), middle, normed_ffn, logits_grad,
            target_t, small, pack, spread,
            cut={7: out_cut}, flops=4 * dense_flops,
        )
        grad_heads = swap_seq(send)
        (grad_own,) = once(
            attention_back_kernel,
            [shape((seq_count, tok_count, local_width + 2 * HD), bf16)],
            heads, grad_heads, bias, cos_all, sin_all,
            flops=10 * head_local * group_tok * group_tok * HD,
        )
        (qkv_block_grad,) = once(
            qkv_weight_kernel,
            [shape((shard_count, shard_rows, half_width), bf16)],
            normed_all, grad_own, small_grad, spread, flops=2 * dense_flops,
        )
        sent, qkv_block_grad = lax.optimization_barrier((swap_seq(grad_own), qkv_block_grad))
        grad_hidden, grad_low, gains[layer] = once(
            before_attention_kernel,
            [
                shape((tok_count, width), f32),
                shape((tok_count, width), bf16),
                shape((shard_count, HD), f32),
            ],
            sent, qkv_w, qkv_w, qkv_w, spread, small, below, grad_middle,
            cut={
                1: ((1, row, shard_rows),),
                2: ((1, row + shard_rows, shard_rows),),
                3: ((1, row + 2 * shard_rows, shard_rows), (2, 0, 2 * KVHEADS * HD)),
            },
            flops=4 * dense_flops,
        )
        branches[layer], attendeds[layer], sums[layer] = branch, attended, summed
        if layer > 0:
            grad_blocks = around_seq(grad_low)
            waiting = (qkv_block_grad,)
    (out_block_grad,) = once(
        out_weight_kernel,
        [shape((shard_count, 2 * LAYERS * out_rows, half_width), bf16)],
        place, *around_seq(jnp.stack(branches)), *attendeds, *gains,
        scalar=True, flops=2 * dense_flops,
    )

    def shard_sum(block):
        block = block.reshape((shard_count // 2, 2) + block.shape[1:])
        own = lax.dynamic_index_in_dim(block, core, 1, False)
        other = swap_cores(lax.dynamic_index_in_dim(block, 1 - core, 1, False))
        block = (own.astype(f32) + other.astype(f32)).astype(bf16)
        return jnp.sum(swap_chips(block).astype(f32), axis=0)

    qkv_sum = shard_sum(qkv_block_grad)
    out_sum = shard_sum(out_block_grad)
    out_sums = [out_sum[2 * out_rows * n : 2 * out_rows * (n + 1)] for n in range(LAYERS)]
    own_rows = spread_qkv(qkv_sum, out_sums[0])
    above_rows = spread_qkv(sums[0][local_experts * expert_rows :].astype(f32), out_sums[1])
    gate_grads, up_grads, down_grads = once(
        expert_grads_kernel,
        [
            shape((LAYERS,) + w_gate.shape[1:], f32),
            shape((LAYERS,) + w_up.shape[1:], f32),
            shape((LAYERS,) + w_down.shape[1:], f32),
        ],
        *sums,
        cut={0: ((0, 0, local_experts * expert_rows),)},
    )
    query_grads, key_grads, value_grads, out_grads, small_grads = once(
        dense_grads_kernel,
        [
            shape((dense_rows, LAYERS, HEADS * HD), f32),
            shape((dense_rows, LAYERS, KVHEADS * HD), f32),
            shape((dense_rows, LAYERS, KVHEADS * HD), f32),
            shape((dense_rows, LAYERS, width), f32),
            shape((LAYERS, dense_rows, HD), f32),
        ],
        own_rows, above_rows, *out_sums,
    )
    return (
        result[None],
        grad_hidden[None],
        small_grads[:, :, expert_count],
        query_grads.transpose(1, 0, 2),
        key_grads.transpose(1, 0, 2),
        value_grads.transpose(1, 0, 2),
        out_grads.transpose(1, 0, 2),
        small_grads[:, :, expert_count + 1],
        small_grads[:, :, :expert_count],
        gate_grads,
        up_grads,
        down_grads,
    )


def solution(mesh):
    in_specs = (
        P("fsdp", "seq", None),
        P("fsdp", "seq", None),
        P(None, "fsdp", "seq", None),
        P(None, "fsdp", "seq", None),
        P("fsdp", None),
        P(None, ("seq", "fsdp")),
        P(None, ("seq", "fsdp"), None),
        P(None, ("seq", "fsdp"), None),
        P(None, ("seq", "fsdp"), None),
        P(None, ("seq", "fsdp"), None),
        P(None, ("seq", "fsdp")),
        P(None, ("seq", "fsdp"), None),
        P(None, "seq", "fsdp", None),
        P(None, "seq", "fsdp", None),
        P(None, "seq", "fsdp", None),
    )
    out_specs = (
        P("fsdp", "seq", None),
        P("fsdp", "seq", None),
        P(None, ("seq", "fsdp")),
        P(None, ("seq", "fsdp"), None),
        P(None, ("seq", "fsdp"), None),
        P(None, ("seq", "fsdp"), None),
        P(None, ("seq", "fsdp"), None),
        P(None, ("seq", "fsdp")),
        P(None, ("seq", "fsdp"), None),
        P(None, "seq", "fsdp", None),
        P(None, "seq", "fsdp", None),
        P(None, "seq", "fsdp", None),
    )
    return jax.shard_map(
        per_device, mesh=mesh, in_specs=in_specs, out_specs=out_specs, check_vma=False
    )
```

```python
import functools

import jax
import jax.numpy as jnp
import numpy as np
from jax import lax
from jax.experimental import pallas as pl
from jax.experimental.pallas import tpu as pltpu
from jax.sharding import PartitionSpec as P

HEADS = 12
KVHEADS = 2
HD = 128
TOPK = 4
LAYERS = 2
NCONT = 4

norm_eps = 1e-06
rope_base = 10000.0
masked_value = -1e30

bf16 = jnp.bfloat16
f32 = jnp.float32
VMEM_BYTES = 64 * 1024 * 1024 - 256 * 1024


def group_tables(segment_row, prompt_len):
    cont_len = segment_row.shape[0]
    onehot = (segment_row[:, None] == jnp.arange(NCONT, dtype=jnp.int32)[None, :]).astype(jnp.int32)
    counts = jnp.sum(onehot, axis=0)
    starts = jnp.cumsum(counts) - counts
    seg_begin = jnp.sum(onehot * starts[None, :], axis=1)
    within = jnp.arange(cont_len, dtype=jnp.int32) - seg_begin
    positions = jnp.concatenate([jnp.arange(prompt_len, dtype=jnp.int32), prompt_len + within])
    labels = jnp.concatenate([jnp.full((prompt_len,), -1, jnp.int32), segment_row])
    frequency = rope_base ** (-(jnp.arange(HD // 2, dtype=jnp.float32) * 2.0 / HD))
    angles = positions.astype(jnp.float32)[:, None] * frequency[None, :]
    return (jnp.cos(angles), jnp.sin(angles), labels)


def slot_table(routes_t, order_t, expert_count, capacity):
    pair_expert = routes_t.reshape(-1)
    pair_order = order_t.reshape(-1)
    same_expert = pair_expert[:, None] == pair_expert[None, :]
    earlier = pair_order[None, :] < pair_order[:, None]
    pair_slot = jnp.sum(jnp.logical_and(same_expert, earlier).astype(jnp.int32), axis=1)
    target = jnp.where(
        pair_slot < capacity, pair_expert * capacity + pair_slot, expert_count * capacity
    )
    return target.reshape(routes_t.shape)


def nn(left, right):
    return lax.dot_general(left, right, (((1,), (0,)), ((), ())), preferred_element_type=f32)


def nt(left, right):
    return lax.dot_general(left, right, (((1,), (1,)), ((), ())), preferred_element_type=f32)


def tn(left, right):
    return lax.dot_general(left, right, (((0,), (0,)), ((), ())), preferred_element_type=f32)


def split(value):
    high = value.astype(bf16)
    return high, (value - high.astype(f32)).astype(bf16)


class Late:
    def __init__(self, ref, copy):
        self.ref, self.copy, self.shape = ref, copy, ref.shape
        copy.start()

    def wait(self):
        if self.copy is not None:
            self.copy.wait()
            self.copy = None

    def __getitem__(self, index):
        self.wait()
        return self.ref[index]


class Out:
    def __init__(self, ref, copies):
        self.ref, self.copies, self.shape = ref, copies, ref.shape
        self.sent = [False] * len(copies)

    def send(self, piece=None):
        for n in range(len(self.copies)) if piece is None else (piece,):
            if not self.sent[n]:
                self.copies[n].start()
                self.sent[n] = True

    def __getitem__(self, index):
        return self.ref[index]

    def __setitem__(self, index, value):
        self.ref[index] = value


def cost(args, outs, flops):
    moved = sum(int(np.prod(a.shape)) * a.dtype.itemsize for a in (*args, *outs))
    return pl.CostEstimate(flops=flops, bytes_accessed=moved, transcendentals=0)


def once(kernel, outs, *args, scalar=False, cut=None, pieces=None, flops=0):
    cut, pieces = cut or {}, pieces or {}
    hbm = pl.BlockSpec(memory_space=pltpu.HBM)
    late = [n for n in range(len(args)) if not (scalar and n == 0)]
    specs = [hbm] * len(args)
    if scalar:
        specs[0] = pl.BlockSpec(memory_space=pltpu.SMEM)
    scratch = []
    for n in late:
        dims = list(args[n].shape)
        for dim, start, size in cut.get(n, ()):
            dims[dim] = size
        scratch.append(pltpu.VMEM(tuple(dims), args[n].dtype))
    scratch += [pltpu.VMEM(o.shape, o.dtype) for o in outs]
    parts = [pieces.get(n, (0, 1)) for n in range(len(outs))]
    scratch.append(pltpu.SemaphoreType.DMA((len(late) + sum(count for _, count in parts),)))

    def body(*refs):
        ins = list(refs[: len(args)])
        out_refs = refs[len(args) : len(args) + len(outs)]
        rooms = refs[len(args) + len(outs) : -1]
        sems = refs[-1]
        for i, n in enumerate(late):
            source = ins[n]
            for dim, start, size in cut.get(n, ()):
                if callable(start):
                    start = pl.multiple_of(start(ins[0][0]), 16 if dim == 1 else HD)
                source = source.at[(slice(None),) * dim + (pl.ds(start, size),)]
            ins[n] = Late(rooms[i], pltpu.make_async_copy(source, rooms[i], sems.at[i]))
        results = []
        used = len(late)
        for i, out in enumerate(out_refs):
            room = rooms[len(late) + i]
            dim, count = parts[i]
            size = room.shape[dim] // count
            copies = []
            for n in range(count):
                at = (slice(None),) * dim + (pl.ds(n * size, size),)
                copies.append(pltpu.make_async_copy(room.at[at], out.at[at], sems.at[used]))
                used += 1
            results.append(Out(room, copies))
        kernel(*ins, *results)
        for result in results:
            result.send()
        for n in late:
            ins[n].wait()
        for result in results:
            for copy in result.copies:
                copy.wait()

    return pl.pallas_call(
        body,
        out_shape=list(outs),
        in_specs=specs,
        out_specs=[hbm] * len(outs),
        scratch_shapes=scratch,
        compiler_params=pltpu.CompilerParams(vmem_limit_bytes=VMEM_BYTES),
        cost_estimate=cost(args, outs, flops),
    )(*args)


def shape(dims, dtype):
    return jax.ShapeDtypeStruct(dims, dtype)


def normalize(value, gain):
    inverse = lax.rsqrt(jnp.mean(value * value, axis=-1, keepdims=True) + norm_eps)
    return value * inverse * gain


def normalize_back(value, gain, grad):
    inverse = lax.rsqrt(jnp.mean(value * value, axis=-1, keepdims=True) + norm_eps)
    unit = value * inverse
    grad_gain = jnp.sum(grad * unit, axis=0, keepdims=True)
    scaled = grad * gain
    grad_value = inverse * (scaled - unit * jnp.mean(scaled * unit, axis=-1, keepdims=True))
    return grad_value, grad_gain


def to_gathered(parts, order):
    count = len(parts)
    share = parts[0].shape[1] // count
    done = []
    for j in range(count):
        piece = jnp.concatenate([part[:, j * share : (j + 1) * share] for part in parts], axis=1)
        done.append(nn(piece, order))
    return jnp.concatenate(done, axis=1)


def to_natural(value, order):
    count = value.shape[1] // order.shape[0]
    size = order.shape[0]
    share = size // count
    done = [nt(value[:, j * size : (j + 1) * size], order) for j in range(count)]
    return [
        jnp.concatenate([part[:, s * share : (s + 1) * share] for part in done], axis=1)
        for s in range(count)
    ]


def column_blocks(value, count):
    size = value.shape[1] // count
    return [value[:, s * size : (s + 1) * size] for s in range(count)]


def turn(block, cosines, sines):
    return block * cosines + pltpu.roll(block, HD // 2, 1) * sines


def smooth_parts(value):
    root = np.float32(np.sqrt(2.0 / np.pi))
    square = value * value
    high = jnp.tanh(root * (value + 0.044715 * value * square))
    half = 0.5 * (1.0 + high)
    slope = half + 0.5 * value * (1.0 - high * high) * root * (1.0 + 3 * 0.044715 * square)
    return value * half, slope


def choose(target_t, slots):
    place = lax.broadcasted_iota(jnp.int32, (slots, target_t.shape[1]), 0)
    total = jnp.zeros(place.shape, f32)
    for k in range(TOPK):
        total = total + jnp.where(place == target_t[k : k + 1], 1.0, 0.0)
    return total


def choose_weighted(target_t, gates_t, slots):
    place = lax.broadcasted_iota(jnp.int32, (slots, target_t.shape[1]), 0)
    total = jnp.zeros(place.shape, f32)
    for k in range(TOPK):
        total = total + jnp.where(place == target_t[k : k + 1], gates_t[k : k + 1], 0.0)
    return total


def input_kernel(
    middle, combined, gates_t, target_t, small, spread, normed_ref, hidden_ref
):
    expert_count = 8
    hidden = middle[...] + mix(combined[...], gates_t[...], target_t[...])
    hidden_ref[...] = hidden
    hidden_ref.send()
    gain = small[expert_count : expert_count + 1].astype(f32)
    normed = normalize(hidden, gain).astype(bf16)
    count = normed.shape[1] // spread.shape[0]
    normed_ref[...] = to_gathered(column_blocks(normed, count), spread[...]).astype(bf16)


def mix(combined, gates_t, target_t):
    high, low = split(choose_weighted(target_t, gates_t, combined.shape[0]))
    tokens = high.shape[1]
    both = tn(jnp.concatenate([high, low], axis=1), combined)
    return both[:tokens] + both[tokens:]


def result_kernel(middle, combined, gates_t, target_t, result_ref):
    mixture = mix(combined[...], gates_t[...], target_t[...])
    result_ref[...] = (middle[...] + mixture).astype(bf16)


def attend(rows, weight, cosines, sines, bias_ref, heads_ref, out_ref):
    seq_count, tokens, columns = heads_ref.shape
    group = seq_count * tokens
    local = columns // HD - 2
    prompt = group // 2
    raw = nn(rows, weight)
    heads = []
    for j in range(local + 2):
        block = raw[:, j * HD : (j + 1) * HD]
        if j <= local:
            block = turn(block, cosines, sines)
        heads.append(block.astype(bf16))
        heads_ref[:, :, j * HD : (j + 1) * HD] = heads[j].reshape(seq_count, tokens, HD)
    heads_ref.send()
    key, value = heads[local], heads[local + 1]
    scale = HD ** (-0.5)
    for j in range(local):
        query = heads[j]
        for rows, seen in ((slice(0, prompt), prompt), (slice(prompt, group), group)):
            scores = nt(query[rows], key[:seen]) * scale + bias_ref[rows, :seen]
            peak = jnp.max(scores, axis=-1, keepdims=True)
            weights = jnp.exp(scores - peak)
            weights = weights / jnp.sum(weights, axis=-1, keepdims=True)
            part = nn(weights.astype(bf16), value[:seen]).astype(bf16)
            first = rows.start // tokens
            out_ref[first : first + prompt // tokens, :, j * HD : (j + 1) * HD] = part.reshape(
                prompt // tokens, tokens, HD
            )


def first_attention_kernel(
    place, own, one, two, three, weight, spread, cosines, sines, bias_ref,
    heads_ref, out_ref, normed_ref, small_ref,
):
    expert_count = 8
    me = place[0]
    seq_count, tokens, width = normed_ref.shape
    columns = heads_ref.shape[2]
    count = small_ref.shape[1]
    extras = weight[:, columns:].astype(f32).T.astype(bf16)
    extras = jnp.concatenate([extras[:count], extras[HD : HD + count]], axis=0)
    small = jnp.concatenate(to_natural(extras, spread[...]), axis=1)
    small_ref[0] = small[:count].astype(bf16)
    small_ref[1] = small[count:].astype(bf16)
    small_ref.send()
    gain = small[expert_count : expert_count + 1]
    for k, block in enumerate((own, one, two, three)):
        normed = normalize(block[...].astype(f32), gain).astype(bf16)
        normed = to_gathered(column_blocks(normed, seq_count), spread[...]).astype(bf16)
        normed_ref[lax.rem(me + k, seq_count)] = normed
    normed_ref.send()
    rows = normed_ref[...].reshape(seq_count * tokens, width)
    attend(rows, weight[:, :columns], cosines[...], sines[...], bias_ref, heads_ref, out_ref)


def next_attention_kernel(
    place, own, one, two, three, weight, cosines, sines, bias_ref, heads_ref, out_ref, normed_ref
):
    me = place[0]
    seq_count, tokens, width = normed_ref.shape
    weight = weight[...].reshape(width, weight.shape[2])[:, : heads_ref.shape[2]]
    for k, block in enumerate((own, one, two, three)):
        normed_ref[lax.rem(me + k, seq_count)] = block[...]
    normed_ref.send()
    rows = normed_ref[...].reshape(seq_count * tokens, width)
    attend(rows, weight, cosines[...], sines[...], bias_ref, heads_ref, out_ref)


def gates_of(logits, routes_t, rows):
    expert_count = 8
    tokens = logits.shape[1]
    chosen = []
    for k in range(TOPK):
        route = routes_t[k : k + 1]
        value = jnp.zeros((1, tokens), f32)
        for e in range(expert_count):
            value = value + jnp.where(route == e, logits[e : e + 1], 0.0)
        chosen.append(value)
    peak = functools.reduce(jnp.maximum, chosen)
    powers = [jnp.exp(value - peak) for value in chosen]
    total = functools.reduce(jnp.add, powers)
    gates = [power / total for power in powers]
    return jnp.concatenate(gates + [jnp.zeros((rows - TOPK, tokens), f32)], axis=0)


def after_attention_kernel(
    back, spread, hidden, small, out_w, routes_t, middle_ref, normed_ref, gates_ref
):
    expert_count = 8
    seq_count, tokens, part = back.shape
    width = seq_count * part
    attended = to_gathered([back[s] for s in range(seq_count)], spread[...]).astype(bf16)
    rows = out_w.shape[1] // 2
    half = out_w.shape[2]
    for side in range(2):
        weight = out_w[:, side * rows : (side + 1) * rows].reshape(width, half)
        cols = slice(side * half, (side + 1) * half)
        middle_ref[:, cols] = hidden[:, cols].astype(f32) + nn(attended, weight)
    middle_ref.send()
    middle = middle_ref[...]
    gain = small[expert_count + 1 : expert_count + 2].astype(f32)
    normed = normalize(middle, gain).astype(bf16)
    normed_ref[...] = normed
    normed_ref.send()
    gates_ref[...] = gates_of(nt(small[...], normed), routes_t[...], gates_ref.shape[0])


def down_parts(block):
    shards, rows, half = block.shape
    wide = block.astype(f32)
    left = wide[:, : rows // 2].reshape(shards * rows // 2, half).astype(bf16)
    right = wide[:, rows // 2 :].reshape(shards * rows // 2, half).astype(bf16)
    return left, right


def expert_kernel(place, own, one, two, three, targets, routes, small, *rest):
    me = place[0]
    blocks = (own, one, two, three)
    out_ref, rows_ref, gate_ref, up_ref, gates_ref = rest[-5:]
    weights = rest[:-5]
    sources, experts, capacity, width = out_ref.shape
    half = width // 2
    for e in range(experts):
        gate_w, up_w, down_w = weights[3 * e : 3 * e + 3]
        first = (me * experts + e) * capacity
        parts = []
        for k, block in enumerate(blocks):
            hot = choose(targets[lax.rem(me + k, sources)] - first, capacity)
            parts.append(nn(hot.astype(bf16), block[...]))
        tokens = jnp.concatenate(parts, axis=0).astype(bf16)
        rows_ref[e] = tokens
        rows_ref.send(e)
        gate_val = nn(tokens, gate_w[...].reshape(width, half))
        gate_ref[e] = gate_val.astype(bf16)
        gate_ref.send(e)
        up_val = nn(tokens, up_w[...].reshape(width, half))
        up_ref[e] = up_val.astype(bf16)
        up_ref.send(e)
        activated, slope = smooth_parts(gate_val)
        inner = (activated * up_val).astype(bf16)
        for side, part in enumerate(down_parts(down_w[...])):
            done = nn(inner, part).astype(bf16)
            for k in range(sources):
                out_ref[lax.rem(me + k, sources), e, :, side * half : (side + 1) * half] = done[
                    k * capacity : (k + 1) * capacity
                ]
        out_ref.send(e)
    for k, block in enumerate(blocks):
        logits = nt(small[...], block[...])
        gates_ref[k] = gates_of(logits, routes[lax.rem(me + k, sources)], gates_ref.shape[1])


def logits_grad_kernel(grad, combined, gates_t, routes_t, target_t, logits_ref):
    tokens = grad.shape[0]
    slots = combined.shape[0]
    high, low = split(grad[...])
    products = nt(combined[...], jnp.concatenate([high, low], axis=0))
    products = products[:, :tokens] + products[:, tokens:]
    place = lax.broadcasted_iota(jnp.int32, (slots, tokens), 0)
    grad_gates = [
        jnp.sum(jnp.where(place == target_t[k : k + 1], products, 0.0), axis=0, keepdims=True)
        for k in range(TOPK)
    ]
    gates = [gates_t[k : k + 1] for k in range(TOPK)]
    center = functools.reduce(jnp.add, [a * b for a, b in zip(gates, grad_gates)])
    label = lax.broadcasted_iota(jnp.int32, logits_ref.shape, 0)
    total = jnp.zeros(logits_ref.shape, f32)
    for k in range(TOPK):
        choice = gates[k] * (grad_gates[k] - center)
        total = total + jnp.where(label == routes_t[k : k + 1], choice, 0.0)
    logits_ref[...] = total.astype(bf16)


def expert_back_kernel(
    place, own, one, two, three, targets, gates, down_first, gate_ref, up_ref, *rest
):
    me = place[0]
    blocks = (own, one, two, three)
    out_ref, rows_ref, gate_grad_ref, up_grad_ref, inner_ref = rest[-5:]
    weights = (down_first,) + rest[:-5]
    sources, experts, capacity, width = out_ref.shape
    half = width // 2
    for e in range(experts):
        down_w, gate_w, up_w = weights[3 * e : 3 * e + 3]
        shards, rows, _ = gate_w.shape
        first = (me * experts + e) * capacity
        parts = []
        for k, block in enumerate(blocks):
            target = targets[lax.rem(me + k, sources)] - first
            hot = jnp.concatenate(split(choose_weighted(target, gates[k], capacity)), axis=1)
            twice = jnp.concatenate([block[...], block[...]], axis=0)
            parts.append(nn(hot, twice))
        grad = jnp.concatenate(parts, axis=0).astype(bf16)
        rows_ref[e] = grad
        rows_ref.send(e)
        left, right = down_parts(down_w[...])
        grad_inner = nt(grad[:, :half], left) + nt(grad[:, half:], right)
        up_val = up_ref[e].astype(f32)
        activated, slope = smooth_parts(gate_ref[e].astype(f32))
        inner_ref[e] = (activated * up_val).astype(bf16)
        inner_ref.send(e)
        gate_grad_ref[e] = (grad_inner * up_val * slope).astype(bf16)
        gate_grad_ref.send(e)
        up_grad_ref[e] = (grad_inner * activated).astype(bf16)
        up_grad_ref.send(e)
        parts = 4
        some, size = shards // parts, shards * rows // parts
        for c in range(parts):
            at = slice(c * some, (c + 1) * some)
            total = nt(gate_grad_ref[e], gate_w[at].reshape(size, half))
            total = total + nt(up_grad_ref[e], up_w[at].reshape(size, half))
            total = total.astype(bf16)
            for k in range(sources):
                out_ref[lax.rem(me + k, sources), e, :, c * size : (c + 1) * size] = total[
                    k * capacity : (k + 1) * capacity
                ]
        out_ref.send(e)


def expert_weight_kernel(rows_ref, grad_ref, gate_grad_ref, up_grad_ref, inner_ref, pack_ref):
    weight_grads(rows_ref, grad_ref, gate_grad_ref, up_grad_ref, inner_ref, (pack_ref,), None)


def expert_weight_apart_kernel(
    core, rows_ref, grad_ref, gate_grad_ref, up_grad_ref, inner_ref, extra, own_ref, other_ref
):
    outs = (own_ref, other_ref)
    at = weight_grads(rows_ref, grad_ref, gate_grad_ref, up_grad_ref, inner_ref, outs, core[0])
    keep_shards(outs, core[0], at, extra[...])


def keep_shards(outs, core, at, value):
    shards, rows, half = value.shape
    if core is None:
        outs[0][:, at : at + rows] = value
    else:
        value = value.reshape(shards // 2, 2, rows, half)
        outs[0][:, at : at + rows] = jnp.where(core == 0, value[:, 0], value[:, 1])
        outs[1][:, at : at + rows] = jnp.where(core == 0, value[:, 1], value[:, 0])
    for out in outs:
        for piece in range(at // 16, (at + rows) // 16):
            out.send(piece)


def weight_grads(rows_ref, grad_ref, gate_grad_ref, up_grad_ref, inner_ref, outs, core):
    experts, _, width = rows_ref.shape
    half = outs[0].shape[2]
    shards = outs[0].shape[0] * len(outs)
    rows = width // shards
    at = 0
    for e in range(experts):
        grads = jnp.concatenate([gate_grad_ref[e], up_grad_ref[e]], axis=1)
        both = tn(rows_ref[e], grads).astype(bf16)
        keep_shards(outs, core, at, both[:, :half].reshape(shards, rows, half))
        keep_shards(outs, core, at + rows, both[:, half:].reshape(shards, rows, half))
        down = tn(inner_ref[e], grad_ref[e])
        left = down[:, :half].reshape(shards, rows // 2, half)
        right = down[:, half:].reshape(shards, rows // 2, half)
        down = jnp.concatenate([left, right], axis=1).astype(bf16)
        keep_shards(outs, core, at + 2 * rows, down)
        at += 3 * rows
    return at


def after_experts_kernel(
    grad, sent, middle, normed, logits_grad, target_t, small, out_w, spread,
    grad_ref, branch_ref, send_ref, small_ref,
):
    expert_count = 8
    seq_count, tokens, part = send_ref.shape
    width = seq_count * part
    chosen = choose(target_t[...], sent.shape[0]).astype(bf16)
    grad_normed = tn(chosen, sent[...]) + tn(logits_grad[...], small[...])
    router = nn(logits_grad[...], normed[...])
    gain = small[expert_count + 1 : expert_count + 2].astype(f32)
    grad_value, grad_gain = normalize_back(middle[...], gain, grad_normed)
    label = lax.broadcasted_iota(jnp.int32, small_ref.shape, 0)
    small_ref[...] = jnp.where(label == expert_count + 1, grad_gain, router)
    grad_middle = grad[...] + grad_value
    grad_ref[...] = grad_middle
    grad_ref.send()
    branch = grad_middle.astype(bf16)
    branch_ref[...] = branch
    branch_ref.send()
    rows = out_w.shape[1] // 2
    half = out_w.shape[2]
    parts = [
        nt(branch[:, :half], out_w[:, :rows].reshape(width, half)),
        nt(branch[:, half:], out_w[:, rows:].reshape(width, half)),
    ]
    attended = (parts[0] + parts[1]).astype(bf16)
    for s, block in enumerate(to_natural(attended, spread[...])):
        send_ref[s] = block.astype(bf16)


def attention_back_kernel(heads_ref, grad_ref, bias_ref, cosines, sines, out_ref):
    seq_count, tokens, columns = heads_ref.shape
    group = seq_count * tokens
    heads = heads_ref[...].reshape(group, columns)
    grads = grad_ref[...].reshape(group, grad_ref.shape[2])
    local = columns // HD - 2
    prompt = group // 2
    key = heads[:, local * HD : (local + 1) * HD]
    value = heads[:, (local + 1) * HD :]
    scale = HD ** (-0.5)

    def keep(at, block):
        out_ref[:, :, at * HD : (at + 1) * HD] = block.astype(bf16).reshape(seq_count, tokens, HD)

    cosines, sines = cosines[...], sines[...]

    def unturn(block):
        return block * cosines - pltpu.roll(block, HD // 2, 1) * sines

    grad_key = [jnp.zeros((prompt, HD), f32), jnp.zeros((prompt, HD), f32)]
    grad_value = [jnp.zeros((prompt, HD), f32), jnp.zeros((prompt, HD), f32)]
    for j in range(local):
        query = heads[:, j * HD : (j + 1) * HD]
        grad = grads[:, j * HD : (j + 1) * HD]
        grad_query = []
        for rows, seen in ((slice(0, prompt), prompt), (slice(prompt, group), group)):
            scores = nt(query[rows], key[:seen]) * scale + bias_ref[rows, :seen]
            peak = jnp.max(scores, axis=-1, keepdims=True)
            weights = jnp.exp(scores - peak)
            weights = weights / jnp.sum(weights, axis=-1, keepdims=True)
            grad_weights = nt(grad[rows], value[:seen])
            center = jnp.sum(weights * grad_weights, axis=-1, keepdims=True)
            grad_scores = (weights * (grad_weights - center)).astype(bf16)
            low = weights.astype(bf16)
            grad_query.append(nn(grad_scores, key[:seen]) * scale)
            for side in range(seen // prompt):
                cols = slice(side * prompt, (side + 1) * prompt)
                grad_key[side] = grad_key[side] + tn(grad_scores[:, cols], query[rows])
                grad_value[side] = grad_value[side] + tn(low[:, cols], grad[rows])
        keep(j, unturn(jnp.concatenate(grad_query, axis=0)))
    keep(local, unturn(jnp.concatenate(grad_key, axis=0) * scale))
    keep(local + 1, jnp.concatenate(grad_value, axis=0))


def before_attention_kernel(
    sent, left_w, right_w, kv_w, spread, small, hidden, grad_middle, out_ref, low_ref, gain_ref
):
    expert_count = 8
    seq_count, tokens, columns = sent.shape
    local = columns // HD - 2
    share = seq_count // KVHEADS
    blocks = [sent[s, :, : local * HD] for s in range(seq_count)]
    for at in (local, local + 1):
        for c in range(KVHEADS):
            total = jnp.zeros((tokens, HD), f32)
            for s in range(c * share, (c + 1) * share):
                total = total + sent[s, :, at * HD : (at + 1) * HD].astype(f32)
            blocks.append(total.astype(bf16))
    raw = jnp.concatenate(blocks, axis=1)
    at, total = 0, 0.0
    for part in (left_w, right_w, kv_w):
        shards, rows, columns = part.shape
        weight = part[...].reshape(shards * rows, columns)
        total = total + nt(raw[:, at : at + columns], weight)
        at += columns
    high, low = split(total)
    both = to_natural(jnp.concatenate([high, low], axis=0), spread[...])
    both = jnp.concatenate(both, axis=1)
    grad_normed = both[:tokens] + both[tokens:]
    gain = small[expert_count : expert_count + 1].astype(f32)
    grad_value, grad_gain = normalize_back(hidden[...].astype(f32), gain, grad_normed)
    total = grad_middle[...] + grad_value
    low_ref[...] = total.astype(bf16)
    low_ref.send()
    out_ref[...] = total
    out_ref.send()
    shards = gain_ref.shape[0]
    width = grad_gain.shape[1]
    share = width // seq_count
    part = share // shards
    shard = lax.broadcasted_iota(jnp.int32, (shards, width), 0)
    at = lax.broadcasted_iota(jnp.int32, (shards, width), 1)
    kept = jnp.where(at % share // part == shard, grad_gain, 0.0).astype(bf16)
    source = lax.broadcasted_iota(jnp.int32, (width, HD), 0)
    wanted = lax.broadcasted_iota(jnp.int32, (width, HD), 1)
    place = source // share * part + source % part
    gain_ref[...] = nn(kept, jnp.where(place == wanted, 1.0, 0.0).astype(bf16))


def qkv_weight_kernel(normed, grads, small, spread, out_ref):
    seq_count, tokens, columns = grads.shape
    shards, rows, wide = out_ref.shape
    inputs = normed[...].reshape(seq_count * tokens, normed.shape[2])
    total = tn(inputs, grads[...].reshape(seq_count * tokens, columns))
    out_ref[:, :, :columns] = total.astype(bf16).reshape(shards, rows, columns)
    extra = column_blocks(small[...].astype(bf16), seq_count)
    extra = to_gathered(extra, spread[...])
    extra = jnp.concatenate([extra, jnp.zeros((HD - extra.shape[0], extra.shape[1]), f32)], axis=0).T
    out_ref[:, :, columns:] = extra.astype(bf16).reshape(shards, rows, wide - columns)


def out_weight_kernel(place, *rest):
    out_ref = rest[-1]
    me = place[0]
    around = len(rest) // LAYERS - 2
    blocks, rest = rest[: LAYERS * around], rest[LAYERS * around :]
    shards, rows, half = out_ref.shape
    rows = rows // (2 * LAYERS)
    for layer in range(LAYERS):
        attended, gain = rest[layer], rest[LAYERS + layer]
        seq_count, tokens, part = attended.shape
        valid = part // shards
        branch = [block[...] for block in blocks[layer * around : (layer + 1) * around]]
        branch = jnp.concatenate(branch, axis=0)
        heads = jnp.concatenate(
            [attended[lax.rem(me + k, seq_count)] for k in range(seq_count)], axis=0
        )
        place_in = lax.broadcasted_iota(jnp.int32, (part, shards * rows), 0)
        place_out = lax.broadcasted_iota(jnp.int32, (part, shards * rows), 1)
        source = place_out // rows * valid + place_out % rows
        same = jnp.logical_and(place_in == source, place_out % rows < valid)
        heads = nn(heads, jnp.where(same, 1.0, 0.0).astype(bf16)).astype(bf16)
        wide = jnp.concatenate([gain[...], jnp.zeros((shards, half - HD), f32)], axis=1)
        row = lax.broadcasted_iota(jnp.int32, (shards, rows, half), 1)
        for side in range(2):
            total = tn(heads, branch[:, side * half : (side + 1) * half])
            total = total.reshape(shards, rows, half)
            if side == 0:
                total = jnp.where(row == valid, wide[:, None, :], total)
            at = (2 * layer + side) * rows
            out_ref[:, at : at + rows] = total.astype(bf16)


def expert_grads_kernel(*refs):
    sums, (gate_ref, up_ref, down_ref) = refs[:LAYERS], refs[LAYERS:]
    rows = gate_ref.shape[2]
    half = gate_ref.shape[3]
    for layer in range(LAYERS):
        block = sums[layer][...].astype(f32)
        for e in range(gate_ref.shape[1]):
            at = 3 * rows * e
            gate_ref[layer, e] = block[at : at + rows]
            up_ref[layer, e] = block[at + rows : at + 2 * rows]
            at += 2 * rows
            down_ref[layer, e, :, :half] = block[at : at + rows // 2]
            down_ref[layer, e, :, half:] = block[at + rows // 2 : at + rows]


def dense_grads_kernel(*refs):
    blocks, outs = refs[:LAYERS], refs[LAYERS : 2 * LAYERS]
    query_ref, key_ref, value_ref, out_ref, small_ref = refs[2 * LAYERS :]
    seq_count, rows, columns = blocks[0].shape
    local = columns - 3 * HD
    share = seq_count // KVHEADS
    for layer in range(LAYERS):
        parts = [blocks[layer][s].astype(f32) for s in range(seq_count)]
        for s in range(seq_count):
            query_ref[:, layer, s * local : (s + 1) * local] = parts[s][:, :local]
        for c in range(KVHEADS):
            total = functools.reduce(jnp.add, parts[c * share : (c + 1) * share])
            key_ref[:, layer, c * HD : (c + 1) * HD] = total[:, local : local + HD]
            value_ref[:, layer, c * HD : (c + 1) * HD] = total[:, local + HD : local + 2 * HD]
        total = functools.reduce(jnp.add, parts)
        small_ref[layer] = total[:, local + 2 * HD :]
        block = outs[layer][...].astype(f32)
        half = block.shape[1]
        out_ref[:, layer, :half] = block[:rows]
        out_ref[:, layer, half:] = block[block.shape[0] // 2 :][:rows]


def swap_seq(block):
    return lax.all_to_all(block, "seq", split_axis=0, concat_axis=0, tiled=True)


def around_seq(block):
    count = lax.axis_size("seq")
    others = [
        lax.ppermute(block, "seq", [((i + k) % count, i) for i in range(count)])
        for k in range(1, count)
    ]
    return [block] + others


def halves(block):
    cut = block.shape[-1] // 2
    return jnp.concatenate([block[..., :cut], block[..., cut:]], axis=-2)


def per_device(
    tokens_in,
    cotangent,
    routes,
    order,
    segment_ids,
    gain_attn,
    w_query,
    w_key,
    w_value,
    w_out,
    gain_ffn,
    w_router,
    w_gate,
    w_up,
    w_down,
):
    tok_count = tokens_in.shape[1]
    width = tokens_in.shape[2]
    seq_count = lax.axis_size("seq")
    shard_count = lax.axis_size("fsdp")
    seq_index = lax.axis_index("seq")
    place = jnp.full((1,), seq_index, jnp.int32)
    core_place = jnp.full((1,), lax.rem(lax.axis_index("fsdp"), 2), jnp.int32)
    group_tok = seq_count * tok_count
    prompt_len = group_tok - segment_ids.shape[1]
    local_experts = w_gate.shape[1]
    expert_count = local_experts * seq_count
    capacity = 9 * tok_count * TOPK // (8 * expert_count)
    total_slots = expert_count * capacity
    head_local = HEADS // seq_count
    local_width = head_local * HD
    dense_rows = w_query.shape[1]
    shard_rows = dense_rows * seq_count
    gate_rows = w_gate.shape[2]
    down_rows = w_down.shape[2]
    expert_rows = 2 * gate_rows + 2 * down_rows
    qkv_width = (HEADS + 2 * KVHEADS) * HD
    half_width = width // 2
    inner_width = w_gate.shape[3]
    slot_rows = seq_count * capacity

    cos_half, sin_half, labels = group_tables(segment_ids[0], prompt_len)
    cos_all = jnp.concatenate([cos_half, cos_half], axis=1)
    sin_all = jnp.concatenate([-sin_half, sin_half], axis=1)
    cos_own = lax.dynamic_slice_in_dim(cos_all, seq_index * tok_count, tok_count, 0)
    sin_own = lax.dynamic_slice_in_dim(sin_all, seq_index * tok_count, tok_count, 0)
    key_pos = jnp.arange(group_tok, dtype=jnp.int32)
    allowed = jnp.logical_and(
        key_pos[None, :] <= key_pos[:, None],
        jnp.logical_or(key_pos[None, :] < prompt_len, labels[None, :] == labels[:, None]),
    )
    bias = jnp.where(allowed, 0.0, masked_value)

    column = jnp.arange(width // seq_count, dtype=jnp.int32)
    natural = (
        column % shard_rows // dense_rows * (width // seq_count // seq_count)
        + column // shard_rows * dense_rows
        + column % dense_rows
    )
    spread = (column[:, None] == natural[None, :]).astype(bf16)

    def small_rows_of(layer):
        return jnp.concatenate(
            [
                w_router[layer],
                gain_attn[layer][:, None],
                gain_ffn[layer][:, None],
                jnp.zeros((dense_rows, HD - 2 - expert_count), bf16),
            ],
            axis=1,
        )

    def dense_rows_of(layer):
        return jnp.concatenate(
            [w_query[layer], w_key[layer], w_value[layer], small_rows_of(layer), w_out[layer]],
            axis=1,
        )

    def spread_seq(dense):
        dense = swap_seq(jnp.broadcast_to(dense[None], (seq_count,) + dense.shape))
        return dense.reshape(shard_rows, dense.shape[2])

    def own_columns(weight):
        pick = seq_index * KVHEADS // seq_count
        starts = (seq_index * local_width, (HEADS + pick) * HD, (HEADS + KVHEADS + pick) * HD)
        parts = [
            lax.dynamic_slice_in_dim(weight, start, size, 1)
            for start, size in zip(starts, (local_width, HD, HD))
        ]
        return jnp.concatenate(parts + [weight[:, qkv_width : qkv_width + HD]], axis=1)

    def expert_part(layer):
        return [
            part
            for e in range(local_experts)
            for part in (w_gate[layer, e], w_up[layer, e], halves(w_down[layer, e]))
        ]

    def out_part(dense):
        return [halves(dense[:, qkv_width + HD :])]

    def qkv_part(dense):
        wide = jnp.concatenate(
            [dense[:, : qkv_width + HD], jnp.zeros((shard_rows, HD), bf16)], axis=1
        )
        return [wide[:, at : at + half_width] for at in range(0, wide.shape[1], half_width)]

    def fetch(parts):
        return lax.all_gather(jnp.concatenate(parts, axis=0), "fsdp", axis=0, tiled=False)

    core = lax.rem(lax.axis_index("fsdp"), 2)
    chips = [[i + c for i in range(0, shard_count, 2)] for c in range(2)]

    def swap_chips(block):
        return lax.all_to_all(
            block, "fsdp", split_axis=0, concat_axis=0, tiled=True, axis_index_groups=chips
        )

    def swap_cores(block):
        return lax.ppermute(block, "fsdp", [(i, i ^ 1) for i in range(shard_count)])

    def both_cores(block):
        other = swap_cores(block)
        first = jnp.where(core == 0, block, other)
        second = jnp.where(core == 0, other, block)
        return jnp.stack([first, second], axis=1).reshape((shard_count,) + block.shape[1:])

    def to_chips(block):
        return swap_chips(jnp.broadcast_to(block[None], (shard_count // 2,) + block.shape))

    weight_parts = [
        (e * expert_rows + k * gate_rows, gate_rows) for e in range(local_experts) for k in range(3)
    ]
    back_parts = [weight_parts[3 * e + k] for e in range(local_experts) for k in (2, 0, 1)]
    out_cut = ((1, local_experts * expert_rows, 2 * shard_rows),)

    slots_shape = shape((seq_count, local_experts, capacity, width), bf16)
    inner_shape = (local_experts, slot_rows, inner_width)
    expert_flops = 6 * total_slots * width * inner_width
    dense_flops = 2 * tok_count * width * width
    records = []
    hidden = tokens_in[0]
    dense = spread_seq(jnp.concatenate([dense_rows_of(0), small_rows_of(1)], axis=1))
    columns = jnp.concatenate([own_columns(dense), dense[:, -HD:]], axis=1)
    dense = dense[:, :-HD]
    columns, hidden = lax.optimization_barrier((columns, hidden))
    token_blocks = around_seq(hidden)
    packs = [fetch(expert_part(0) + out_part(dense)), None]
    columns = to_chips(columns)
    pairs = jnp.concatenate(
        [array[layer, 0].T for array in (routes, order) for layer in range(LAYERS)], axis=0
    )
    pairs = swap_seq(jnp.broadcast_to(pairs[None], (seq_count,) + pairs.shape))
    pairs = pairs.reshape(seq_count, 2, LAYERS, TOPK, tok_count)
    slots_of = functools.partial(slot_table, expert_count=expert_count, capacity=capacity)
    all_routes = [pairs[:, 0, layer] for layer in range(LAYERS)]
    all_targets = [
        jax.vmap(slots_of)(pairs[:, 0, layer], pairs[:, 1, layer]) for layer in range(LAYERS)
    ]
    targets = [lax.dynamic_index_in_dim(t, seq_index, 0, False) for t in all_targets]
    routes_ts = [lax.dynamic_index_in_dim(t, seq_index, 0, False) for t in all_routes]
    early = (token_blocks, all_targets, all_routes, targets, routes_ts)
    columns, early = lax.optimization_barrier((columns, early + (cos_all, sin_all, bias, spread)))
    token_blocks, all_targets, all_routes, targets, routes_ts, cos_all, sin_all, bias, spread = early
    first_columns = both_cores(columns).reshape(width, columns.shape[2])
    first_columns, grad_rows = lax.optimization_barrier((first_columns, cotangent[0]))
    grad_blocks = around_seq(grad_rows)
    own_at = local_experts * expert_rows + 2 * shard_rows
    heads_shape = shape((seq_count, tok_count, local_width + 2 * HD), bf16)
    attended_shape = shape((seq_count, tok_count, local_width), bf16)
    normed_shape = shape((seq_count, tok_count, width), bf16)
    small_shape = shape((LAYERS, 2 * expert_count, width), bf16)
    attention_flops = 4 * head_local * group_tok * group_tok * HD + 2 * dense_flops
    for layer in range(LAYERS):
        pack, routes_t, target_t = packs[layer], routes_ts[layer], targets[layer]
        if layer == 0:
            heads, attended, normed_all, smalls = once(
                first_attention_kernel,
                [heads_shape, attended_shape, normed_shape, small_shape],
                place, *token_blocks, first_columns, spread, cos_all, sin_all, bias,
                scalar=True, flops=attention_flops + 4 * dense_flops,
            )
            small = smalls[layer]
        else:
            small = smalls[layer]
            normed_p, hidden = once(
                input_kernel,
                [shape((tok_count, width), bf16), shape((tok_count, width), f32)],
                middle, combined, gates_t, above_target, small, spread, flops=2 * dense_flops,
            )
            heads, attended, normed_all = once(
                next_attention_kernel,
                [heads_shape, attended_shape, normed_shape],
                place, *around_seq(normed_p), pack, cos_all, sin_all, bias,
                scalar=True, cut={5: ((1, own_at, shard_rows),)}, flops=attention_flops,
            )
        if layer == 0:
            attended, next_rows = lax.optimization_barrier((attended, dense_rows_of(1)))
            back = swap_seq(attended)
            next_dense = spread_seq(next_rows)
            next_parts = expert_part(1) + out_part(next_dense) + [own_columns(next_dense)]
            next_parts = jnp.concatenate(next_parts, axis=0)
            tied = lax.optimization_barrier((pack, next_parts, back, grad_blocks))
            pack, next_parts, back, grad_blocks = tied
            packs = [pack, fetch([next_parts])]
        else:
            back = swap_seq(attended)
            qkv_parts = jnp.concatenate(qkv_part(dense) + qkv_part(next_dense), axis=0)
            qkv_parts, back = lax.optimization_barrier((qkv_parts, back))
            qkv_w = fetch([qkv_parts])
        middle, normed_ffn, gates_t = once(
            after_attention_kernel,
            [
                shape((tok_count, width), f32),
                shape((tok_count, width), bf16),
                shape((2 * TOPK, tok_count), f32),
            ],
            back, spread, hidden, small, pack, routes_t,
            cut={4: out_cut}, flops=3 * dense_flops,
        )
        expert_out, received, gate_val, up_val, all_gates = once(
            expert_kernel,
            [
                slots_shape,
                shape((local_experts, slot_rows, width), bf16),
                shape(inner_shape, bf16),
                shape(inner_shape, bf16),
                shape((seq_count, 2 * TOPK, tok_count), f32),
            ],
            place, *around_seq(normed_ffn), all_targets[layer], all_routes[layer], small,
            *[pack] * len(weight_parts),
            scalar=True,
            cut={n + 8: ((1, *part),) for n, part in enumerate(weight_parts)},
            pieces={n: (1 if n == 0 else 0, local_experts) for n in range(4)},
            flops=expert_flops,
        )
        combined = swap_seq(expert_out).reshape(total_slots, width)
        above_target = target_t
        records.append(
            (
                (pack, small, routes_t, target_t),
                (hidden, normed_all, heads, attended),
                (middle, normed_ffn, gates_t, combined),
                (received, gate_val, up_val, all_gates),
            )
        )
    (result,) = once(
        result_kernel, [shape((tok_count, width), bf16)], middle, combined, gates_t, target_t,
        flops=dense_flops,
    )

    def scatter(block):
        return lax.psum_scatter(block, "fsdp", scatter_dimension=0, tiled=False)

    def spread_qkv(block, out_block):
        gain = out_block[dense_rows, :shard_rows]
        label = jnp.arange(local_width + 3 * HD)[None, :]
        block = jnp.where(label == local_width + 2 * HD + expert_count, gain[:, None], block)
        return swap_seq(block.reshape(seq_count, dense_rows, local_width + 3 * HD))

    def shard_sum(block):
        block = block.reshape((shard_count // 2, 2) + block.shape[1:])
        own = lax.dynamic_index_in_dim(block, core, 1, False)
        other = swap_cores(lax.dynamic_index_in_dim(block, 1 - core, 1, False))
        block = (own.astype(f32) + other.astype(f32)).astype(bf16)
        return jnp.sum(swap_chips(block).astype(f32), axis=0)

    out_rows = 16

    grad_hidden = cotangent[0].astype(f32)
    sums, gains = [None] * LAYERS, [None] * LAYERS
    branches, attendeds = [None] * LAYERS, [None] * LAYERS
    waiting = None
    for layer in range(LAYERS - 1, -1, -1):
        weights, attn_saved, mid_saved, expert_saved = records[layer]
        pack, small, routes_t, target_t = weights
        row = layer * 3 * shard_rows
        below, normed_all, heads, attended = attn_saved
        middle, normed_ffn, gates_t, combined = mid_saved
        received, gate_val, up_val, all_gates = expert_saved
        if waiting is None:
            tied = lax.optimization_barrier((grad_blocks, qkv_w, result, combined))
            grad_blocks, qkv_w, result, combined = tied
        else:
            grad_blocks, waiting = lax.optimization_barrier((grad_blocks, waiting))
        grad_rows, grad_expert, gate_grad, up_grad, inner = once(
            expert_back_kernel,
            [slots_shape, shape((local_experts, slot_rows, width), bf16)]
            + [shape(inner_shape, bf16)] * 3,
            place, *grad_blocks, all_targets[layer], all_gates, pack, gate_val, up_val,
            *[pack] * (len(back_parts) - 1),
            scalar=True,
            cut={n + 9 if n else 7: ((1, *part),) for n, part in enumerate(back_parts)},
            pieces={n: (1 if n == 0 else 0, local_experts) for n in range(5)},
            flops=expert_flops,
        )
        if layer < LAYERS - 1:
            tied = lax.optimization_barrier((grad_blocks, branches[layer + 1]))
            grad_rows, branches[layer + 1] = lax.optimization_barrier((grad_rows, around_seq(tied[1])))
        (logits_grad,) = once(
            logits_grad_kernel,
            [shape((2 * expert_count, tok_count), bf16)],
            grad_hidden, combined, gates_t, routes_t, target_t, flops=3 * dense_flops,
        )
        sent = swap_seq(grad_rows)
        sources = (received, grad_expert, gate_grad, up_grad, inner)
        pack_rows = local_experts * expert_rows
        if layer == LAYERS - 1:
            (packed,) = once(
                expert_weight_kernel,
                [shape((shard_count, pack_rows, half_width), bf16)],
                *sources, pieces={0: (1, pack_rows // 16)}, flops=expert_flops,
            )
        else:
            pack_rows += shard_rows
            packed = once(
                expert_weight_apart_kernel,
                [shape((shard_count // 2, pack_rows, half_width), bf16)] * 2,
                core_place, *sources, *waiting,
                scalar=True, pieces={n: (1, pack_rows // 16) for n in range(2)}, flops=expert_flops,
            )
        sent, packed, logits_grad = lax.optimization_barrier((sent, packed, logits_grad))
        if layer == LAYERS - 1:
            summed = scatter(packed)
        grad_middle, branch, send, small_grad = once(
            after_experts_kernel,
            [
                shape((tok_count, width), f32),
                shape((tok_count, width), bf16),
                shape((seq_count, tok_count, local_width), bf16),
                shape((2 * expert_count, width), f32),
            ],
            grad_hidden, sent.reshape(total_slots, width), middle, normed_ffn, logits_grad,
            target_t, small, pack, spread,
            cut={7: out_cut}, flops=4 * dense_flops,
        )
        grad_heads = swap_seq(send)
        if layer < LAYERS - 1:
            packed = (packed[0].astype(f32) + swap_cores(packed[1]).astype(f32)).astype(bf16)
            tied = lax.optimization_barrier((packed, sums[layer + 1], grad_heads))
            packed, sums[layer + 1], grad_heads = tied
            summed = lax.psum_scatter(
                packed.reshape(-1, half_width), "fsdp", scatter_dimension=0, tiled=True,
                axis_index_groups=chips,
            )
        (grad_own,) = once(
            attention_back_kernel,
            [shape((seq_count, tok_count, local_width + 2 * HD), bf16)],
            heads, grad_heads, bias, cos_all, sin_all,
            flops=10 * head_local * group_tok * group_tok * HD,
        )
        (qkv_block_grad,) = once(
            qkv_weight_kernel,
            [shape((shard_count, shard_rows, half_width), bf16)],
            normed_all, grad_own, small_grad, spread, flops=2 * dense_flops,
        )
        sent, qkv_block_grad = lax.optimization_barrier((swap_seq(grad_own), qkv_block_grad))
        grad_hidden, grad_low, gains[layer] = once(
            before_attention_kernel,
            [
                shape((tok_count, width), f32),
                shape((tok_count, width), bf16),
                shape((shard_count, HD), f32),
            ],
            sent, qkv_w, qkv_w, qkv_w, spread, small, below, grad_middle,
            cut={
                1: ((1, row, shard_rows),),
                2: ((1, row + shard_rows, shard_rows),),
                3: ((1, row + 2 * shard_rows, shard_rows), (2, 0, 2 * KVHEADS * HD)),
            },
            flops=4 * dense_flops,
        )
        branches[layer], attendeds[layer], sums[layer] = branch, attended, summed
        if layer > 0:
            grad_blocks = around_seq(grad_low)
            waiting = (qkv_block_grad,)
    qkv_sum = shard_sum(qkv_block_grad)
    branches[0] = around_seq(branches[0])
    branches[0], qkv_sum = lax.optimization_barrier((branches[0], qkv_sum))
    (out_block_grad,) = once(
        out_weight_kernel,
        [shape((shard_count, 2 * LAYERS * out_rows, half_width), bf16)],
        place, *branches[0], *branches[1], *attendeds, *gains,
        scalar=True, flops=2 * dense_flops,
    )

    out_sum = shard_sum(out_block_grad)
    out_sums = [out_sum[2 * out_rows * n : 2 * out_rows * (n + 1)] for n in range(LAYERS)]
    own_rows = spread_qkv(qkv_sum, out_sums[0])
    above_rows = spread_qkv(sums[0][local_experts * expert_rows :].astype(f32), out_sums[1])
    gate_grads, up_grads, down_grads = once(
        expert_grads_kernel,
        [
            shape((LAYERS,) + w_gate.shape[1:], f32),
            shape((LAYERS,) + w_up.shape[1:], f32),
            shape((LAYERS,) + w_down.shape[1:], f32),
        ],
        *sums,
        cut={0: ((0, 0, local_experts * expert_rows),)},
    )
    query_grads, key_grads, value_grads, out_grads, small_grads = once(
        dense_grads_kernel,
        [
            shape((dense_rows, LAYERS, HEADS * HD), f32),
            shape((dense_rows, LAYERS, KVHEADS * HD), f32),
            shape((dense_rows, LAYERS, KVHEADS * HD), f32),
            shape((dense_rows, LAYERS, width), f32),
            shape((LAYERS, dense_rows, HD), f32),
        ],
        own_rows, above_rows, *out_sums,
    )
    return (
        result[None],
        grad_hidden[None],
        small_grads[:, :, expert_count],
        query_grads.transpose(1, 0, 2),
        key_grads.transpose(1, 0, 2),
        value_grads.transpose(1, 0, 2),
        out_grads.transpose(1, 0, 2),
        small_grads[:, :, expert_count + 1],
        small_grads[:, :, :expert_count],
        gate_grads,
        up_grads,
        down_grads,
    )


def solution(mesh):
    in_specs = (
        P("fsdp", "seq", None),
        P("fsdp", "seq", None),
        P(None, "fsdp", "seq", None),
        P(None, "fsdp", "seq", None),
        P("fsdp", None),
        P(None, ("seq", "fsdp")),
        P(None, ("seq", "fsdp"), None),
        P(None, ("seq", "fsdp"), None),
        P(None, ("seq", "fsdp"), None),
        P(None, ("seq", "fsdp"), None),
        P(None, ("seq", "fsdp")),
        P(None, ("seq", "fsdp"), None),
        P(None, "seq", "fsdp", None),
        P(None, "seq", "fsdp", None),
        P(None, "seq", "fsdp", None),
    )
    out_specs = (
        P("fsdp", "seq", None),
        P("fsdp", "seq", None),
        P(None, ("seq", "fsdp")),
        P(None, ("seq", "fsdp"), None),
        P(None, ("seq", "fsdp"), None),
        P(None, ("seq", "fsdp"), None),
        P(None, ("seq", "fsdp"), None),
        P(None, ("seq", "fsdp")),
        P(None, ("seq", "fsdp"), None),
        P(None, "seq", "fsdp", None),
        P(None, "seq", "fsdp", None),
        P(None, "seq", "fsdp", None),
    )
    return jax.shard_map(
        per_device, mesh=mesh, in_specs=in_specs, out_specs=out_specs, check_vma=False
    )
```

```python
import functools

import jax
import jax.numpy as jnp
import numpy as np
from jax import lax
from jax.experimental import pallas as pl
from jax.experimental.pallas import tpu as pltpu
from jax.sharding import PartitionSpec as P

HEADS = 12
KVHEADS = 2
HD = 128
TOPK = 4
LAYERS = 2
NCONT = 4

norm_eps = 1e-06
rope_base = 10000.0
masked_value = -1e30

bf16 = jnp.bfloat16
f32 = jnp.float32
VMEM_BYTES = 64 * 1024 * 1024 - 256 * 1024


def group_tables(segment_row, prompt_len):
    cont_len = segment_row.shape[0]
    onehot = (segment_row[:, None] == jnp.arange(NCONT, dtype=jnp.int32)[None, :]).astype(jnp.int32)
    counts = jnp.sum(onehot, axis=0)
    starts = jnp.cumsum(counts) - counts
    seg_begin = jnp.sum(onehot * starts[None, :], axis=1)
    within = jnp.arange(cont_len, dtype=jnp.int32) - seg_begin
    positions = jnp.concatenate([jnp.arange(prompt_len, dtype=jnp.int32), prompt_len + within])
    labels = jnp.concatenate([jnp.full((prompt_len,), -1, jnp.int32), segment_row])
    frequency = rope_base ** (-(jnp.arange(HD // 2, dtype=jnp.float32) * 2.0 / HD))
    angles = positions.astype(jnp.float32)[:, None] * frequency[None, :]
    return (jnp.cos(angles), jnp.sin(angles), labels)


def slot_table(routes_t, order_t, expert_count, capacity):
    pair_expert = routes_t.reshape(-1)
    pair_order = order_t.reshape(-1)
    same_expert = pair_expert[:, None] == pair_expert[None, :]
    earlier = pair_order[None, :] < pair_order[:, None]
    pair_slot = jnp.sum(jnp.logical_and(same_expert, earlier).astype(jnp.int32), axis=1)
    target = jnp.where(
        pair_slot < capacity, pair_expert * capacity + pair_slot, expert_count * capacity
    )
    return target.reshape(routes_t.shape)


def nn(left, right):
    return lax.dot_general(left, right, (((1,), (0,)), ((), ())), preferred_element_type=f32)


def nt(left, right):
    return lax.dot_general(left, right, (((1,), (1,)), ((), ())), preferred_element_type=f32)


def tn(left, right):
    return lax.dot_general(left, right, (((0,), (0,)), ((), ())), preferred_element_type=f32)


def split(value):
    high = value.astype(bf16)
    return high, (value - high.astype(f32)).astype(bf16)


class Late:
    def __init__(self, ref, copy):
        self.ref, self.copy, self.shape = ref, copy, ref.shape
        copy.start()

    def wait(self):
        if self.copy is not None:
            self.copy.wait()
            self.copy = None

    def __getitem__(self, index):
        self.wait()
        return self.ref[index]


class Out:
    def __init__(self, ref, copies):
        self.ref, self.copies, self.shape = ref, copies, ref.shape
        self.sent = [False] * len(copies)

    def send(self, piece=None):
        for n in range(len(self.copies)) if piece is None else (piece,):
            if not self.sent[n]:
                self.copies[n].start()
                self.sent[n] = True

    def __getitem__(self, index):
        return self.ref[index]

    def __setitem__(self, index, value):
        self.ref[index] = value


def cost(args, outs, flops):
    moved = sum(int(np.prod(a.shape)) * a.dtype.itemsize for a in (*args, *outs))
    return pl.CostEstimate(flops=flops, bytes_accessed=moved, transcendentals=0)


def once(kernel, outs, *args, scalar=False, cut=None, pieces=None, flops=0):
    cut, pieces = cut or {}, pieces or {}
    hbm = pl.BlockSpec(memory_space=pltpu.HBM)
    late = [n for n in range(len(args)) if not (scalar and n == 0)]
    specs = [hbm] * len(args)
    if scalar:
        specs[0] = pl.BlockSpec(memory_space=pltpu.SMEM)
    scratch = []
    for n in late:
        dims = list(args[n].shape)
        for dim, start, size in cut.get(n, ()):
            dims[dim] = size
        scratch.append(pltpu.VMEM(tuple(dims), args[n].dtype))
    scratch += [pltpu.VMEM(o.shape, o.dtype) for o in outs]
    parts = [pieces.get(n, (0, 1)) for n in range(len(outs))]
    scratch.append(pltpu.SemaphoreType.DMA((len(late) + sum(count for _, count in parts),)))

    def body(*refs):
        ins = list(refs[: len(args)])
        out_refs = refs[len(args) : len(args) + len(outs)]
        rooms = refs[len(args) + len(outs) : -1]
        sems = refs[-1]
        for i, n in enumerate(late):
            source = ins[n]
            for dim, start, size in cut.get(n, ()):
                if callable(start):
                    start = pl.multiple_of(start(ins[0][0]), 16 if dim == 1 else HD)
                source = source.at[(slice(None),) * dim + (pl.ds(start, size),)]
            ins[n] = Late(rooms[i], pltpu.make_async_copy(source, rooms[i], sems.at[i]))
        results = []
        used = len(late)
        for i, out in enumerate(out_refs):
            room = rooms[len(late) + i]
            dim, count = parts[i]
            size = room.shape[dim] // count
            copies = []
            for n in range(count):
                at = (slice(None),) * dim + (pl.ds(n * size, size),)
                copies.append(pltpu.make_async_copy(room.at[at], out.at[at], sems.at[used]))
                used += 1
            results.append(Out(room, copies))
        kernel(*ins, *results)
        for result in results:
            result.send()
        for n in late:
            ins[n].wait()
        for result in results:
            for copy in result.copies:
                copy.wait()

    return pl.pallas_call(
        body,
        out_shape=list(outs),
        in_specs=specs,
        out_specs=[hbm] * len(outs),
        scratch_shapes=scratch,
        compiler_params=pltpu.CompilerParams(vmem_limit_bytes=VMEM_BYTES),
        cost_estimate=cost(args, outs, flops),
    )(*args)


def shape(dims, dtype):
    return jax.ShapeDtypeStruct(dims, dtype)


def normalize(value, gain):
    inverse = lax.rsqrt(jnp.mean(value * value, axis=-1, keepdims=True) + norm_eps)
    return value * inverse * gain


def normalize_back(value, gain, grad):
    inverse = lax.rsqrt(jnp.mean(value * value, axis=-1, keepdims=True) + norm_eps)
    unit = value * inverse
    grad_gain = jnp.sum(grad * unit, axis=0, keepdims=True)
    scaled = grad * gain
    grad_value = inverse * (scaled - unit * jnp.mean(scaled * unit, axis=-1, keepdims=True))
    return grad_value, grad_gain


def to_gathered(parts, order):
    count = len(parts)
    share = parts[0].shape[1] // count
    done = []
    for j in range(count):
        piece = jnp.concatenate([part[:, j * share : (j + 1) * share] for part in parts], axis=1)
        done.append(nn(piece, order))
    return jnp.concatenate(done, axis=1)


def to_natural(value, order):
    count = value.shape[1] // order.shape[0]
    size = order.shape[0]
    share = size // count
    done = [nt(value[:, j * size : (j + 1) * size], order) for j in range(count)]
    return [
        jnp.concatenate([part[:, s * share : (s + 1) * share] for part in done], axis=1)
        for s in range(count)
    ]


def column_blocks(value, count):
    size = value.shape[1] // count
    return [value[:, s * size : (s + 1) * size] for s in range(count)]


def turn(block, cosines, sines):
    return block * cosines + pltpu.roll(block, HD // 2, 1) * sines


def smooth_parts(value):
    root = np.float32(np.sqrt(2.0 / np.pi))
    square = value * value
    high = jnp.tanh(root * (value + 0.044715 * value * square))
    half = 0.5 * (1.0 + high)
    slope = half + 0.5 * value * (1.0 - high * high) * root * (1.0 + 3 * 0.044715 * square)
    return value * half, slope


def choose(target_t, slots):
    place = lax.broadcasted_iota(jnp.int32, (slots, target_t.shape[1]), 0)
    total = jnp.zeros(place.shape, f32)
    for k in range(TOPK):
        total = total + jnp.where(place == target_t[k : k + 1], 1.0, 0.0)
    return total


def choose_weighted(target_t, gates_t, slots):
    place = lax.broadcasted_iota(jnp.int32, (slots, target_t.shape[1]), 0)
    total = jnp.zeros(place.shape, f32)
    for k in range(TOPK):
        total = total + jnp.where(place == target_t[k : k + 1], gates_t[k : k + 1], 0.0)
    return total


def input_kernel(
    middle, combined, gates_t, target_t, small, spread, normed_ref, hidden_ref
):
    expert_count = 8
    hidden = middle[...] + mix(combined[...], gates_t[...], target_t[...])
    hidden_ref[...] = hidden
    hidden_ref.send()
    gain = small[expert_count : expert_count + 1].astype(f32)
    normed = normalize(hidden, gain).astype(bf16)
    count = normed.shape[1] // spread.shape[0]
    normed_ref[...] = to_gathered(column_blocks(normed, count), spread[...]).astype(bf16)


def mix(combined, gates_t, target_t):
    high, low = split(choose_weighted(target_t, gates_t, combined.shape[0]))
    tokens = high.shape[1]
    both = tn(jnp.concatenate([high, low], axis=1), combined)
    return both[:tokens] + both[tokens:]


def result_kernel(middle, combined, gates_t, target_t, result_ref):
    mixture = mix(combined[...], gates_t[...], target_t[...])
    result_ref[...] = (middle[...] + mixture).astype(bf16)


def attend(rows, weight, cosines, sines, bias_ref, heads_ref, out_ref):
    seq_count, tokens, columns = heads_ref.shape
    group = seq_count * tokens
    local = columns // HD - 2
    prompt = group // 2
    raw = nn(rows, weight)
    heads = []
    for j in range(local + 2):
        block = raw[:, j * HD : (j + 1) * HD]
        if j <= local:
            block = turn(block, cosines, sines)
        heads.append(block.astype(bf16))
        heads_ref[:, :, j * HD : (j + 1) * HD] = heads[j].reshape(seq_count, tokens, HD)
    heads_ref.send()
    key, value = heads[local], heads[local + 1]
    scale = HD ** (-0.5)
    for j in range(local):
        query = heads[j]
        for rows, seen in ((slice(0, prompt), prompt), (slice(prompt, group), group)):
            scores = nt(query[rows], key[:seen]) * scale + bias_ref[rows, :seen]
            peak = jnp.max(scores, axis=-1, keepdims=True)
            weights = jnp.exp(scores - peak)
            weights = weights / jnp.sum(weights, axis=-1, keepdims=True)
            part = nn(weights.astype(bf16), value[:seen]).astype(bf16)
            first = rows.start // tokens
            out_ref[first : first + prompt // tokens, :, j * HD : (j + 1) * HD] = part.reshape(
                prompt // tokens, tokens, HD
            )


def first_attention_kernel(
    place, own, one, two, three, weight, spread, cosines, sines, bias_ref,
    heads_ref, out_ref, normed_ref, small_ref,
):
    expert_count = 8
    me = place[0]
    seq_count, tokens, width = normed_ref.shape
    columns = heads_ref.shape[2]
    count = small_ref.shape[1]
    extras = weight[:, columns:].astype(f32).T.astype(bf16)
    extras = jnp.concatenate([extras[:count], extras[HD : HD + count]], axis=0)
    small = jnp.concatenate(to_natural(extras, spread[...]), axis=1)
    small_ref[0] = small[:count].astype(bf16)
    small_ref[1] = small[count:].astype(bf16)
    small_ref.send()
    gain = small[expert_count : expert_count + 1]
    for k, block in enumerate((own, one, two, three)):
        normed = normalize(block[...].astype(f32), gain).astype(bf16)
        normed = to_gathered(column_blocks(normed, seq_count), spread[...]).astype(bf16)
        normed_ref[lax.rem(me + k, seq_count)] = normed
    normed_ref.send()
    rows = normed_ref[...].reshape(seq_count * tokens, width)
    attend(rows, weight[:, :columns], cosines[...], sines[...], bias_ref, heads_ref, out_ref)


def next_attention_kernel(
    place, own, one, two, three, weight, cosines, sines, bias_ref, heads_ref, out_ref, normed_ref
):
    me = place[0]
    seq_count, tokens, width = normed_ref.shape
    weight = weight[...].reshape(width, weight.shape[2])[:, : heads_ref.shape[2]]
    for k, block in enumerate((own, one, two, three)):
        normed_ref[lax.rem(me + k, seq_count)] = block[...]
    normed_ref.send()
    rows = normed_ref[...].reshape(seq_count * tokens, width)
    attend(rows, weight, cosines[...], sines[...], bias_ref, heads_ref, out_ref)


def gates_of(logits, routes_t, rows):
    expert_count = 8
    tokens = logits.shape[1]
    chosen = []
    for k in range(TOPK):
        route = routes_t[k : k + 1]
        value = jnp.zeros((1, tokens), f32)
        for e in range(expert_count):
            value = value + jnp.where(route == e, logits[e : e + 1], 0.0)
        chosen.append(value)
    peak = functools.reduce(jnp.maximum, chosen)
    powers = [jnp.exp(value - peak) for value in chosen]
    total = functools.reduce(jnp.add, powers)
    gates = [power / total for power in powers]
    return jnp.concatenate(gates + [jnp.zeros((rows - TOPK, tokens), f32)], axis=0)


def after_attention_kernel(
    back, spread, hidden, small, out_w, routes_t, middle_ref, normed_ref, gates_ref
):
    expert_count = 8
    seq_count, tokens, part = back.shape
    width = seq_count * part
    attended = to_gathered([back[s] for s in range(seq_count)], spread[...]).astype(bf16)
    rows = out_w.shape[1] // 2
    half = out_w.shape[2]
    for side in range(2):
        weight = out_w[:, side * rows : (side + 1) * rows].reshape(width, half)
        cols = slice(side * half, (side + 1) * half)
        middle_ref[:, cols] = hidden[:, cols].astype(f32) + nn(attended, weight)
    middle_ref.send()
    middle = middle_ref[...]
    gain = small[expert_count + 1 : expert_count + 2].astype(f32)
    normed = normalize(middle, gain).astype(bf16)
    normed_ref[...] = normed
    normed_ref.send()
    gates_ref[...] = gates_of(nt(small[...], normed), routes_t[...], gates_ref.shape[0])


def down_parts(block):
    shards, rows, half = block.shape
    wide = block.astype(f32)
    left = wide[:, : rows // 2].reshape(shards * rows // 2, half).astype(bf16)
    right = wide[:, rows // 2 :].reshape(shards * rows // 2, half).astype(bf16)
    return left, right


def expert_kernel(place, own, one, two, three, targets, routes, small, *rest):
    me = place[0]
    blocks = (own, one, two, three)
    out_ref, rows_ref, gate_ref, up_ref, gates_ref = rest[-5:]
    weights = rest[:-5]
    sources, experts, capacity, width = out_ref.shape
    half = width // 2
    for e in range(experts):
        gate_w, up_w, down_w = weights[3 * e : 3 * e + 3]
        first = (me * experts + e) * capacity
        parts = []
        for k, block in enumerate(blocks):
            hot = choose(targets[lax.rem(me + k, sources)] - first, capacity)
            parts.append(nn(hot.astype(bf16), block[...]))
        tokens = jnp.concatenate(parts, axis=0).astype(bf16)
        rows_ref[e] = tokens
        rows_ref.send(e)
        gate_val = nn(tokens, gate_w[...].reshape(width, half))
        gate_ref[e] = gate_val.astype(bf16)
        gate_ref.send(e)
        up_val = nn(tokens, up_w[...].reshape(width, half))
        up_ref[e] = up_val.astype(bf16)
        up_ref.send(e)
        activated, slope = smooth_parts(gate_val)
        inner = (activated * up_val).astype(bf16)
        for side, part in enumerate(down_parts(down_w[...])):
            done = nn(inner, part).astype(bf16)
            for k in range(sources):
                out_ref[lax.rem(me + k, sources), e, :, side * half : (side + 1) * half] = done[
                    k * capacity : (k + 1) * capacity
                ]
        out_ref.send(e)
    for k, block in enumerate(blocks):
        logits = nt(small[...], block[...])
        gates_ref[k] = gates_of(logits, routes[lax.rem(me + k, sources)], gates_ref.shape[1])


def logits_grad_kernel(grad, combined, gates_t, routes_t, target_t, logits_ref):
    tokens = grad.shape[0]
    slots = combined.shape[0]
    high, low = split(grad[...])
    products = nt(combined[...], jnp.concatenate([high, low], axis=0))
    products = products[:, :tokens] + products[:, tokens:]
    place = lax.broadcasted_iota(jnp.int32, (slots, tokens), 0)
    grad_gates = [
        jnp.sum(jnp.where(place == target_t[k : k + 1], products, 0.0), axis=0, keepdims=True)
        for k in range(TOPK)
    ]
    gates = [gates_t[k : k + 1] for k in range(TOPK)]
    center = functools.reduce(jnp.add, [a * b for a, b in zip(gates, grad_gates)])
    label = lax.broadcasted_iota(jnp.int32, logits_ref.shape, 0)
    total = jnp.zeros(logits_ref.shape, f32)
    for k in range(TOPK):
        choice = gates[k] * (grad_gates[k] - center)
        total = total + jnp.where(label == routes_t[k : k + 1], choice, 0.0)
    logits_ref[...] = total.astype(bf16)


def expert_back_kernel(
    place, own, one, two, three, targets, gates, down_first, gate_ref, up_ref, *rest
):
    me = place[0]
    blocks = (own, one, two, three)
    out_ref, keep_ref = rest[-2:]
    weights = (down_first,) + rest[:-2]
    sources, experts, capacity, width = out_ref.shape
    half = width // 2
    for e in range(experts):
        down_w, gate_w, up_w = weights[3 * e : 3 * e + 3]
        shards, rows, _ = gate_w.shape
        first = (me * experts + e) * capacity
        parts = []
        for k, block in enumerate(blocks):
            target = targets[lax.rem(me + k, sources)] - first
            hot = jnp.concatenate(split(choose_weighted(target, gates[k], capacity)), axis=1)
            twice = jnp.concatenate([block[...], block[...]], axis=0)
            parts.append(nn(hot, twice))
        grad = jnp.concatenate(parts, axis=0).astype(bf16)
        keep_ref[e, :, :width] = grad
        left, right = down_parts(down_w[...])
        grad_inner = nt(grad[:, :half], left) + nt(grad[:, half:], right)
        up_val = up_ref[e].astype(f32)
        activated, slope = smooth_parts(gate_ref[e].astype(f32))
        gate_at, up_at, inner_at = (slice(width + n * half, width + (n + 1) * half) for n in range(3))
        keep_ref[e, :, gate_at] = (grad_inner * up_val * slope).astype(bf16)
        keep_ref[e, :, up_at] = (grad_inner * activated).astype(bf16)
        keep_ref[e, :, inner_at] = (activated * up_val).astype(bf16)
        keep_ref.send(e)
        parts = 4
        some, size = shards // parts, shards * rows // parts
        for c in range(parts):
            at = slice(c * some, (c + 1) * some)
            total = nt(keep_ref[e, :, gate_at], gate_w[at].reshape(size, half))
            total = total + nt(keep_ref[e, :, up_at], up_w[at].reshape(size, half))
            total = total.astype(bf16)
            for k in range(sources):
                out_ref[lax.rem(me + k, sources), e, :, c * size : (c + 1) * size] = total[
                    k * capacity : (k + 1) * capacity
                ]
        out_ref.send(e)


def pick_kernel(rows, other_rows, pick, out_ref):
    count = rows.shape[1]
    for e in range(rows.shape[0]):
        out_ref[e, :count] = nn(rows[e], pick[...]).astype(bf16)
        out_ref[e, count:] = nn(other_rows[e], pick[...]).astype(bf16)
        out_ref.send(e)


def expert_weight_kernel(tokens, pick_inner, keep, other_keep, *rest):
    pack_ref = rest[-1]
    chips, _, half = pack_ref.shape
    experts = tokens.shape[0]
    width = 2 * tokens.shape[2]
    count = width // (2 * chips)
    at = 0

    def send():
        for piece in range(at // 16, (at + count) // 16):
            pack_ref.send(piece)

    for e in range(experts):
        grads = jnp.concatenate([keep[e], other_keep[e]], axis=0)
        both = tn(tokens[e], grads[:, width : width + 2 * half]).astype(bf16)
        for n in range(2):
            block = both[:, n * half : (n + 1) * half].reshape(chips, count, half)
            pack_ref[:, at : at + count] = block
            send()
            at += count
        inner = nn(grads[:, width + 2 * half :], pick_inner[...]).astype(bf16)
        down = tn(inner, grads[:, :width])
        left = down[:, :half].reshape(chips, count // 2, half)
        right = down[:, half:].reshape(chips, count // 2, half)
        pack_ref[:, at : at + count] = jnp.concatenate([left, right], axis=1).astype(bf16)
        send()
        at += count
    if len(rest) > 1:
        own, other = rest[:2]
        pack_ref[:, at : at + count] = (own[...].astype(f32) + other[...].astype(f32)).astype(bf16)
        send()


def keep_shards(own_ref, other_ref, core, at, value):
    shards, rows, columns = value.shape
    value = value.reshape(shards // 2, 2, rows, columns)
    own_ref[:, at : at + rows] = jnp.where(core == 0, value[:, 0], value[:, 1])
    other_ref[:, at : at + rows] = jnp.where(core == 0, value[:, 1], value[:, 0])


def after_experts_kernel(
    grad, sent, middle, normed, logits_grad, target_t, small, out_w, spread,
    grad_ref, branch_ref, send_ref, small_ref,
):
    expert_count = 8
    seq_count, tokens, part = send_ref.shape
    width = seq_count * part
    chosen = choose(target_t[...], sent.shape[0]).astype(bf16)
    grad_normed = tn(chosen, sent[...]) + tn(logits_grad[...], small[...])
    router = nn(logits_grad[...], normed[...])
    gain = small[expert_count + 1 : expert_count + 2].astype(f32)
    grad_value, grad_gain = normalize_back(middle[...], gain, grad_normed)
    label = lax.broadcasted_iota(jnp.int32, small_ref.shape, 0)
    small_ref[...] = jnp.where(label == expert_count + 1, grad_gain, router)
    grad_middle = grad[...] + grad_value
    grad_ref[...] = grad_middle
    grad_ref.send()
    branch = grad_middle.astype(bf16)
    branch_ref[...] = branch
    branch_ref.send()
    rows = out_w.shape[1] // 2
    half = out_w.shape[2]
    parts = [
        nt(branch[:, :half], out_w[:, :rows].reshape(width, half)),
        nt(branch[:, half:], out_w[:, rows:].reshape(width, half)),
    ]
    attended = (parts[0] + parts[1]).astype(bf16)
    for s, block in enumerate(to_natural(attended, spread[...])):
        send_ref[s] = block.astype(bf16)


def attention_back_kernel(heads_ref, grad_ref, bias_ref, cosines, sines, out_ref):
    seq_count, tokens, columns = heads_ref.shape
    group = seq_count * tokens
    heads = heads_ref[...].reshape(group, columns)
    grads = grad_ref[...].reshape(group, grad_ref.shape[2])
    local = columns // HD - 2
    prompt = group // 2
    key = heads[:, local * HD : (local + 1) * HD]
    value = heads[:, (local + 1) * HD :]
    scale = HD ** (-0.5)

    def keep(at, block):
        out_ref[:, :, at * HD : (at + 1) * HD] = block.astype(bf16).reshape(seq_count, tokens, HD)

    cosines, sines = cosines[...], sines[...]

    def unturn(block):
        return block * cosines - pltpu.roll(block, HD // 2, 1) * sines

    grad_key = [jnp.zeros((prompt, HD), f32), jnp.zeros((prompt, HD), f32)]
    grad_value = [jnp.zeros((prompt, HD), f32), jnp.zeros((prompt, HD), f32)]
    for j in range(local):
        query = heads[:, j * HD : (j + 1) * HD]
        grad = grads[:, j * HD : (j + 1) * HD]
        grad_query = []
        for rows, seen in ((slice(0, prompt), prompt), (slice(prompt, group), group)):
            scores = nt(query[rows], key[:seen]) * scale + bias_ref[rows, :seen]
            peak = jnp.max(scores, axis=-1, keepdims=True)
            weights = jnp.exp(scores - peak)
            weights = weights / jnp.sum(weights, axis=-1, keepdims=True)
            grad_weights = nt(grad[rows], value[:seen])
            center = jnp.sum(weights * grad_weights, axis=-1, keepdims=True)
            grad_scores = (weights * (grad_weights - center)).astype(bf16)
            low = weights.astype(bf16)
            grad_query.append(nn(grad_scores, key[:seen]) * scale)
            for side in range(seen // prompt):
                cols = slice(side * prompt, (side + 1) * prompt)
                grad_key[side] = grad_key[side] + tn(grad_scores[:, cols], query[rows])
                grad_value[side] = grad_value[side] + tn(low[:, cols], grad[rows])
        keep(j, unturn(jnp.concatenate(grad_query, axis=0)))
    keep(local, unturn(jnp.concatenate(grad_key, axis=0) * scale))
    keep(local + 1, jnp.concatenate(grad_value, axis=0))


def before_attention_kernel(
    sent, left_w, right_w, kv_w, spread, small, hidden, grad_middle, out_ref, low_ref, gain_ref
):
    expert_count = 8
    seq_count, tokens, columns = sent.shape
    local = columns // HD - 2
    share = seq_count // KVHEADS
    blocks = [sent[s, :, : local * HD] for s in range(seq_count)]
    for at in (local, local + 1):
        for c in range(KVHEADS):
            total = jnp.zeros((tokens, HD), f32)
            for s in range(c * share, (c + 1) * share):
                total = total + sent[s, :, at * HD : (at + 1) * HD].astype(f32)
            blocks.append(total.astype(bf16))
    raw = jnp.concatenate(blocks, axis=1)
    at, total = 0, 0.0
    for part in (left_w, right_w, kv_w):
        shards, rows, columns = part.shape
        weight = part[...].reshape(shards * rows, columns)
        total = total + nt(raw[:, at : at + columns], weight)
        at += columns
    high, low = split(total)
    both = to_natural(jnp.concatenate([high, low], axis=0), spread[...])
    both = jnp.concatenate(both, axis=1)
    grad_normed = both[:tokens] + both[tokens:]
    gain = small[expert_count : expert_count + 1].astype(f32)
    grad_value, grad_gain = normalize_back(hidden[...].astype(f32), gain, grad_normed)
    total = grad_middle[...] + grad_value
    low_ref[...] = total.astype(bf16)
    low_ref.send()
    out_ref[...] = total
    out_ref.send()
    shards = gain_ref.shape[0]
    width = grad_gain.shape[1]
    share = width // seq_count
    part = share // shards
    shard = lax.broadcasted_iota(jnp.int32, (shards, width), 0)
    at = lax.broadcasted_iota(jnp.int32, (shards, width), 1)
    kept = jnp.where(at % share // part == shard, grad_gain, 0.0).astype(bf16)
    source = lax.broadcasted_iota(jnp.int32, (width, HD), 0)
    wanted = lax.broadcasted_iota(jnp.int32, (width, HD), 1)
    place = source // share * part + source % part
    gain_ref[...] = nn(kept, jnp.where(place == wanted, 1.0, 0.0).astype(bf16))


def qkv_weight_kernel(place, normed, grads, small, spread, own_ref, other_ref):
    seq_count, tokens, columns = grads.shape
    chips, rows, wide = own_ref.shape
    shards = 2 * chips
    inputs = normed[...].reshape(seq_count * tokens, normed.shape[2])
    total = tn(inputs, grads[...].reshape(seq_count * tokens, columns))
    extra = column_blocks(small[...].astype(bf16), seq_count)
    extra = to_gathered(extra, spread[...])
    extra = jnp.concatenate([extra, jnp.zeros((HD - extra.shape[0], extra.shape[1]), f32)], axis=0).T
    total = jnp.concatenate([total, extra], axis=1).astype(bf16).reshape(shards, rows, wide)
    keep_shards(own_ref, other_ref, place[1], 0, total)


def out_weight_kernel(place, *rest):
    own_ref, other_ref = rest[-2:]
    rest = rest[:-2]
    me = place[0]
    around = len(rest) // LAYERS - 2
    blocks, rest = rest[: LAYERS * around], rest[LAYERS * around :]
    chips, rows, half = own_ref.shape
    shards = 2 * chips
    rows = rows // (2 * LAYERS)
    for layer in range(LAYERS):
        attended, gain = rest[layer], rest[LAYERS + layer]
        seq_count, tokens, part = attended.shape
        valid = part // shards
        branch = [block[...] for block in blocks[layer * around : (layer + 1) * around]]
        branch = jnp.concatenate(branch, axis=0)
        heads = jnp.concatenate(
            [attended[lax.rem(me + k, seq_count)] for k in range(seq_count)], axis=0
        )
        place_in = lax.broadcasted_iota(jnp.int32, (part, shards * rows), 0)
        place_out = lax.broadcasted_iota(jnp.int32, (part, shards * rows), 1)
        source = place_out // rows * valid + place_out % rows
        same = jnp.logical_and(place_in == source, place_out % rows < valid)
        heads = nn(heads, jnp.where(same, 1.0, 0.0).astype(bf16)).astype(bf16)
        wide = jnp.concatenate([gain[...], jnp.zeros((shards, half - HD), f32)], axis=1)
        row = lax.broadcasted_iota(jnp.int32, (shards, rows, half), 1)
        for side in range(2):
            total = tn(heads, branch[:, side * half : (side + 1) * half])
            total = total.reshape(shards, rows, half)
            if side == 0:
                total = jnp.where(row == valid, wide[:, None, :], total)
            at = (2 * layer + side) * rows
            keep_shards(own_ref, other_ref, place[1], at, total.astype(bf16))


def expert_grads_kernel(*refs):
    sums, (gate_ref, up_ref, down_ref) = refs[:LAYERS], refs[LAYERS:]
    rows = gate_ref.shape[2]
    half = gate_ref.shape[3]
    for layer in range(LAYERS):
        block = sums[layer][...].astype(f32)
        for e in range(gate_ref.shape[1]):
            at = 3 * rows * e
            gate_ref[layer, e] = block[at : at + rows]
            up_ref[layer, e] = block[at + rows : at + 2 * rows]
            at += 2 * rows
            down_ref[layer, e, :, :half] = block[at : at + rows // 2]
            down_ref[layer, e, :, half:] = block[at + rows // 2 : at + rows]


def dense_grads_kernel(*refs):
    blocks, outs = refs[:LAYERS], refs[LAYERS : 2 * LAYERS]
    query_ref, key_ref, value_ref, out_ref, small_ref = refs[2 * LAYERS :]
    seq_count, rows, columns = blocks[0].shape
    local = columns - 3 * HD
    share = seq_count // KVHEADS
    for layer in range(LAYERS):
        parts = [blocks[layer][s].astype(f32) for s in range(seq_count)]
        for s in range(seq_count):
            query_ref[:, layer, s * local : (s + 1) * local] = parts[s][:, :local]
        for c in range(KVHEADS):
            total = functools.reduce(jnp.add, parts[c * share : (c + 1) * share])
            key_ref[:, layer, c * HD : (c + 1) * HD] = total[:, local : local + HD]
            value_ref[:, layer, c * HD : (c + 1) * HD] = total[:, local + HD : local + 2 * HD]
        total = functools.reduce(jnp.add, parts)
        small_ref[layer] = total[:, local + 2 * HD :]
        block = outs[layer][...].astype(f32)
        half = block.shape[1]
        out_ref[:, layer, :half] = block[:rows]
        out_ref[:, layer, half:] = block[block.shape[0] // 2 :][:rows]


def swap_seq(block):
    return lax.all_to_all(block, "seq", split_axis=0, concat_axis=0, tiled=True)


def around_seq(block):
    count = lax.axis_size("seq")
    others = [
        lax.ppermute(block, "seq", [((i + k) % count, i) for i in range(count)])
        for k in range(1, count)
    ]
    return [block] + others


def halves(block):
    cut = block.shape[-1] // 2
    return jnp.concatenate([block[..., :cut], block[..., cut:]], axis=-2)


def per_device(
    tokens_in,
    cotangent,
    routes,
    order,
    segment_ids,
    gain_attn,
    w_query,
    w_key,
    w_value,
    w_out,
    gain_ffn,
    w_router,
    w_gate,
    w_up,
    w_down,
):
    tok_count = tokens_in.shape[1]
    width = tokens_in.shape[2]
    seq_count = lax.axis_size("seq")
    shard_count = lax.axis_size("fsdp")
    seq_index = lax.axis_index("seq")
    core = lax.rem(lax.axis_index("fsdp"), 2)
    place = jnp.stack([seq_index, core]).astype(jnp.int32)
    group_tok = seq_count * tok_count
    prompt_len = group_tok - segment_ids.shape[1]
    local_experts = w_gate.shape[1]
    expert_count = local_experts * seq_count
    capacity = 9 * tok_count * TOPK // (8 * expert_count)
    total_slots = expert_count * capacity
    head_local = HEADS // seq_count
    local_width = head_local * HD
    dense_rows = w_query.shape[1]
    shard_rows = dense_rows * seq_count
    gate_rows = w_gate.shape[2]
    down_rows = w_down.shape[2]
    expert_rows = 2 * gate_rows + 2 * down_rows
    qkv_width = (HEADS + 2 * KVHEADS) * HD
    half_width = width // 2
    inner_width = w_gate.shape[3]
    slot_rows = seq_count * capacity

    cos_half, sin_half, labels = group_tables(segment_ids[0], prompt_len)
    cos_all = jnp.concatenate([cos_half, cos_half], axis=1)
    sin_all = jnp.concatenate([-sin_half, sin_half], axis=1)
    cos_own = lax.dynamic_slice_in_dim(cos_all, seq_index * tok_count, tok_count, 0)
    sin_own = lax.dynamic_slice_in_dim(sin_all, seq_index * tok_count, tok_count, 0)
    key_pos = jnp.arange(group_tok, dtype=jnp.int32)
    allowed = jnp.logical_and(
        key_pos[None, :] <= key_pos[:, None],
        jnp.logical_or(key_pos[None, :] < prompt_len, labels[None, :] == labels[:, None]),
    )
    bias = jnp.where(allowed, 0.0, masked_value)

    column = jnp.arange(width // seq_count, dtype=jnp.int32)
    natural = (
        column % shard_rows // dense_rows * (width // seq_count // seq_count)
        + column // shard_rows * dense_rows
        + column % dense_rows
    )
    spread = (column[:, None] == natural[None, :]).astype(bf16)

    def small_rows_of(layer):
        return jnp.concatenate(
            [
                w_router[layer],
                gain_attn[layer][:, None],
                gain_ffn[layer][:, None],
                jnp.zeros((dense_rows, HD - 2 - expert_count), bf16),
            ],
            axis=1,
        )

    def dense_rows_of(layer):
        return jnp.concatenate(
            [w_query[layer], w_key[layer], w_value[layer], small_rows_of(layer), w_out[layer]],
            axis=1,
        )

    def shards_of_core(count):
        rows = count // shard_count
        wanted = jnp.arange(count // 2, dtype=jnp.int32)
        wanted = (wanted // rows * 2 + core) * rows + wanted % rows
        return (jnp.arange(count, dtype=jnp.int32)[:, None] == wanted[None, :]).astype(bf16)

    picks = (shards_of_core(width), shards_of_core(inner_width))

    def spread_seq(dense):
        dense = swap_seq(jnp.broadcast_to(dense[None], (seq_count,) + dense.shape))
        return dense.reshape(shard_rows, dense.shape[2])

    def own_columns(weight):
        pick = seq_index * KVHEADS // seq_count
        starts = (seq_index * local_width, (HEADS + pick) * HD, (HEADS + KVHEADS + pick) * HD)
        parts = [
            lax.dynamic_slice_in_dim(weight, start, size, 1)
            for start, size in zip(starts, (local_width, HD, HD))
        ]
        return jnp.concatenate(parts + [weight[:, qkv_width : qkv_width + HD]], axis=1)

    def expert_part(layer):
        return [
            part
            for e in range(local_experts)
            for part in (w_gate[layer, e], w_up[layer, e], halves(w_down[layer, e]))
        ]

    def out_part(dense):
        return [halves(dense[:, qkv_width + HD :])]

    def qkv_part(dense):
        wide = jnp.concatenate(
            [dense[:, : qkv_width + HD], jnp.zeros((shard_rows, HD), bf16)], axis=1
        )
        return [wide[:, at : at + half_width] for at in range(0, wide.shape[1], half_width)]

    def fetch(parts):
        return lax.all_gather(jnp.concatenate(parts, axis=0), "fsdp", axis=0, tiled=False)

    chips = [[i + c for i in range(0, shard_count, 2)] for c in range(2)]

    def swap_chips(block):
        return lax.all_to_all(
            block, "fsdp", split_axis=0, concat_axis=0, tiled=True, axis_index_groups=chips
        )

    def swap_cores(block):
        return lax.ppermute(block, "fsdp", [(i, i ^ 1) for i in range(shard_count)])

    def both_cores(block):
        other = swap_cores(block)
        first = jnp.where(core == 0, block, other)
        second = jnp.where(core == 0, other, block)
        return jnp.stack([first, second], axis=1).reshape((shard_count,) + block.shape[1:])

    def to_chips(block):
        return swap_chips(jnp.broadcast_to(block[None], (shard_count // 2,) + block.shape))

    weight_parts = [
        (e * expert_rows + k * gate_rows, gate_rows) for e in range(local_experts) for k in range(3)
    ]
    back_parts = [weight_parts[3 * e + k] for e in range(local_experts) for k in (2, 0, 1)]
    out_cut = ((1, local_experts * expert_rows, 2 * shard_rows),)

    slots_shape = shape((seq_count, local_experts, capacity, width), bf16)
    inner_shape = (local_experts, slot_rows, inner_width)
    expert_flops = 6 * total_slots * width * inner_width
    dense_flops = 2 * tok_count * width * width
    records = []
    hidden = tokens_in[0]
    dense = spread_seq(jnp.concatenate([dense_rows_of(0), small_rows_of(1)], axis=1))
    columns = jnp.concatenate([own_columns(dense), dense[:, -HD:]], axis=1)
    dense = dense[:, :-HD]
    columns, hidden = lax.optimization_barrier((columns, hidden))
    token_blocks = around_seq(hidden)
    packs = [fetch(expert_part(0) + out_part(dense)), None]
    columns = to_chips(columns)
    pairs = jnp.concatenate(
        [array[layer, 0].T for array in (routes, order) for layer in range(LAYERS)], axis=0
    )
    pairs = swap_seq(jnp.broadcast_to(pairs[None], (seq_count,) + pairs.shape))
    pairs = pairs.reshape(seq_count, 2, LAYERS, TOPK, tok_count)
    slots_of = functools.partial(slot_table, expert_count=expert_count, capacity=capacity)
    all_routes = [pairs[:, 0, layer] for layer in range(LAYERS)]
    all_targets = [
        jax.vmap(slots_of)(pairs[:, 0, layer], pairs[:, 1, layer]) for layer in range(LAYERS)
    ]
    targets = [lax.dynamic_index_in_dim(t, seq_index, 0, False) for t in all_targets]
    routes_ts = [lax.dynamic_index_in_dim(t, seq_index, 0, False) for t in all_routes]
    early = (token_blocks, all_targets, all_routes, targets, routes_ts)
    early = early + (cos_all, sin_all, bias, spread, picks)
    columns, early = lax.optimization_barrier((columns, early))
    token_blocks, all_targets, all_routes, targets, routes_ts = early[:5]
    cos_all, sin_all, bias, spread, picks = early[5:]
    first_columns = both_cores(columns).reshape(width, columns.shape[2])
    first_columns, grad_rows = lax.optimization_barrier((first_columns, cotangent[0]))
    grad_blocks = around_seq(grad_rows)
    own_at = local_experts * expert_rows + 2 * shard_rows
    heads_shape = shape((seq_count, tok_count, local_width + 2 * HD), bf16)
    attended_shape = shape((seq_count, tok_count, local_width), bf16)
    normed_shape = shape((seq_count, tok_count, width), bf16)
    small_shape = shape((LAYERS, 2 * expert_count, width), bf16)
    attention_flops = 4 * head_local * group_tok * group_tok * HD + 2 * dense_flops
    for layer in range(LAYERS):
        pack, routes_t, target_t = packs[layer], routes_ts[layer], targets[layer]
        if layer == 0:
            heads, attended, normed_all, smalls = once(
                first_attention_kernel,
                [heads_shape, attended_shape, normed_shape, small_shape],
                place, *token_blocks, first_columns, spread, cos_all, sin_all, bias,
                scalar=True, flops=attention_flops + 4 * dense_flops,
            )
            small = smalls[layer]
        else:
            small = smalls[layer]
            normed_p, hidden = once(
                input_kernel,
                [shape((tok_count, width), bf16), shape((tok_count, width), f32)],
                middle, combined, gates_t, above_target, small, spread, flops=2 * dense_flops,
            )
            heads, attended, normed_all = once(
                next_attention_kernel,
                [heads_shape, attended_shape, normed_shape],
                place, *around_seq(normed_p), pack, cos_all, sin_all, bias,
                scalar=True, cut={5: ((1, own_at, shard_rows),)}, flops=attention_flops,
            )
        if layer == 0:
            attended, next_rows = lax.optimization_barrier((attended, dense_rows_of(1)))
            back = swap_seq(attended)
            next_dense = spread_seq(next_rows)
            next_parts = expert_part(1) + out_part(next_dense) + [own_columns(next_dense)]
            next_parts = jnp.concatenate(next_parts, axis=0)
            tied = lax.optimization_barrier((pack, next_parts, back, grad_blocks))
            pack, next_parts, back, grad_blocks = tied
            packs = [pack, fetch([next_parts])]
        else:
            back = swap_seq(attended)
            qkv_parts = jnp.concatenate(qkv_part(dense) + qkv_part(next_dense), axis=0)
            qkv_parts, back = lax.optimization_barrier((qkv_parts, back))
            qkv_w = fetch([qkv_parts])
        middle, normed_ffn, gates_t = once(
            after_attention_kernel,
            [
                shape((tok_count, width), f32),
                shape((tok_count, width), bf16),
                shape((2 * TOPK, tok_count), f32),
            ],
            back, spread, hidden, small, pack, routes_t,
            cut={4: out_cut}, flops=3 * dense_flops,
        )
        expert_out, received, gate_val, up_val, all_gates = once(
            expert_kernel,
            [
                slots_shape,
                shape((local_experts, slot_rows, width), bf16),
                shape(inner_shape, bf16),
                shape(inner_shape, bf16),
                shape((seq_count, 2 * TOPK, tok_count), f32),
            ],
            place, *around_seq(normed_ffn), all_targets[layer], all_routes[layer], small,
            *[pack] * len(weight_parts),
            scalar=True,
            cut={n + 8: ((1, *part),) for n, part in enumerate(weight_parts)},
            pieces={n: (1 if n == 0 else 0, local_experts) for n in range(4)},
            flops=expert_flops,
        )
        (picked,) = once(
            pick_kernel,
            [shape((local_experts, 2 * slot_rows, width // 2), bf16)],
            received, swap_cores(received), picks[0],
            pieces={0: (0, local_experts)}, flops=expert_flops // 3,
        )
        combined, picked = lax.optimization_barrier(
            (swap_seq(expert_out).reshape(total_slots, width), picked)
        )
        above_target = target_t
        records.append(
            (
                (pack, small, routes_t, target_t),
                (hidden, normed_all, heads, attended),
                (middle, normed_ffn, gates_t, combined),
                (picked, gate_val, up_val, all_gates),
            )
        )
    (result,) = once(
        result_kernel, [shape((tok_count, width), bf16)], middle, combined, gates_t, target_t,
        flops=dense_flops,
    )

    def spread_qkv(block, out_block):
        gain = out_block[dense_rows, :shard_rows]
        label = jnp.arange(local_width + 3 * HD)[None, :]
        block = jnp.where(label == local_width + 2 * HD + expert_count, gain[:, None], block)
        return swap_seq(block.reshape(seq_count, dense_rows, local_width + 3 * HD))

    def shard_sum(blocks):
        own, other = blocks
        block = (own.astype(f32) + swap_cores(other).astype(f32)).astype(bf16)
        return jnp.sum(swap_chips(block).astype(f32), axis=0)

    out_rows = 16

    grad_hidden = cotangent[0].astype(f32)
    sums, gains = [None] * LAYERS, [None] * LAYERS
    branches, attendeds = [None] * LAYERS, [None] * LAYERS
    waiting = None
    for layer in range(LAYERS - 1, -1, -1):
        weights, attn_saved, mid_saved, expert_saved = records[layer]
        pack, small, routes_t, target_t = weights
        row = layer * 3 * shard_rows
        below, normed_all, heads, attended = attn_saved
        middle, normed_ffn, gates_t, combined = mid_saved
        picked, gate_val, up_val, all_gates = expert_saved
        if waiting is None:
            tied = lax.optimization_barrier((grad_blocks, qkv_w, result, combined))
            grad_blocks, qkv_w, result, combined = tied
        else:
            grad_blocks, waiting = lax.optimization_barrier((grad_blocks, waiting))
        grad_rows, kept = once(
            expert_back_kernel,
            [slots_shape, shape((local_experts, slot_rows, width + 3 * inner_width), bf16)],
            place, *grad_blocks, all_targets[layer], all_gates, pack, gate_val, up_val,
            *[pack] * (len(back_parts) - 1),
            scalar=True,
            cut={n + 9 if n else 7: ((1, *part),) for n, part in enumerate(back_parts)},
            pieces={0: (1, local_experts), 1: (0, local_experts)},
            flops=expert_flops,
        )
        if layer < LAYERS - 1:
            tied = lax.optimization_barrier((grad_blocks, branches[layer + 1]))
            grad_rows, branches[layer + 1] = lax.optimization_barrier((grad_rows, around_seq(tied[1])))
        (logits_grad,) = once(
            logits_grad_kernel,
            [shape((2 * expert_count, tok_count), bf16)],
            grad_hidden, combined, gates_t, routes_t, target_t, flops=3 * dense_flops,
        )
        sent = swap_seq(grad_rows)
        extra = () if layer == LAYERS - 1 else waiting
        pack_rows = local_experts * expert_rows + (shard_rows if extra else 0)
        (packed,) = once(
            expert_weight_kernel,
            [shape((shard_count // 2, pack_rows, half_width), bf16)],
            picked, picks[1], kept, swap_cores(kept), *extra,
            pieces={0: (1, pack_rows // 16)}, flops=2 * expert_flops,
        )
        sent, packed_too, logits_grad = lax.optimization_barrier((sent, packed, logits_grad))
        if layer < LAYERS - 1:
            packed, sums[layer + 1] = lax.optimization_barrier((packed, sums[layer + 1]))
        summed = lax.psum_scatter(
            packed.reshape(-1, half_width), "fsdp", scatter_dimension=0, tiled=True,
            axis_index_groups=chips,
        )
        grad_middle, branch, send, small_grad = once(
            after_experts_kernel,
            [
                shape((tok_count, width), f32),
                shape((tok_count, width), bf16),
                shape((seq_count, tok_count, local_width), bf16),
                shape((2 * expert_count, width), f32),
            ],
            grad_hidden, sent.reshape(total_slots, width), middle, normed_ffn, logits_grad,
            target_t, small, pack, spread,
            cut={7: out_cut}, flops=4 * dense_flops,
        )
        grad_heads = swap_seq(send)
        (grad_own,) = once(
            attention_back_kernel,
            [shape((seq_count, tok_count, local_width + 2 * HD), bf16)],
            heads, grad_heads, bias, cos_all, sin_all,
            flops=10 * head_local * group_tok * group_tok * HD,
        )
        qkv_block_grad = once(
            qkv_weight_kernel,
            [shape((shard_count // 2, shard_rows, half_width), bf16)] * 2,
            place, normed_all, grad_own, small_grad, spread, scalar=True, flops=2 * dense_flops,
        )
        sent, qkv_block_grad = lax.optimization_barrier((swap_seq(grad_own), qkv_block_grad))
        grad_hidden, grad_low, gains[layer] = once(
            before_attention_kernel,
            [
                shape((tok_count, width), f32),
                shape((tok_count, width), bf16),
                shape((shard_count, HD), f32),
            ],
            sent, qkv_w, qkv_w, qkv_w, spread, small, below, grad_middle,
            cut={
                1: ((1, row, shard_rows),),
                2: ((1, row + shard_rows, shard_rows),),
                3: ((1, row + 2 * shard_rows, shard_rows), (2, 0, 2 * KVHEADS * HD)),
            },
            flops=4 * dense_flops,
        )
        branches[layer], attendeds[layer], sums[layer] = branch, attended, summed
        if layer > 0:
            grad_blocks = around_seq(grad_low)
            waiting = (qkv_block_grad[0], swap_cores(qkv_block_grad[1]))
    qkv_sum = shard_sum(qkv_block_grad)
    branches[0] = around_seq(branches[0])
    branches[0], qkv_sum = lax.optimization_barrier((branches[0], qkv_sum))
    out_block_grad = once(
        out_weight_kernel,
        [shape((shard_count // 2, 2 * LAYERS * out_rows, half_width), bf16)] * 2,
        place, *branches[0], *branches[1], *attendeds, *gains,
        scalar=True, flops=2 * dense_flops,
    )

    out_sum = shard_sum(out_block_grad)
    out_sums = [out_sum[2 * out_rows * n : 2 * out_rows * (n + 1)] for n in range(LAYERS)]
    own_rows = spread_qkv(qkv_sum, out_sums[0])
    above_rows = spread_qkv(sums[0][local_experts * expert_rows :].astype(f32), out_sums[1])
    gate_grads, up_grads, down_grads = once(
        expert_grads_kernel,
        [
            shape((LAYERS,) + w_gate.shape[1:], f32),
            shape((LAYERS,) + w_up.shape[1:], f32),
            shape((LAYERS,) + w_down.shape[1:], f32),
        ],
        *sums,
        cut={0: ((0, 0, local_experts * expert_rows),)},
    )
    query_grads, key_grads, value_grads, out_grads, small_grads = once(
        dense_grads_kernel,
        [
            shape((dense_rows, LAYERS, HEADS * HD), f32),
            shape((dense_rows, LAYERS, KVHEADS * HD), f32),
            shape((dense_rows, LAYERS, KVHEADS * HD), f32),
            shape((dense_rows, LAYERS, width), f32),
            shape((LAYERS, dense_rows, HD), f32),
        ],
        own_rows, above_rows, *out_sums,
    )
    return (
        result[None],
        grad_hidden[None],
        small_grads[:, :, expert_count],
        query_grads.transpose(1, 0, 2),
        key_grads.transpose(1, 0, 2),
        value_grads.transpose(1, 0, 2),
        out_grads.transpose(1, 0, 2),
        small_grads[:, :, expert_count + 1],
        small_grads[:, :, :expert_count],
        gate_grads,
        up_grads,
        down_grads,
    )


def solution(mesh):
    in_specs = (
        P("fsdp", "seq", None),
        P("fsdp", "seq", None),
        P(None, "fsdp", "seq", None),
        P(None, "fsdp", "seq", None),
        P("fsdp", None),
        P(None, ("seq", "fsdp")),
        P(None, ("seq", "fsdp"), None),
        P(None, ("seq", "fsdp"), None),
        P(None, ("seq", "fsdp"), None),
        P(None, ("seq", "fsdp"), None),
        P(None, ("seq", "fsdp")),
        P(None, ("seq", "fsdp"), None),
        P(None, "seq", "fsdp", None),
        P(None, "seq", "fsdp", None),
        P(None, "seq", "fsdp", None),
    )
    out_specs = (
        P("fsdp", "seq", None),
        P("fsdp", "seq", None),
        P(None, ("seq", "fsdp")),
        P(None, ("seq", "fsdp"), None),
        P(None, ("seq", "fsdp"), None),
        P(None, ("seq", "fsdp"), None),
        P(None, ("seq", "fsdp"), None),
        P(None, ("seq", "fsdp")),
        P(None, ("seq", "fsdp"), None),
        P(None, "seq", "fsdp", None),
        P(None, "seq", "fsdp", None),
        P(None, "seq", "fsdp", None),
    )
    return jax.shard_map(
        per_device, mesh=mesh, in_specs=in_specs, out_specs=out_specs, check_vma=False
    )
```

```python
import functools

import jax
import jax.numpy as jnp
import numpy as np
from jax import lax
from jax.experimental import pallas as pl
from jax.experimental.pallas import tpu as pltpu
from jax.sharding import PartitionSpec as P

HEADS = 12
KVHEADS = 2
HD = 128
TOPK = 4
LAYERS = 2
NCONT = 4

norm_eps = 1e-06
rope_base = 10000.0
masked_value = -1e30

bf16 = jnp.bfloat16
f32 = jnp.float32
VMEM_BYTES = 64 * 1024 * 1024 - 256 * 1024


def group_tables(segment_row, prompt_len):
    cont_len = segment_row.shape[0]
    onehot = (segment_row[:, None] == jnp.arange(NCONT, dtype=jnp.int32)[None, :]).astype(jnp.int32)
    counts = jnp.sum(onehot, axis=0)
    starts = jnp.cumsum(counts) - counts
    seg_begin = jnp.sum(onehot * starts[None, :], axis=1)
    within = jnp.arange(cont_len, dtype=jnp.int32) - seg_begin
    positions = jnp.concatenate([jnp.arange(prompt_len, dtype=jnp.int32), prompt_len + within])
    labels = jnp.concatenate([jnp.full((prompt_len,), -1, jnp.int32), segment_row])
    frequency = rope_base ** (-(jnp.arange(HD // 2, dtype=jnp.float32) * 2.0 / HD))
    angles = positions.astype(jnp.float32)[:, None] * frequency[None, :]
    return (jnp.cos(angles), jnp.sin(angles), labels)


def slot_table(routes_t, order_t, expert_count, capacity):
    pair_expert = routes_t.reshape(-1)
    pair_order = order_t.reshape(-1)
    same_expert = pair_expert[:, None] == pair_expert[None, :]
    earlier = pair_order[None, :] < pair_order[:, None]
    pair_slot = jnp.sum(jnp.logical_and(same_expert, earlier).astype(jnp.int32), axis=1)
    target = jnp.where(
        pair_slot < capacity, pair_expert * capacity + pair_slot, expert_count * capacity
    )
    return target.reshape(routes_t.shape)


def nn(left, right):
    return lax.dot_general(left, right, (((1,), (0,)), ((), ())), preferred_element_type=f32)


def nt(left, right):
    return lax.dot_general(left, right, (((1,), (1,)), ((), ())), preferred_element_type=f32)


def tn(left, right):
    return lax.dot_general(left, right, (((0,), (0,)), ((), ())), preferred_element_type=f32)


def split(value):
    high = value.astype(bf16)
    return high, (value - high.astype(f32)).astype(bf16)


class Late:
    def __init__(self, ref, copy):
        self.ref, self.copy, self.shape = ref, copy, ref.shape
        copy.start()

    def wait(self):
        if self.copy is not None:
            self.copy.wait()
            self.copy = None

    def __getitem__(self, index):
        self.wait()
        return self.ref[index]


class Out:
    def __init__(self, ref, copies):
        self.ref, self.copies, self.shape = ref, copies, ref.shape
        self.sent = [False] * len(copies)

    def send(self, piece=None):
        for n in range(len(self.copies)) if piece is None else (piece,):
            if not self.sent[n]:
                self.copies[n].start()
                self.sent[n] = True

    def __getitem__(self, index):
        return self.ref[index]

    def __setitem__(self, index, value):
        self.ref[index] = value


def cost(args, outs, flops):
    moved = sum(int(np.prod(a.shape)) * a.dtype.itemsize for a in (*args, *outs))
    return pl.CostEstimate(flops=flops, bytes_accessed=moved, transcendentals=0)


def once(kernel, outs, *args, scalar=False, cut=None, pieces=None, flops=0):
    cut, pieces = cut or {}, pieces or {}
    hbm = pl.BlockSpec(memory_space=pltpu.HBM)
    late = [n for n in range(len(args)) if not (scalar and n == 0)]
    specs = [hbm] * len(args)
    if scalar:
        specs[0] = pl.BlockSpec(memory_space=pltpu.SMEM)
    scratch = []
    for n in late:
        dims = list(args[n].shape)
        for dim, start, size in cut.get(n, ()):
            dims[dim] = size
        scratch.append(pltpu.VMEM(tuple(dims), args[n].dtype))
    scratch += [pltpu.VMEM(o.shape, o.dtype) for o in outs]
    parts = [pieces.get(n, (0, 1)) for n in range(len(outs))]
    scratch.append(pltpu.SemaphoreType.DMA((len(late) + sum(count for _, count in parts),)))

    def body(*refs):
        ins = list(refs[: len(args)])
        out_refs = refs[len(args) : len(args) + len(outs)]
        rooms = refs[len(args) + len(outs) : -1]
        sems = refs[-1]
        for i, n in enumerate(late):
            source = ins[n]
            for dim, start, size in cut.get(n, ()):
                if callable(start):
                    start = pl.multiple_of(start(ins[0][0]), 16 if dim == 1 else HD)
                source = source.at[(slice(None),) * dim + (pl.ds(start, size),)]
            ins[n] = Late(rooms[i], pltpu.make_async_copy(source, rooms[i], sems.at[i]))
        results = []
        used = len(late)
        for i, out in enumerate(out_refs):
            room = rooms[len(late) + i]
            dim, count = parts[i]
            size = room.shape[dim] // count
            copies = []
            for n in range(count):
                at = (slice(None),) * dim + (pl.ds(n * size, size),)
                copies.append(pltpu.make_async_copy(room.at[at], out.at[at], sems.at[used]))
                used += 1
            results.append(Out(room, copies))
        kernel(*ins, *results)
        for result in results:
            result.send()
        for n in late:
            ins[n].wait()
        for result in results:
            for copy in result.copies:
                copy.wait()

    return pl.pallas_call(
        body,
        out_shape=list(outs),
        in_specs=specs,
        out_specs=[hbm] * len(outs),
        scratch_shapes=scratch,
        compiler_params=pltpu.CompilerParams(vmem_limit_bytes=VMEM_BYTES),
        cost_estimate=cost(args, outs, flops),
    )(*args)


def shape(dims, dtype):
    return jax.ShapeDtypeStruct(dims, dtype)


def normalize(value, gain):
    inverse = lax.rsqrt(jnp.mean(value * value, axis=-1, keepdims=True) + norm_eps)
    return value * inverse * gain


def normalize_back(value, gain, grad):
    inverse = lax.rsqrt(jnp.mean(value * value, axis=-1, keepdims=True) + norm_eps)
    unit = value * inverse
    grad_gain = jnp.sum(grad * unit, axis=0, keepdims=True)
    scaled = grad * gain
    grad_value = inverse * (scaled - unit * jnp.mean(scaled * unit, axis=-1, keepdims=True))
    return grad_value, grad_gain


def to_gathered(parts, order):
    count = len(parts)
    share = parts[0].shape[1] // count
    done = []
    for j in range(count):
        piece = jnp.concatenate([part[:, j * share : (j + 1) * share] for part in parts], axis=1)
        done.append(nn(piece, order))
    return jnp.concatenate(done, axis=1)


def to_natural(value, order):
    count = value.shape[1] // order.shape[0]
    size = order.shape[0]
    share = size // count
    done = [nt(value[:, j * size : (j + 1) * size], order) for j in range(count)]
    return [
        jnp.concatenate([part[:, s * share : (s + 1) * share] for part in done], axis=1)
        for s in range(count)
    ]


def column_blocks(value, count):
    size = value.shape[1] // count
    return [value[:, s * size : (s + 1) * size] for s in range(count)]


def turn(block, cosines, sines):
    return block * cosines + pltpu.roll(block, HD // 2, 1) * sines


def smooth_parts(value):
    root = np.float32(np.sqrt(2.0 / np.pi))
    square = value * value
    high = jnp.tanh(root * (value + 0.044715 * value * square))
    half = 0.5 * (1.0 + high)
    slope = half + 0.5 * value * (1.0 - high * high) * root * (1.0 + 3 * 0.044715 * square)
    return value * half, slope


def choose(target_t, slots):
    place = lax.broadcasted_iota(jnp.int32, (slots, target_t.shape[1]), 0)
    total = jnp.zeros(place.shape, f32)
    for k in range(TOPK):
        total = total + jnp.where(place == target_t[k : k + 1], 1.0, 0.0)
    return total


def choose_weighted(target_t, gates_t, slots):
    place = lax.broadcasted_iota(jnp.int32, (slots, target_t.shape[1]), 0)
    total = jnp.zeros(place.shape, f32)
    for k in range(TOPK):
        total = total + jnp.where(place == target_t[k : k + 1], gates_t[k : k + 1], 0.0)
    return total


def input_kernel(
    middle, combined, gates_t, target_t, small, spread, normed_ref, hidden_ref
):
    expert_count = 8
    hidden = middle[...] + mix(combined[...], gates_t[...], target_t[...])
    hidden_ref[...] = hidden
    hidden_ref.send()
    gain = small[expert_count : expert_count + 1].astype(f32)
    normed = normalize(hidden, gain).astype(bf16)
    count = normed.shape[1] // spread.shape[0]
    normed_ref[...] = to_gathered(column_blocks(normed, count), spread[...]).astype(bf16)


def mix(combined, gates_t, target_t):
    high, low = split(choose_weighted(target_t, gates_t, combined.shape[0]))
    tokens = high.shape[1]
    both = tn(jnp.concatenate([high, low], axis=1), combined)
    return both[:tokens] + both[tokens:]


def result_kernel(middle, combined, gates_t, target_t, result_ref):
    mixture = mix(combined[...], gates_t[...], target_t[...])
    result_ref[...] = (middle[...] + mixture).astype(bf16)


def attend(rows, weight, cosines, sines, bias_ref, heads_ref, out_ref):
    seq_count, tokens, columns = heads_ref.shape
    group = seq_count * tokens
    local = columns // HD - 2
    prompt = group // 2
    raw = nn(rows, weight)
    heads = []
    for j in range(local + 2):
        block = raw[:, j * HD : (j + 1) * HD]
        if j <= local:
            block = turn(block, cosines, sines)
        heads.append(block.astype(bf16))
        heads_ref[:, :, j * HD : (j + 1) * HD] = heads[j].reshape(seq_count, tokens, HD)
    heads_ref.send()
    key, value = heads[local], heads[local + 1]
    scale = HD ** (-0.5)
    for j in range(local):
        query = heads[j]
        for rows, seen in ((slice(0, prompt), prompt), (slice(prompt, group), group)):
            scores = nt(query[rows], key[:seen]) * scale + bias_ref[rows, :seen]
            peak = jnp.max(scores, axis=-1, keepdims=True)
            weights = jnp.exp(scores - peak)
            weights = weights / jnp.sum(weights, axis=-1, keepdims=True)
            part = nn(weights.astype(bf16), value[:seen]).astype(bf16)
            first = rows.start // tokens
            out_ref[first : first + prompt // tokens, :, j * HD : (j + 1) * HD] = part.reshape(
                prompt // tokens, tokens, HD
            )


def first_attention_kernel(
    place, own, one, two, three, weight, spread, cosines, sines, bias_ref,
    heads_ref, out_ref, normed_ref, small_ref,
):
    expert_count = 8
    me = place[0]
    seq_count, tokens, width = normed_ref.shape
    columns = heads_ref.shape[2]
    count = small_ref.shape[1]
    extras = weight[:, columns:].astype(f32).T.astype(bf16)
    extras = jnp.concatenate([extras[:count], extras[HD : HD + count]], axis=0)
    small = jnp.concatenate(to_natural(extras, spread[...]), axis=1)
    small_ref[0] = small[:count].astype(bf16)
    small_ref[1] = small[count:].astype(bf16)
    small_ref.send()
    gain = small[expert_count : expert_count + 1]
    for k, block in enumerate((own, one, two, three)):
        normed = normalize(block[...].astype(f32), gain).astype(bf16)
        normed = to_gathered(column_blocks(normed, seq_count), spread[...]).astype(bf16)
        normed_ref[lax.rem(me + k, seq_count)] = normed
    normed_ref.send()
    rows = normed_ref[...].reshape(seq_count * tokens, width)
    attend(rows, weight[:, :columns], cosines[...], sines[...], bias_ref, heads_ref, out_ref)


def next_attention_kernel(
    place, own, one, two, three, weight, cosines, sines, bias_ref, heads_ref, out_ref, normed_ref
):
    me = place[0]
    seq_count, tokens, width = normed_ref.shape
    weight = weight[...].reshape(width, weight.shape[2])[:, : heads_ref.shape[2]]
    for k, block in enumerate((own, one, two, three)):
        normed_ref[lax.rem(me + k, seq_count)] = block[...]
    normed_ref.send()
    rows = normed_ref[...].reshape(seq_count * tokens, width)
    attend(rows, weight, cosines[...], sines[...], bias_ref, heads_ref, out_ref)


def gates_of(logits, routes_t, rows):
    expert_count = 8
    tokens = logits.shape[1]
    chosen = []
    for k in range(TOPK):
        route = routes_t[k : k + 1]
        value = jnp.zeros((1, tokens), f32)
        for e in range(expert_count):
            value = value + jnp.where(route == e, logits[e : e + 1], 0.0)
        chosen.append(value)
    peak = functools.reduce(jnp.maximum, chosen)
    powers = [jnp.exp(value - peak) for value in chosen]
    total = functools.reduce(jnp.add, powers)
    gates = [power / total for power in powers]
    return jnp.concatenate(gates + [jnp.zeros((rows - TOPK, tokens), f32)], axis=0)


def after_attention_kernel(
    back, spread, hidden, small, out_w, routes_t, middle_ref, normed_ref, gates_ref
):
    expert_count = 8
    seq_count, tokens, part = back.shape
    width = seq_count * part
    attended = to_gathered([back[s] for s in range(seq_count)], spread[...]).astype(bf16)
    rows = out_w.shape[1] // 2
    half = out_w.shape[2]
    for side in range(2):
        weight = out_w[:, side * rows : (side + 1) * rows].reshape(width, half)
        cols = slice(side * half, (side + 1) * half)
        middle_ref[:, cols] = hidden[:, cols].astype(f32) + nn(attended, weight)
    middle_ref.send()
    middle = middle_ref[...]
    gain = small[expert_count + 1 : expert_count + 2].astype(f32)
    normed = normalize(middle, gain).astype(bf16)
    normed_ref[...] = normed
    normed_ref.send()
    gates_ref[...] = gates_of(nt(small[...], normed), routes_t[...], gates_ref.shape[0])


def down_parts(block):
    shards, rows, half = block.shape
    wide = block.astype(f32)
    left = wide[:, : rows // 2].reshape(shards * rows // 2, half).astype(bf16)
    right = wide[:, rows // 2 :].reshape(shards * rows // 2, half).astype(bf16)
    return left, right


def expert_kernel(place, own, one, two, three, targets, routes, small, *rest):
    me = place[0]
    blocks = (own, one, two, three)
    out_ref, rows_ref, gate_ref, up_ref, gates_ref = rest[-5:]
    weights = rest[:-5]
    sources, experts, capacity, width = out_ref.shape
    half = width // 2
    for e in range(experts):
        gate_w, up_w, down_w = weights[3 * e : 3 * e + 3]
        first = (me * experts + e) * capacity
        parts = []
        for k, block in enumerate(blocks):
            hot = choose(targets[lax.rem(me + k, sources)] - first, capacity)
            parts.append(nn(hot.astype(bf16), block[...]))
        tokens = jnp.concatenate(parts, axis=0).astype(bf16)
        rows_ref[e] = tokens
        rows_ref.send(e)
        gate_val = nn(tokens, gate_w[...].reshape(width, half))
        gate_ref[e] = gate_val.astype(bf16)
        gate_ref.send(e)
        up_val = nn(tokens, up_w[...].reshape(width, half))
        up_ref[e] = up_val.astype(bf16)
        up_ref.send(e)
        activated, slope = smooth_parts(gate_val)
        inner = (activated * up_val).astype(bf16)
        for side, part in enumerate(down_parts(down_w[...])):
            done = nn(inner, part).astype(bf16)
            for k in range(sources):
                out_ref[lax.rem(me + k, sources), e, :, side * half : (side + 1) * half] = done[
                    k * capacity : (k + 1) * capacity
                ]
        out_ref.send(e)
    for k, block in enumerate(blocks):
        logits = nt(small[...], block[...])
        gates_ref[k] = gates_of(logits, routes[lax.rem(me + k, sources)], gates_ref.shape[1])


def logits_grad_kernel(grad, combined, gates_t, routes_t, target_t, logits_ref):
    tokens = grad.shape[0]
    slots = combined.shape[0]
    high, low = split(grad[...])
    products = nt(combined[...], jnp.concatenate([high, low], axis=0))
    products = products[:, :tokens] + products[:, tokens:]
    place = lax.broadcasted_iota(jnp.int32, (slots, tokens), 0)
    grad_gates = [
        jnp.sum(jnp.where(place == target_t[k : k + 1], products, 0.0), axis=0, keepdims=True)
        for k in range(TOPK)
    ]
    gates = [gates_t[k : k + 1] for k in range(TOPK)]
    center = functools.reduce(jnp.add, [a * b for a, b in zip(gates, grad_gates)])
    label = lax.broadcasted_iota(jnp.int32, logits_ref.shape, 0)
    total = jnp.zeros(logits_ref.shape, f32)
    for k in range(TOPK):
        choice = gates[k] * (grad_gates[k] - center)
        total = total + jnp.where(label == routes_t[k : k + 1], choice, 0.0)
    logits_ref[...] = total.astype(bf16)


def expert_back_kernel(
    place, own, one, two, three, targets, gates, down_first, gate_ref, up_ref, *rest
):
    me = place[0]
    blocks = (own, one, two, three)
    out_ref, keep_ref = rest[-2:]
    weights = (down_first,) + rest[:-2]
    sources, experts, capacity, width = out_ref.shape
    half = width // 2
    for e in range(experts):
        down_w, gate_w, up_w = weights[3 * e : 3 * e + 3]
        shards, rows, _ = gate_w.shape
        first = (me * experts + e) * capacity
        parts = []
        for k, block in enumerate(blocks):
            target = targets[lax.rem(me + k, sources)] - first
            hot = jnp.concatenate(split(choose_weighted(target, gates[k], capacity)), axis=1)
            twice = jnp.concatenate([block[...], block[...]], axis=0)
            parts.append(nn(hot, twice))
        grad = jnp.concatenate(parts, axis=0).astype(bf16)
        keep_ref[e, :, :width] = grad
        left, right = down_parts(down_w[...])
        grad_inner = nt(grad[:, :half], left) + nt(grad[:, half:], right)
        up_val = up_ref[e].astype(f32)
        activated, slope = smooth_parts(gate_ref[e].astype(f32))
        gate_at, up_at, inner_at = (slice(width + n * half, width + (n + 1) * half) for n in range(3))
        keep_ref[e, :, gate_at] = (grad_inner * up_val * slope).astype(bf16)
        keep_ref[e, :, up_at] = (grad_inner * activated).astype(bf16)
        keep_ref[e, :, inner_at] = (activated * up_val).astype(bf16)
        keep_ref.send(e)
        parts = 4
        some, size = shards // parts, shards * rows // parts
        for c in range(parts):
            at = slice(c * some, (c + 1) * some)
            total = nt(keep_ref[e, :, gate_at], gate_w[at].reshape(size, half))
            total = total + nt(keep_ref[e, :, up_at], up_w[at].reshape(size, half))
            total = total.astype(bf16)
            for k in range(sources):
                out_ref[lax.rem(me + k, sources), e, :, c * size : (c + 1) * size] = total[
                    k * capacity : (k + 1) * capacity
                ]
        out_ref.send(e)


def pick_kernel(rows, other_rows, pick, out_ref):
    count = rows.shape[1]
    for e in range(rows.shape[0]):
        out_ref[e, :count] = nn(rows[e], pick[...]).astype(bf16)
        out_ref[e, count:] = nn(other_rows[e], pick[...]).astype(bf16)
        out_ref.send(e)


def expert_weight_kernel(tokens, pick_inner, keep, other_keep, *rest):
    pack_ref = rest[-1]
    chips, _, half = pack_ref.shape
    experts = tokens.shape[0]
    width = 2 * tokens.shape[2]
    count = width // (2 * chips)
    at = 0

    def send():
        for piece in range(at // 16, (at + count) // 16):
            pack_ref.send(piece)

    for e in range(experts):
        grads = jnp.concatenate([keep[e], other_keep[e]], axis=0)
        both = tn(tokens[e], grads[:, width : width + 2 * half]).astype(bf16)
        for n in range(2):
            block = both[:, n * half : (n + 1) * half].reshape(chips, count, half)
            pack_ref[:, at : at + count] = block
            send()
            at += count
        inner = nn(grads[:, width + 2 * half :], pick_inner[...]).astype(bf16)
        down = tn(inner, grads[:, :width])
        left = down[:, :half].reshape(chips, count // 2, half)
        right = down[:, half:].reshape(chips, count // 2, half)
        pack_ref[:, at : at + count] = jnp.concatenate([left, right], axis=1).astype(bf16)
        send()
        at += count
    if len(rest) > 1:
        own, other = rest[:2]
        pack_ref[:, at : at + count] = (own[...].astype(f32) + other[...].astype(f32)).astype(bf16)
        send()


def keep_shards(own_ref, other_ref, core, at, value):
    shards, rows, columns = value.shape
    value = value.reshape(shards // 2, 2, rows, columns)
    own_ref[:, at : at + rows] = jnp.where(core == 0, value[:, 0], value[:, 1])
    other_ref[:, at : at + rows] = jnp.where(core == 0, value[:, 1], value[:, 0])


def after_experts_kernel(
    grad, sent, middle, normed, logits_grad, target_t, small, out_w, spread,
    grad_ref, branch_ref, send_ref, small_ref,
):
    expert_count = 8
    seq_count, tokens, part = send_ref.shape
    width = seq_count * part
    chosen = choose(target_t[...], sent.shape[0]).astype(bf16)
    grad_normed = tn(chosen, sent[...]) + tn(logits_grad[...], small[...])
    router = nn(logits_grad[...], normed[...])
    gain = small[expert_count + 1 : expert_count + 2].astype(f32)
    grad_value, grad_gain = normalize_back(middle[...], gain, grad_normed)
    label = lax.broadcasted_iota(jnp.int32, small_ref.shape, 0)
    small_ref[...] = jnp.where(label == expert_count + 1, grad_gain, router)
    grad_middle = grad[...] + grad_value
    grad_ref[...] = grad_middle
    grad_ref.send()
    branch = grad_middle.astype(bf16)
    branch_ref[...] = branch
    branch_ref.send()
    rows = out_w.shape[1] // 2
    half = out_w.shape[2]
    parts = [
        nt(branch[:, :half], out_w[:, :rows].reshape(width, half)),
        nt(branch[:, half:], out_w[:, rows:].reshape(width, half)),
    ]
    attended = (parts[0] + parts[1]).astype(bf16)
    for s, block in enumerate(to_natural(attended, spread[...])):
        send_ref[s] = block.astype(bf16)


def attention_back_kernel(heads_ref, grad_ref, bias_ref, cosines, sines, out_ref):
    seq_count, tokens, columns = heads_ref.shape
    group = seq_count * tokens
    heads = heads_ref[...].reshape(group, columns)
    grads = grad_ref[...].reshape(group, grad_ref.shape[2])
    local = columns // HD - 2
    prompt = group // 2
    key = heads[:, local * HD : (local + 1) * HD]
    value = heads[:, (local + 1) * HD :]
    scale = HD ** (-0.5)

    def keep(at, block):
        out_ref[:, :, at * HD : (at + 1) * HD] = block.astype(bf16).reshape(seq_count, tokens, HD)

    cosines, sines = cosines[...], sines[...]

    def unturn(block):
        return block * cosines - pltpu.roll(block, HD // 2, 1) * sines

    grad_key = [jnp.zeros((prompt, HD), f32), jnp.zeros((prompt, HD), f32)]
    grad_value = [jnp.zeros((prompt, HD), f32), jnp.zeros((prompt, HD), f32)]
    for j in range(local):
        query = heads[:, j * HD : (j + 1) * HD]
        grad = grads[:, j * HD : (j + 1) * HD]
        grad_query = []
        for rows, seen in ((slice(0, prompt), prompt), (slice(prompt, group), group)):
            scores = nt(query[rows], key[:seen]) * scale + bias_ref[rows, :seen]
            peak = jnp.max(scores, axis=-1, keepdims=True)
            weights = jnp.exp(scores - peak)
            weights = weights / jnp.sum(weights, axis=-1, keepdims=True)
            grad_weights = nt(grad[rows], value[:seen])
            center = jnp.sum(weights * grad_weights, axis=-1, keepdims=True)
            grad_scores = (weights * (grad_weights - center)).astype(bf16)
            low = weights.astype(bf16)
            grad_query.append(nn(grad_scores, key[:seen]) * scale)
            for side in range(seen // prompt):
                cols = slice(side * prompt, (side + 1) * prompt)
                grad_key[side] = grad_key[side] + tn(grad_scores[:, cols], query[rows])
                grad_value[side] = grad_value[side] + tn(low[:, cols], grad[rows])
        keep(j, unturn(jnp.concatenate(grad_query, axis=0)))
    keep(local, unturn(jnp.concatenate(grad_key, axis=0) * scale))
    keep(local + 1, jnp.concatenate(grad_value, axis=0))


def before_attention_kernel(
    sent, left_w, right_w, kv_w, spread, small, hidden, grad_middle, out_ref, low_ref, gain_ref
):
    expert_count = 8
    seq_count, tokens, columns = sent.shape
    local = columns // HD - 2
    share = seq_count // KVHEADS
    blocks = [sent[s, :, : local * HD] for s in range(seq_count)]
    for at in (local, local + 1):
        for c in range(KVHEADS):
            total = jnp.zeros((tokens, HD), f32)
            for s in range(c * share, (c + 1) * share):
                total = total + sent[s, :, at * HD : (at + 1) * HD].astype(f32)
            blocks.append(total.astype(bf16))
    raw = jnp.concatenate(blocks, axis=1)
    at, total = 0, 0.0
    for part in (left_w, right_w, kv_w):
        shards, rows, columns = part.shape
        weight = part[...].reshape(shards * rows, columns)
        total = total + nt(raw[:, at : at + columns], weight)
        at += columns
    high, low = split(total)
    both = to_natural(jnp.concatenate([high, low], axis=0), spread[...])
    both = jnp.concatenate(both, axis=1)
    grad_normed = both[:tokens] + both[tokens:]
    gain = small[expert_count : expert_count + 1].astype(f32)
    grad_value, grad_gain = normalize_back(hidden[...].astype(f32), gain, grad_normed)
    total = grad_middle[...] + grad_value
    low_ref[...] = total.astype(bf16)
    low_ref.send()
    out_ref[...] = total
    out_ref.send()
    shards = gain_ref.shape[0]
    width = grad_gain.shape[1]
    share = width // seq_count
    part = share // shards
    shard = lax.broadcasted_iota(jnp.int32, (shards, width), 0)
    at = lax.broadcasted_iota(jnp.int32, (shards, width), 1)
    kept = jnp.where(at % share // part == shard, grad_gain, 0.0).astype(bf16)
    source = lax.broadcasted_iota(jnp.int32, (width, HD), 0)
    wanted = lax.broadcasted_iota(jnp.int32, (width, HD), 1)
    place = source // share * part + source % part
    gain_ref[...] = nn(kept, jnp.where(place == wanted, 1.0, 0.0).astype(bf16))


def qkv_weight_kernel(place, normed, grads, small, spread, own_ref, other_ref):
    seq_count, tokens, columns = grads.shape
    chips, rows, wide = own_ref.shape
    shards = 2 * chips
    inputs = normed[...].reshape(seq_count * tokens, normed.shape[2])
    total = tn(inputs, grads[...].reshape(seq_count * tokens, columns))
    extra = column_blocks(small[...].astype(bf16), seq_count)
    extra = to_gathered(extra, spread[...])
    extra = jnp.concatenate([extra, jnp.zeros((HD - extra.shape[0], extra.shape[1]), f32)], axis=0).T
    total = jnp.concatenate([total, extra], axis=1).astype(bf16).reshape(shards, rows, wide)
    keep_shards(own_ref, other_ref, place[1], 0, total)


def out_weight_kernel(place, *rest):
    own_ref, other_ref = rest[-2:]
    rest = rest[:-2]
    me = place[0]
    around = len(rest) // LAYERS - 2
    blocks, rest = rest[: LAYERS * around], rest[LAYERS * around :]
    chips, rows, half = own_ref.shape
    shards = 2 * chips
    rows = rows // (2 * LAYERS)
    for layer in range(LAYERS):
        attended, gain = rest[layer], rest[LAYERS + layer]
        seq_count, tokens, part = attended.shape
        valid = part // shards
        branch = [block[...] for block in blocks[layer * around : (layer + 1) * around]]
        branch = jnp.concatenate(branch, axis=0)
        heads = jnp.concatenate(
            [attended[lax.rem(me + k, seq_count)] for k in range(seq_count)], axis=0
        )
        place_in = lax.broadcasted_iota(jnp.int32, (part, shards * rows), 0)
        place_out = lax.broadcasted_iota(jnp.int32, (part, shards * rows), 1)
        source = place_out // rows * valid + place_out % rows
        same = jnp.logical_and(place_in == source, place_out % rows < valid)
        heads = nn(heads, jnp.where(same, 1.0, 0.0).astype(bf16)).astype(bf16)
        wide = jnp.concatenate([gain[...], jnp.zeros((shards, half - HD), f32)], axis=1)
        row = lax.broadcasted_iota(jnp.int32, (shards, rows, half), 1)
        for side in range(2):
            total = tn(heads, branch[:, side * half : (side + 1) * half])
            total = total.reshape(shards, rows, half)
            if side == 0:
                total = jnp.where(row == valid, wide[:, None, :], total)
            at = (2 * layer + side) * rows
            keep_shards(own_ref, other_ref, place[1], at, total.astype(bf16))


def expert_grads_kernel(*refs):
    sums, (gate_ref, up_ref, down_ref) = refs[:LAYERS], refs[LAYERS:]
    rows = gate_ref.shape[2]
    half = gate_ref.shape[3]
    for layer in range(LAYERS):
        block = sums[layer][...].astype(f32)
        for e in range(gate_ref.shape[1]):
            at = 3 * rows * e
            gate_ref[layer, e] = block[at : at + rows]
            up_ref[layer, e] = block[at + rows : at + 2 * rows]
            at += 2 * rows
            down_ref[layer, e, :, :half] = block[at : at + rows // 2]
            down_ref[layer, e, :, half:] = block[at + rows // 2 : at + rows]


def dense_grads_kernel(*refs):
    blocks, outs = refs[0], refs[1 : 1 + LAYERS]
    query_ref, key_ref, value_ref, out_ref, small_ref = refs[1 + LAYERS :]
    seq_count, _, rows, columns = blocks.shape
    local = columns - 3 * HD
    share = seq_count // KVHEADS
    for layer in range(LAYERS):
        parts = [blocks[s, layer].astype(f32) for s in range(seq_count)]
        for s in range(seq_count):
            query_ref[:, layer, s * local : (s + 1) * local] = parts[s][:, :local]
        for c in range(KVHEADS):
            total = functools.reduce(jnp.add, parts[c * share : (c + 1) * share])
            key_ref[:, layer, c * HD : (c + 1) * HD] = total[:, local : local + HD]
            value_ref[:, layer, c * HD : (c + 1) * HD] = total[:, local + HD : local + 2 * HD]
        total = functools.reduce(jnp.add, parts)
        small_ref[layer] = total[:, local + 2 * HD :]
        block = outs[layer][...].astype(f32)
        half = block.shape[1]
        out_ref[:, layer, :half] = block[:rows]
        out_ref[:, layer, half:] = block[block.shape[0] // 2 :][:rows]


def swap_seq(block):
    return lax.all_to_all(block, "seq", split_axis=0, concat_axis=0, tiled=True)


def around_seq(block):
    count = lax.axis_size("seq")
    others = [
        lax.ppermute(block, "seq", [((i + k) % count, i) for i in range(count)])
        for k in range(1, count)
    ]
    return [block] + others


def halves(block):
    cut = block.shape[-1] // 2
    return jnp.concatenate([block[..., :cut], block[..., cut:]], axis=-2)


def per_device(
    tokens_in,
    cotangent,
    routes,
    order,
    segment_ids,
    gain_attn,
    w_query,
    w_key,
    w_value,
    w_out,
    gain_ffn,
    w_router,
    w_gate,
    w_up,
    w_down,
):
    tok_count = tokens_in.shape[1]
    width = tokens_in.shape[2]
    seq_count = lax.axis_size("seq")
    shard_count = lax.axis_size("fsdp")
    seq_index = lax.axis_index("seq")
    core = lax.rem(lax.axis_index("fsdp"), 2)
    place = jnp.stack([seq_index, core]).astype(jnp.int32)
    group_tok = seq_count * tok_count
    prompt_len = group_tok - segment_ids.shape[1]
    local_experts = w_gate.shape[1]
    expert_count = local_experts * seq_count
    capacity = 9 * tok_count * TOPK // (8 * expert_count)
    total_slots = expert_count * capacity
    head_local = HEADS // seq_count
    local_width = head_local * HD
    dense_rows = w_query.shape[1]
    shard_rows = dense_rows * seq_count
    gate_rows = w_gate.shape[2]
    down_rows = w_down.shape[2]
    expert_rows = 2 * gate_rows + 2 * down_rows
    qkv_width = (HEADS + 2 * KVHEADS) * HD
    half_width = width // 2
    inner_width = w_gate.shape[3]
    slot_rows = seq_count * capacity

    cos_half, sin_half, labels = group_tables(segment_ids[0], prompt_len)
    cos_all = jnp.concatenate([cos_half, cos_half], axis=1)
    sin_all = jnp.concatenate([-sin_half, sin_half], axis=1)
    cos_own = lax.dynamic_slice_in_dim(cos_all, seq_index * tok_count, tok_count, 0)
    sin_own = lax.dynamic_slice_in_dim(sin_all, seq_index * tok_count, tok_count, 0)
    key_pos = jnp.arange(group_tok, dtype=jnp.int32)
    allowed = jnp.logical_and(
        key_pos[None, :] <= key_pos[:, None],
        jnp.logical_or(key_pos[None, :] < prompt_len, labels[None, :] == labels[:, None]),
    )
    bias = jnp.where(allowed, 0.0, masked_value)

    column = jnp.arange(width // seq_count, dtype=jnp.int32)
    natural = (
        column % shard_rows // dense_rows * (width // seq_count // seq_count)
        + column // shard_rows * dense_rows
        + column % dense_rows
    )
    spread = (column[:, None] == natural[None, :]).astype(bf16)

    def small_rows_of(layer):
        return jnp.concatenate(
            [
                w_router[layer],
                gain_attn[layer][:, None],
                gain_ffn[layer][:, None],
                jnp.zeros((dense_rows, HD - 2 - expert_count), bf16),
            ],
            axis=1,
        )

    def dense_rows_of(layer):
        return jnp.concatenate(
            [w_query[layer], w_key[layer], w_value[layer], small_rows_of(layer), w_out[layer]],
            axis=1,
        )

    def shards_of_core(count):
        rows = count // shard_count
        wanted = jnp.arange(count // 2, dtype=jnp.int32)
        wanted = (wanted // rows * 2 + core) * rows + wanted % rows
        return (jnp.arange(count, dtype=jnp.int32)[:, None] == wanted[None, :]).astype(bf16)

    picks = (shards_of_core(width), shards_of_core(inner_width))

    def spread_seq(dense):
        dense = swap_seq(jnp.broadcast_to(dense[None], (seq_count,) + dense.shape))
        return dense.reshape(shard_rows, dense.shape[2])

    def own_columns(weight):
        pick = seq_index * KVHEADS // seq_count
        starts = (seq_index * local_width, (HEADS + pick) * HD, (HEADS + KVHEADS + pick) * HD)
        parts = [
            lax.dynamic_slice_in_dim(weight, start, size, 1)
            for start, size in zip(starts, (local_width, HD, HD))
        ]
        return jnp.concatenate(parts + [weight[:, qkv_width : qkv_width + HD]], axis=1)

    def expert_part(layer):
        return [
            part
            for e in range(local_experts)
            for part in (w_gate[layer, e], w_up[layer, e], halves(w_down[layer, e]))
        ]

    def out_part(dense):
        return [halves(dense[:, qkv_width + HD :])]

    def qkv_part(dense):
        wide = jnp.concatenate(
            [dense[:, : qkv_width + HD], jnp.zeros((shard_rows, HD), bf16)], axis=1
        )
        return [wide[:, at : at + half_width] for at in range(0, wide.shape[1], half_width)]

    def fetch(parts):
        return lax.all_gather(jnp.concatenate(parts, axis=0), "fsdp", axis=0, tiled=False)

    chips = [[i + c for i in range(0, shard_count, 2)] for c in range(2)]

    def swap_chips(block):
        return lax.all_to_all(
            block, "fsdp", split_axis=0, concat_axis=0, tiled=True, axis_index_groups=chips
        )

    def swap_cores(block):
        return lax.ppermute(block, "fsdp", [(i, i ^ 1) for i in range(shard_count)])

    def both_cores(block):
        other = swap_cores(block)
        first = jnp.where(core == 0, block, other)
        second = jnp.where(core == 0, other, block)
        return jnp.stack([first, second], axis=1).reshape((shard_count,) + block.shape[1:])

    def to_chips(block):
        return swap_chips(jnp.broadcast_to(block[None], (shard_count // 2,) + block.shape))

    weight_parts = [
        (e * expert_rows + k * gate_rows, gate_rows) for e in range(local_experts) for k in range(3)
    ]
    back_parts = [weight_parts[3 * e + k] for e in range(local_experts) for k in (2, 0, 1)]
    out_cut = ((1, local_experts * expert_rows, 2 * shard_rows),)

    slots_shape = shape((seq_count, local_experts, capacity, width), bf16)
    inner_shape = (local_experts, slot_rows, inner_width)
    expert_flops = 6 * total_slots * width * inner_width
    dense_flops = 2 * tok_count * width * width
    records = []
    hidden = tokens_in[0]
    dense = spread_seq(jnp.concatenate([dense_rows_of(0), small_rows_of(1)], axis=1))
    columns = jnp.concatenate([own_columns(dense), dense[:, -HD:]], axis=1)
    dense = dense[:, :-HD]
    columns, hidden = lax.optimization_barrier((columns, hidden))
    token_blocks = around_seq(hidden)
    packs = [fetch(expert_part(0) + out_part(dense)), None]
    columns = to_chips(columns)
    pairs = jnp.concatenate(
        [array[layer, 0].T for array in (routes, order) for layer in range(LAYERS)], axis=0
    )
    pairs = swap_seq(jnp.broadcast_to(pairs[None], (seq_count,) + pairs.shape))
    pairs = pairs.reshape(seq_count, 2, LAYERS, TOPK, tok_count)
    slots_of = functools.partial(slot_table, expert_count=expert_count, capacity=capacity)
    all_routes = [pairs[:, 0, layer] for layer in range(LAYERS)]
    all_targets = [
        jax.vmap(slots_of)(pairs[:, 0, layer], pairs[:, 1, layer]) for layer in range(LAYERS)
    ]
    targets = [lax.dynamic_index_in_dim(t, seq_index, 0, False) for t in all_targets]
    routes_ts = [lax.dynamic_index_in_dim(t, seq_index, 0, False) for t in all_routes]
    early = (token_blocks, all_targets, all_routes, targets, routes_ts)
    early = early + (cos_all, sin_all, bias, spread, picks)
    columns, early = lax.optimization_barrier((columns, early))
    token_blocks, all_targets, all_routes, targets, routes_ts = early[:5]
    cos_all, sin_all, bias, spread, picks = early[5:]
    first_columns = both_cores(columns).reshape(width, columns.shape[2])
    first_columns, grad_rows = lax.optimization_barrier((first_columns, cotangent[0]))
    grad_blocks = around_seq(grad_rows)
    own_at = local_experts * expert_rows + 2 * shard_rows
    heads_shape = shape((seq_count, tok_count, local_width + 2 * HD), bf16)
    attended_shape = shape((seq_count, tok_count, local_width), bf16)
    normed_shape = shape((seq_count, tok_count, width), bf16)
    small_shape = shape((LAYERS, 2 * expert_count, width), bf16)
    attention_flops = 4 * head_local * group_tok * group_tok * HD + 2 * dense_flops
    for layer in range(LAYERS):
        pack, routes_t, target_t = packs[layer], routes_ts[layer], targets[layer]
        if layer == 0:
            heads, attended, normed_all, smalls = once(
                first_attention_kernel,
                [heads_shape, attended_shape, normed_shape, small_shape],
                place, *token_blocks, first_columns, spread, cos_all, sin_all, bias,
                scalar=True, flops=attention_flops + 4 * dense_flops,
            )
            small = smalls[layer]
        else:
            small = smalls[layer]
            normed_p, hidden = once(
                input_kernel,
                [shape((tok_count, width), bf16), shape((tok_count, width), f32)],
                middle, combined, gates_t, above_target, small, spread, flops=2 * dense_flops,
            )
            heads, attended, normed_all = once(
                next_attention_kernel,
                [heads_shape, attended_shape, normed_shape],
                place, *around_seq(normed_p), pack, cos_all, sin_all, bias,
                scalar=True, cut={5: ((1, own_at, shard_rows),)}, flops=attention_flops,
            )
        if layer == 0:
            attended, next_rows = lax.optimization_barrier((attended, dense_rows_of(1)))
            back = swap_seq(attended)
            next_dense = spread_seq(next_rows)
            next_parts = expert_part(1) + out_part(next_dense) + [own_columns(next_dense)]
            next_parts = jnp.concatenate(next_parts, axis=0)
            tied = lax.optimization_barrier((pack, next_parts, back, grad_blocks))
            pack, next_parts, back, grad_blocks = tied
            packs = [pack, fetch([next_parts])]
        else:
            back = swap_seq(attended)
            qkv_parts = jnp.concatenate(qkv_part(dense) + qkv_part(next_dense), axis=0)
            qkv_parts, back = lax.optimization_barrier((qkv_parts, back))
            qkv_w = fetch([qkv_parts])
        middle, normed_ffn, gates_t = once(
            after_attention_kernel,
            [
                shape((tok_count, width), f32),
                shape((tok_count, width), bf16),
                shape((2 * TOPK, tok_count), f32),
            ],
            back, spread, hidden, small, pack, routes_t,
            cut={4: out_cut}, flops=3 * dense_flops,
        )
        expert_out, received, gate_val, up_val, all_gates = once(
            expert_kernel,
            [
                slots_shape,
                shape((local_experts, slot_rows, width), bf16),
                shape(inner_shape, bf16),
                shape(inner_shape, bf16),
                shape((seq_count, 2 * TOPK, tok_count), f32),
            ],
            place, *around_seq(normed_ffn), all_targets[layer], all_routes[layer], small,
            *[pack] * len(weight_parts),
            scalar=True,
            cut={n + 8: ((1, *part),) for n, part in enumerate(weight_parts)},
            pieces={n: (1 if n == 0 else 0, local_experts) for n in range(4)},
            flops=expert_flops,
        )
        (picked,) = once(
            pick_kernel,
            [shape((local_experts, 2 * slot_rows, width // 2), bf16)],
            received, swap_cores(received), picks[0],
            pieces={0: (0, local_experts)}, flops=expert_flops // 3,
        )
        combined, picked = lax.optimization_barrier(
            (swap_seq(expert_out).reshape(total_slots, width), picked)
        )
        above_target = target_t
        records.append(
            (
                (pack, small, routes_t, target_t),
                (hidden, normed_all, heads, attended),
                (middle, normed_ffn, gates_t, combined),
                (picked, gate_val, up_val, all_gates),
            )
        )
    (result,) = once(
        result_kernel, [shape((tok_count, width), bf16)], middle, combined, gates_t, target_t,
        flops=dense_flops,
    )

    def with_gain(block, out_block):
        gain = out_block[dense_rows, :shard_rows]
        label = jnp.arange(half_width)[None, :]
        return jnp.where(label == local_width + 2 * HD + expert_count, gain[:, None], block)

    def shard_sum(blocks):
        own, other = blocks
        block = (own.astype(f32) + swap_cores(other).astype(f32)).astype(bf16)
        return jnp.sum(swap_chips(block).astype(f32), axis=0)

    out_rows = 16

    grad_hidden = cotangent[0].astype(f32)
    sums, gains = [None] * LAYERS, [None] * LAYERS
    branches, attendeds = [None] * LAYERS, [None] * LAYERS
    waiting = None
    for layer in range(LAYERS - 1, -1, -1):
        weights, attn_saved, mid_saved, expert_saved = records[layer]
        pack, small, routes_t, target_t = weights
        row = layer * 3 * shard_rows
        below, normed_all, heads, attended = attn_saved
        middle, normed_ffn, gates_t, combined = mid_saved
        picked, gate_val, up_val, all_gates = expert_saved
        if waiting is None:
            tied = lax.optimization_barrier((grad_blocks, qkv_w, result, combined))
            grad_blocks, qkv_w, result, combined = tied
        else:
            grad_blocks, waiting = lax.optimization_barrier((grad_blocks, waiting))
        grad_rows, kept = once(
            expert_back_kernel,
            [slots_shape, shape((local_experts, slot_rows, width + 3 * inner_width), bf16)],
            place, *grad_blocks, all_targets[layer], all_gates, pack, gate_val, up_val,
            *[pack] * (len(back_parts) - 1),
            scalar=True,
            cut={n + 9 if n else 7: ((1, *part),) for n, part in enumerate(back_parts)},
            pieces={0: (1, local_experts), 1: (0, local_experts)},
            flops=expert_flops,
        )
        (logits_grad,) = once(
            logits_grad_kernel,
            [shape((2 * expert_count, tok_count), bf16)],
            grad_hidden, combined, gates_t, routes_t, target_t, flops=3 * dense_flops,
        )
        sent = swap_seq(grad_rows)
        extra = () if layer == LAYERS - 1 else waiting
        pack_rows = local_experts * expert_rows + (shard_rows if extra else 0)
        (packed,) = once(
            expert_weight_kernel,
            [shape((shard_count // 2, pack_rows, half_width), bf16)],
            picked, picks[1], kept, swap_cores(kept), *extra,
            pieces={0: (1, pack_rows // 16)}, flops=2 * expert_flops,
        )
        sent, packed, logits_grad = lax.optimization_barrier((sent, packed, logits_grad))
        if layer < LAYERS - 1:
            packed, sums[layer + 1] = lax.optimization_barrier((packed, sums[layer + 1]))
        summed = lax.psum_scatter(
            packed.reshape(-1, half_width), "fsdp", scatter_dimension=0, tiled=True,
            axis_index_groups=chips,
        )
        grad_middle, branch, send, small_grad = once(
            after_experts_kernel,
            [
                shape((tok_count, width), f32),
                shape((tok_count, width), bf16),
                shape((seq_count, tok_count, local_width), bf16),
                shape((2 * expert_count, width), f32),
            ],
            grad_hidden, sent.reshape(total_slots, width), middle, normed_ffn, logits_grad,
            target_t, small, pack, spread,
            cut={7: out_cut}, flops=4 * dense_flops,
        )
        grad_heads = swap_seq(send)
        if layer == 0:
            tied = lax.optimization_barrier((grad_heads, branch, branches[1]))
            grad_heads, branches = tied[0], [around_seq(block) for block in tied[1:]]
        (grad_own,) = once(
            attention_back_kernel,
            [shape((seq_count, tok_count, local_width + 2 * HD), bf16)],
            heads, grad_heads, bias, cos_all, sin_all,
            flops=10 * head_local * group_tok * group_tok * HD,
        )
        qkv_block_grad = once(
            qkv_weight_kernel,
            [shape((shard_count // 2, shard_rows, half_width), bf16)] * 2,
            place, normed_all, grad_own, small_grad, spread, scalar=True, flops=2 * dense_flops,
        )
        sent, qkv_block_grad = lax.optimization_barrier((swap_seq(grad_own), qkv_block_grad))
        grad_hidden, grad_low, gains[layer] = once(
            before_attention_kernel,
            [
                shape((tok_count, width), f32),
                shape((tok_count, width), bf16),
                shape((shard_count, HD), f32),
            ],
            sent, qkv_w, qkv_w, qkv_w, spread, small, below, grad_middle,
            cut={
                1: ((1, row, shard_rows),),
                2: ((1, row + shard_rows, shard_rows),),
                3: ((1, row + 2 * shard_rows, shard_rows), (2, 0, 2 * KVHEADS * HD)),
            },
            flops=4 * dense_flops,
        )
        attendeds[layer], sums[layer] = attended, summed
        if layer > 0:
            branches[layer] = branch
            grad_blocks = around_seq(grad_low)
            waiting = (qkv_block_grad[0], swap_cores(qkv_block_grad[1]))
    grad_hidden, gains[0], branches = lax.optimization_barrier((grad_hidden, gains[0], branches))
    out_block_grad = once(
        out_weight_kernel,
        [shape((shard_count // 2, 2 * LAYERS * out_rows, half_width), bf16)] * 2,
        place, *branches[0], *branches[1], *attendeds, *gains,
        scalar=True, flops=2 * dense_flops,
    )
    qkv_sum, out_block_grad = lax.optimization_barrier((shard_sum(qkv_block_grad), out_block_grad))
    out_sum = shard_sum(out_block_grad)
    out_sums = [out_sum[2 * out_rows * n : 2 * out_rows * (n + 1)] for n in range(LAYERS)]
    above = sums[0][local_experts * expert_rows :].astype(f32)
    rows = [with_gain(qkv_sum, out_sums[0]), with_gain(above, out_sums[1])]
    rows = jnp.stack(rows).reshape(LAYERS, seq_count, dense_rows, half_width)
    rows = swap_seq(rows.transpose(1, 0, 2, 3))
    gate_grads, up_grads, down_grads = once(
        expert_grads_kernel,
        [
            shape((LAYERS,) + w_gate.shape[1:], f32),
            shape((LAYERS,) + w_up.shape[1:], f32),
            shape((LAYERS,) + w_down.shape[1:], f32),
        ],
        *sums,
        cut={0: ((0, 0, local_experts * expert_rows),)},
    )
    query_grads, key_grads, value_grads, out_grads, small_grads = once(
        dense_grads_kernel,
        [
            shape((dense_rows, LAYERS, HEADS * HD), f32),
            shape((dense_rows, LAYERS, KVHEADS * HD), f32),
            shape((dense_rows, LAYERS, KVHEADS * HD), f32),
            shape((dense_rows, LAYERS, width), f32),
            shape((LAYERS, dense_rows, HD), f32),
        ],
        rows, *out_sums,
    )
    return (
        result[None],
        grad_hidden[None],
        small_grads[:, :, expert_count],
        query_grads.transpose(1, 0, 2),
        key_grads.transpose(1, 0, 2),
        value_grads.transpose(1, 0, 2),
        out_grads.transpose(1, 0, 2),
        small_grads[:, :, expert_count + 1],
        small_grads[:, :, :expert_count],
        gate_grads,
        up_grads,
        down_grads,
    )


def solution(mesh):
    in_specs = (
        P("fsdp", "seq", None),
        P("fsdp", "seq", None),
        P(None, "fsdp", "seq", None),
        P(None, "fsdp", "seq", None),
        P("fsdp", None),
        P(None, ("seq", "fsdp")),
        P(None, ("seq", "fsdp"), None),
        P(None, ("seq", "fsdp"), None),
        P(None, ("seq", "fsdp"), None),
        P(None, ("seq", "fsdp"), None),
        P(None, ("seq", "fsdp")),
        P(None, ("seq", "fsdp"), None),
        P(None, "seq", "fsdp", None),
        P(None, "seq", "fsdp", None),
        P(None, "seq", "fsdp", None),
    )
    out_specs = (
        P("fsdp", "seq", None),
        P("fsdp", "seq", None),
        P(None, ("seq", "fsdp")),
        P(None, ("seq", "fsdp"), None),
        P(None, ("seq", "fsdp"), None),
        P(None, ("seq", "fsdp"), None),
        P(None, ("seq", "fsdp"), None),
        P(None, ("seq", "fsdp")),
        P(None, ("seq", "fsdp"), None),
        P(None, "seq", "fsdp", None),
        P(None, "seq", "fsdp", None),
        P(None, "seq", "fsdp", None),
    )
    return jax.shard_map(
        per_device, mesh=mesh, in_specs=in_specs, out_specs=out_specs, check_vma=False
    )
```

```python
import functools

import jax
import jax.numpy as jnp
import numpy as np
from jax import lax
from jax.experimental import pallas as pl
from jax.experimental.pallas import tpu as pltpu
from jax.sharding import PartitionSpec as P

HEADS = 12
KVHEADS = 2
HD = 128
TOPK = 4
LAYERS = 2
NCONT = 4

norm_eps = 1e-06
rope_base = 10000.0
masked_value = -1e30

bf16 = jnp.bfloat16
f32 = jnp.float32
VMEM_BYTES = 64 * 1024 * 1024 - 256 * 1024


def group_tables(segment_row, prompt_len):
    cont_len = segment_row.shape[0]
    onehot = (segment_row[:, None] == jnp.arange(NCONT, dtype=jnp.int32)[None, :]).astype(jnp.int32)
    counts = jnp.sum(onehot, axis=0)
    starts = jnp.cumsum(counts) - counts
    seg_begin = jnp.sum(onehot * starts[None, :], axis=1)
    within = jnp.arange(cont_len, dtype=jnp.int32) - seg_begin
    positions = jnp.concatenate([jnp.arange(prompt_len, dtype=jnp.int32), prompt_len + within])
    labels = jnp.concatenate([jnp.full((prompt_len,), -1, jnp.int32), segment_row])
    frequency = rope_base ** (-(jnp.arange(HD // 2, dtype=jnp.float32) * 2.0 / HD))
    angles = positions.astype(jnp.float32)[:, None] * frequency[None, :]
    return (jnp.cos(angles), jnp.sin(angles), labels)


def slot_table(routes_t, order_t, expert_count, capacity):
    pair_expert = routes_t.reshape(-1)
    pair_order = order_t.reshape(-1)
    same_expert = pair_expert[:, None] == pair_expert[None, :]
    earlier = pair_order[None, :] < pair_order[:, None]
    pair_slot = jnp.sum(jnp.logical_and(same_expert, earlier).astype(jnp.int32), axis=1)
    target = jnp.where(
        pair_slot < capacity, pair_expert * capacity + pair_slot, expert_count * capacity
    )
    return target.reshape(routes_t.shape)


def nn(left, right):
    return lax.dot_general(left, right, (((1,), (0,)), ((), ())), preferred_element_type=f32)


def nt(left, right):
    return lax.dot_general(left, right, (((1,), (1,)), ((), ())), preferred_element_type=f32)


def tn(left, right):
    return lax.dot_general(left, right, (((0,), (0,)), ((), ())), preferred_element_type=f32)


def split(value):
    high = value.astype(bf16)
    return high, (value - high.astype(f32)).astype(bf16)


class Late:
    def __init__(self, ref, copy):
        self.ref, self.copy, self.shape = ref, copy, ref.shape
        copy.start()

    def wait(self):
        if self.copy is not None:
            self.copy.wait()
            self.copy = None

    def __getitem__(self, index):
        self.wait()
        return self.ref[index]


class Out:
    def __init__(self, ref, copies):
        self.ref, self.copies, self.shape = ref, copies, ref.shape
        self.sent = [False] * len(copies)

    def send(self, piece=None):
        for n in range(len(self.copies)) if piece is None else (piece,):
            if not self.sent[n]:
                self.copies[n].start()
                self.sent[n] = True

    def __getitem__(self, index):
        return self.ref[index]

    def __setitem__(self, index, value):
        self.ref[index] = value


def cost(args, outs, flops):
    moved = sum(int(np.prod(a.shape)) * a.dtype.itemsize for a in (*args, *outs))
    return pl.CostEstimate(flops=flops, bytes_accessed=moved, transcendentals=0)


def once(kernel, outs, *args, scalar=False, cut=None, pieces=None, flops=0):
    cut, pieces = cut or {}, pieces or {}
    hbm = pl.BlockSpec(memory_space=pltpu.HBM)
    late = [n for n in range(len(args)) if not (scalar and n == 0)]
    specs = [hbm] * len(args)
    if scalar:
        specs[0] = pl.BlockSpec(memory_space=pltpu.SMEM)
    scratch = []
    for n in late:
        dims = list(args[n].shape)
        for dim, start, size in cut.get(n, ()):
            dims[dim] = size
        scratch.append(pltpu.VMEM(tuple(dims), args[n].dtype))
    scratch += [pltpu.VMEM(o.shape, o.dtype) for o in outs]
    parts = [pieces.get(n, (0, 1)) for n in range(len(outs))]
    scratch.append(pltpu.SemaphoreType.DMA((len(late) + sum(count for _, count in parts),)))

    def body(*refs):
        ins = list(refs[: len(args)])
        out_refs = refs[len(args) : len(args) + len(outs)]
        rooms = refs[len(args) + len(outs) : -1]
        sems = refs[-1]
        for i, n in enumerate(late):
            source = ins[n]
            for dim, start, size in cut.get(n, ()):
                if callable(start):
                    start = pl.multiple_of(start(ins[0][0]), 16 if dim == 1 else HD)
                source = source.at[(slice(None),) * dim + (pl.ds(start, size),)]
            ins[n] = Late(rooms[i], pltpu.make_async_copy(source, rooms[i], sems.at[i]))
        results = []
        used = len(late)
        for i, out in enumerate(out_refs):
            room = rooms[len(late) + i]
            dim, count = parts[i]
            size = room.shape[dim] // count
            copies = []
            for n in range(count):
                at = (slice(None),) * dim + (pl.ds(n * size, size),)
                copies.append(pltpu.make_async_copy(room.at[at], out.at[at], sems.at[used]))
                used += 1
            results.append(Out(room, copies))
        kernel(*ins, *results)
        for result in results:
            result.send()
        for n in late:
            ins[n].wait()
        for result in results:
            for copy in result.copies:
                copy.wait()

    return pl.pallas_call(
        body,
        out_shape=list(outs),
        in_specs=specs,
        out_specs=[hbm] * len(outs),
        scratch_shapes=scratch,
        compiler_params=pltpu.CompilerParams(vmem_limit_bytes=VMEM_BYTES),
        cost_estimate=cost(args, outs, flops),
    )(*args)


def shape(dims, dtype):
    return jax.ShapeDtypeStruct(dims, dtype)


def normalize(value, gain):
    inverse = lax.rsqrt(jnp.mean(value * value, axis=-1, keepdims=True) + norm_eps)
    return value * inverse * gain


def normalize_back(value, gain, grad):
    inverse = lax.rsqrt(jnp.mean(value * value, axis=-1, keepdims=True) + norm_eps)
    unit = value * inverse
    grad_gain = jnp.sum(grad * unit, axis=0, keepdims=True)
    scaled = grad * gain
    grad_value = inverse * (scaled - unit * jnp.mean(scaled * unit, axis=-1, keepdims=True))
    return grad_value, grad_gain


def to_gathered(parts, order):
    count = len(parts)
    share = parts[0].shape[1] // count
    done = []
    for j in range(count):
        piece = jnp.concatenate([part[:, j * share : (j + 1) * share] for part in parts], axis=1)
        done.append(nn(piece, order))
    return jnp.concatenate(done, axis=1)


def to_natural(value, order):
    count = value.shape[1] // order.shape[0]
    size = order.shape[0]
    share = size // count
    done = [nt(value[:, j * size : (j + 1) * size], order) for j in range(count)]
    return [
        jnp.concatenate([part[:, s * share : (s + 1) * share] for part in done], axis=1)
        for s in range(count)
    ]


def column_blocks(value, count):
    size = value.shape[1] // count
    return [value[:, s * size : (s + 1) * size] for s in range(count)]


def turn(block, cosines, sines):
    return block * cosines + pltpu.roll(block, HD // 2, 1) * sines


def smooth_parts(value):
    root = np.float32(np.sqrt(2.0 / np.pi))
    square = value * value
    high = jnp.tanh(root * (value + 0.044715 * value * square))
    half = 0.5 * (1.0 + high)
    slope = half + 0.5 * value * (1.0 - high * high) * root * (1.0 + 3 * 0.044715 * square)
    return value * half, slope


def choose(target_t, slots):
    place = lax.broadcasted_iota(jnp.int32, (slots, target_t.shape[1]), 0)
    total = jnp.zeros(place.shape, f32)
    for k in range(TOPK):
        total = total + jnp.where(place == target_t[k : k + 1], 1.0, 0.0)
    return total


def choose_weighted(target_t, gates_t, slots):
    place = lax.broadcasted_iota(jnp.int32, (slots, target_t.shape[1]), 0)
    total = jnp.zeros(place.shape, f32)
    for k in range(TOPK):
        total = total + jnp.where(place == target_t[k : k + 1], gates_t[k : k + 1], 0.0)
    return total


def input_kernel(
    middle, combined, gates_t, target_t, small, spread, normed_ref, hidden_ref
):
    expert_count = 8
    hidden = middle[...] + mix(combined[...], gates_t[...], target_t[...])
    hidden_ref[...] = hidden
    hidden_ref.send()
    gain = small[expert_count : expert_count + 1].astype(f32)
    normed = normalize(hidden, gain).astype(bf16)
    count = normed.shape[1] // spread.shape[0]
    normed_ref[...] = to_gathered(column_blocks(normed, count), spread[...]).astype(bf16)


def mix(combined, gates_t, target_t):
    high, low = split(choose_weighted(target_t, gates_t, combined.shape[0]))
    tokens = high.shape[1]
    both = tn(jnp.concatenate([high, low], axis=1), combined)
    return both[:tokens] + both[tokens:]


def result_kernel(middle, combined, gates_t, target_t, result_ref):
    mixture = mix(combined[...], gates_t[...], target_t[...])
    result_ref[...] = (middle[...] + mixture).astype(bf16)


def attend(rows, weight, cosines, sines, bias_ref, heads_ref, out_ref):
    seq_count, tokens, columns = heads_ref.shape
    group = seq_count * tokens
    local = columns // HD - 2
    prompt = group // 2
    raw = nn(rows, weight)
    heads = []
    for j in range(local + 2):
        block = raw[:, j * HD : (j + 1) * HD]
        if j <= local:
            block = turn(block, cosines, sines)
        heads.append(block.astype(bf16))
        heads_ref[:, :, j * HD : (j + 1) * HD] = heads[j].reshape(seq_count, tokens, HD)
    heads_ref.send()
    key, value = heads[local], heads[local + 1]
    scale = HD ** (-0.5)
    for j in range(local):
        query = heads[j]
        for rows, seen in ((slice(0, prompt), prompt), (slice(prompt, group), group)):
            scores = nt(query[rows], key[:seen]) * scale + bias_ref[rows, :seen]
            peak = jnp.max(scores, axis=-1, keepdims=True)
            weights = jnp.exp(scores - peak)
            weights = weights / jnp.sum(weights, axis=-1, keepdims=True)
            part = nn(weights.astype(bf16), value[:seen]).astype(bf16)
            first = rows.start // tokens
            out_ref[first : first + prompt // tokens, :, j * HD : (j + 1) * HD] = part.reshape(
                prompt // tokens, tokens, HD
            )


def first_attention_kernel(
    place, own, one, two, three, weight, spread, cosines, sines, bias_ref,
    heads_ref, out_ref, normed_ref, small_ref,
):
    expert_count = 8
    me = place[0]
    seq_count, tokens, width = normed_ref.shape
    columns = heads_ref.shape[2]
    count = small_ref.shape[1]
    extras = weight[:, columns:].astype(f32).T.astype(bf16)
    extras = jnp.concatenate([extras[:count], extras[HD : HD + count]], axis=0)
    small = jnp.concatenate(to_natural(extras, spread[...]), axis=1)
    small_ref[0] = small[:count].astype(bf16)
    small_ref[1] = small[count:].astype(bf16)
    small_ref.send()
    gain = small[expert_count : expert_count + 1]
    for k, block in enumerate((own, one, two, three)):
        normed = normalize(block[...].astype(f32), gain).astype(bf16)
        normed = to_gathered(column_blocks(normed, seq_count), spread[...]).astype(bf16)
        normed_ref[lax.rem(me + k, seq_count)] = normed
    normed_ref.send()
    rows = normed_ref[...].reshape(seq_count * tokens, width)
    attend(rows, weight[:, :columns], cosines[...], sines[...], bias_ref, heads_ref, out_ref)


def next_attention_kernel(
    place, own, one, two, three, weight, cosines, sines, bias_ref, heads_ref, out_ref, normed_ref
):
    me = place[0]
    seq_count, tokens, width = normed_ref.shape
    weight = weight[...].reshape(width, weight.shape[2])[:, : heads_ref.shape[2]]
    for k, block in enumerate((own, one, two, three)):
        normed_ref[lax.rem(me + k, seq_count)] = block[...]
    normed_ref.send()
    rows = normed_ref[...].reshape(seq_count * tokens, width)
    attend(rows, weight, cosines[...], sines[...], bias_ref, heads_ref, out_ref)


def gates_of(logits, routes_t, rows):
    expert_count = 8
    tokens = logits.shape[1]
    chosen = []
    for k in range(TOPK):
        route = routes_t[k : k + 1]
        value = jnp.zeros((1, tokens), f32)
        for e in range(expert_count):
            value = value + jnp.where(route == e, logits[e : e + 1], 0.0)
        chosen.append(value)
    peak = functools.reduce(jnp.maximum, chosen)
    powers = [jnp.exp(value - peak) for value in chosen]
    total = functools.reduce(jnp.add, powers)
    gates = [power / total for power in powers]
    return jnp.concatenate(gates + [jnp.zeros((rows - TOPK, tokens), f32)], axis=0)


def after_attention_kernel(
    back, spread, hidden, small, out_w, routes_t, middle_ref, normed_ref, gates_ref, attended_ref
):
    expert_count = 8
    seq_count, tokens, part = back.shape
    width = seq_count * part
    attended = to_gathered([back[s] for s in range(seq_count)], spread[...]).astype(bf16)
    attended_ref[...] = attended
    attended_ref.send()
    rows = out_w.shape[1] // 2
    half = out_w.shape[2]
    for side in range(2):
        weight = out_w[:, side * rows : (side + 1) * rows].reshape(width, half)
        cols = slice(side * half, (side + 1) * half)
        middle_ref[:, cols] = hidden[:, cols].astype(f32) + nn(attended, weight)
    middle_ref.send()
    middle = middle_ref[...]
    gain = small[expert_count + 1 : expert_count + 2].astype(f32)
    normed = normalize(middle, gain).astype(bf16)
    normed_ref[...] = normed
    normed_ref.send()
    gates_ref[...] = gates_of(nt(small[...], normed), routes_t[...], gates_ref.shape[0])


def down_parts(block):
    shards, rows, half = block.shape
    wide = block.astype(f32)
    left = wide[:, : rows // 2].reshape(shards * rows // 2, half).astype(bf16)
    right = wide[:, rows // 2 :].reshape(shards * rows // 2, half).astype(bf16)
    return left, right


def expert_kernel(place, own, one, two, three, targets, routes, small, *rest):
    me = place[0]
    blocks = (own, one, two, three)
    out_ref, rows_ref, gate_ref, up_ref, gates_ref = rest[-5:]
    weights = rest[:-5]
    sources, experts, capacity, width = out_ref.shape
    half = width // 2
    for e in range(experts):
        gate_w, up_w, down_w = weights[3 * e : 3 * e + 3]
        first = (me * experts + e) * capacity
        parts = []
        for k, block in enumerate(blocks):
            hot = choose(targets[lax.rem(me + k, sources)] - first, capacity)
            parts.append(nn(hot.astype(bf16), block[...]))
        tokens = jnp.concatenate(parts, axis=0).astype(bf16)
        rows_ref[e] = tokens
        rows_ref.send(e)
        gate_val = nn(tokens, gate_w[...].reshape(width, half))
        gate_ref[e] = gate_val.astype(bf16)
        gate_ref.send(e)
        up_val = nn(tokens, up_w[...].reshape(width, half))
        up_ref[e] = up_val.astype(bf16)
        up_ref.send(e)
        activated, slope = smooth_parts(gate_val)
        inner = (activated * up_val).astype(bf16)
        for side, part in enumerate(down_parts(down_w[...])):
            done = nn(inner, part).astype(bf16)
            for k in range(sources):
                out_ref[lax.rem(me + k, sources), e, :, side * half : (side + 1) * half] = done[
                    k * capacity : (k + 1) * capacity
                ]
        out_ref.send(e)
    for k, block in enumerate(blocks):
        logits = nt(small[...], block[...])
        gates_ref[k] = gates_of(logits, routes[lax.rem(me + k, sources)], gates_ref.shape[1])


def logits_grad_kernel(grad, combined, gates_t, routes_t, target_t, logits_ref):
    tokens = grad.shape[0]
    slots = combined.shape[0]
    high, low = split(grad[...])
    products = nt(combined[...], jnp.concatenate([high, low], axis=0))
    products = products[:, :tokens] + products[:, tokens:]
    place = lax.broadcasted_iota(jnp.int32, (slots, tokens), 0)
    grad_gates = [
        jnp.sum(jnp.where(place == target_t[k : k + 1], products, 0.0), axis=0, keepdims=True)
        for k in range(TOPK)
    ]
    gates = [gates_t[k : k + 1] for k in range(TOPK)]
    center = functools.reduce(jnp.add, [a * b for a, b in zip(gates, grad_gates)])
    label = lax.broadcasted_iota(jnp.int32, logits_ref.shape, 0)
    total = jnp.zeros(logits_ref.shape, f32)
    for k in range(TOPK):
        choice = gates[k] * (grad_gates[k] - center)
        total = total + jnp.where(label == routes_t[k : k + 1], choice, 0.0)
    logits_ref[...] = total.astype(bf16)


def expert_back_kernel(
    place, own, one, two, three, targets, gates, down_first, gate_ref, up_ref, *rest
):
    me = place[0]
    blocks = (own, one, two, three)
    out_ref, keep_ref = rest[-2:]
    weights = (down_first,) + rest[:-2]
    sources, experts, capacity, width = out_ref.shape
    half = width // 2
    for e in range(experts):
        down_w, gate_w, up_w = weights[3 * e : 3 * e + 3]
        shards, rows, _ = gate_w.shape
        first = (me * experts + e) * capacity
        parts = []
        for k, block in enumerate(blocks):
            target = targets[lax.rem(me + k, sources)] - first
            hot = jnp.concatenate(split(choose_weighted(target, gates[k], capacity)), axis=1)
            twice = jnp.concatenate([block[...], block[...]], axis=0)
            parts.append(nn(hot, twice))
        grad = jnp.concatenate(parts, axis=0).astype(bf16)
        keep_ref[e, :, :width] = grad
        left, right = down_parts(down_w[...])
        grad_inner = nt(grad[:, :half], left) + nt(grad[:, half:], right)
        up_val = up_ref[e].astype(f32)
        activated, slope = smooth_parts(gate_ref[e].astype(f32))
        gate_at, up_at, inner_at = (slice(width + n * half, width + (n + 1) * half) for n in range(3))
        keep_ref[e, :, gate_at] = (grad_inner * up_val * slope).astype(bf16)
        keep_ref[e, :, up_at] = (grad_inner * activated).astype(bf16)
        keep_ref[e, :, inner_at] = (activated * up_val).astype(bf16)
        keep_ref.send(e)
        parts = 4
        some, size = shards // parts, shards * rows // parts
        for c in range(parts):
            at = slice(c * some, (c + 1) * some)
            total = nt(keep_ref[e, :, gate_at], gate_w[at].reshape(size, half))
            total = total + nt(keep_ref[e, :, up_at], up_w[at].reshape(size, half))
            total = total.astype(bf16)
            for k in range(sources):
                out_ref[lax.rem(me + k, sources), e, :, c * size : (c + 1) * size] = total[
                    k * capacity : (k + 1) * capacity
                ]
        out_ref.send(e)


def pick_kernel(rows, other_rows, attended, other_attended, pick, out_ref, attended_ref):
    count = rows.shape[1]
    for e in range(rows.shape[0]):
        out_ref[e, :count] = nn(rows[e], pick[...]).astype(bf16)
        out_ref[e, count:] = nn(other_rows[e], pick[...]).astype(bf16)
        out_ref.send(e)
    both = jnp.concatenate([attended[...], other_attended[...]], axis=0)
    attended_ref[...] = nn(both, pick[...]).astype(bf16)


def expert_weight_kernel(core, tokens, pick_inner, keep, other_keep, *rest):
    pack_ref = rest[-1]
    chips, _, half = pack_ref.shape
    experts = tokens.shape[0]
    width = 2 * tokens.shape[2]
    count = width // (2 * chips)
    at = 0

    def send():
        for piece in range(at // 16, (at + count) // 16):
            pack_ref.send(piece)

    for e in range(experts):
        grads = jnp.concatenate([keep[e], other_keep[e]], axis=0)
        both = tn(tokens[e], grads[:, width : width + 2 * half]).astype(bf16)
        for n in range(2):
            block = both[:, n * half : (n + 1) * half].reshape(chips, count, half)
            pack_ref[:, at : at + count] = block
            send()
            at += count
        inner = nn(grads[:, width + 2 * half :], pick_inner[...]).astype(bf16)
        down = tn(inner, grads[:, :width])
        left = down[:, :half].reshape(chips, count // 2, half)
        right = down[:, half:].reshape(chips, count // 2, half)
        pack_ref[:, at : at + count] = jnp.concatenate([left, right], axis=1).astype(bf16)
        send()
        at += count
    if len(rest) > 1:
        dense_part(core[0], rest[:-1], pack_ref, at)


def dense_kernel(core, *refs):
    dense_part(core[0], refs[:-1], refs[-1], 0)


def dense_part(core, refs, pack_ref, at):
    qkv, other_qkv, gain, other_gain, spread, attended, branch, other_branch = refs
    expert_count = 8
    chips, rows, half = qkv.shape
    width = gain.shape[1]
    blocks = column_blocks((gain[...] + other_gain[...]).astype(bf16), width // spread.shape[0])
    gains = to_gathered(blocks, spread[...])
    count = gains.shape[0]
    gains = jnp.where(lax.broadcasted_iota(jnp.int32, gains.shape, 0) == 0, gains, 0.0)
    below = jnp.zeros((HD - expert_count - count, width), f32)
    gains = jnp.concatenate([jnp.zeros((expert_count, width), f32), gains, below], axis=0).T
    gains = gains.reshape(chips, 2, rows, HD)
    gains = jnp.where(core == 0, gains[:, 0], gains[:, 1])
    total = qkv[...].astype(f32) + other_qkv[...].astype(f32)
    pack_ref[:, at : at + rows, : half - HD] = total[:, :, : half - HD].astype(bf16)
    pack_ref[:, at : at + rows, half - HD :] = (total[:, :, half - HD :] + gains).astype(bf16)
    grads = jnp.concatenate([branch[...], other_branch[...]], axis=0)
    total = tn(attended[...], grads).astype(bf16)
    for side in range(2):
        at += rows
        block = total[:, side * half : (side + 1) * half]
        pack_ref[:, at : at + rows] = block.reshape(chips, rows, half)


def keep_shards(own_ref, other_ref, core, at, value):
    shards, rows, columns = value.shape
    value = value.reshape(shards // 2, 2, rows, columns)
    own_ref[:, at : at + rows] = jnp.where(core == 0, value[:, 0], value[:, 1])
    other_ref[:, at : at + rows] = jnp.where(core == 0, value[:, 1], value[:, 0])


def after_experts_kernel(
    grad, sent, middle, normed, logits_grad, target_t, small, out_w, spread,
    grad_ref, branch_ref, send_ref, small_ref,
):
    expert_count = 8
    seq_count, tokens, part = send_ref.shape
    width = seq_count * part
    chosen = choose(target_t[...], sent.shape[0]).astype(bf16)
    grad_normed = tn(chosen, sent[...]) + tn(logits_grad[...], small[...])
    router = nn(logits_grad[...], normed[...])
    gain = small[expert_count + 1 : expert_count + 2].astype(f32)
    grad_value, grad_gain = normalize_back(middle[...], gain, grad_normed)
    label = lax.broadcasted_iota(jnp.int32, small_ref.shape, 0)
    small_ref[...] = jnp.where(label == expert_count + 1, grad_gain, router)
    grad_middle = grad[...] + grad_value
    grad_ref[...] = grad_middle
    grad_ref.send()
    branch = grad_middle.astype(bf16)
    branch_ref[...] = branch
    branch_ref.send()
    rows = out_w.shape[1] // 2
    half = out_w.shape[2]
    parts = [
        nt(branch[:, :half], out_w[:, :rows].reshape(width, half)),
        nt(branch[:, half:], out_w[:, rows:].reshape(width, half)),
    ]
    attended = (parts[0] + parts[1]).astype(bf16)
    for s, block in enumerate(to_natural(attended, spread[...])):
        send_ref[s] = block.astype(bf16)


def attention_back_kernel(heads_ref, grad_ref, bias_ref, cosines, sines, out_ref):
    seq_count, tokens, columns = heads_ref.shape
    group = seq_count * tokens
    heads = heads_ref[...].reshape(group, columns)
    grads = grad_ref[...].reshape(group, grad_ref.shape[2])
    local = columns // HD - 2
    prompt = group // 2
    key = heads[:, local * HD : (local + 1) * HD]
    value = heads[:, (local + 1) * HD :]
    scale = HD ** (-0.5)

    def keep(at, block):
        out_ref[:, :, at * HD : (at + 1) * HD] = block.astype(bf16).reshape(seq_count, tokens, HD)

    cosines, sines = cosines[...], sines[...]

    def unturn(block):
        return block * cosines - pltpu.roll(block, HD // 2, 1) * sines

    grad_key = [jnp.zeros((prompt, HD), f32), jnp.zeros((prompt, HD), f32)]
    grad_value = [jnp.zeros((prompt, HD), f32), jnp.zeros((prompt, HD), f32)]
    for j in range(local):
        query = heads[:, j * HD : (j + 1) * HD]
        grad = grads[:, j * HD : (j + 1) * HD]
        grad_query = []
        for rows, seen in ((slice(0, prompt), prompt), (slice(prompt, group), group)):
            scores = nt(query[rows], key[:seen]) * scale + bias_ref[rows, :seen]
            peak = jnp.max(scores, axis=-1, keepdims=True)
            weights = jnp.exp(scores - peak)
            weights = weights / jnp.sum(weights, axis=-1, keepdims=True)
            grad_weights = nt(grad[rows], value[:seen])
            center = jnp.sum(weights * grad_weights, axis=-1, keepdims=True)
            grad_scores = (weights * (grad_weights - center)).astype(bf16)
            low = weights.astype(bf16)
            grad_query.append(nn(grad_scores, key[:seen]) * scale)
            for side in range(seen // prompt):
                cols = slice(side * prompt, (side + 1) * prompt)
                grad_key[side] = grad_key[side] + tn(grad_scores[:, cols], query[rows])
                grad_value[side] = grad_value[side] + tn(low[:, cols], grad[rows])
        keep(j, unturn(jnp.concatenate(grad_query, axis=0)))
    keep(local, unturn(jnp.concatenate(grad_key, axis=0) * scale))
    keep(local + 1, jnp.concatenate(grad_value, axis=0))


def before_attention_kernel(
    sent, left_w, right_w, kv_w, spread, small, hidden, grad_middle, out_ref, low_ref, gain_ref
):
    expert_count = 8
    seq_count, tokens, columns = sent.shape
    local = columns // HD - 2
    share = seq_count // KVHEADS
    blocks = [sent[s, :, : local * HD] for s in range(seq_count)]
    for at in (local, local + 1):
        for c in range(KVHEADS):
            total = jnp.zeros((tokens, HD), f32)
            for s in range(c * share, (c + 1) * share):
                total = total + sent[s, :, at * HD : (at + 1) * HD].astype(f32)
            blocks.append(total.astype(bf16))
    raw = jnp.concatenate(blocks, axis=1)
    at, total = 0, 0.0
    for part in (left_w, right_w, kv_w):
        shards, rows, columns = part.shape
        weight = part[...].reshape(shards * rows, columns)
        total = total + nt(raw[:, at : at + columns], weight)
        at += columns
    high, low = split(total)
    both = to_natural(jnp.concatenate([high, low], axis=0), spread[...])
    both = jnp.concatenate(both, axis=1)
    grad_normed = both[:tokens] + both[tokens:]
    gain = small[expert_count : expert_count + 1].astype(f32)
    grad_value, grad_gain = normalize_back(hidden[...].astype(f32), gain, grad_normed)
    total = grad_middle[...] + grad_value
    low_ref[...] = total.astype(bf16)
    low_ref.send()
    out_ref[...] = total
    out_ref.send()
    gain_ref[...] = jnp.broadcast_to(grad_gain, gain_ref.shape)


def qkv_weight_kernel(core, normed, grads, small, spread, own_ref, other_ref):
    seq_count, tokens, columns = grads.shape
    chips, rows, wide = own_ref.shape
    shards = 2 * chips
    inputs = normed[...].reshape(seq_count * tokens, normed.shape[2])
    total = tn(inputs, grads[...].reshape(seq_count * tokens, columns))
    extra = column_blocks(small[...].astype(bf16), seq_count)
    extra = to_gathered(extra, spread[...])
    extra = jnp.concatenate([extra, jnp.zeros((HD - extra.shape[0], extra.shape[1]), f32)], axis=0).T
    total = jnp.concatenate([total, extra], axis=1).astype(bf16).reshape(shards, rows, wide)
    keep_shards(own_ref, other_ref, core[0], 0, total)


def expert_grads_kernel(*refs):
    sums, (gate_ref, up_ref, down_ref) = refs[:LAYERS], refs[LAYERS:]
    rows = gate_ref.shape[2]
    half = gate_ref.shape[3]
    for layer in range(LAYERS):
        block = sums[layer][...].astype(f32)
        for e in range(gate_ref.shape[1]):
            at = 3 * rows * e
            gate_ref[layer, e] = block[at : at + rows]
            up_ref[layer, e] = block[at + rows : at + 2 * rows]
            at += 2 * rows
            down_ref[layer, e, :, :half] = block[at : at + rows // 2]
            down_ref[layer, e, :, half:] = block[at + rows // 2 : at + rows]


def dense_grads_kernel(*refs):
    blocks = refs[0]
    query_ref, key_ref, value_ref, out_ref, small_ref = refs[1:]
    seq_count, _, _, rows, columns = blocks.shape
    local = columns - 3 * HD
    share = seq_count // KVHEADS
    for layer in range(LAYERS):
        parts = [blocks[s, layer, 0].astype(f32) for s in range(seq_count)]
        for s in range(seq_count):
            query_ref[:, layer, s * local : (s + 1) * local] = parts[s][:, :local]
        for c in range(KVHEADS):
            total = functools.reduce(jnp.add, parts[c * share : (c + 1) * share])
            key_ref[:, layer, c * HD : (c + 1) * HD] = total[:, local : local + HD]
            value_ref[:, layer, c * HD : (c + 1) * HD] = total[:, local + HD : local + 2 * HD]
        total = functools.reduce(jnp.add, parts)
        small_ref[layer] = total[:, local + 2 * HD :]
        for side in range(2):
            sides = [blocks[s, layer, 1 + side].astype(f32) for s in range(seq_count)]
            total = functools.reduce(jnp.add, sides)
            out_ref[:, layer, side * columns : (side + 1) * columns] = total


def swap_seq(block):
    return lax.all_to_all(block, "seq", split_axis=0, concat_axis=0, tiled=True)


def around_seq(block):
    count = lax.axis_size("seq")
    others = [
        lax.ppermute(block, "seq", [((i + k) % count, i) for i in range(count)])
        for k in range(1, count)
    ]
    return [block] + others


def halves(block):
    cut = block.shape[-1] // 2
    return jnp.concatenate([block[..., :cut], block[..., cut:]], axis=-2)


def per_device(
    tokens_in,
    cotangent,
    routes,
    order,
    segment_ids,
    gain_attn,
    w_query,
    w_key,
    w_value,
    w_out,
    gain_ffn,
    w_router,
    w_gate,
    w_up,
    w_down,
):
    tok_count = tokens_in.shape[1]
    width = tokens_in.shape[2]
    seq_count = lax.axis_size("seq")
    shard_count = lax.axis_size("fsdp")
    seq_index = lax.axis_index("seq")
    core = lax.rem(lax.axis_index("fsdp"), 2)
    place = jnp.full((1,), seq_index, jnp.int32)
    core_place = jnp.full((1,), core, jnp.int32)
    group_tok = seq_count * tok_count
    prompt_len = group_tok - segment_ids.shape[1]
    local_experts = w_gate.shape[1]
    expert_count = local_experts * seq_count
    capacity = 9 * tok_count * TOPK // (8 * expert_count)
    total_slots = expert_count * capacity
    head_local = HEADS // seq_count
    local_width = head_local * HD
    dense_rows = w_query.shape[1]
    shard_rows = dense_rows * seq_count
    gate_rows = w_gate.shape[2]
    down_rows = w_down.shape[2]
    expert_rows = 2 * gate_rows + 2 * down_rows
    qkv_width = (HEADS + 2 * KVHEADS) * HD
    half_width = width // 2
    inner_width = w_gate.shape[3]
    slot_rows = seq_count * capacity

    cos_half, sin_half, labels = group_tables(segment_ids[0], prompt_len)
    cos_all = jnp.concatenate([cos_half, cos_half], axis=1)
    sin_all = jnp.concatenate([-sin_half, sin_half], axis=1)
    cos_own = lax.dynamic_slice_in_dim(cos_all, seq_index * tok_count, tok_count, 0)
    sin_own = lax.dynamic_slice_in_dim(sin_all, seq_index * tok_count, tok_count, 0)
    key_pos = jnp.arange(group_tok, dtype=jnp.int32)
    allowed = jnp.logical_and(
        key_pos[None, :] <= key_pos[:, None],
        jnp.logical_or(key_pos[None, :] < prompt_len, labels[None, :] == labels[:, None]),
    )
    bias = jnp.where(allowed, 0.0, masked_value)

    column = jnp.arange(width // seq_count, dtype=jnp.int32)
    natural = (
        column % shard_rows // dense_rows * (width // seq_count // seq_count)
        + column // shard_rows * dense_rows
        + column % dense_rows
    )
    spread = (column[:, None] == natural[None, :]).astype(bf16)

    def small_rows_of(layer):
        return jnp.concatenate(
            [
                w_router[layer],
                gain_attn[layer][:, None],
                gain_ffn[layer][:, None],
                jnp.zeros((dense_rows, HD - 2 - expert_count), bf16),
            ],
            axis=1,
        )

    def dense_rows_of(layer):
        return jnp.concatenate(
            [w_query[layer], w_key[layer], w_value[layer], small_rows_of(layer), w_out[layer]],
            axis=1,
        )

    def shards_of_core(count):
        rows = count // shard_count
        wanted = jnp.arange(count // 2, dtype=jnp.int32)
        wanted = (wanted // rows * 2 + core) * rows + wanted % rows
        return (jnp.arange(count, dtype=jnp.int32)[:, None] == wanted[None, :]).astype(bf16)

    picks = (shards_of_core(width), shards_of_core(inner_width))

    def spread_seq(dense):
        dense = swap_seq(jnp.broadcast_to(dense[None], (seq_count,) + dense.shape))
        return dense.reshape(shard_rows, dense.shape[2])

    def own_columns(weight):
        pick = seq_index * KVHEADS // seq_count
        starts = (seq_index * local_width, (HEADS + pick) * HD, (HEADS + KVHEADS + pick) * HD)
        parts = [
            lax.dynamic_slice_in_dim(weight, start, size, 1)
            for start, size in zip(starts, (local_width, HD, HD))
        ]
        return jnp.concatenate(parts + [weight[:, qkv_width : qkv_width + HD]], axis=1)

    def expert_part(layer):
        return [
            part
            for e in range(local_experts)
            for part in (w_gate[layer, e], w_up[layer, e], halves(w_down[layer, e]))
        ]

    def out_part(dense):
        return [halves(dense[:, qkv_width + HD :])]

    def qkv_part(dense):
        wide = jnp.concatenate(
            [dense[:, : qkv_width + HD], jnp.zeros((shard_rows, HD), bf16)], axis=1
        )
        return [wide[:, at : at + half_width] for at in range(0, wide.shape[1], half_width)]

    def fetch(parts):
        return lax.all_gather(jnp.concatenate(parts, axis=0), "fsdp", axis=0, tiled=False)

    chips = [[i + c for i in range(0, shard_count, 2)] for c in range(2)]

    def swap_chips(block):
        return lax.all_to_all(
            block, "fsdp", split_axis=0, concat_axis=0, tiled=True, axis_index_groups=chips
        )

    def swap_cores(block):
        return lax.ppermute(block, "fsdp", [(i, i ^ 1) for i in range(shard_count)])

    def both_cores(block):
        other = swap_cores(block)
        first = jnp.where(core == 0, block, other)
        second = jnp.where(core == 0, other, block)
        return jnp.stack([first, second], axis=1).reshape((shard_count,) + block.shape[1:])

    def to_chips(block):
        return swap_chips(jnp.broadcast_to(block[None], (shard_count // 2,) + block.shape))

    weight_parts = [
        (e * expert_rows + k * gate_rows, gate_rows) for e in range(local_experts) for k in range(3)
    ]
    back_parts = [weight_parts[3 * e + k] for e in range(local_experts) for k in (2, 0, 1)]
    out_cut = ((1, local_experts * expert_rows, 2 * shard_rows),)

    slots_shape = shape((seq_count, local_experts, capacity, width), bf16)
    inner_shape = (local_experts, slot_rows, inner_width)
    expert_flops = 6 * total_slots * width * inner_width
    dense_flops = 2 * tok_count * width * width
    records = []
    hidden = tokens_in[0]
    dense = spread_seq(jnp.concatenate([dense_rows_of(0), small_rows_of(1)], axis=1))
    columns = jnp.concatenate([own_columns(dense), dense[:, -HD:]], axis=1)
    dense = dense[:, :-HD]
    columns, hidden = lax.optimization_barrier((columns, hidden))
    token_blocks = around_seq(hidden)
    packs = [fetch(expert_part(0) + out_part(dense)), None]
    columns = to_chips(columns)
    pairs = jnp.concatenate(
        [array[layer, 0].T for array in (routes, order) for layer in range(LAYERS)], axis=0
    )
    pairs = swap_seq(jnp.broadcast_to(pairs[None], (seq_count,) + pairs.shape))
    pairs = pairs.reshape(seq_count, 2, LAYERS, TOPK, tok_count)
    slots_of = functools.partial(slot_table, expert_count=expert_count, capacity=capacity)
    all_routes = [pairs[:, 0, layer] for layer in range(LAYERS)]
    all_targets = [
        jax.vmap(slots_of)(pairs[:, 0, layer], pairs[:, 1, layer]) for layer in range(LAYERS)
    ]
    targets = [lax.dynamic_index_in_dim(t, seq_index, 0, False) for t in all_targets]
    routes_ts = [lax.dynamic_index_in_dim(t, seq_index, 0, False) for t in all_routes]
    early = (token_blocks, all_targets, all_routes, targets, routes_ts)
    early = early + (cos_all, sin_all, bias, spread, picks)
    columns, early = lax.optimization_barrier((columns, early))
    token_blocks, all_targets, all_routes, targets, routes_ts = early[:5]
    cos_all, sin_all, bias, spread, picks = early[5:]
    first_columns = both_cores(columns).reshape(width, columns.shape[2])
    first_columns, grad_rows = lax.optimization_barrier((first_columns, cotangent[0]))
    grad_blocks = around_seq(grad_rows)
    own_at = local_experts * expert_rows + 2 * shard_rows
    heads_shape = shape((seq_count, tok_count, local_width + 2 * HD), bf16)
    attended_shape = shape((seq_count, tok_count, local_width), bf16)
    normed_shape = shape((seq_count, tok_count, width), bf16)
    small_shape = shape((LAYERS, 2 * expert_count, width), bf16)
    attention_flops = 4 * head_local * group_tok * group_tok * HD + 2 * dense_flops
    for layer in range(LAYERS):
        pack, routes_t, target_t = packs[layer], routes_ts[layer], targets[layer]
        if layer == 0:
            heads, attended, normed_all, smalls = once(
                first_attention_kernel,
                [heads_shape, attended_shape, normed_shape, small_shape],
                place, *token_blocks, first_columns, spread, cos_all, sin_all, bias,
                scalar=True, flops=attention_flops + 4 * dense_flops,
            )
            small = smalls[layer]
        else:
            small = smalls[layer]
            normed_p, hidden = once(
                input_kernel,
                [shape((tok_count, width), bf16), shape((tok_count, width), f32)],
                middle, combined, gates_t, above_target, small, spread, flops=2 * dense_flops,
            )
            heads, attended, normed_all = once(
                next_attention_kernel,
                [heads_shape, attended_shape, normed_shape],
                place, *around_seq(normed_p), pack, cos_all, sin_all, bias,
                scalar=True, cut={5: ((1, own_at, shard_rows),)}, flops=attention_flops,
            )
        if layer == 0:
            attended, next_rows = lax.optimization_barrier((attended, dense_rows_of(1)))
            back = swap_seq(attended)
            next_dense = spread_seq(next_rows)
            next_parts = expert_part(1) + out_part(next_dense) + [own_columns(next_dense)]
            next_parts = jnp.concatenate(next_parts, axis=0)
            tied = lax.optimization_barrier((pack, next_parts, back, grad_blocks))
            pack, next_parts, back, grad_blocks = tied
            packs = [pack, fetch([next_parts])]
        else:
            back = swap_seq(attended)
            qkv_parts = jnp.concatenate(qkv_part(dense) + qkv_part(next_dense), axis=0)
            qkv_parts, back = lax.optimization_barrier((qkv_parts, back))
            qkv_w = fetch([qkv_parts])
        middle, normed_ffn, gates_t, attended_p = once(
            after_attention_kernel,
            [
                shape((tok_count, width), f32),
                shape((tok_count, width), bf16),
                shape((2 * TOPK, tok_count), f32),
                shape((tok_count, width), bf16),
            ],
            back, spread, hidden, small, pack, routes_t,
            cut={4: out_cut}, flops=3 * dense_flops,
        )
        expert_out, received, gate_val, up_val, all_gates = once(
            expert_kernel,
            [
                slots_shape,
                shape((local_experts, slot_rows, width), bf16),
                shape(inner_shape, bf16),
                shape(inner_shape, bf16),
                shape((seq_count, 2 * TOPK, tok_count), f32),
            ],
            place, *around_seq(normed_ffn), all_targets[layer], all_routes[layer], small,
            *[pack] * len(weight_parts),
            scalar=True,
            cut={n + 8: ((1, *part),) for n, part in enumerate(weight_parts)},
            pieces={n: (1 if n == 0 else 0, local_experts) for n in range(4)},
            flops=expert_flops,
        )
        picked = once(
            pick_kernel,
            [
                shape((local_experts, 2 * slot_rows, width // 2), bf16),
                shape((2 * tok_count, width // 2), bf16),
            ],
            received, swap_cores(received), attended_p, swap_cores(attended_p), picks[0],
            pieces={0: (0, local_experts)}, flops=expert_flops // 3,
        )
        combined, picked = lax.optimization_barrier(
            (swap_seq(expert_out).reshape(total_slots, width), picked)
        )
        above_target = target_t
        records.append(
            (
                (pack, small, routes_t, target_t),
                (hidden, normed_all, heads),
                (middle, normed_ffn, gates_t, combined),
                (picked, gate_val, up_val, all_gates),
            )
        )
    (result,) = once(
        result_kernel, [shape((tok_count, width), bf16)], middle, combined, gates_t, target_t,
        flops=dense_flops,
    )

    grad_hidden = cotangent[0].astype(f32)
    sums = [None] * LAYERS
    waiting = None
    for layer in range(LAYERS - 1, -1, -1):
        weights, attn_saved, mid_saved, expert_saved = records[layer]
        pack, small, routes_t, target_t = weights
        row = layer * 3 * shard_rows
        below, normed_all, heads = attn_saved
        middle, normed_ffn, gates_t, combined = mid_saved
        picked, gate_val, up_val, all_gates = expert_saved
        if waiting is None:
            tied = lax.optimization_barrier((grad_blocks, qkv_w, result, combined))
            grad_blocks, qkv_w, result, combined = tied
        else:
            grad_blocks, waiting = lax.optimization_barrier((grad_blocks, waiting))
        grad_rows, kept = once(
            expert_back_kernel,
            [slots_shape, shape((local_experts, slot_rows, width + 3 * inner_width), bf16)],
            place, *grad_blocks, all_targets[layer], all_gates, pack, gate_val, up_val,
            *[pack] * (len(back_parts) - 1),
            scalar=True,
            cut={n + 9 if n else 7: ((1, *part),) for n, part in enumerate(back_parts)},
            pieces={0: (1, local_experts), 1: (0, local_experts)},
            flops=expert_flops,
        )
        (logits_grad,) = once(
            logits_grad_kernel,
            [shape((2 * expert_count, tok_count), bf16)],
            grad_hidden, combined, gates_t, routes_t, target_t, flops=3 * dense_flops,
        )
        sent = swap_seq(grad_rows)
        extra = () if layer == LAYERS - 1 else waiting
        pack_rows = local_experts * expert_rows + (3 * shard_rows if extra else 0)
        (packed,) = once(
            expert_weight_kernel,
            [shape((shard_count // 2, pack_rows, half_width), bf16)],
            core_place, picked[0], picks[1], kept, swap_cores(kept), *extra,
            scalar=True, pieces={0: (1, pack_rows // 16)}, flops=2 * expert_flops,
        )
        sent, packed, logits_grad = lax.optimization_barrier((sent, packed, logits_grad))
        if layer < LAYERS - 1:
            packed, sums[layer + 1] = lax.optimization_barrier((packed, sums[layer + 1]))
        summed = lax.psum_scatter(
            packed.reshape(-1, half_width), "fsdp", scatter_dimension=0, tiled=True,
            axis_index_groups=chips,
        )
        grad_middle, branch, send, small_grad = once(
            after_experts_kernel,
            [
                shape((tok_count, width), f32),
                shape((tok_count, width), bf16),
                shape((seq_count, tok_count, local_width), bf16),
                shape((2 * expert_count, width), f32),
            ],
            grad_hidden, sent.reshape(total_slots, width), middle, normed_ffn, logits_grad,
            target_t, small, pack, spread,
            cut={7: out_cut}, flops=4 * dense_flops,
        )
        grad_heads = swap_seq(send)
        (grad_own,) = once(
            attention_back_kernel,
            [shape((seq_count, tok_count, local_width + 2 * HD), bf16)],
            heads, grad_heads, bias, cos_all, sin_all,
            flops=10 * head_local * group_tok * group_tok * HD,
        )
        qkv_block_grad = once(
            qkv_weight_kernel,
            [shape((shard_count // 2, shard_rows, half_width), bf16)] * 2,
            core_place, normed_all, grad_own, small_grad, spread, scalar=True, flops=2 * dense_flops,
        )
        sent, qkv_block_grad = lax.optimization_barrier((swap_seq(grad_own), qkv_block_grad))
        grad_hidden, grad_low, gain_grad = once(
            before_attention_kernel,
            [
                shape((tok_count, width), f32),
                shape((tok_count, width), bf16),
                shape((8, width), f32),
            ],
            sent, qkv_w, qkv_w, qkv_w, spread, small, below, grad_middle,
            cut={
                1: ((1, row, shard_rows),),
                2: ((1, row + shard_rows, shard_rows),),
                3: ((1, row + 2 * shard_rows, shard_rows), (2, 0, 2 * KVHEADS * HD)),
            },
            flops=4 * dense_flops,
        )
        sums[layer] = summed
        dense_sources = (
            qkv_block_grad[0], swap_cores(qkv_block_grad[1]), gain_grad, swap_cores(gain_grad),
            spread, picked[1], branch, swap_cores(branch),
        )
        if layer > 0:
            grad_blocks, waiting = around_seq(grad_low), dense_sources
    (dense_pack,) = once(
        dense_kernel,
        [shape((shard_count // 2, 3 * shard_rows, half_width), bf16)],
        core_place, *dense_sources, scalar=True, flops=2 * dense_flops,
    )
    dense_sum = jnp.sum(swap_chips(dense_pack).astype(f32), axis=0).astype(bf16)
    rows = jnp.stack([dense_sum, sums[0][local_experts * expert_rows :]])
    rows = rows.reshape(LAYERS, 3, seq_count, dense_rows, half_width).transpose(2, 0, 1, 3, 4)
    rows = swap_seq(rows)
    gate_grads, up_grads, down_grads = once(
        expert_grads_kernel,
        [
            shape((LAYERS,) + w_gate.shape[1:], f32),
            shape((LAYERS,) + w_up.shape[1:], f32),
            shape((LAYERS,) + w_down.shape[1:], f32),
        ],
        *sums,
        cut={0: ((0, 0, local_experts * expert_rows),)},
    )
    query_grads, key_grads, value_grads, out_grads, small_grads = once(
        dense_grads_kernel,
        [
            shape((dense_rows, LAYERS, HEADS * HD), f32),
            shape((dense_rows, LAYERS, KVHEADS * HD), f32),
            shape((dense_rows, LAYERS, KVHEADS * HD), f32),
            shape((dense_rows, LAYERS, width), f32),
            shape((LAYERS, dense_rows, HD), f32),
        ],
        rows,
    )
    return (
        result[None],
        grad_hidden[None],
        small_grads[:, :, expert_count],
        query_grads.transpose(1, 0, 2),
        key_grads.transpose(1, 0, 2),
        value_grads.transpose(1, 0, 2),
        out_grads.transpose(1, 0, 2),
        small_grads[:, :, expert_count + 1],
        small_grads[:, :, :expert_count],
        gate_grads,
        up_grads,
        down_grads,
    )


def solution(mesh):
    in_specs = (
        P("fsdp", "seq", None),
        P("fsdp", "seq", None),
        P(None, "fsdp", "seq", None),
        P(None, "fsdp", "seq", None),
        P("fsdp", None),
        P(None, ("seq", "fsdp")),
        P(None, ("seq", "fsdp"), None),
        P(None, ("seq", "fsdp"), None),
        P(None, ("seq", "fsdp"), None),
        P(None, ("seq", "fsdp"), None),
        P(None, ("seq", "fsdp")),
        P(None, ("seq", "fsdp"), None),
        P(None, "seq", "fsdp", None),
        P(None, "seq", "fsdp", None),
        P(None, "seq", "fsdp", None),
    )
    out_specs = (
        P("fsdp", "seq", None),
        P("fsdp", "seq", None),
        P(None, ("seq", "fsdp")),
        P(None, ("seq", "fsdp"), None),
        P(None, ("seq", "fsdp"), None),
        P(None, ("seq", "fsdp"), None),
        P(None, ("seq", "fsdp"), None),
        P(None, ("seq", "fsdp")),
        P(None, ("seq", "fsdp"), None),
        P(None, "seq", "fsdp", None),
        P(None, "seq", "fsdp", None),
        P(None, "seq", "fsdp", None),
    )
    return jax.shard_map(
        per_device, mesh=mesh, in_specs=in_specs, out_specs=out_specs, check_vma=False
    )
```

```python
import functools

import jax
import jax.numpy as jnp
import numpy as np
from jax import lax
from jax.experimental import pallas as pl
from jax.experimental.pallas import tpu as pltpu
from jax.sharding import PartitionSpec as P

HEADS = 12
KVHEADS = 2
HD = 128
TOPK = 4
LAYERS = 2
NCONT = 4

norm_eps = 1e-06
rope_base = 10000.0
masked_value = -1e30

bf16 = jnp.bfloat16
f32 = jnp.float32
VMEM_BYTES = 64 * 1024 * 1024 - 256 * 1024


def group_tables(segment_row, prompt_len):
    cont_len = segment_row.shape[0]
    onehot = (segment_row[:, None] == jnp.arange(NCONT, dtype=jnp.int32)[None, :]).astype(jnp.int32)
    counts = jnp.sum(onehot, axis=0)
    starts = jnp.cumsum(counts) - counts
    seg_begin = jnp.sum(onehot * starts[None, :], axis=1)
    within = jnp.arange(cont_len, dtype=jnp.int32) - seg_begin
    positions = jnp.concatenate([jnp.arange(prompt_len, dtype=jnp.int32), prompt_len + within])
    labels = jnp.concatenate([jnp.full((prompt_len,), -1, jnp.int32), segment_row])
    frequency = rope_base ** (-(jnp.arange(HD // 2, dtype=jnp.float32) * 2.0 / HD))
    angles = positions.astype(jnp.float32)[:, None] * frequency[None, :]
    return (jnp.cos(angles), jnp.sin(angles), labels)


def slot_table(routes_t, order_t, expert_count, capacity):
    pair_expert = routes_t.reshape(-1)
    pair_order = order_t.reshape(-1)
    same_expert = pair_expert[:, None] == pair_expert[None, :]
    earlier = pair_order[None, :] < pair_order[:, None]
    pair_slot = jnp.sum(jnp.logical_and(same_expert, earlier).astype(jnp.int32), axis=1)
    target = jnp.where(
        pair_slot < capacity, pair_expert * capacity + pair_slot, expert_count * capacity
    )
    return target.reshape(routes_t.shape)


def nn(left, right):
    return lax.dot_general(left, right, (((1,), (0,)), ((), ())), preferred_element_type=f32)


def nt(left, right):
    return lax.dot_general(left, right, (((1,), (1,)), ((), ())), preferred_element_type=f32)


def tn(left, right):
    return lax.dot_general(left, right, (((0,), (0,)), ((), ())), preferred_element_type=f32)


def split(value):
    high = value.astype(bf16)
    return high, (value - high.astype(f32)).astype(bf16)


class Late:
    def __init__(self, ref, copy):
        self.ref, self.copy, self.shape = ref, copy, ref.shape
        copy.start()

    def wait(self):
        if self.copy is not None:
            self.copy.wait()
            self.copy = None

    def __getitem__(self, index):
        self.wait()
        return self.ref[index]


class Out:
    def __init__(self, ref, copies):
        self.ref, self.copies, self.shape = ref, copies, ref.shape
        self.sent = [False] * len(copies)

    def send(self, piece=None):
        for n in range(len(self.copies)) if piece is None else (piece,):
            if not self.sent[n]:
                self.copies[n].start()
                self.sent[n] = True

    def __getitem__(self, index):
        return self.ref[index]

    def __setitem__(self, index, value):
        self.ref[index] = value


def cost(args, outs, flops):
    moved = sum(int(np.prod(a.shape)) * a.dtype.itemsize for a in (*args, *outs))
    return pl.CostEstimate(flops=flops, bytes_accessed=moved, transcendentals=0)


def once(kernel, outs, *args, scalar=False, cut=None, pieces=None, flops=0):
    cut, pieces = cut or {}, pieces or {}
    hbm = pl.BlockSpec(memory_space=pltpu.HBM)
    late = [n for n in range(len(args)) if not (scalar and n == 0)]
    specs = [hbm] * len(args)
    if scalar:
        specs[0] = pl.BlockSpec(memory_space=pltpu.SMEM)
    scratch = []
    for n in late:
        dims = list(args[n].shape)
        for dim, start, size in cut.get(n, ()):
            dims[dim] = size
        scratch.append(pltpu.VMEM(tuple(dims), args[n].dtype))
    scratch += [pltpu.VMEM(o.shape, o.dtype) for o in outs]
    parts = [pieces.get(n, (0, 1)) for n in range(len(outs))]
    scratch.append(pltpu.SemaphoreType.DMA((len(late) + sum(count for _, count in parts),)))

    def body(*refs):
        ins = list(refs[: len(args)])
        out_refs = refs[len(args) : len(args) + len(outs)]
        rooms = refs[len(args) + len(outs) : -1]
        sems = refs[-1]
        for i, n in enumerate(late):
            source = ins[n]
            for dim, start, size in cut.get(n, ()):
                if callable(start):
                    start = pl.multiple_of(start(ins[0][0]), 16 if dim == 1 else HD)
                source = source.at[(slice(None),) * dim + (pl.ds(start, size),)]
            ins[n] = Late(rooms[i], pltpu.make_async_copy(source, rooms[i], sems.at[i]))
        results = []
        used = len(late)
        for i, out in enumerate(out_refs):
            room = rooms[len(late) + i]
            dim, count = parts[i]
            size = room.shape[dim] // count
            copies = []
            for n in range(count):
                at = (slice(None),) * dim + (pl.ds(n * size, size),)
                copies.append(pltpu.make_async_copy(room.at[at], out.at[at], sems.at[used]))
                used += 1
            results.append(Out(room, copies))
        kernel(*ins, *results)
        for result in results:
            result.send()
        for n in late:
            ins[n].wait()
        for result in results:
            for copy in result.copies:
                copy.wait()

    return pl.pallas_call(
        body,
        out_shape=list(outs),
        in_specs=specs,
        out_specs=[hbm] * len(outs),
        scratch_shapes=scratch,
        compiler_params=pltpu.CompilerParams(vmem_limit_bytes=VMEM_BYTES),
        cost_estimate=cost(args, outs, flops),
    )(*args)


def shape(dims, dtype):
    return jax.ShapeDtypeStruct(dims, dtype)


def normalize(value, gain):
    inverse = lax.rsqrt(jnp.mean(value * value, axis=-1, keepdims=True) + norm_eps)
    return value * inverse * gain


def normalize_back(value, gain, grad):
    inverse = lax.rsqrt(jnp.mean(value * value, axis=-1, keepdims=True) + norm_eps)
    unit = value * inverse
    grad_gain = jnp.sum(grad * unit, axis=0, keepdims=True)
    scaled = grad * gain
    grad_value = inverse * (scaled - unit * jnp.mean(scaled * unit, axis=-1, keepdims=True))
    return grad_value, grad_gain


def to_gathered(parts, order):
    count = len(parts)
    share = parts[0].shape[1] // count
    done = []
    for j in range(count):
        piece = jnp.concatenate([part[:, j * share : (j + 1) * share] for part in parts], axis=1)
        done.append(nn(piece, order))
    return jnp.concatenate(done, axis=1)


def to_natural(value, order):
    count = value.shape[1] // order.shape[0]
    size = order.shape[0]
    share = size // count
    done = [nt(value[:, j * size : (j + 1) * size], order) for j in range(count)]
    return [
        jnp.concatenate([part[:, s * share : (s + 1) * share] for part in done], axis=1)
        for s in range(count)
    ]


def column_blocks(value, count):
    size = value.shape[1] // count
    return [value[:, s * size : (s + 1) * size] for s in range(count)]


def turn(block, cosines, sines):
    return block * cosines + pltpu.roll(block, HD // 2, 1) * sines


def smooth_parts(value):
    root = np.float32(np.sqrt(2.0 / np.pi))
    square = value * value
    high = jnp.tanh(root * (value + 0.044715 * value * square))
    half = 0.5 * (1.0 + high)
    slope = half + 0.5 * value * (1.0 - high * high) * root * (1.0 + 3 * 0.044715 * square)
    return value * half, slope


def choose(target_t, slots):
    place = lax.broadcasted_iota(jnp.int32, (slots, target_t.shape[1]), 0)
    total = jnp.zeros(place.shape, f32)
    for k in range(TOPK):
        total = total + jnp.where(place == target_t[k : k + 1], 1.0, 0.0)
    return total


def choose_weighted(target_t, gates_t, slots):
    place = lax.broadcasted_iota(jnp.int32, (slots, target_t.shape[1]), 0)
    total = jnp.zeros(place.shape, f32)
    for k in range(TOPK):
        total = total + jnp.where(place == target_t[k : k + 1], gates_t[k : k + 1], 0.0)
    return total


def input_kernel(
    middle, combined, gates_t, target_t, small, spread, normed_ref, hidden_ref
):
    expert_count = 8
    hidden = middle[...] + mix(combined[...], gates_t[...], target_t[...])
    hidden_ref[...] = hidden
    hidden_ref.send()
    gain = small[expert_count : expert_count + 1].astype(f32)
    normed = normalize(hidden, gain).astype(bf16)
    count = normed.shape[1] // spread.shape[0]
    normed_ref[...] = to_gathered(column_blocks(normed, count), spread[...]).astype(bf16)


def mix(combined, gates_t, target_t):
    high, low = split(choose_weighted(target_t, gates_t, combined.shape[0]))
    tokens = high.shape[1]
    both = tn(jnp.concatenate([high, low], axis=1), combined)
    return both[:tokens] + both[tokens:]


def result_kernel(middle, combined, gates_t, target_t, result_ref):
    mixture = mix(combined[...], gates_t[...], target_t[...])
    result_ref[...] = (middle[...] + mixture).astype(bf16)


def attend(rows, weight, cosines, sines, bias_ref, heads_ref, out_ref):
    seq_count, tokens, columns = heads_ref.shape
    group = seq_count * tokens
    local = columns // HD - 2
    prompt = group // 2
    raw = nn(rows, weight)
    heads = []
    for j in range(local + 2):
        block = raw[:, j * HD : (j + 1) * HD]
        if j <= local:
            block = turn(block, cosines, sines)
        heads.append(block.astype(bf16))
        heads_ref[:, :, j * HD : (j + 1) * HD] = heads[j].reshape(seq_count, tokens, HD)
    heads_ref.send()
    key, value = heads[local], heads[local + 1]
    scale = HD ** (-0.5)
    for j in range(local):
        query = heads[j]
        for rows, seen in ((slice(0, prompt), prompt), (slice(prompt, group), group)):
            scores = nt(query[rows], key[:seen]) * scale + bias_ref[rows, :seen]
            peak = jnp.max(scores, axis=-1, keepdims=True)
            weights = jnp.exp(scores - peak)
            weights = weights / jnp.sum(weights, axis=-1, keepdims=True)
            part = nn(weights.astype(bf16), value[:seen]).astype(bf16)
            first = rows.start // tokens
            out_ref[first : first + prompt // tokens, :, j * HD : (j + 1) * HD] = part.reshape(
                prompt // tokens, tokens, HD
            )


def first_attention_kernel(
    place, own, one, two, three, weight, spread, cosines, sines, bias_ref,
    heads_ref, out_ref, normed_ref, small_ref,
):
    expert_count = 8
    me = place[0]
    seq_count, tokens, width = normed_ref.shape
    columns = heads_ref.shape[2]
    count = small_ref.shape[1]
    extras = weight[:, columns:].astype(f32).T.astype(bf16)
    extras = jnp.concatenate([extras[:count], extras[HD : HD + count]], axis=0)
    small = jnp.concatenate(to_natural(extras, spread[...]), axis=1)
    small_ref[0] = small[:count].astype(bf16)
    small_ref[1] = small[count:].astype(bf16)
    small_ref.send()
    gain = small[expert_count : expert_count + 1]
    for k, block in enumerate((own, one, two, three)):
        normed = normalize(block[...].astype(f32), gain).astype(bf16)
        normed = to_gathered(column_blocks(normed, seq_count), spread[...]).astype(bf16)
        normed_ref[lax.rem(me + k, seq_count)] = normed
    normed_ref.send()
    rows = normed_ref[...].reshape(seq_count * tokens, width)
    attend(rows, weight[:, :columns], cosines[...], sines[...], bias_ref, heads_ref, out_ref)


def next_attention_kernel(
    place, own, one, two, three, weight, cosines, sines, bias_ref, heads_ref, out_ref, normed_ref
):
    me = place[0]
    seq_count, tokens, width = normed_ref.shape
    weight = weight[...].reshape(width, weight.shape[2])[:, : heads_ref.shape[2]]
    for k, block in enumerate((own, one, two, three)):
        normed_ref[lax.rem(me + k, seq_count)] = block[...]
    normed_ref.send()
    rows = normed_ref[...].reshape(seq_count * tokens, width)
    attend(rows, weight, cosines[...], sines[...], bias_ref, heads_ref, out_ref)


def gates_of(logits, routes_t, rows):
    expert_count = 8
    tokens = logits.shape[1]
    chosen = []
    for k in range(TOPK):
        route = routes_t[k : k + 1]
        value = jnp.zeros((1, tokens), f32)
        for e in range(expert_count):
            value = value + jnp.where(route == e, logits[e : e + 1], 0.0)
        chosen.append(value)
    peak = functools.reduce(jnp.maximum, chosen)
    powers = [jnp.exp(value - peak) for value in chosen]
    total = functools.reduce(jnp.add, powers)
    gates = [power / total for power in powers]
    return jnp.concatenate(gates + [jnp.zeros((rows - TOPK, tokens), f32)], axis=0)


def after_attention_kernel(
    back, spread, hidden, small, out_w, routes_t, middle_ref, normed_ref, gates_ref, attended_ref
):
    expert_count = 8
    seq_count, tokens, part = back.shape
    width = seq_count * part
    attended = to_gathered([back[s] for s in range(seq_count)], spread[...]).astype(bf16)
    attended_ref[...] = attended
    attended_ref.send()
    rows = out_w.shape[1] // 2
    half = out_w.shape[2]
    for side in range(2):
        weight = out_w[:, side * rows : (side + 1) * rows].reshape(width, half)
        cols = slice(side * half, (side + 1) * half)
        middle_ref[:, cols] = hidden[:, cols].astype(f32) + nn(attended, weight)
    middle_ref.send()
    middle = middle_ref[...]
    gain = small[expert_count + 1 : expert_count + 2].astype(f32)
    normed = normalize(middle, gain).astype(bf16)
    normed_ref[...] = normed
    normed_ref.send()
    gates_ref[...] = gates_of(nt(small[...], normed), routes_t[...], gates_ref.shape[0])


def down_parts(block):
    shards, rows, half = block.shape
    wide = block.astype(f32)
    left = wide[:, : rows // 2].reshape(shards * rows // 2, half).astype(bf16)
    right = wide[:, rows // 2 :].reshape(shards * rows // 2, half).astype(bf16)
    return left, right


def expert_kernel(place, own, one, two, three, targets, routes, small, *rest):
    me = place[0]
    blocks = (own, one, two, three)
    out_ref, rows_ref, gate_ref, up_ref, gates_ref = rest[-5:]
    weights = rest[:-5]
    sources, experts, capacity, width = out_ref.shape
    half = width // 2
    for e in range(experts):
        gate_w, up_w, down_w = weights[3 * e : 3 * e + 3]
        first = (me * experts + e) * capacity
        parts = []
        for k, block in enumerate(blocks):
            hot = choose(targets[lax.rem(me + k, sources)] - first, capacity)
            parts.append(nn(hot.astype(bf16), block[...]))
        tokens = jnp.concatenate(parts, axis=0).astype(bf16)
        rows_ref[e] = tokens
        rows_ref.send(e)
        gate_val = nn(tokens, gate_w[...].reshape(width, half))
        gate_ref[e] = gate_val.astype(bf16)
        gate_ref.send(e)
        up_val = nn(tokens, up_w[...].reshape(width, half))
        up_ref[e] = up_val.astype(bf16)
        up_ref.send(e)
        activated, slope = smooth_parts(gate_val)
        inner = (activated * up_val).astype(bf16)
        for side, part in enumerate(down_parts(down_w[...])):
            done = nn(inner, part).astype(bf16)
            for k in range(sources):
                out_ref[lax.rem(me + k, sources), e, :, side * half : (side + 1) * half] = done[
                    k * capacity : (k + 1) * capacity
                ]
        out_ref.send(e)
    for k, block in enumerate(blocks):
        logits = nt(small[...], block[...])
        gates_ref[k] = gates_of(logits, routes[lax.rem(me + k, sources)], gates_ref.shape[1])


def logits_grad_kernel(grad, combined, gates_t, routes_t, target_t, logits_ref):
    tokens = grad.shape[0]
    slots = combined.shape[0]
    high, low = split(grad[...])
    products = nt(combined[...], jnp.concatenate([high, low], axis=0))
    products = products[:, :tokens] + products[:, tokens:]
    place = lax.broadcasted_iota(jnp.int32, (slots, tokens), 0)
    grad_gates = [
        jnp.sum(jnp.where(place == target_t[k : k + 1], products, 0.0), axis=0, keepdims=True)
        for k in range(TOPK)
    ]
    gates = [gates_t[k : k + 1] for k in range(TOPK)]
    center = functools.reduce(jnp.add, [a * b for a, b in zip(gates, grad_gates)])
    label = lax.broadcasted_iota(jnp.int32, logits_ref.shape, 0)
    total = jnp.zeros(logits_ref.shape, f32)
    for k in range(TOPK):
        choice = gates[k] * (grad_gates[k] - center)
        total = total + jnp.where(label == routes_t[k : k + 1], choice, 0.0)
    logits_ref[...] = total.astype(bf16)


def expert_back_kernel(
    place, own, one, two, three, targets, gates, down_first, gate_ref, up_ref, *rest
):
    me = place[0]
    blocks = (own, one, two, three)
    out_ref, keep_ref = rest[-2:]
    weights = (down_first,) + rest[:-2]
    sources, experts, capacity, width = out_ref.shape
    half = width // 2
    for e in range(experts):
        down_w, gate_w, up_w = weights[3 * e : 3 * e + 3]
        shards, rows, _ = gate_w.shape
        first = (me * experts + e) * capacity
        parts = []
        for k, block in enumerate(blocks):
            target = targets[lax.rem(me + k, sources)] - first
            hot = jnp.concatenate(split(choose_weighted(target, gates[k], capacity)), axis=1)
            twice = jnp.concatenate([block[...], block[...]], axis=0)
            parts.append(nn(hot, twice))
        grad = jnp.concatenate(parts, axis=0).astype(bf16)
        keep_ref[e, :, :width] = grad
        left, right = down_parts(down_w[...])
        grad_inner = nt(grad[:, :half], left) + nt(grad[:, half:], right)
        up_val = up_ref[e].astype(f32)
        activated, slope = smooth_parts(gate_ref[e].astype(f32))
        gate_at, up_at, inner_at = (slice(width + n * half, width + (n + 1) * half) for n in range(3))
        keep_ref[e, :, gate_at] = (grad_inner * up_val * slope).astype(bf16)
        keep_ref[e, :, up_at] = (grad_inner * activated).astype(bf16)
        keep_ref[e, :, inner_at] = (activated * up_val).astype(bf16)
        keep_ref.send(e)
        parts = 4
        some, size = shards // parts, shards * rows // parts
        for c in range(parts):
            at = slice(c * some, (c + 1) * some)
            total = nt(keep_ref[e, :, gate_at], gate_w[at].reshape(size, half))
            total = total + nt(keep_ref[e, :, up_at], up_w[at].reshape(size, half))
            total = total.astype(bf16)
            for k in range(sources):
                out_ref[lax.rem(me + k, sources), e, :, c * size : (c + 1) * size] = total[
                    k * capacity : (k + 1) * capacity
                ]
        out_ref.send(e)


def pick_kernel(rows, other_rows, attended, other_attended, pick, out_ref, attended_ref):
    count = rows.shape[1]
    for e in range(rows.shape[0]):
        out_ref[e, :count] = nn(rows[e], pick[...]).astype(bf16)
        out_ref[e, count:] = nn(other_rows[e], pick[...]).astype(bf16)
        out_ref.send(e)
    both = jnp.concatenate([attended[...], other_attended[...]], axis=0)
    attended_ref[...] = nn(both, pick[...]).astype(bf16)


def expert_weight_kernel(core, tokens, pick_inner, keep, other_keep, *rest):
    pack_ref = rest[-1]
    chips, _, half = pack_ref.shape
    experts = tokens.shape[0]
    width = 2 * tokens.shape[2]
    count = width // (2 * chips)
    at = 0

    def send():
        for piece in range(at // 16, (at + count) // 16):
            pack_ref.send(piece)

    for e in range(experts):
        grads = jnp.concatenate([keep[e], other_keep[e]], axis=0)
        both = tn(tokens[e], grads[:, width : width + 2 * half]).astype(bf16)
        for n in range(2):
            block = both[:, n * half : (n + 1) * half].reshape(chips, count, half)
            pack_ref[:, at : at + count] = block
            send()
            at += count
        inner = nn(grads[:, width + 2 * half :], pick_inner[...]).astype(bf16)
        down = tn(inner, grads[:, :width])
        left = down[:, :half].reshape(chips, count // 2, half)
        right = down[:, half:].reshape(chips, count // 2, half)
        pack_ref[:, at : at + count] = jnp.concatenate([left, right], axis=1).astype(bf16)
        send()
        at += count
    if len(rest) > 1:
        dense_part(core[0], rest[:-1], pack_ref, at)


def dense_kernel(core, *refs):
    dense_part(core[0], refs[:-1], refs[-1], 0)


def dense_part(core, refs, pack_ref, at):
    qkv, other_qkv, gain, other_gain, spread, attended, branch, other_branch = refs
    expert_count = 8
    chips, rows, half = qkv.shape
    width = gain.shape[1]
    blocks = column_blocks((gain[...] + other_gain[...]).astype(bf16), width // spread.shape[0])
    gains = to_gathered(blocks, spread[...])
    count = gains.shape[0]
    gains = jnp.where(lax.broadcasted_iota(jnp.int32, gains.shape, 0) == 0, gains, 0.0)
    below = jnp.zeros((HD - expert_count - count, width), f32)
    gains = jnp.concatenate([jnp.zeros((expert_count, width), f32), gains, below], axis=0).T
    gains = gains.reshape(chips, 2, rows, HD)
    gains = jnp.where(core == 0, gains[:, 0], gains[:, 1])
    total = qkv[...].astype(f32) + other_qkv[...].astype(f32)
    pack_ref[:, at : at + rows, : half - HD] = total[:, :, : half - HD].astype(bf16)
    pack_ref[:, at : at + rows, half - HD :] = (total[:, :, half - HD :] + gains).astype(bf16)
    grads = jnp.concatenate([branch[...], other_branch[...]], axis=0)
    total = tn(attended[...], grads).astype(bf16)
    for side in range(2):
        at += rows
        block = total[:, side * half : (side + 1) * half]
        pack_ref[:, at : at + rows] = block.reshape(chips, rows, half)


def keep_shards(own_ref, other_ref, core, at, value):
    shards, rows, columns = value.shape
    value = value.reshape(shards // 2, 2, rows, columns)
    own_ref[:, at : at + rows] = jnp.where(core == 0, value[:, 0], value[:, 1])
    other_ref[:, at : at + rows] = jnp.where(core == 0, value[:, 1], value[:, 0])


def after_experts_kernel(
    grad, sent, middle, normed, logits_grad, target_t, small, out_w, spread,
    grad_ref, branch_ref, send_ref, small_ref,
):
    expert_count = 8
    seq_count, tokens, part = send_ref.shape
    width = seq_count * part
    chosen = choose(target_t[...], sent.shape[0]).astype(bf16)
    grad_normed = tn(chosen, sent[...]) + tn(logits_grad[...], small[...])
    router = nn(logits_grad[...], normed[...])
    gain = small[expert_count + 1 : expert_count + 2].astype(f32)
    grad_value, grad_gain = normalize_back(middle[...], gain, grad_normed)
    label = lax.broadcasted_iota(jnp.int32, small_ref.shape, 0)
    small_ref[...] = jnp.where(label == expert_count + 1, grad_gain, router)
    grad_middle = grad[...] + grad_value
    grad_ref[...] = grad_middle
    grad_ref.send()
    branch = grad_middle.astype(bf16)
    branch_ref[...] = branch
    branch_ref.send()
    rows = out_w.shape[1] // 2
    half = out_w.shape[2]
    parts = [
        nt(branch[:, :half], out_w[:, :rows].reshape(width, half)),
        nt(branch[:, half:], out_w[:, rows:].reshape(width, half)),
    ]
    attended = (parts[0] + parts[1]).astype(bf16)
    for s, block in enumerate(to_natural(attended, spread[...])):
        send_ref[s] = block.astype(bf16)


def attention_back_kernel(heads_ref, grad_ref, bias_ref, cosines, sines, out_ref):
    seq_count, tokens, columns = heads_ref.shape
    group = seq_count * tokens
    heads = heads_ref[...].reshape(group, columns)
    grads = grad_ref[...].reshape(group, grad_ref.shape[2])
    local = columns // HD - 2
    prompt = group // 2
    key = heads[:, local * HD : (local + 1) * HD]
    value = heads[:, (local + 1) * HD :]
    scale = HD ** (-0.5)

    def keep(at, block):
        out_ref[:, :, at * HD : (at + 1) * HD] = block.astype(bf16).reshape(seq_count, tokens, HD)

    cosines, sines = cosines[...], sines[...]

    def unturn(block):
        return block * cosines - pltpu.roll(block, HD // 2, 1) * sines

    grad_key = [jnp.zeros((prompt, HD), f32), jnp.zeros((prompt, HD), f32)]
    grad_value = [jnp.zeros((prompt, HD), f32), jnp.zeros((prompt, HD), f32)]
    for j in range(local):
        query = heads[:, j * HD : (j + 1) * HD]
        grad = grads[:, j * HD : (j + 1) * HD]
        grad_query = []
        for rows, seen in ((slice(0, prompt), prompt), (slice(prompt, group), group)):
            scores = nt(query[rows], key[:seen]) * scale + bias_ref[rows, :seen]
            peak = jnp.max(scores, axis=-1, keepdims=True)
            weights = jnp.exp(scores - peak)
            weights = weights / jnp.sum(weights, axis=-1, keepdims=True)
            grad_weights = nt(grad[rows], value[:seen])
            center = jnp.sum(weights * grad_weights, axis=-1, keepdims=True)
            grad_scores = (weights * (grad_weights - center)).astype(bf16)
            low = weights.astype(bf16)
            grad_query.append(nn(grad_scores, key[:seen]) * scale)
            for side in range(seen // prompt):
                cols = slice(side * prompt, (side + 1) * prompt)
                grad_key[side] = grad_key[side] + tn(grad_scores[:, cols], query[rows])
                grad_value[side] = grad_value[side] + tn(low[:, cols], grad[rows])
        keep(j, unturn(jnp.concatenate(grad_query, axis=0)))
    keep(local, unturn(jnp.concatenate(grad_key, axis=0) * scale))
    keep(local + 1, jnp.concatenate(grad_value, axis=0))


def before_attention_kernel(
    sent, left_w, right_w, kv_w, spread, small, hidden, grad_middle, out_ref, low_ref, gain_ref
):
    expert_count = 8
    seq_count, tokens, columns = sent.shape
    local = columns // HD - 2
    share = seq_count // KVHEADS
    blocks = [sent[s, :, : local * HD] for s in range(seq_count)]
    for at in (local, local + 1):
        for c in range(KVHEADS):
            total = jnp.zeros((tokens, HD), f32)
            for s in range(c * share, (c + 1) * share):
                total = total + sent[s, :, at * HD : (at + 1) * HD].astype(f32)
            blocks.append(total.astype(bf16))
    raw = jnp.concatenate(blocks, axis=1)
    at, total = 0, 0.0
    for part in (left_w, right_w, kv_w):
        shards, rows, columns = part.shape
        weight = part[...].reshape(shards * rows, columns)
        total = total + nt(raw[:, at : at + columns], weight)
        at += columns
    high, low = split(total)
    both = to_natural(jnp.concatenate([high, low], axis=0), spread[...])
    both = jnp.concatenate(both, axis=1)
    grad_normed = both[:tokens] + both[tokens:]
    gain = small[expert_count : expert_count + 1].astype(f32)
    grad_value, grad_gain = normalize_back(hidden[...].astype(f32), gain, grad_normed)
    total = grad_middle[...] + grad_value
    low_ref[...] = total.astype(bf16)
    low_ref.send()
    out_ref[...] = total
    out_ref.send()
    gain_ref[...] = jnp.broadcast_to(grad_gain, gain_ref.shape)


def qkv_weight_kernel(core, normed, grads, small, spread, own_ref, other_ref):
    seq_count, tokens, columns = grads.shape
    chips, rows, wide = own_ref.shape
    shards = 2 * chips
    inputs = normed[...].reshape(seq_count * tokens, normed.shape[2])
    total = tn(inputs, grads[...].reshape(seq_count * tokens, columns))
    extra = column_blocks(small[...].astype(bf16), seq_count)
    extra = to_gathered(extra, spread[...])
    extra = jnp.concatenate([extra, jnp.zeros((HD - extra.shape[0], extra.shape[1]), f32)], axis=0).T
    total = jnp.concatenate([total, extra], axis=1).astype(bf16).reshape(shards, rows, wide)
    keep_shards(own_ref, other_ref, core[0], 0, total)


def expert_grads_kernel(*refs):
    sums, (gate_ref, up_ref, down_ref) = refs[:LAYERS], refs[LAYERS:]
    rows = gate_ref.shape[2]
    half = gate_ref.shape[3]
    for layer in range(LAYERS):
        block = sums[layer][...].astype(f32)
        for e in range(gate_ref.shape[1]):
            at = 3 * rows * e
            gate_ref[layer, e] = block[at : at + rows]
            up_ref[layer, e] = block[at + rows : at + 2 * rows]
            at += 2 * rows
            down_ref[layer, e, :, :half] = block[at : at + rows // 2]
            down_ref[layer, e, :, half:] = block[at + rows // 2 : at + rows]


def arrange_kernel(first, above, out_ref):
    seq_count, blocks, padded, half = out_ref.shape
    parts = blocks // LAYERS
    rows = first.shape[0] // (parts * seq_count)
    below = jnp.zeros((padded - rows, half), f32)
    for layer, ref in enumerate((first, above)):
        total = ref[...].astype(f32)
        for part in range(parts):
            for s in range(seq_count):
                at = (part * seq_count + s) * rows
                block = jnp.concatenate([total[at : at + rows], below], axis=0)
                out_ref[s, layer * parts + part] = block.astype(bf16)


def dense_grads_kernel(
    blocks, query_ref, key_ref, value_ref, out_ref, router_ref, gain_attn_ref, gain_ffn_ref
):
    seq_count, count, _, columns = blocks.shape
    parts = count // LAYERS
    rows, expert_count = query_ref.shape[0], router_ref.shape[1]
    local = columns - 3 * HD
    share = seq_count // KVHEADS
    for layer in range(LAYERS):
        whole = [blocks[s, layer * parts].astype(f32) for s in range(seq_count)]
        for s in range(seq_count):
            query_ref[:, layer, s * local : (s + 1) * local] = whole[s][:rows, :local]
        for c in range(KVHEADS):
            total = functools.reduce(jnp.add, whole[c * share : (c + 1) * share])[:rows]
            key_ref[:, layer, c * HD : (c + 1) * HD] = total[:, local : local + HD]
            value_ref[:, layer, c * HD : (c + 1) * HD] = total[:, local + HD : local + 2 * HD]
        small = functools.reduce(jnp.add, [block[:, local + 2 * HD :] for block in whole]).T
        router_ref[layer] = small[:expert_count, :rows]
        gain_attn_ref[layer : layer + 1] = small[expert_count : expert_count + 1, :rows]
        gain_ffn_ref[layer : layer + 1] = small[expert_count + 1 : expert_count + 2, :rows]
        for side in range(2):
            sides = [blocks[s, layer * parts + 1 + side].astype(f32) for s in range(seq_count)]
            total = functools.reduce(jnp.add, sides)[:rows]
            out_ref[:, layer, side * columns : (side + 1) * columns] = total


def swap_seq(block):
    return lax.all_to_all(block, "seq", split_axis=0, concat_axis=0, tiled=True)


def around_seq(block):
    count = lax.axis_size("seq")
    others = [
        lax.ppermute(block, "seq", [((i + k) % count, i) for i in range(count)])
        for k in range(1, count)
    ]
    return [block] + others


def halves(block):
    cut = block.shape[-1] // 2
    return jnp.concatenate([block[..., :cut], block[..., cut:]], axis=-2)


def per_device(
    tokens_in,
    cotangent,
    routes,
    order,
    segment_ids,
    gain_attn,
    w_query,
    w_key,
    w_value,
    w_out,
    gain_ffn,
    w_router,
    w_gate,
    w_up,
    w_down,
):
    tok_count = tokens_in.shape[1]
    width = tokens_in.shape[2]
    seq_count = lax.axis_size("seq")
    shard_count = lax.axis_size("fsdp")
    seq_index = lax.axis_index("seq")
    core = lax.rem(lax.axis_index("fsdp"), 2)
    place = jnp.full((1,), seq_index, jnp.int32)
    core_place = jnp.full((1,), core, jnp.int32)
    group_tok = seq_count * tok_count
    prompt_len = group_tok - segment_ids.shape[1]
    local_experts = w_gate.shape[1]
    expert_count = local_experts * seq_count
    capacity = 9 * tok_count * TOPK // (8 * expert_count)
    total_slots = expert_count * capacity
    head_local = HEADS // seq_count
    local_width = head_local * HD
    dense_rows = w_query.shape[1]
    shard_rows = dense_rows * seq_count
    gate_rows = w_gate.shape[2]
    down_rows = w_down.shape[2]
    expert_rows = 2 * gate_rows + 2 * down_rows
    qkv_width = (HEADS + 2 * KVHEADS) * HD
    half_width = width // 2
    inner_width = w_gate.shape[3]
    slot_rows = seq_count * capacity

    cos_half, sin_half, labels = group_tables(segment_ids[0], prompt_len)
    cos_all = jnp.concatenate([cos_half, cos_half], axis=1)
    sin_all = jnp.concatenate([-sin_half, sin_half], axis=1)
    cos_own = lax.dynamic_slice_in_dim(cos_all, seq_index * tok_count, tok_count, 0)
    sin_own = lax.dynamic_slice_in_dim(sin_all, seq_index * tok_count, tok_count, 0)
    key_pos = jnp.arange(group_tok, dtype=jnp.int32)
    allowed = jnp.logical_and(
        key_pos[None, :] <= key_pos[:, None],
        jnp.logical_or(key_pos[None, :] < prompt_len, labels[None, :] == labels[:, None]),
    )
    bias = jnp.where(allowed, 0.0, masked_value)

    column = jnp.arange(width // seq_count, dtype=jnp.int32)
    natural = (
        column % shard_rows // dense_rows * (width // seq_count // seq_count)
        + column // shard_rows * dense_rows
        + column % dense_rows
    )
    spread = (column[:, None] == natural[None, :]).astype(bf16)

    def small_rows_of(layer):
        return jnp.concatenate(
            [
                w_router[layer],
                gain_attn[layer][:, None],
                gain_ffn[layer][:, None],
                jnp.zeros((dense_rows, HD - 2 - expert_count), bf16),
            ],
            axis=1,
        )

    def dense_rows_of(layer):
        return jnp.concatenate(
            [w_query[layer], w_key[layer], w_value[layer], small_rows_of(layer), w_out[layer]],
            axis=1,
        )

    def shards_of_core(count):
        rows = count // shard_count
        wanted = jnp.arange(count // 2, dtype=jnp.int32)
        wanted = (wanted // rows * 2 + core) * rows + wanted % rows
        return (jnp.arange(count, dtype=jnp.int32)[:, None] == wanted[None, :]).astype(bf16)

    picks = (shards_of_core(width), shards_of_core(inner_width))

    def spread_seq(dense):
        dense = swap_seq(jnp.broadcast_to(dense[None], (seq_count,) + dense.shape))
        return dense.reshape(shard_rows, dense.shape[2])

    def own_columns(weight):
        pick = seq_index * KVHEADS // seq_count
        starts = (seq_index * local_width, (HEADS + pick) * HD, (HEADS + KVHEADS + pick) * HD)
        parts = [
            lax.dynamic_slice_in_dim(weight, start, size, 1)
            for start, size in zip(starts, (local_width, HD, HD))
        ]
        return jnp.concatenate(parts + [weight[:, qkv_width : qkv_width + HD]], axis=1)

    def expert_part(layer):
        return [
            part
            for e in range(local_experts)
            for part in (w_gate[layer, e], w_up[layer, e], halves(w_down[layer, e]))
        ]

    def out_part(dense):
        return [halves(dense[:, qkv_width + HD :])]

    def qkv_part(dense):
        wide = jnp.concatenate(
            [dense[:, : qkv_width + HD], jnp.zeros((shard_rows, HD), bf16)], axis=1
        )
        return [wide[:, at : at + half_width] for at in range(0, wide.shape[1], half_width)]

    def fetch(parts):
        return lax.all_gather(jnp.concatenate(parts, axis=0), "fsdp", axis=0, tiled=False)

    chips = [[i + c for i in range(0, shard_count, 2)] for c in range(2)]

    def swap_chips(block):
        return lax.all_to_all(
            block, "fsdp", split_axis=0, concat_axis=0, tiled=True, axis_index_groups=chips
        )

    def swap_cores(block):
        return lax.ppermute(block, "fsdp", [(i, i ^ 1) for i in range(shard_count)])

    def both_cores(block):
        other = swap_cores(block)
        first = jnp.where(core == 0, block, other)
        second = jnp.where(core == 0, other, block)
        return jnp.stack([first, second], axis=1).reshape((shard_count,) + block.shape[1:])

    def to_chips(block):
        return swap_chips(jnp.broadcast_to(block[None], (shard_count // 2,) + block.shape))

    weight_parts = [
        (e * expert_rows + k * gate_rows, gate_rows) for e in range(local_experts) for k in range(3)
    ]
    back_parts = [weight_parts[3 * e + k] for e in range(local_experts) for k in (2, 0, 1)]
    out_cut = ((1, local_experts * expert_rows, 2 * shard_rows),)

    slots_shape = shape((seq_count, local_experts, capacity, width), bf16)
    inner_shape = (local_experts, slot_rows, inner_width)
    expert_flops = 6 * total_slots * width * inner_width
    dense_flops = 2 * tok_count * width * width
    records = []
    hidden = tokens_in[0]
    dense = spread_seq(jnp.concatenate([dense_rows_of(0), small_rows_of(1)], axis=1))
    columns = jnp.concatenate([own_columns(dense), dense[:, -HD:]], axis=1)
    dense = dense[:, :-HD]
    both_rows = jnp.concatenate([hidden, cotangent[0]], axis=0)
    columns, both_rows = lax.optimization_barrier((columns, both_rows))
    both_blocks = around_seq(both_rows)
    packs = [fetch(expert_part(0) + out_part(dense)), None]
    columns = to_chips(columns)
    pairs = jnp.concatenate(
        [array[layer, 0].T for array in (routes, order) for layer in range(LAYERS)], axis=0
    )
    pairs = swap_seq(jnp.broadcast_to(pairs[None], (seq_count,) + pairs.shape))
    pairs = pairs.reshape(seq_count, 2, LAYERS, TOPK, tok_count)
    slots_of = functools.partial(slot_table, expert_count=expert_count, capacity=capacity)
    all_routes = [pairs[:, 0, layer] for layer in range(LAYERS)]
    all_targets = [
        jax.vmap(slots_of)(pairs[:, 0, layer], pairs[:, 1, layer]) for layer in range(LAYERS)
    ]
    targets = [lax.dynamic_index_in_dim(t, seq_index, 0, False) for t in all_targets]
    routes_ts = [lax.dynamic_index_in_dim(t, seq_index, 0, False) for t in all_routes]
    early = (both_blocks, all_targets, all_routes, targets, routes_ts)
    early = early + (cos_all, sin_all, bias, spread, picks)
    columns, early = lax.optimization_barrier((columns, early))
    both_blocks, all_targets, all_routes, targets, routes_ts = early[:5]
    cos_all, sin_all, bias, spread, picks = early[5:]
    first_columns = both_cores(columns).reshape(width, columns.shape[2])
    grad_blocks, grad_cut = both_blocks, ((0, tok_count, tok_count),)
    own_at = local_experts * expert_rows + 2 * shard_rows
    heads_shape = shape((seq_count, tok_count, local_width + 2 * HD), bf16)
    attended_shape = shape((seq_count, tok_count, local_width), bf16)
    normed_shape = shape((seq_count, tok_count, width), bf16)
    small_shape = shape((LAYERS, 2 * expert_count, width), bf16)
    attention_flops = 4 * head_local * group_tok * group_tok * HD + 2 * dense_flops
    for layer in range(LAYERS):
        pack, routes_t, target_t = packs[layer], routes_ts[layer], targets[layer]
        if layer == 0:
            heads, attended, normed_all, smalls = once(
                first_attention_kernel,
                [heads_shape, attended_shape, normed_shape, small_shape],
                place, *both_blocks, first_columns, spread, cos_all, sin_all, bias,
                scalar=True, cut={n: ((0, 0, tok_count),) for n in range(1, 5)}, flops=attention_flops + 4 * dense_flops,
            )
            small = smalls[layer]
        else:
            small = smalls[layer]
            normed_p, hidden = once(
                input_kernel,
                [shape((tok_count, width), bf16), shape((tok_count, width), f32)],
                middle, combined, gates_t, above_target, small, spread, flops=2 * dense_flops,
            )
            heads, attended, normed_all = once(
                next_attention_kernel,
                [heads_shape, attended_shape, normed_shape],
                place, *around_seq(normed_p), pack, cos_all, sin_all, bias,
                scalar=True, cut={5: ((1, own_at, shard_rows),)}, flops=attention_flops,
            )
        if layer == 0:
            back, next_rows = lax.optimization_barrier((swap_seq(attended), dense_rows_of(1)))
            next_dense = spread_seq(next_rows)
            next_parts = expert_part(1) + out_part(next_dense) + [own_columns(next_dense)]
            next_parts = jnp.concatenate(next_parts, axis=0)
            pack, next_parts, back = lax.optimization_barrier((pack, next_parts, back))
            packs = [pack, fetch([next_parts])]
        else:
            back = swap_seq(attended)
            qkv_parts = jnp.concatenate(qkv_part(dense) + qkv_part(next_dense), axis=0)
            qkv_parts, back = lax.optimization_barrier((qkv_parts, back))
            qkv_w = fetch([qkv_parts])
        middle, normed_ffn, gates_t, attended_p = once(
            after_attention_kernel,
            [
                shape((tok_count, width), f32),
                shape((tok_count, width), bf16),
                shape((2 * TOPK, tok_count), f32),
                shape((tok_count, width), bf16),
            ],
            back, spread, hidden, small, pack, routes_t,
            cut={4: out_cut}, flops=3 * dense_flops,
        )
        expert_out, received, gate_val, up_val, all_gates = once(
            expert_kernel,
            [
                slots_shape,
                shape((local_experts, slot_rows, width), bf16),
                shape(inner_shape, bf16),
                shape(inner_shape, bf16),
                shape((seq_count, 2 * TOPK, tok_count), f32),
            ],
            place, *around_seq(normed_ffn), all_targets[layer], all_routes[layer], small,
            *[pack] * len(weight_parts),
            scalar=True,
            cut={n + 8: ((1, *part),) for n, part in enumerate(weight_parts)},
            pieces={n: (1 if n == 0 else 0, local_experts) for n in range(4)},
            flops=expert_flops,
        )
        picked = once(
            pick_kernel,
            [
                shape((local_experts, 2 * slot_rows, width // 2), bf16),
                shape((2 * tok_count, width // 2), bf16),
            ],
            received, swap_cores(received), attended_p, swap_cores(attended_p), picks[0],
            pieces={0: (0, local_experts)}, flops=expert_flops // 3,
        )
        combined, picked = lax.optimization_barrier(
            (swap_seq(expert_out).reshape(total_slots, width), picked)
        )
        above_target = target_t
        records.append(
            (
                (pack, small, routes_t, target_t),
                (hidden, normed_all, heads),
                (middle, normed_ffn, gates_t, combined),
                (picked, gate_val, up_val, all_gates),
            )
        )
    (result,) = once(
        result_kernel, [shape((tok_count, width), bf16)], middle, combined, gates_t, target_t,
        flops=dense_flops,
    )

    grad_hidden = cotangent[0].astype(f32)
    sums = [None] * LAYERS
    waiting = None
    for layer in range(LAYERS - 1, -1, -1):
        weights, attn_saved, mid_saved, expert_saved = records[layer]
        pack, small, routes_t, target_t = weights
        row = layer * 3 * shard_rows
        below, normed_all, heads = attn_saved
        middle, normed_ffn, gates_t, combined = mid_saved
        picked, gate_val, up_val, all_gates = expert_saved
        if waiting is None:
            tied = lax.optimization_barrier((grad_blocks, qkv_w, result, combined))
            grad_blocks, qkv_w, result, combined = tied
        else:
            grad_blocks, waiting = lax.optimization_barrier((grad_blocks, waiting))
        grad_rows, kept = once(
            expert_back_kernel,
            [slots_shape, shape((local_experts, slot_rows, width + 3 * inner_width), bf16)],
            place, *grad_blocks, all_targets[layer], all_gates, pack, gate_val, up_val,
            *[pack] * (len(back_parts) - 1),
            scalar=True,
            cut={n + 9 if n else 7: ((1, *part),) for n, part in enumerate(back_parts)}
            | {n: grad_cut for n in range(1, 5)},
            pieces={0: (1, local_experts), 1: (0, local_experts)},
            flops=expert_flops,
        )
        (logits_grad,) = once(
            logits_grad_kernel,
            [shape((2 * expert_count, tok_count), bf16)],
            grad_hidden, combined, gates_t, routes_t, target_t, flops=3 * dense_flops,
        )
        sent = swap_seq(grad_rows)
        extra = () if layer == LAYERS - 1 else waiting
        pack_rows = local_experts * expert_rows + (3 * shard_rows if extra else 0)
        (packed,) = once(
            expert_weight_kernel,
            [shape((shard_count // 2, pack_rows, half_width), bf16)],
            core_place, picked[0], picks[1], kept, swap_cores(kept), *extra,
            scalar=True, pieces={0: (1, pack_rows // 16)}, flops=2 * expert_flops,
        )
        sent, packed, logits_grad = lax.optimization_barrier((sent, packed, logits_grad))
        if layer < LAYERS - 1:
            packed, sums[layer + 1] = lax.optimization_barrier((packed, sums[layer + 1]))
        summed = lax.psum_scatter(
            packed.reshape(-1, half_width), "fsdp", scatter_dimension=0, tiled=True,
            axis_index_groups=chips,
        )
        grad_middle, branch, send, small_grad = once(
            after_experts_kernel,
            [
                shape((tok_count, width), f32),
                shape((tok_count, width), bf16),
                shape((seq_count, tok_count, local_width), bf16),
                shape((2 * expert_count, width), f32),
            ],
            grad_hidden, sent.reshape(total_slots, width), middle, normed_ffn, logits_grad,
            target_t, small, pack, spread,
            cut={7: out_cut}, flops=4 * dense_flops,
        )
        grad_heads = swap_seq(send)
        (grad_own,) = once(
            attention_back_kernel,
            [shape((seq_count, tok_count, local_width + 2 * HD), bf16)],
            heads, grad_heads, bias, cos_all, sin_all,
            flops=10 * head_local * group_tok * group_tok * HD,
        )
        qkv_block_grad = once(
            qkv_weight_kernel,
            [shape((shard_count // 2, shard_rows, half_width), bf16)] * 2,
            core_place, normed_all, grad_own, small_grad, spread, scalar=True, flops=2 * dense_flops,
        )
        sent, qkv_block_grad = lax.optimization_barrier((swap_seq(grad_own), qkv_block_grad))
        grad_hidden, grad_low, gain_grad = once(
            before_attention_kernel,
            [
                shape((tok_count, width), f32),
                shape((tok_count, width), bf16),
                shape((8, width), f32),
            ],
            sent, qkv_w, qkv_w, qkv_w, spread, small, below, grad_middle,
            cut={
                1: ((1, row, shard_rows),),
                2: ((1, row + shard_rows, shard_rows),),
                3: ((1, row + 2 * shard_rows, shard_rows), (2, 0, 2 * KVHEADS * HD)),
            },
            flops=4 * dense_flops,
        )
        sums[layer] = summed
        dense_sources = (
            qkv_block_grad[0], swap_cores(qkv_block_grad[1]), gain_grad, swap_cores(gain_grad),
            spread, picked[1], branch, swap_cores(branch),
        )
        if layer > 0:
            grad_blocks, grad_cut, waiting = around_seq(grad_low), (), dense_sources
    (dense_pack,) = once(
        dense_kernel,
        [shape((shard_count // 2, 3 * shard_rows, half_width), bf16)],
        core_place, *dense_sources, scalar=True, flops=2 * dense_flops,
    )
    dense_sum = jnp.sum(swap_chips(dense_pack).astype(f32), axis=0).astype(bf16)
    (rows,) = once(
        arrange_kernel,
        [shape((seq_count, 3 * LAYERS, 16, half_width), bf16)],
        dense_sum, sums[0], cut={1: ((0, local_experts * expert_rows, 3 * shard_rows),)},
    )
    rows = swap_seq(rows)
    gate_grads, up_grads, down_grads = once(
        expert_grads_kernel,
        [
            shape((LAYERS,) + w_gate.shape[1:], f32),
            shape((LAYERS,) + w_up.shape[1:], f32),
            shape((LAYERS,) + w_down.shape[1:], f32),
        ],
        *sums,
        cut={0: ((0, 0, local_experts * expert_rows),)},
    )
    query_grads, key_grads, value_grads, out_grads, router_grads, *gain_grads = once(
        dense_grads_kernel,
        [
            shape((dense_rows, LAYERS, HEADS * HD), f32),
            shape((dense_rows, LAYERS, KVHEADS * HD), f32),
            shape((dense_rows, LAYERS, KVHEADS * HD), f32),
            shape((dense_rows, LAYERS, width), f32),
            shape((LAYERS, expert_count, dense_rows), f32),
            shape((LAYERS, dense_rows), f32),
            shape((LAYERS, dense_rows), f32),
        ],
        rows,
    )
    return (
        result[None],
        grad_hidden[None],
        gain_grads[0],
        query_grads.transpose(1, 0, 2),
        key_grads.transpose(1, 0, 2),
        value_grads.transpose(1, 0, 2),
        out_grads.transpose(1, 0, 2),
        gain_grads[1],
        router_grads.transpose(0, 2, 1),
        gate_grads,
        up_grads,
        down_grads,
    )


def solution(mesh):
    in_specs = (
        P("fsdp", "seq", None),
        P("fsdp", "seq", None),
        P(None, "fsdp", "seq", None),
        P(None, "fsdp", "seq", None),
        P("fsdp", None),
        P(None, ("seq", "fsdp")),
        P(None, ("seq", "fsdp"), None),
        P(None, ("seq", "fsdp"), None),
        P(None, ("seq", "fsdp"), None),
        P(None, ("seq", "fsdp"), None),
        P(None, ("seq", "fsdp")),
        P(None, ("seq", "fsdp"), None),
        P(None, "seq", "fsdp", None),
        P(None, "seq", "fsdp", None),
        P(None, "seq", "fsdp", None),
    )
    out_specs = (
        P("fsdp", "seq", None),
        P("fsdp", "seq", None),
        P(None, ("seq", "fsdp")),
        P(None, ("seq", "fsdp"), None),
        P(None, ("seq", "fsdp"), None),
        P(None, ("seq", "fsdp"), None),
        P(None, ("seq", "fsdp"), None),
        P(None, ("seq", "fsdp")),
        P(None, ("seq", "fsdp"), None),
        P(None, "seq", "fsdp", None),
        P(None, "seq", "fsdp", None),
        P(None, "seq", "fsdp", None),
    )
    return jax.shard_map(
        per_device, mesh=mesh, in_specs=in_specs, out_specs=out_specs, check_vma=False
    )
```

```python
import functools

import jax
import jax.numpy as jnp
import numpy as np
from jax import lax
from jax.experimental import pallas as pl
from jax.experimental.pallas import tpu as pltpu
from jax.sharding import PartitionSpec as P

HEADS = 12
KVHEADS = 2
HD = 128
TOPK = 4
LAYERS = 2
NCONT = 4

norm_eps = 1e-06
rope_base = 10000.0
masked_value = -1e30

bf16 = jnp.bfloat16
f32 = jnp.float32
VMEM_BYTES = 64 * 1024 * 1024 - 256 * 1024


def group_tables(segment_row, prompt_len):
    cont_len = segment_row.shape[0]
    onehot = (segment_row[:, None] == jnp.arange(NCONT, dtype=jnp.int32)[None, :]).astype(jnp.int32)
    counts = jnp.sum(onehot, axis=0)
    starts = jnp.cumsum(counts) - counts
    seg_begin = jnp.sum(onehot * starts[None, :], axis=1)
    within = jnp.arange(cont_len, dtype=jnp.int32) - seg_begin
    positions = jnp.concatenate([jnp.arange(prompt_len, dtype=jnp.int32), prompt_len + within])
    labels = jnp.concatenate([jnp.full((prompt_len,), -1, jnp.int32), segment_row])
    frequency = rope_base ** (-(jnp.arange(HD // 2, dtype=jnp.float32) * 2.0 / HD))
    angles = positions.astype(jnp.float32)[:, None] * frequency[None, :]
    return (jnp.cos(angles), jnp.sin(angles), labels)


def slot_table(routes_t, order_t, expert_count, capacity):
    pair_expert = routes_t.reshape(-1)
    pair_order = order_t.reshape(-1)
    same_expert = pair_expert[:, None] == pair_expert[None, :]
    earlier = pair_order[None, :] < pair_order[:, None]
    pair_slot = jnp.sum(jnp.logical_and(same_expert, earlier).astype(jnp.int32), axis=1)
    target = jnp.where(
        pair_slot < capacity, pair_expert * capacity + pair_slot, expert_count * capacity
    )
    return target.reshape(routes_t.shape)


def nn(left, right):
    return lax.dot_general(left, right, (((1,), (0,)), ((), ())), preferred_element_type=f32)


def nt(left, right):
    return lax.dot_general(left, right, (((1,), (1,)), ((), ())), preferred_element_type=f32)


def tn(left, right):
    return lax.dot_general(left, right, (((0,), (0,)), ((), ())), preferred_element_type=f32)


def split(value):
    high = value.astype(bf16)
    return high, (value - high.astype(f32)).astype(bf16)


class Late:
    def __init__(self, ref, copy):
        self.ref, self.copy, self.shape = ref, copy, ref.shape
        copy.start()

    def wait(self):
        if self.copy is not None:
            self.copy.wait()
            self.copy = None

    def __getitem__(self, index):
        self.wait()
        return self.ref[index]


class Out:
    def __init__(self, ref, copies):
        self.ref, self.copies, self.shape = ref, copies, ref.shape
        self.sent = [False] * len(copies)

    def send(self, piece=None):
        for n in range(len(self.copies)) if piece is None else (piece,):
            if not self.sent[n]:
                self.copies[n].start()
                self.sent[n] = True

    def __getitem__(self, index):
        return self.ref[index]

    def __setitem__(self, index, value):
        self.ref[index] = value


def cost(args, outs, flops):
    moved = sum(int(np.prod(a.shape)) * a.dtype.itemsize for a in (*args, *outs))
    return pl.CostEstimate(flops=flops, bytes_accessed=moved, transcendentals=0)


def once(kernel, outs, *args, scalar=False, cut=None, pieces=None, flops=0):
    cut, pieces = cut or {}, pieces or {}
    hbm = pl.BlockSpec(memory_space=pltpu.HBM)
    late = [n for n in range(len(args)) if not (scalar and n == 0)]
    specs = [hbm] * len(args)
    if scalar:
        specs[0] = pl.BlockSpec(memory_space=pltpu.SMEM)
    scratch = []
    for n in late:
        dims = list(args[n].shape)
        for dim, start, size in cut.get(n, ()):
            dims[dim] = size
        scratch.append(pltpu.VMEM(tuple(dims), args[n].dtype))
    scratch += [pltpu.VMEM(o.shape, o.dtype) for o in outs]
    parts = [pieces.get(n, (0, 1)) for n in range(len(outs))]
    scratch.append(pltpu.SemaphoreType.DMA((len(late) + sum(count for _, count in parts),)))

    def body(*refs):
        ins = list(refs[: len(args)])
        out_refs = refs[len(args) : len(args) + len(outs)]
        rooms = refs[len(args) + len(outs) : -1]
        sems = refs[-1]
        for i, n in enumerate(late):
            source = ins[n]
            for dim, start, size in cut.get(n, ()):
                if callable(start):
                    start = pl.multiple_of(start(ins[0][0]), 16 if dim == 1 else HD)
                source = source.at[(slice(None),) * dim + (pl.ds(start, size),)]
            ins[n] = Late(rooms[i], pltpu.make_async_copy(source, rooms[i], sems.at[i]))
        results = []
        used = len(late)
        for i, out in enumerate(out_refs):
            room = rooms[len(late) + i]
            dim, count = parts[i]
            size = room.shape[dim] // count
            copies = []
            for n in range(count):
                at = (slice(None),) * dim + (pl.ds(n * size, size),)
                copies.append(pltpu.make_async_copy(room.at[at], out.at[at], sems.at[used]))
                used += 1
            results.append(Out(room, copies))
        kernel(*ins, *results)
        for result in results:
            result.send()
        for n in late:
            ins[n].wait()
        for result in results:
            for copy in result.copies:
                copy.wait()

    return pl.pallas_call(
        body,
        out_shape=list(outs),
        in_specs=specs,
        out_specs=[hbm] * len(outs),
        scratch_shapes=scratch,
        compiler_params=pltpu.CompilerParams(vmem_limit_bytes=VMEM_BYTES),
        cost_estimate=cost(args, outs, flops),
    )(*args)


def shape(dims, dtype):
    return jax.ShapeDtypeStruct(dims, dtype)


def normalize(value, gain):
    inverse = lax.rsqrt(jnp.mean(value * value, axis=-1, keepdims=True) + norm_eps)
    return value * inverse * gain


def normalize_back(value, gain, grad):
    inverse = lax.rsqrt(jnp.mean(value * value, axis=-1, keepdims=True) + norm_eps)
    unit = value * inverse
    grad_gain = jnp.sum(grad * unit, axis=0, keepdims=True)
    scaled = grad * gain
    grad_value = inverse * (scaled - unit * jnp.mean(scaled * unit, axis=-1, keepdims=True))
    return grad_value, grad_gain


def to_gathered(parts, order):
    count = len(parts)
    share = parts[0].shape[1] // count
    done = []
    for j in range(count):
        piece = jnp.concatenate([part[:, j * share : (j + 1) * share] for part in parts], axis=1)
        done.append(nn(piece, order))
    return jnp.concatenate(done, axis=1)


def to_natural(value, order):
    count = value.shape[1] // order.shape[0]
    size = order.shape[0]
    share = size // count
    done = [nt(value[:, j * size : (j + 1) * size], order) for j in range(count)]
    return [
        jnp.concatenate([part[:, s * share : (s + 1) * share] for part in done], axis=1)
        for s in range(count)
    ]


def column_blocks(value, count):
    size = value.shape[1] // count
    return [value[:, s * size : (s + 1) * size] for s in range(count)]


def turn(block, cosines, sines):
    return block * cosines + pltpu.roll(block, HD // 2, 1) * sines


def smooth_parts(value):
    root = np.float32(np.sqrt(2.0 / np.pi))
    square = value * value
    high = jnp.tanh(root * (value + 0.044715 * value * square))
    half = 0.5 * (1.0 + high)
    slope = half + 0.5 * value * (1.0 - high * high) * root * (1.0 + 3 * 0.044715 * square)
    return value * half, slope


def choose(target_t, slots):
    place = lax.broadcasted_iota(jnp.int32, (slots, target_t.shape[1]), 0)
    total = jnp.zeros(place.shape, f32)
    for k in range(TOPK):
        total = total + jnp.where(place == target_t[k : k + 1], 1.0, 0.0)
    return total


def choose_weighted(target_t, gates_t, slots):
    place = lax.broadcasted_iota(jnp.int32, (slots, target_t.shape[1]), 0)
    total = jnp.zeros(place.shape, f32)
    for k in range(TOPK):
        total = total + jnp.where(place == target_t[k : k + 1], gates_t[k : k + 1], 0.0)
    return total


def input_kernel(
    middle, combined, gates_t, target_t, small, spread, normed_ref, hidden_ref
):
    expert_count = 8
    hidden = middle[...] + mix(combined[...], gates_t[...], target_t[...])
    hidden_ref[...] = hidden
    hidden_ref.send()
    gain = small[expert_count : expert_count + 1].astype(f32)
    normed = normalize(hidden, gain).astype(bf16)
    count = normed.shape[1] // spread.shape[0]
    normed_ref[...] = to_gathered(column_blocks(normed, count), spread[...]).astype(bf16)


def mix(combined, gates_t, target_t):
    high, low = split(choose_weighted(target_t, gates_t, combined.shape[0]))
    tokens = high.shape[1]
    both = tn(jnp.concatenate([high, low], axis=1), combined)
    return both[:tokens] + both[tokens:]


def result_kernel(middle, combined, gates_t, target_t, result_ref):
    mixture = mix(combined[...], gates_t[...], target_t[...])
    result_ref[...] = (middle[...] + mixture).astype(bf16)


def attend(rows, weight, cosines, sines, bias_ref, heads_ref, out_ref):
    seq_count, tokens, columns = heads_ref.shape
    group = seq_count * tokens
    local = columns // HD - 2
    prompt = group // 2
    raw = nn(rows, weight)
    heads = []
    for j in range(local + 2):
        block = raw[:, j * HD : (j + 1) * HD]
        if j <= local:
            block = turn(block, cosines, sines)
        heads.append(block.astype(bf16))
        heads_ref[:, :, j * HD : (j + 1) * HD] = heads[j].reshape(seq_count, tokens, HD)
    heads_ref.send()
    key, value = heads[local], heads[local + 1]
    scale = HD ** (-0.5)
    for j in range(local):
        query = heads[j]
        for rows, seen in ((slice(0, prompt), prompt), (slice(prompt, group), group)):
            scores = nt(query[rows], key[:seen]) * scale + bias_ref[rows, :seen]
            peak = jnp.max(scores, axis=-1, keepdims=True)
            weights = jnp.exp(scores - peak)
            weights = weights / jnp.sum(weights, axis=-1, keepdims=True)
            part = nn(weights.astype(bf16), value[:seen]).astype(bf16)
            first = rows.start // tokens
            out_ref[first : first + prompt // tokens, :, j * HD : (j + 1) * HD] = part.reshape(
                prompt // tokens, tokens, HD
            )


def first_attention_kernel(
    place, own, one, two, three, weight, spread, cosines, sines, bias_ref,
    heads_ref, out_ref, normed_ref, small_ref,
):
    expert_count = 8
    me = place[0]
    seq_count, tokens, width = normed_ref.shape
    columns = heads_ref.shape[2]
    count = small_ref.shape[1]
    extras = weight[:, columns:].astype(f32).T.astype(bf16)
    extras = jnp.concatenate([extras[:count], extras[HD : HD + count]], axis=0)
    small = jnp.concatenate(to_natural(extras, spread[...]), axis=1)
    small_ref[0] = small[:count].astype(bf16)
    small_ref[1] = small[count:].astype(bf16)
    small_ref.send()
    gain = small[expert_count : expert_count + 1]
    for k, block in enumerate((own, one, two, three)):
        normed = normalize(block[...].astype(f32), gain).astype(bf16)
        normed = to_gathered(column_blocks(normed, seq_count), spread[...]).astype(bf16)
        normed_ref[lax.rem(me + k, seq_count)] = normed
    normed_ref.send()
    rows = normed_ref[...].reshape(seq_count * tokens, width)
    attend(rows, weight[:, :columns], cosines[...], sines[...], bias_ref, heads_ref, out_ref)


def next_attention_kernel(
    place, own, one, two, three, weight, cosines, sines, bias_ref, heads_ref, out_ref, normed_ref
):
    me = place[0]
    seq_count, tokens, width = normed_ref.shape
    weight = weight[...].reshape(width, weight.shape[2])[:, : heads_ref.shape[2]]
    for k, block in enumerate((own, one, two, three)):
        normed_ref[lax.rem(me + k, seq_count)] = block[...]
    normed_ref.send()
    rows = normed_ref[...].reshape(seq_count * tokens, width)
    attend(rows, weight, cosines[...], sines[...], bias_ref, heads_ref, out_ref)


def gates_of(logits, routes_t, rows):
    expert_count = 8
    tokens = logits.shape[1]
    chosen = []
    for k in range(TOPK):
        route = routes_t[k : k + 1]
        value = jnp.zeros((1, tokens), f32)
        for e in range(expert_count):
            value = value + jnp.where(route == e, logits[e : e + 1], 0.0)
        chosen.append(value)
    peak = functools.reduce(jnp.maximum, chosen)
    powers = [jnp.exp(value - peak) for value in chosen]
    total = functools.reduce(jnp.add, powers)
    gates = [power / total for power in powers]
    return jnp.concatenate(gates + [jnp.zeros((rows - TOPK, tokens), f32)], axis=0)


def after_attention_kernel(
    back, spread, hidden, small, out_w, routes_t, middle_ref, normed_ref, gates_ref, attended_ref
):
    expert_count = 8
    seq_count, tokens, part = back.shape
    width = seq_count * part
    attended = to_gathered([back[s] for s in range(seq_count)], spread[...]).astype(bf16)
    attended_ref[...] = attended
    attended_ref.send()
    rows = out_w.shape[1] // 2
    half = out_w.shape[2]
    for side in range(2):
        weight = out_w[:, side * rows : (side + 1) * rows].reshape(width, half)
        cols = slice(side * half, (side + 1) * half)
        middle_ref[:, cols] = hidden[:, cols].astype(f32) + nn(attended, weight)
    middle_ref.send()
    middle = middle_ref[...]
    gain = small[expert_count + 1 : expert_count + 2].astype(f32)
    normed = normalize(middle, gain).astype(bf16)
    normed_ref[...] = normed
    normed_ref.send()
    gates_ref[...] = gates_of(nt(small[...], normed), routes_t[...], gates_ref.shape[0])


def down_parts(block):
    shards, rows, half = block.shape
    wide = block.astype(f32)
    left = wide[:, : rows // 2].reshape(shards * rows // 2, half).astype(bf16)
    right = wide[:, rows // 2 :].reshape(shards * rows // 2, half).astype(bf16)
    return left, right


def expert_kernel(place, own, one, two, three, targets, routes, small, *rest):
    me = place[0]
    blocks = (own, one, two, three)
    out_ref, rows_ref, gate_ref, up_ref, gates_ref = rest[-5:]
    weights = rest[:-5]
    sources, experts, capacity, width = out_ref.shape
    half = width // 2
    for e in range(experts):
        gate_w, up_w, down_w = weights[3 * e : 3 * e + 3]
        first = (me * experts + e) * capacity
        parts = []
        for k, block in enumerate(blocks):
            hot = choose(targets[lax.rem(me + k, sources)] - first, capacity)
            parts.append(nn(hot.astype(bf16), block[...]))
        tokens = jnp.concatenate(parts, axis=0).astype(bf16)
        rows_ref[e] = tokens
        rows_ref.send(e)
        gate_val = nn(tokens, gate_w[...].reshape(width, half))
        gate_ref[e] = gate_val.astype(bf16)
        gate_ref.send(e)
        up_val = nn(tokens, up_w[...].reshape(width, half))
        up_ref[e] = up_val.astype(bf16)
        up_ref.send(e)
        activated, slope = smooth_parts(gate_val)
        inner = (activated * up_val).astype(bf16)
        for side, part in enumerate(down_parts(down_w[...])):
            done = nn(inner, part).astype(bf16)
            for k in range(sources):
                out_ref[lax.rem(me + k, sources), e, :, side * half : (side + 1) * half] = done[
                    k * capacity : (k + 1) * capacity
                ]
        out_ref.send(e)
    for k, block in enumerate(blocks):
        logits = nt(small[...], block[...])
        gates_ref[k] = gates_of(logits, routes[lax.rem(me + k, sources)], gates_ref.shape[1])


def logits_grad_kernel(grad, combined, gates_t, routes_t, target_t, logits_ref):
    tokens = grad.shape[0]
    slots = combined.shape[0]
    high, low = split(grad[...])
    products = nt(combined[...], jnp.concatenate([high, low], axis=0))
    products = products[:, :tokens] + products[:, tokens:]
    place = lax.broadcasted_iota(jnp.int32, (slots, tokens), 0)
    grad_gates = [
        jnp.sum(jnp.where(place == target_t[k : k + 1], products, 0.0), axis=0, keepdims=True)
        for k in range(TOPK)
    ]
    gates = [gates_t[k : k + 1] for k in range(TOPK)]
    center = functools.reduce(jnp.add, [a * b for a, b in zip(gates, grad_gates)])
    label = lax.broadcasted_iota(jnp.int32, logits_ref.shape, 0)
    total = jnp.zeros(logits_ref.shape, f32)
    for k in range(TOPK):
        choice = gates[k] * (grad_gates[k] - center)
        total = total + jnp.where(label == routes_t[k : k + 1], choice, 0.0)
    logits_ref[...] = total.astype(bf16)


def expert_back_kernel(
    place, own, one, two, three, targets, gates, down_first, gate_ref, up_ref, *rest
):
    me = place[0]
    blocks = (own, one, two, three)
    out_ref, keep_ref = rest[-2:]
    weights = (down_first,) + rest[:-2]
    sources, experts, capacity, width = out_ref.shape
    half = width // 2
    for e in range(experts):
        down_w, gate_w, up_w = weights[3 * e : 3 * e + 3]
        shards, rows, _ = gate_w.shape
        first = (me * experts + e) * capacity
        parts = []
        for k, block in enumerate(blocks):
            target = targets[lax.rem(me + k, sources)] - first
            hot = jnp.concatenate(split(choose_weighted(target, gates[k], capacity)), axis=1)
            twice = jnp.concatenate([block[...], block[...]], axis=0)
            parts.append(nn(hot, twice))
        grad = jnp.concatenate(parts, axis=0).astype(bf16)
        keep_ref[e, :, :width] = grad
        left, right = down_parts(down_w[...])
        grad_inner = nt(grad[:, :half], left) + nt(grad[:, half:], right)
        up_val = up_ref[e].astype(f32)
        activated, slope = smooth_parts(gate_ref[e].astype(f32))
        gate_at, up_at, inner_at = (slice(width + n * half, width + (n + 1) * half) for n in range(3))
        keep_ref[e, :, gate_at] = (grad_inner * up_val * slope).astype(bf16)
        keep_ref[e, :, up_at] = (grad_inner * activated).astype(bf16)
        keep_ref[e, :, inner_at] = (activated * up_val).astype(bf16)
        keep_ref.send(e)
        parts = 4
        some, size = shards // parts, shards * rows // parts
        for c in range(parts):
            at = slice(c * some, (c + 1) * some)
            total = nt(keep_ref[e, :, gate_at], gate_w[at].reshape(size, half))
            total = total + nt(keep_ref[e, :, up_at], up_w[at].reshape(size, half))
            total = total.astype(bf16)
            for k in range(sources):
                out_ref[lax.rem(me + k, sources), e, :, c * size : (c + 1) * size] = total[
                    k * capacity : (k + 1) * capacity
                ]
        out_ref.send(e)


def pick_kernel(rows, other_rows, attended, other_attended, pick, out_ref, attended_ref):
    count = rows.shape[1]
    for e in range(rows.shape[0]):
        out_ref[e, :count] = nn(rows[e], pick[...]).astype(bf16)
        out_ref[e, count:] = nn(other_rows[e], pick[...]).astype(bf16)
        out_ref.send(e)
    both = jnp.concatenate([attended[...], other_attended[...]], axis=0)
    attended_ref[...] = nn(both, pick[...]).astype(bf16)


def expert_weight_kernel(core, tokens, pick_inner, keep, other_keep, *rest):
    pack_ref = rest[-1]
    chips, _, half = pack_ref.shape
    experts = tokens.shape[0]
    width = 2 * tokens.shape[2]
    count = width // (2 * chips)
    at = 0

    def send():
        for piece in range(at // 16, (at + count) // 16):
            pack_ref.send(piece)

    for e in range(experts):
        grads = jnp.concatenate([keep[e], other_keep[e]], axis=0)
        both = tn(tokens[e], grads[:, width : width + 2 * half]).astype(bf16)
        for n in range(2):
            block = both[:, n * half : (n + 1) * half].reshape(chips, count, half)
            pack_ref[:, at : at + count] = block
            send()
            at += count
        inner = nn(grads[:, width + 2 * half :], pick_inner[...]).astype(bf16)
        down = tn(inner, grads[:, :width])
        left = down[:, :half].reshape(chips, count // 2, half)
        right = down[:, half:].reshape(chips, count // 2, half)
        pack_ref[:, at : at + count] = jnp.concatenate([left, right], axis=1).astype(bf16)
        send()
        at += count
    if len(rest) > 1:
        dense_part(core[0], rest[:-1], pack_ref, at)


def dense_kernel(core, *refs):
    dense_part(core[0], refs[:-1], refs[-1], 0)


def dense_part(core, refs, pack_ref, at):
    qkv, other_qkv, gain, other_gain, spread, attended, branch, other_branch = refs
    expert_count = 8
    chips, rows, half = qkv.shape
    width = gain.shape[1]
    blocks = column_blocks((gain[...] + other_gain[...]).astype(bf16), width // spread.shape[0])
    gains = to_gathered(blocks, spread[...])
    count = gains.shape[0]
    gains = jnp.where(lax.broadcasted_iota(jnp.int32, gains.shape, 0) == 0, gains, 0.0)
    below = jnp.zeros((HD - expert_count - count, width), f32)
    gains = jnp.concatenate([jnp.zeros((expert_count, width), f32), gains, below], axis=0).T
    gains = gains.reshape(chips, 2, rows, HD)
    gains = jnp.where(core == 0, gains[:, 0], gains[:, 1])
    total = qkv[...].astype(f32) + other_qkv[...].astype(f32)
    pack_ref[:, at : at + rows, : half - HD] = total[:, :, : half - HD].astype(bf16)
    pack_ref[:, at : at + rows, half - HD :] = (total[:, :, half - HD :] + gains).astype(bf16)
    grads = jnp.concatenate([branch[...], other_branch[...]], axis=0)
    total = tn(attended[...], grads).astype(bf16)
    for side in range(2):
        at += rows
        block = total[:, side * half : (side + 1) * half]
        pack_ref[:, at : at + rows] = block.reshape(chips, rows, half)


def keep_shards(own_ref, other_ref, core, at, value):
    shards, rows, columns = value.shape
    value = value.reshape(shards // 2, 2, rows, columns)
    own_ref[:, at : at + rows] = jnp.where(core == 0, value[:, 0], value[:, 1])
    other_ref[:, at : at + rows] = jnp.where(core == 0, value[:, 1], value[:, 0])


def after_experts_kernel(
    grad, sent, middle, normed, logits_grad, target_t, small, out_w, spread,
    grad_ref, branch_ref, send_ref, small_ref,
):
    expert_count = 8
    seq_count, tokens, part = send_ref.shape
    width = seq_count * part
    chosen = choose(target_t[...], sent.shape[0]).astype(bf16)
    grad_normed = tn(chosen, sent[...]) + tn(logits_grad[...], small[...])
    router = nn(logits_grad[...], normed[...])
    gain = small[expert_count + 1 : expert_count + 2].astype(f32)
    grad_value, grad_gain = normalize_back(middle[...], gain, grad_normed)
    label = lax.broadcasted_iota(jnp.int32, small_ref.shape, 0)
    small_ref[...] = jnp.where(label == expert_count + 1, grad_gain, router)
    grad_middle = grad[...] + grad_value
    grad_ref[...] = grad_middle
    grad_ref.send()
    branch = grad_middle.astype(bf16)
    branch_ref[...] = branch
    branch_ref.send()
    rows = out_w.shape[1] // 2
    half = out_w.shape[2]
    parts = [
        nt(branch[:, :half], out_w[:, :rows].reshape(width, half)),
        nt(branch[:, half:], out_w[:, rows:].reshape(width, half)),
    ]
    attended = (parts[0] + parts[1]).astype(bf16)
    for s, block in enumerate(to_natural(attended, spread[...])):
        send_ref[s] = block.astype(bf16)


def attention_back_kernel(heads_ref, grad_ref, bias_ref, cosines, sines, out_ref):
    seq_count, tokens, columns = heads_ref.shape
    group = seq_count * tokens
    heads = heads_ref[...].reshape(group, columns)
    grads = grad_ref[...].reshape(group, grad_ref.shape[2])
    local = columns // HD - 2
    prompt = group // 2
    key = heads[:, local * HD : (local + 1) * HD]
    value = heads[:, (local + 1) * HD :]
    scale = HD ** (-0.5)

    def keep(at, block):
        out_ref[:, :, at * HD : (at + 1) * HD] = block.astype(bf16).reshape(seq_count, tokens, HD)

    cosines, sines = cosines[...], sines[...]

    def unturn(block):
        return block * cosines - pltpu.roll(block, HD // 2, 1) * sines

    grad_key = [jnp.zeros((prompt, HD), f32), jnp.zeros((prompt, HD), f32)]
    grad_value = [jnp.zeros((prompt, HD), f32), jnp.zeros((prompt, HD), f32)]
    for j in range(local):
        query = heads[:, j * HD : (j + 1) * HD]
        grad = grads[:, j * HD : (j + 1) * HD]
        grad_query = []
        for rows, seen in ((slice(0, prompt), prompt), (slice(prompt, group), group)):
            scores = nt(query[rows], key[:seen]) * scale + bias_ref[rows, :seen]
            peak = jnp.max(scores, axis=-1, keepdims=True)
            weights = jnp.exp(scores - peak)
            weights = weights / jnp.sum(weights, axis=-1, keepdims=True)
            grad_weights = nt(grad[rows], value[:seen])
            center = jnp.sum(weights * grad_weights, axis=-1, keepdims=True)
            grad_scores = (weights * (grad_weights - center)).astype(bf16)
            low = weights.astype(bf16)
            grad_query.append(nn(grad_scores, key[:seen]) * scale)
            for side in range(seen // prompt):
                cols = slice(side * prompt, (side + 1) * prompt)
                grad_key[side] = grad_key[side] + tn(grad_scores[:, cols], query[rows])
                grad_value[side] = grad_value[side] + tn(low[:, cols], grad[rows])
        keep(j, unturn(jnp.concatenate(grad_query, axis=0)))
    keep(local, unturn(jnp.concatenate(grad_key, axis=0) * scale))
    keep(local + 1, jnp.concatenate(grad_value, axis=0))


def before_attention_kernel(
    sent, left_w, right_w, kv_w, spread, small, hidden, grad_middle, out_ref, low_ref, gain_ref
):
    expert_count = 8
    seq_count, tokens, columns = sent.shape
    local = columns // HD - 2
    share = seq_count // KVHEADS
    blocks = [sent[s, :, : local * HD] for s in range(seq_count)]
    for at in (local, local + 1):
        for c in range(KVHEADS):
            total = jnp.zeros((tokens, HD), f32)
            for s in range(c * share, (c + 1) * share):
                total = total + sent[s, :, at * HD : (at + 1) * HD].astype(f32)
            blocks.append(total.astype(bf16))
    raw = jnp.concatenate(blocks, axis=1)
    at, total = 0, 0.0
    for part in (left_w, right_w, kv_w):
        shards, rows, columns = part.shape
        weight = part[...].reshape(shards * rows, columns)
        total = total + nt(raw[:, at : at + columns], weight)
        at += columns
    high, low = split(total)
    both = to_natural(jnp.concatenate([high, low], axis=0), spread[...])
    both = jnp.concatenate(both, axis=1)
    grad_normed = both[:tokens] + both[tokens:]
    gain = small[expert_count : expert_count + 1].astype(f32)
    grad_value, grad_gain = normalize_back(hidden[...].astype(f32), gain, grad_normed)
    total = grad_middle[...] + grad_value
    low_ref[...] = total.astype(bf16)
    low_ref.send()
    out_ref[...] = total
    out_ref.send()
    gain_ref[...] = jnp.broadcast_to(grad_gain, gain_ref.shape)


def qkv_weight_kernel(core, normed, grads, small, spread, own_ref, other_ref):
    seq_count, tokens, columns = grads.shape
    chips, rows, wide = own_ref.shape
    shards = 2 * chips
    inputs = normed[...].reshape(seq_count * tokens, normed.shape[2])
    total = tn(inputs, grads[...].reshape(seq_count * tokens, columns))
    extra = column_blocks(small[...].astype(bf16), seq_count)
    extra = to_gathered(extra, spread[...])
    extra = jnp.concatenate([extra, jnp.zeros((HD - extra.shape[0], extra.shape[1]), f32)], axis=0).T
    total = jnp.concatenate([total, extra], axis=1).astype(bf16).reshape(shards, rows, wide)
    keep_shards(own_ref, other_ref, core[0], 0, total)


def expert_grads_kernel(*refs):
    sums, (gate_ref, up_ref, down_ref) = refs[:LAYERS], refs[LAYERS:]
    rows = gate_ref.shape[2]
    half = gate_ref.shape[3]
    for layer in range(LAYERS):
        block = sums[layer][...].astype(f32)
        for e in range(gate_ref.shape[1]):
            at = 3 * rows * e
            gate_ref[layer, e] = block[at : at + rows]
            up_ref[layer, e] = block[at + rows : at + 2 * rows]
            at += 2 * rows
            down_ref[layer, e, :, :half] = block[at : at + rows // 2]
            down_ref[layer, e, :, half:] = block[at + rows // 2 : at + rows]


def arrange_kernel(first, above, out_ref):
    seq_count, blocks, padded, half = out_ref.shape
    parts = blocks // LAYERS
    rows = first.shape[0] // (parts * seq_count)
    below = jnp.zeros((padded - rows, half), f32)
    for layer, ref in enumerate((first, above)):
        total = ref[...].astype(f32)
        for part in range(parts):
            for s in range(seq_count):
                at = (part * seq_count + s) * rows
                block = jnp.concatenate([total[at : at + rows], below], axis=0)
                out_ref[s, layer * parts + part] = block.astype(bf16)


def dense_grads_kernel(
    blocks, query_ref, key_ref, value_ref, out_ref, router_ref, gain_attn_ref, gain_ffn_ref
):
    seq_count, count, _, columns = blocks.shape
    parts = count // LAYERS
    rows, expert_count = query_ref.shape[0], router_ref.shape[1]
    local = columns - 3 * HD
    share = seq_count // KVHEADS
    for layer in range(LAYERS):
        whole = [blocks[s, layer * parts].astype(f32) for s in range(seq_count)]
        for s in range(seq_count):
            query_ref[:, layer, s * local : (s + 1) * local] = whole[s][:rows, :local]
        for c in range(KVHEADS):
            total = functools.reduce(jnp.add, whole[c * share : (c + 1) * share])[:rows]
            key_ref[:, layer, c * HD : (c + 1) * HD] = total[:, local : local + HD]
            value_ref[:, layer, c * HD : (c + 1) * HD] = total[:, local + HD : local + 2 * HD]
        small = functools.reduce(jnp.add, [block[:, local + 2 * HD :] for block in whole]).T
        router_ref[layer] = small[:expert_count, :rows]
        gain_attn_ref[layer : layer + 1] = small[expert_count : expert_count + 1, :rows]
        gain_ffn_ref[layer : layer + 1] = small[expert_count + 1 : expert_count + 2, :rows]
        for side in range(2):
            sides = [blocks[s, layer * parts + 1 + side].astype(f32) for s in range(seq_count)]
            total = functools.reduce(jnp.add, sides)[:rows]
            out_ref[:, layer, side * columns : (side + 1) * columns] = total


def swap_seq(block):
    return lax.all_to_all(block, "seq", split_axis=0, concat_axis=0, tiled=True)


def around_seq(block):
    count = lax.axis_size("seq")
    others = [
        lax.ppermute(block, "seq", [((i + k) % count, i) for i in range(count)])
        for k in range(1, count)
    ]
    return [block] + others


def halves(block):
    cut = block.shape[-1] // 2
    return jnp.concatenate([block[..., :cut], block[..., cut:]], axis=-2)


def per_device(
    tokens_in,
    cotangent,
    routes,
    order,
    segment_ids,
    gain_attn,
    w_query,
    w_key,
    w_value,
    w_out,
    gain_ffn,
    w_router,
    w_gate,
    w_up,
    w_down,
):
    tok_count = tokens_in.shape[1]
    width = tokens_in.shape[2]
    seq_count = lax.axis_size("seq")
    shard_count = lax.axis_size("fsdp")
    seq_index = lax.axis_index("seq")
    core = lax.rem(lax.axis_index("fsdp"), 2)
    place = jnp.full((1,), seq_index, jnp.int32)
    core_place = jnp.full((1,), core, jnp.int32)
    group_tok = seq_count * tok_count
    prompt_len = group_tok - segment_ids.shape[1]
    local_experts = w_gate.shape[1]
    expert_count = local_experts * seq_count
    capacity = 9 * tok_count * TOPK // (8 * expert_count)
    total_slots = expert_count * capacity
    head_local = HEADS // seq_count
    local_width = head_local * HD
    dense_rows = w_query.shape[1]
    shard_rows = dense_rows * seq_count
    gate_rows = w_gate.shape[2]
    down_rows = w_down.shape[2]
    expert_rows = 2 * gate_rows + 2 * down_rows
    qkv_width = (HEADS + 2 * KVHEADS) * HD
    half_width = width // 2
    inner_width = w_gate.shape[3]
    slot_rows = seq_count * capacity

    cos_half, sin_half, labels = group_tables(segment_ids[0], prompt_len)
    cos_all = jnp.concatenate([cos_half, cos_half], axis=1)
    sin_all = jnp.concatenate([-sin_half, sin_half], axis=1)
    cos_own = lax.dynamic_slice_in_dim(cos_all, seq_index * tok_count, tok_count, 0)
    sin_own = lax.dynamic_slice_in_dim(sin_all, seq_index * tok_count, tok_count, 0)
    key_pos = jnp.arange(group_tok, dtype=jnp.int32)
    allowed = jnp.logical_and(
        key_pos[None, :] <= key_pos[:, None],
        jnp.logical_or(key_pos[None, :] < prompt_len, labels[None, :] == labels[:, None]),
    )
    bias = jnp.where(allowed, 0.0, masked_value)

    column = jnp.arange(width // seq_count, dtype=jnp.int32)
    natural = (
        column % shard_rows // dense_rows * (width // seq_count // seq_count)
        + column // shard_rows * dense_rows
        + column % dense_rows
    )
    spread = (column[:, None] == natural[None, :]).astype(bf16)

    def small_rows_of(layer):
        return jnp.concatenate(
            [
                w_router[layer],
                gain_attn[layer][:, None],
                gain_ffn[layer][:, None],
                jnp.zeros((dense_rows, HD - 2 - expert_count), bf16),
            ],
            axis=1,
        )

    def dense_rows_of(layer):
        return jnp.concatenate(
            [w_query[layer], w_key[layer], w_value[layer], small_rows_of(layer), w_out[layer]],
            axis=1,
        )

    def shards_of_core(count):
        rows = count // shard_count
        wanted = jnp.arange(count // 2, dtype=jnp.int32)
        wanted = (wanted // rows * 2 + core) * rows + wanted % rows
        return (jnp.arange(count, dtype=jnp.int32)[:, None] == wanted[None, :]).astype(bf16)

    picks = (shards_of_core(width), shards_of_core(inner_width))

    def spread_seq(dense):
        dense = swap_seq(jnp.broadcast_to(dense[None], (seq_count,) + dense.shape))
        return dense.reshape(shard_rows, dense.shape[2])

    def own_columns(weight):
        pick = seq_index * KVHEADS // seq_count
        starts = (seq_index * local_width, (HEADS + pick) * HD, (HEADS + KVHEADS + pick) * HD)
        parts = [
            lax.dynamic_slice_in_dim(weight, start, size, 1)
            for start, size in zip(starts, (local_width, HD, HD))
        ]
        return jnp.concatenate(parts + [weight[:, qkv_width : qkv_width + HD]], axis=1)

    def expert_part(layer):
        return [
            part
            for e in range(local_experts)
            for part in (w_gate[layer, e], w_up[layer, e], halves(w_down[layer, e]))
        ]

    def out_part(dense):
        return [halves(dense[:, qkv_width + HD :])]

    def qkv_part(dense):
        wide = jnp.concatenate(
            [dense[:, : qkv_width + HD], jnp.zeros((shard_rows, HD), bf16)], axis=1
        )
        return [wide[:, at : at + half_width] for at in range(0, wide.shape[1], half_width)]

    def fetch(parts):
        return lax.all_gather(jnp.concatenate(parts, axis=0), "fsdp", axis=0, tiled=False)

    chips = [[i + c for i in range(0, shard_count, 2)] for c in range(2)]

    def swap_chips(block):
        return lax.all_to_all(
            block, "fsdp", split_axis=0, concat_axis=0, tiled=True, axis_index_groups=chips
        )

    def swap_cores(block):
        return lax.ppermute(block, "fsdp", [(i, i ^ 1) for i in range(shard_count)])

    def both_cores(block):
        other = swap_cores(block)
        first = jnp.where(core == 0, block, other)
        second = jnp.where(core == 0, other, block)
        return jnp.stack([first, second], axis=1).reshape((shard_count,) + block.shape[1:])

    def to_chips(block):
        return swap_chips(jnp.broadcast_to(block[None], (shard_count // 2,) + block.shape))

    weight_parts = [
        (e * expert_rows + k * gate_rows, gate_rows) for e in range(local_experts) for k in range(3)
    ]
    back_parts = [weight_parts[3 * e + k] for e in range(local_experts) for k in (2, 0, 1)]
    out_cut = ((1, local_experts * expert_rows, 2 * shard_rows),)

    slots_shape = shape((seq_count, local_experts, capacity, width), bf16)
    inner_shape = (local_experts, slot_rows, inner_width)
    expert_flops = 6 * total_slots * width * inner_width
    dense_flops = 2 * tok_count * width * width
    records = []
    hidden = tokens_in[0]
    dense = spread_seq(jnp.concatenate([dense_rows_of(0), dense_rows_of(1)], axis=1))
    dense, next_dense = jnp.split(dense, 2, axis=1)
    next_small = next_dense[:, qkv_width : qkv_width + HD]
    columns = jnp.concatenate([own_columns(dense), next_small], axis=1)
    both_rows = jnp.concatenate([hidden, cotangent[0]], axis=0)
    columns, both_rows = lax.optimization_barrier((columns, both_rows))
    both_blocks = around_seq(both_rows)
    packs = [fetch(expert_part(0) + out_part(dense)), None]
    columns = to_chips(columns)
    pairs = jnp.concatenate(
        [array[layer, 0].T for array in (routes, order) for layer in range(LAYERS)], axis=0
    )
    pairs = swap_seq(jnp.broadcast_to(pairs[None], (seq_count,) + pairs.shape))
    pairs = pairs.reshape(seq_count, 2, LAYERS, TOPK, tok_count)
    slots_of = functools.partial(slot_table, expert_count=expert_count, capacity=capacity)
    all_routes = [pairs[:, 0, layer] for layer in range(LAYERS)]
    all_targets = [
        jax.vmap(slots_of)(pairs[:, 0, layer], pairs[:, 1, layer]) for layer in range(LAYERS)
    ]
    targets = [lax.dynamic_index_in_dim(t, seq_index, 0, False) for t in all_targets]
    routes_ts = [lax.dynamic_index_in_dim(t, seq_index, 0, False) for t in all_routes]
    early = (both_blocks, all_targets, all_routes, targets, routes_ts)
    early = early + (cos_all, sin_all, bias, spread, picks)
    columns, early = lax.optimization_barrier((columns, early))
    both_blocks, all_targets, all_routes, targets, routes_ts = early[:5]
    cos_all, sin_all, bias, spread, picks = early[5:]
    first_columns = both_cores(columns).reshape(width, columns.shape[2])
    grad_blocks, grad_cut = both_blocks, ((0, tok_count, tok_count),)
    own_at = local_experts * expert_rows + 2 * shard_rows
    heads_shape = shape((seq_count, tok_count, local_width + 2 * HD), bf16)
    attended_shape = shape((seq_count, tok_count, local_width), bf16)
    normed_shape = shape((seq_count, tok_count, width), bf16)
    small_shape = shape((LAYERS, 2 * expert_count, width), bf16)
    attention_flops = 4 * head_local * group_tok * group_tok * HD + 2 * dense_flops
    for layer in range(LAYERS):
        pack, routes_t, target_t = packs[layer], routes_ts[layer], targets[layer]
        if layer == 0:
            heads, attended, normed_all, smalls = once(
                first_attention_kernel,
                [heads_shape, attended_shape, normed_shape, small_shape],
                place, *both_blocks, first_columns, spread, cos_all, sin_all, bias,
                scalar=True, cut={n: ((0, 0, tok_count),) for n in range(1, 5)}, flops=attention_flops + 4 * dense_flops,
            )
            small = smalls[layer]
        else:
            small = smalls[layer]
            normed_p, hidden = once(
                input_kernel,
                [shape((tok_count, width), bf16), shape((tok_count, width), f32)],
                middle, combined, gates_t, above_target, small, spread, flops=2 * dense_flops,
            )
            heads, attended, normed_all = once(
                next_attention_kernel,
                [heads_shape, attended_shape, normed_shape],
                place, *around_seq(normed_p), pack, cos_all, sin_all, bias,
                scalar=True, cut={5: ((1, own_at, shard_rows),)}, flops=attention_flops,
            )
        if layer == 0:
            back = swap_seq(attended)
            next_parts = expert_part(1) + out_part(next_dense) + [own_columns(next_dense)]
            next_parts = jnp.concatenate(next_parts, axis=0)
            tied, next_parts = lax.optimization_barrier((pack, next_parts))
            packs = [tied, fetch([next_parts])]
        else:
            back = swap_seq(attended)
            qkv_parts = jnp.concatenate(qkv_part(dense) + qkv_part(next_dense), axis=0)
            qkv_parts, back = lax.optimization_barrier((qkv_parts, back))
            qkv_w = fetch([qkv_parts])
        middle, normed_ffn, gates_t, attended_p = once(
            after_attention_kernel,
            [
                shape((tok_count, width), f32),
                shape((tok_count, width), bf16),
                shape((2 * TOPK, tok_count), f32),
                shape((tok_count, width), bf16),
            ],
            back, spread, hidden, small, pack, routes_t,
            cut={4: out_cut}, flops=3 * dense_flops,
        )
        expert_out, received, gate_val, up_val, all_gates = once(
            expert_kernel,
            [
                slots_shape,
                shape((local_experts, slot_rows, width), bf16),
                shape(inner_shape, bf16),
                shape(inner_shape, bf16),
                shape((seq_count, 2 * TOPK, tok_count), f32),
            ],
            place, *around_seq(normed_ffn), all_targets[layer], all_routes[layer], small,
            *[pack] * len(weight_parts),
            scalar=True,
            cut={n + 8: ((1, *part),) for n, part in enumerate(weight_parts)},
            pieces={n: (1 if n == 0 else 0, local_experts) for n in range(4)},
            flops=expert_flops,
        )
        picked = once(
            pick_kernel,
            [
                shape((local_experts, 2 * slot_rows, width // 2), bf16),
                shape((2 * tok_count, width // 2), bf16),
            ],
            received, swap_cores(received), attended_p, swap_cores(attended_p), picks[0],
            pieces={0: (0, local_experts)}, flops=expert_flops // 3,
        )
        combined, picked = lax.optimization_barrier(
            (swap_seq(expert_out).reshape(total_slots, width), picked)
        )
        above_target = target_t
        records.append(
            (
                (pack, small, routes_t, target_t),
                (hidden, normed_all, heads),
                (middle, normed_ffn, gates_t, combined),
                (picked, gate_val, up_val, all_gates),
            )
        )
    (result,) = once(
        result_kernel, [shape((tok_count, width), bf16)], middle, combined, gates_t, target_t,
        flops=dense_flops,
    )

    grad_hidden = cotangent[0].astype(f32)
    sums = [None] * LAYERS
    waiting = None
    for layer in range(LAYERS - 1, -1, -1):
        weights, attn_saved, mid_saved, expert_saved = records[layer]
        pack, small, routes_t, target_t = weights
        row = layer * 3 * shard_rows
        below, normed_all, heads = attn_saved
        middle, normed_ffn, gates_t, combined = mid_saved
        picked, gate_val, up_val, all_gates = expert_saved
        if waiting is None:
            tied = lax.optimization_barrier((grad_blocks, qkv_w, result, combined))
            grad_blocks, qkv_w, result, combined = tied
        else:
            grad_blocks, waiting = lax.optimization_barrier((grad_blocks, waiting))
        grad_rows, kept = once(
            expert_back_kernel,
            [slots_shape, shape((local_experts, slot_rows, width + 3 * inner_width), bf16)],
            place, *grad_blocks, all_targets[layer], all_gates, pack, gate_val, up_val,
            *[pack] * (len(back_parts) - 1),
            scalar=True,
            cut={n + 9 if n else 7: ((1, *part),) for n, part in enumerate(back_parts)}
            | {n: grad_cut for n in range(1, 5)},
            pieces={0: (1, local_experts), 1: (0, local_experts)},
            flops=expert_flops,
        )
        (logits_grad,) = once(
            logits_grad_kernel,
            [shape((2 * expert_count, tok_count), bf16)],
            grad_hidden, combined, gates_t, routes_t, target_t, flops=3 * dense_flops,
        )
        sent = swap_seq(grad_rows)
        extra = () if layer == LAYERS - 1 else waiting
        pack_rows = local_experts * expert_rows + (3 * shard_rows if extra else 0)
        (packed,) = once(
            expert_weight_kernel,
            [shape((shard_count // 2, pack_rows, half_width), bf16)],
            core_place, picked[0], picks[1], kept, swap_cores(kept), *extra,
            scalar=True, pieces={0: (1, pack_rows // 16)}, flops=2 * expert_flops,
        )
        sent, packed, logits_grad = lax.optimization_barrier((sent, packed, logits_grad))
        if layer < LAYERS - 1:
            packed, sums[layer + 1] = lax.optimization_barrier((packed, sums[layer + 1]))
        summed = lax.psum_scatter(
            packed.reshape(-1, half_width), "fsdp", scatter_dimension=0, tiled=True,
            axis_index_groups=chips,
        )
        grad_middle, branch, send, small_grad = once(
            after_experts_kernel,
            [
                shape((tok_count, width), f32),
                shape((tok_count, width), bf16),
                shape((seq_count, tok_count, local_width), bf16),
                shape((2 * expert_count, width), f32),
            ],
            grad_hidden, sent.reshape(total_slots, width), middle, normed_ffn, logits_grad,
            target_t, small, pack, spread,
            cut={7: out_cut}, flops=4 * dense_flops,
        )
        grad_heads = swap_seq(send)
        (grad_own,) = once(
            attention_back_kernel,
            [shape((seq_count, tok_count, local_width + 2 * HD), bf16)],
            heads, grad_heads, bias, cos_all, sin_all,
            flops=10 * head_local * group_tok * group_tok * HD,
        )
        qkv_block_grad = once(
            qkv_weight_kernel,
            [shape((shard_count // 2, shard_rows, half_width), bf16)] * 2,
            core_place, normed_all, grad_own, small_grad, spread, scalar=True, flops=2 * dense_flops,
        )
        sent, qkv_block_grad = lax.optimization_barrier((swap_seq(grad_own), qkv_block_grad))
        grad_hidden, grad_low, gain_grad = once(
            before_attention_kernel,
            [
                shape((tok_count, width), f32),
                shape((tok_count, width), bf16),
                shape((8, width), f32),
            ],
            sent, qkv_w, qkv_w, qkv_w, spread, small, below, grad_middle,
            cut={
                1: ((1, row, shard_rows),),
                2: ((1, row + shard_rows, shard_rows),),
                3: ((1, row + 2 * shard_rows, shard_rows), (2, 0, 2 * KVHEADS * HD)),
            },
            flops=4 * dense_flops,
        )
        sums[layer] = summed
        dense_sources = (
            qkv_block_grad[0], swap_cores(qkv_block_grad[1]), gain_grad, swap_cores(gain_grad),
            spread, picked[1], branch, swap_cores(branch),
        )
        if layer > 0:
            grad_blocks, grad_cut, waiting = around_seq(grad_low), (), dense_sources
    (dense_pack,) = once(
        dense_kernel,
        [shape((shard_count // 2, 3 * shard_rows, half_width), bf16)],
        core_place, *dense_sources, scalar=True, flops=2 * dense_flops,
    )
    dense_sum = jnp.sum(swap_chips(dense_pack).astype(f32), axis=0).astype(bf16)
    (rows,) = once(
        arrange_kernel,
        [shape((seq_count, 3 * LAYERS, 16, half_width), bf16)],
        dense_sum, sums[0], cut={1: ((0, local_experts * expert_rows, 3 * shard_rows),)},
    )
    rows = swap_seq(rows)
    gate_grads, up_grads, down_grads = once(
        expert_grads_kernel,
        [
            shape((LAYERS,) + w_gate.shape[1:], f32),
            shape((LAYERS,) + w_up.shape[1:], f32),
            shape((LAYERS,) + w_down.shape[1:], f32),
        ],
        *sums,
        cut={0: ((0, 0, local_experts * expert_rows),)},
    )
    query_grads, key_grads, value_grads, out_grads, router_grads, *gain_grads = once(
        dense_grads_kernel,
        [
            shape((dense_rows, LAYERS, HEADS * HD), f32),
            shape((dense_rows, LAYERS, KVHEADS * HD), f32),
            shape((dense_rows, LAYERS, KVHEADS * HD), f32),
            shape((dense_rows, LAYERS, width), f32),
            shape((LAYERS, expert_count, dense_rows), f32),
            shape((LAYERS, dense_rows), f32),
            shape((LAYERS, dense_rows), f32),
        ],
        rows,
    )
    return (
        result[None],
        grad_hidden[None],
        gain_grads[0],
        query_grads.transpose(1, 0, 2),
        key_grads.transpose(1, 0, 2),
        value_grads.transpose(1, 0, 2),
        out_grads.transpose(1, 0, 2),
        gain_grads[1],
        router_grads.transpose(0, 2, 1),
        gate_grads,
        up_grads,
        down_grads,
    )


def solution(mesh):
    in_specs = (
        P("fsdp", "seq", None),
        P("fsdp", "seq", None),
        P(None, "fsdp", "seq", None),
        P(None, "fsdp", "seq", None),
        P("fsdp", None),
        P(None, ("seq", "fsdp")),
        P(None, ("seq", "fsdp"), None),
        P(None, ("seq", "fsdp"), None),
        P(None, ("seq", "fsdp"), None),
        P(None, ("seq", "fsdp"), None),
        P(None, ("seq", "fsdp")),
        P(None, ("seq", "fsdp"), None),
        P(None, "seq", "fsdp", None),
        P(None, "seq", "fsdp", None),
        P(None, "seq", "fsdp", None),
    )
    out_specs = (
        P("fsdp", "seq", None),
        P("fsdp", "seq", None),
        P(None, ("seq", "fsdp")),
        P(None, ("seq", "fsdp"), None),
        P(None, ("seq", "fsdp"), None),
        P(None, ("seq", "fsdp"), None),
        P(None, ("seq", "fsdp"), None),
        P(None, ("seq", "fsdp")),
        P(None, ("seq", "fsdp"), None),
        P(None, "seq", "fsdp", None),
        P(None, "seq", "fsdp", None),
        P(None, "seq", "fsdp", None),
    )
    return jax.shard_map(
        per_device, mesh=mesh, in_specs=in_specs, out_specs=out_specs, check_vma=False
    )
```

```python
import functools

import jax
import jax.numpy as jnp
import numpy as np
from jax import lax
from jax.experimental import pallas as pl
from jax.experimental.pallas import tpu as pltpu
from jax.sharding import PartitionSpec as P

HEADS = 12
KVHEADS = 2
HD = 128
TOPK = 4
LAYERS = 2
NCONT = 4

norm_eps = 1e-06
rope_base = 10000.0
masked_value = -1e30

bf16 = jnp.bfloat16
f32 = jnp.float32
VMEM_BYTES = 64 * 1024 * 1024 - 256 * 1024


def group_tables(segment_row, prompt_len):
    cont_len = segment_row.shape[0]
    onehot = (segment_row[:, None] == jnp.arange(NCONT, dtype=jnp.int32)[None, :]).astype(jnp.int32)
    counts = jnp.sum(onehot, axis=0)
    starts = jnp.cumsum(counts) - counts
    seg_begin = jnp.sum(onehot * starts[None, :], axis=1)
    within = jnp.arange(cont_len, dtype=jnp.int32) - seg_begin
    positions = jnp.concatenate([jnp.arange(prompt_len, dtype=jnp.int32), prompt_len + within])
    labels = jnp.concatenate([jnp.full((prompt_len,), -1, jnp.int32), segment_row])
    frequency = rope_base ** (-(jnp.arange(HD // 2, dtype=jnp.float32) * 2.0 / HD))
    angles = positions.astype(jnp.float32)[:, None] * frequency[None, :]
    return (jnp.cos(angles), jnp.sin(angles), labels)


def slot_table(routes_t, order_t, expert_count, capacity):
    pair_expert = routes_t.reshape(-1)
    pair_order = order_t.reshape(-1)
    same_expert = pair_expert[:, None] == pair_expert[None, :]
    earlier = pair_order[None, :] < pair_order[:, None]
    pair_slot = jnp.sum(jnp.logical_and(same_expert, earlier).astype(jnp.int32), axis=1)
    target = jnp.where(
        pair_slot < capacity, pair_expert * capacity + pair_slot, expert_count * capacity
    )
    return target.reshape(routes_t.shape)


def nn(left, right):
    return lax.dot_general(left, right, (((1,), (0,)), ((), ())), preferred_element_type=f32)


def nt(left, right):
    return lax.dot_general(left, right, (((1,), (1,)), ((), ())), preferred_element_type=f32)


def tn(left, right):
    return lax.dot_general(left, right, (((0,), (0,)), ((), ())), preferred_element_type=f32)


def split(value):
    high = value.astype(bf16)
    return high, (value - high.astype(f32)).astype(bf16)


class Late:
    def __init__(self, ref, copy):
        self.ref, self.copy, self.shape = ref, copy, ref.shape
        copy.start()

    def wait(self):
        if self.copy is not None:
            self.copy.wait()
            self.copy = None

    def __getitem__(self, index):
        self.wait()
        return self.ref[index]


class Out:
    def __init__(self, ref, copies):
        self.ref, self.copies, self.shape = ref, copies, ref.shape
        self.sent = [False] * len(copies)

    def send(self, piece=None):
        for n in range(len(self.copies)) if piece is None else (piece,):
            if not self.sent[n]:
                self.copies[n].start()
                self.sent[n] = True

    def __getitem__(self, index):
        return self.ref[index]

    def __setitem__(self, index, value):
        self.ref[index] = value


def cost(args, outs, flops):
    moved = sum(int(np.prod(a.shape)) * a.dtype.itemsize for a in (*args, *outs))
    return pl.CostEstimate(flops=flops, bytes_accessed=moved, transcendentals=0)


def once(kernel, outs, *args, scalar=False, cut=None, pieces=None, flops=0):
    cut, pieces = cut or {}, pieces or {}
    hbm = pl.BlockSpec(memory_space=pltpu.HBM)
    late = [n for n in range(len(args)) if not (scalar and n == 0)]
    specs = [hbm] * len(args)
    if scalar:
        specs[0] = pl.BlockSpec(memory_space=pltpu.SMEM)
    scratch = []
    for n in late:
        dims = list(args[n].shape)
        for dim, start, size in cut.get(n, ()):
            dims[dim] = size
        scratch.append(pltpu.VMEM(tuple(dims), args[n].dtype))
    scratch += [pltpu.VMEM(o.shape, o.dtype) for o in outs]
    parts = [pieces.get(n, (0, 1)) for n in range(len(outs))]
    scratch.append(pltpu.SemaphoreType.DMA((len(late) + sum(count for _, count in parts),)))

    def body(*refs):
        ins = list(refs[: len(args)])
        out_refs = refs[len(args) : len(args) + len(outs)]
        rooms = refs[len(args) + len(outs) : -1]
        sems = refs[-1]
        for i, n in enumerate(late):
            source = ins[n]
            for dim, start, size in cut.get(n, ()):
                if callable(start):
                    start = pl.multiple_of(start(ins[0][0]), 16 if dim == 1 else HD)
                source = source.at[(slice(None),) * dim + (pl.ds(start, size),)]
            ins[n] = Late(rooms[i], pltpu.make_async_copy(source, rooms[i], sems.at[i]))
        results = []
        used = len(late)
        for i, out in enumerate(out_refs):
            room = rooms[len(late) + i]
            dim, count = parts[i]
            size = room.shape[dim] // count
            copies = []
            for n in range(count):
                at = (slice(None),) * dim + (pl.ds(n * size, size),)
                copies.append(pltpu.make_async_copy(room.at[at], out.at[at], sems.at[used]))
                used += 1
            results.append(Out(room, copies))
        kernel(*ins, *results)
        for result in results:
            result.send()
        for n in late:
            ins[n].wait()
        for result in results:
            for copy in result.copies:
                copy.wait()

    return pl.pallas_call(
        body,
        out_shape=list(outs),
        in_specs=specs,
        out_specs=[hbm] * len(outs),
        scratch_shapes=scratch,
        compiler_params=pltpu.CompilerParams(vmem_limit_bytes=VMEM_BYTES),
        cost_estimate=cost(args, outs, flops),
    )(*args)


def shape(dims, dtype):
    return jax.ShapeDtypeStruct(dims, dtype)


def normalize(value, gain):
    inverse = lax.rsqrt(jnp.mean(value * value, axis=-1, keepdims=True) + norm_eps)
    return value * inverse * gain


def normalize_back(value, gain, grad):
    inverse = lax.rsqrt(jnp.mean(value * value, axis=-1, keepdims=True) + norm_eps)
    unit = value * inverse
    grad_gain = jnp.sum(grad * unit, axis=0, keepdims=True)
    scaled = grad * gain
    grad_value = inverse * (scaled - unit * jnp.mean(scaled * unit, axis=-1, keepdims=True))
    return grad_value, grad_gain


def to_gathered(parts, order):
    count = len(parts)
    share = parts[0].shape[1] // count
    done = []
    for j in range(count):
        piece = jnp.concatenate([part[:, j * share : (j + 1) * share] for part in parts], axis=1)
        done.append(nn(piece, order))
    return jnp.concatenate(done, axis=1)


def to_natural(value, order):
    count = value.shape[1] // order.shape[0]
    size = order.shape[0]
    share = size // count
    done = [nt(value[:, j * size : (j + 1) * size], order) for j in range(count)]
    return [
        jnp.concatenate([part[:, s * share : (s + 1) * share] for part in done], axis=1)
        for s in range(count)
    ]


def column_blocks(value, count):
    size = value.shape[1] // count
    return [value[:, s * size : (s + 1) * size] for s in range(count)]


def turn(block, cosines, sines):
    return block * cosines + pltpu.roll(block, HD // 2, 1) * sines


def smooth_parts(value):
    root = np.float32(np.sqrt(2.0 / np.pi))
    square = value * value
    high = jnp.tanh(root * (value + 0.044715 * value * square))
    half = 0.5 * (1.0 + high)
    slope = half + 0.5 * value * (1.0 - high * high) * root * (1.0 + 3 * 0.044715 * square)
    return value * half, slope


def choose(target_t, slots):
    place = lax.broadcasted_iota(jnp.int32, (slots, target_t.shape[1]), 0)
    total = jnp.zeros(place.shape, f32)
    for k in range(TOPK):
        total = total + jnp.where(place == target_t[k : k + 1], 1.0, 0.0)
    return total


def choose_weighted(target_t, gates_t, slots):
    place = lax.broadcasted_iota(jnp.int32, (slots, target_t.shape[1]), 0)
    total = jnp.zeros(place.shape, f32)
    for k in range(TOPK):
        total = total + jnp.where(place == target_t[k : k + 1], gates_t[k : k + 1], 0.0)
    return total


def input_kernel(
    middle, combined, gates_t, target_t, small, spread, normed_ref, hidden_ref
):
    expert_count = 8
    hidden = middle[...] + mix(combined[...], gates_t[...], target_t[...])
    hidden_ref[...] = hidden
    hidden_ref.send()
    gain = small[expert_count : expert_count + 1].astype(f32)
    normed = normalize(hidden, gain).astype(bf16)
    count = normed.shape[1] // spread.shape[0]
    normed_ref[...] = to_gathered(column_blocks(normed, count), spread[...]).astype(bf16)


def mix(combined, gates_t, target_t):
    high, low = split(choose_weighted(target_t, gates_t, combined.shape[0]))
    tokens = high.shape[1]
    both = tn(jnp.concatenate([high, low], axis=1), combined)
    return both[:tokens] + both[tokens:]


def result_kernel(middle, combined, gates_t, target_t, result_ref):
    mixture = mix(combined[...], gates_t[...], target_t[...])
    result_ref[...] = (middle[...] + mixture).astype(bf16)


def attend(rows, weight, cosines, sines, bias_ref, heads_ref, out_ref):
    seq_count, tokens, columns = heads_ref.shape
    group = seq_count * tokens
    local = columns // HD - 2
    prompt = group // 2
    raw = nn(rows, weight)
    heads = []
    for j in range(local + 2):
        block = raw[:, j * HD : (j + 1) * HD]
        if j <= local:
            block = turn(block, cosines, sines)
        heads.append(block.astype(bf16))
        heads_ref[:, :, j * HD : (j + 1) * HD] = heads[j].reshape(seq_count, tokens, HD)
    heads_ref.send()
    key, value = heads[local], heads[local + 1]
    scale = HD ** (-0.5)
    for j in range(local):
        query = heads[j]
        for rows, seen in ((slice(0, prompt), prompt), (slice(prompt, group), group)):
            scores = nt(query[rows], key[:seen]) * scale + bias_ref[rows, :seen]
            peak = jnp.max(scores, axis=-1, keepdims=True)
            weights = jnp.exp(scores - peak)
            weights = weights / jnp.sum(weights, axis=-1, keepdims=True)
            part = nn(weights.astype(bf16), value[:seen]).astype(bf16)
            first = rows.start // tokens
            out_ref[first : first + prompt // tokens, :, j * HD : (j + 1) * HD] = part.reshape(
                prompt // tokens, tokens, HD
            )


def first_attention_kernel(
    place, own, one, two, three, weight, spread, cosines, sines, bias_ref,
    heads_ref, out_ref, normed_ref, small_ref,
):
    expert_count = 8
    me = place[0]
    seq_count, tokens, width = normed_ref.shape
    columns = heads_ref.shape[2]
    count = small_ref.shape[1]
    extras = weight[:, columns:].astype(f32).T.astype(bf16)
    extras = jnp.concatenate([extras[:count], extras[HD : HD + count]], axis=0)
    small = jnp.concatenate(to_natural(extras, spread[...]), axis=1)
    small_ref[0] = small[:count].astype(bf16)
    small_ref[1] = small[count:].astype(bf16)
    small_ref.send()
    gain = small[expert_count : expert_count + 1]
    for k, block in enumerate((own, one, two, three)):
        normed = normalize(block[...].astype(f32), gain).astype(bf16)
        normed = to_gathered(column_blocks(normed, seq_count), spread[...]).astype(bf16)
        normed_ref[lax.rem(me + k, seq_count)] = normed
    normed_ref.send()
    rows = normed_ref[...].reshape(seq_count * tokens, width)
    attend(rows, weight[:, :columns], cosines[...], sines[...], bias_ref, heads_ref, out_ref)


def next_attention_kernel(
    place, own, one, two, three, weight, cosines, sines, bias_ref, heads_ref, out_ref, normed_ref
):
    me = place[0]
    seq_count, tokens, width = normed_ref.shape
    weight = weight[...].reshape(width, weight.shape[2])[:, : heads_ref.shape[2]]
    for k, block in enumerate((own, one, two, three)):
        normed_ref[lax.rem(me + k, seq_count)] = block[...]
    normed_ref.send()
    rows = normed_ref[...].reshape(seq_count * tokens, width)
    attend(rows, weight, cosines[...], sines[...], bias_ref, heads_ref, out_ref)


def gates_of(logits, routes_t, rows):
    expert_count = 8
    tokens = logits.shape[1]
    chosen = []
    for k in range(TOPK):
        route = routes_t[k : k + 1]
        value = jnp.zeros((1, tokens), f32)
        for e in range(expert_count):
            value = value + jnp.where(route == e, logits[e : e + 1], 0.0)
        chosen.append(value)
    peak = functools.reduce(jnp.maximum, chosen)
    powers = [jnp.exp(value - peak) for value in chosen]
    total = functools.reduce(jnp.add, powers)
    gates = [power / total for power in powers]
    return jnp.concatenate(gates + [jnp.zeros((rows - TOPK, tokens), f32)], axis=0)


def after_attention_kernel(
    back, spread, hidden, small, out_w, routes_t, middle_ref, normed_ref, gates_ref, attended_ref
):
    expert_count = 8
    seq_count, tokens, part = back.shape
    width = seq_count * part
    attended = to_gathered([back[s] for s in range(seq_count)], spread[...]).astype(bf16)
    attended_ref[...] = attended
    attended_ref.send()
    rows = out_w.shape[1] // 2
    half = out_w.shape[2]
    for side in range(2):
        weight = out_w[:, side * rows : (side + 1) * rows].reshape(width, half)
        cols = slice(side * half, (side + 1) * half)
        middle_ref[:, cols] = hidden[:, cols].astype(f32) + nn(attended, weight)
    middle_ref.send()
    middle = middle_ref[...]
    gain = small[expert_count + 1 : expert_count + 2].astype(f32)
    normed = normalize(middle, gain).astype(bf16)
    normed_ref[...] = normed
    normed_ref.send()
    gates_ref[...] = gates_of(nt(small[...], normed), routes_t[...], gates_ref.shape[0])


def down_parts(block):
    shards, rows, half = block.shape
    wide = block.astype(f32)
    left = wide[:, : rows // 2].reshape(shards * rows // 2, half).astype(bf16)
    right = wide[:, rows // 2 :].reshape(shards * rows // 2, half).astype(bf16)
    return left, right


def expert_kernel(place, own, one, two, three, targets, routes, small, *rest):
    me = place[0]
    blocks = (own, one, two, three)
    out_ref, rows_ref, gate_ref, up_ref, gates_ref = rest[-5:]
    weights = rest[:-5]
    sources, experts, capacity, width = out_ref.shape
    half = width // 2
    for e in range(experts):
        gate_w, up_w, down_w = weights[3 * e : 3 * e + 3]
        first = (me * experts + e) * capacity
        parts = []
        for k, block in enumerate(blocks):
            hot = choose(targets[lax.rem(me + k, sources)] - first, capacity)
            parts.append(nn(hot.astype(bf16), block[...]))
        tokens = jnp.concatenate(parts, axis=0).astype(bf16)
        rows_ref[e] = tokens
        rows_ref.send(e)
        gate_val = nn(tokens, gate_w[...].reshape(width, half))
        gate_ref[e] = gate_val.astype(bf16)
        gate_ref.send(e)
        up_val = nn(tokens, up_w[...].reshape(width, half))
        up_ref[e] = up_val.astype(bf16)
        up_ref.send(e)
        activated, slope = smooth_parts(gate_val)
        inner = (activated * up_val).astype(bf16)
        for side, part in enumerate(down_parts(down_w[...])):
            done = nn(inner, part).astype(bf16)
            for k in range(sources):
                out_ref[lax.rem(me + k, sources), e, :, side * half : (side + 1) * half] = done[
                    k * capacity : (k + 1) * capacity
                ]
        out_ref.send(e)
    for k, block in enumerate(blocks):
        logits = nt(small[...], block[...])
        gates_ref[k] = gates_of(logits, routes[lax.rem(me + k, sources)], gates_ref.shape[1])


def logits_grad_kernel(grad, combined, gates_t, routes_t, target_t, logits_ref):
    tokens = grad.shape[0]
    slots = combined.shape[0]
    high, low = split(grad[...])
    products = nt(combined[...], jnp.concatenate([high, low], axis=0))
    products = products[:, :tokens] + products[:, tokens:]
    place = lax.broadcasted_iota(jnp.int32, (slots, tokens), 0)
    grad_gates = [
        jnp.sum(jnp.where(place == target_t[k : k + 1], products, 0.0), axis=0, keepdims=True)
        for k in range(TOPK)
    ]
    gates = [gates_t[k : k + 1] for k in range(TOPK)]
    center = functools.reduce(jnp.add, [a * b for a, b in zip(gates, grad_gates)])
    label = lax.broadcasted_iota(jnp.int32, logits_ref.shape, 0)
    total = jnp.zeros(logits_ref.shape, f32)
    for k in range(TOPK):
        choice = gates[k] * (grad_gates[k] - center)
        total = total + jnp.where(label == routes_t[k : k + 1], choice, 0.0)
    logits_ref[...] = total.astype(bf16)


def expert_back_kernel(
    place, own, one, two, three, targets, gates, down_first, gate_ref, up_ref, *rest
):
    me = place[0]
    blocks = (own, one, two, three)
    out_ref, keep_ref = rest[-2:]
    weights = (down_first,) + rest[:-2]
    sources, experts, capacity, width = out_ref.shape
    half = width // 2
    for e in range(experts):
        down_w, gate_w, up_w = weights[3 * e : 3 * e + 3]
        shards, rows, _ = gate_w.shape
        first = (me * experts + e) * capacity
        parts = []
        for k, block in enumerate(blocks):
            target = targets[lax.rem(me + k, sources)] - first
            hot = jnp.concatenate(split(choose_weighted(target, gates[k], capacity)), axis=1)
            twice = jnp.concatenate([block[...], block[...]], axis=0)
            parts.append(nn(hot, twice))
        grad = jnp.concatenate(parts, axis=0).astype(bf16)
        keep_ref[e, :, :width] = grad
        left, right = down_parts(down_w[...])
        grad_inner = nt(grad[:, :half], left) + nt(grad[:, half:], right)
        up_val = up_ref[e].astype(f32)
        activated, slope = smooth_parts(gate_ref[e].astype(f32))
        gate_at, up_at, inner_at = (slice(width + n * half, width + (n + 1) * half) for n in range(3))
        keep_ref[e, :, gate_at] = (grad_inner * up_val * slope).astype(bf16)
        keep_ref[e, :, up_at] = (grad_inner * activated).astype(bf16)
        keep_ref[e, :, inner_at] = (activated * up_val).astype(bf16)
        keep_ref.send(e)
        parts = 4
        some, size = shards // parts, shards * rows // parts
        for c in range(parts):
            at = slice(c * some, (c + 1) * some)
            total = nt(keep_ref[e, :, gate_at], gate_w[at].reshape(size, half))
            total = total + nt(keep_ref[e, :, up_at], up_w[at].reshape(size, half))
            total = total.astype(bf16)
            for k in range(sources):
                out_ref[lax.rem(me + k, sources), e, :, c * size : (c + 1) * size] = total[
                    k * capacity : (k + 1) * capacity
                ]
        out_ref.send(e)


def pick_kernel(rows, other_rows, attended, other_attended, pick, out_ref, attended_ref):
    count = rows.shape[1]
    for e in range(rows.shape[0]):
        out_ref[e, :count] = nn(rows[e], pick[...]).astype(bf16)
        out_ref[e, count:] = nn(other_rows[e], pick[...]).astype(bf16)
        out_ref.send(e)
    both = jnp.concatenate([attended[...], other_attended[...]], axis=0)
    attended_ref[...] = nn(both, pick[...]).astype(bf16)


def expert_weight_kernel(core, tokens, pick_inner, keep, other_keep, *rest):
    pack_ref = rest[-1]
    chips, _, half = pack_ref.shape
    experts = tokens.shape[0]
    width = 2 * tokens.shape[2]
    count = width // (2 * chips)
    at = 0

    def send():
        for piece in range(at // 16, (at + count) // 16):
            pack_ref.send(piece)

    for e in range(experts):
        grads = jnp.concatenate([keep[e], other_keep[e]], axis=0)
        both = tn(tokens[e], grads[:, width : width + 2 * half]).astype(bf16)
        for n in range(2):
            block = both[:, n * half : (n + 1) * half].reshape(chips, count, half)
            pack_ref[:, at : at + count] = block
            send()
            at += count
        inner = nn(grads[:, width + 2 * half :], pick_inner[...]).astype(bf16)
        down = tn(inner, grads[:, :width])
        left = down[:, :half].reshape(chips, count // 2, half)
        right = down[:, half:].reshape(chips, count // 2, half)
        pack_ref[:, at : at + count] = jnp.concatenate([left, right], axis=1).astype(bf16)
        send()
        at += count
    if len(rest) > 1:
        dense_part(core[0], rest[:-1], pack_ref, at)


def dense_kernel(core, *refs):
    dense_part(core[0], refs[:-1], refs[-1], 0)


def dense_part(core, refs, pack_ref, at):
    qkv, other_qkv, gain, other_gain, spread, attended, branch, other_branch = refs
    expert_count = 8
    chips, rows, half = qkv.shape
    width = gain.shape[1]
    blocks = column_blocks((gain[...] + other_gain[...]).astype(bf16), width // spread.shape[0])
    gains = to_gathered(blocks, spread[...])
    count = gains.shape[0]
    gains = jnp.where(lax.broadcasted_iota(jnp.int32, gains.shape, 0) == 0, gains, 0.0)
    below = jnp.zeros((HD - expert_count - count, width), f32)
    gains = jnp.concatenate([jnp.zeros((expert_count, width), f32), gains, below], axis=0).T
    gains = gains.reshape(chips, 2, rows, HD)
    gains = jnp.where(core == 0, gains[:, 0], gains[:, 1])
    total = qkv[...].astype(f32) + other_qkv[...].astype(f32)
    pack_ref[:, at : at + rows, : half - HD] = total[:, :, : half - HD].astype(bf16)
    pack_ref[:, at : at + rows, half - HD :] = (total[:, :, half - HD :] + gains).astype(bf16)
    grads = jnp.concatenate([branch[...], other_branch[...]], axis=0)
    total = tn(attended[...], grads).astype(bf16)
    for side in range(2):
        at += rows
        block = total[:, side * half : (side + 1) * half]
        pack_ref[:, at : at + rows] = block.reshape(chips, rows, half)


def keep_shards(own_ref, other_ref, core, at, value):
    shards, rows, columns = value.shape
    value = value.reshape(shards // 2, 2, rows, columns)
    own_ref[:, at : at + rows] = jnp.where(core == 0, value[:, 0], value[:, 1])
    other_ref[:, at : at + rows] = jnp.where(core == 0, value[:, 1], value[:, 0])


def after_experts_kernel(
    grad, sent, middle, normed, logits_grad, target_t, small, out_w, spread,
    grad_ref, branch_ref, send_ref, small_ref,
):
    expert_count = 8
    seq_count, tokens, part = send_ref.shape
    width = seq_count * part
    chosen = choose(target_t[...], sent.shape[0]).astype(bf16)
    grad_normed = tn(chosen, sent[...]) + tn(logits_grad[...], small[...])
    router = nn(logits_grad[...], normed[...])
    gain = small[expert_count + 1 : expert_count + 2].astype(f32)
    grad_value, grad_gain = normalize_back(middle[...], gain, grad_normed)
    label = lax.broadcasted_iota(jnp.int32, small_ref.shape, 0)
    small_ref[...] = jnp.where(label == expert_count + 1, grad_gain, router)
    grad_middle = grad[...] + grad_value
    grad_ref[...] = grad_middle
    grad_ref.send()
    branch = grad_middle.astype(bf16)
    branch_ref[...] = branch
    branch_ref.send()
    rows = out_w.shape[1] // 2
    half = out_w.shape[2]
    parts = [
        nt(branch[:, :half], out_w[:, :rows].reshape(width, half)),
        nt(branch[:, half:], out_w[:, rows:].reshape(width, half)),
    ]
    attended = (parts[0] + parts[1]).astype(bf16)
    for s, block in enumerate(to_natural(attended, spread[...])):
        send_ref[s] = block.astype(bf16)


def attention_back_kernel(heads_ref, grad_ref, bias_ref, cosines, sines, out_ref):
    seq_count, tokens, columns = heads_ref.shape
    group = seq_count * tokens
    heads = heads_ref[...].reshape(group, columns)
    grads = grad_ref[...].reshape(group, grad_ref.shape[2])
    local = columns // HD - 2
    prompt = group // 2
    key = heads[:, local * HD : (local + 1) * HD]
    value = heads[:, (local + 1) * HD :]
    scale = HD ** (-0.5)

    def keep(at, block):
        out_ref[:, :, at * HD : (at + 1) * HD] = block.astype(bf16).reshape(seq_count, tokens, HD)

    cosines, sines = cosines[...], sines[...]

    def unturn(block):
        return block * cosines - pltpu.roll(block, HD // 2, 1) * sines

    grad_key = [jnp.zeros((prompt, HD), f32), jnp.zeros((prompt, HD), f32)]
    grad_value = [jnp.zeros((prompt, HD), f32), jnp.zeros((prompt, HD), f32)]
    for j in range(local):
        query = heads[:, j * HD : (j + 1) * HD]
        grad = grads[:, j * HD : (j + 1) * HD]
        grad_query = []
        for rows, seen in ((slice(0, prompt), prompt), (slice(prompt, group), group)):
            scores = nt(query[rows], key[:seen]) * scale + bias_ref[rows, :seen]
            peak = jnp.max(scores, axis=-1, keepdims=True)
            weights = jnp.exp(scores - peak)
            weights = weights / jnp.sum(weights, axis=-1, keepdims=True)
            grad_weights = nt(grad[rows], value[:seen])
            center = jnp.sum(weights * grad_weights, axis=-1, keepdims=True)
            grad_scores = (weights * (grad_weights - center)).astype(bf16)
            low = weights.astype(bf16)
            grad_query.append(nn(grad_scores, key[:seen]) * scale)
            for side in range(seen // prompt):
                cols = slice(side * prompt, (side + 1) * prompt)
                grad_key[side] = grad_key[side] + tn(grad_scores[:, cols], query[rows])
                grad_value[side] = grad_value[side] + tn(low[:, cols], grad[rows])
        keep(j, unturn(jnp.concatenate(grad_query, axis=0)))
    keep(local, unturn(jnp.concatenate(grad_key, axis=0) * scale))
    keep(local + 1, jnp.concatenate(grad_value, axis=0))


def before_attention_kernel(
    sent, left_w, right_w, kv_w, spread, small, hidden, grad_middle, out_ref, low_ref, gain_ref
):
    expert_count = 8
    seq_count, tokens, columns = sent.shape
    local = columns // HD - 2
    share = seq_count // KVHEADS
    blocks = [sent[s, :, : local * HD] for s in range(seq_count)]
    for at in (local, local + 1):
        for c in range(KVHEADS):
            total = jnp.zeros((tokens, HD), f32)
            for s in range(c * share, (c + 1) * share):
                total = total + sent[s, :, at * HD : (at + 1) * HD].astype(f32)
            blocks.append(total.astype(bf16))
    raw = jnp.concatenate(blocks, axis=1)
    at, total = 0, 0.0
    for part in (left_w, right_w, kv_w):
        shards, rows, columns = part.shape
        weight = part[...].reshape(shards * rows, columns)
        total = total + nt(raw[:, at : at + columns], weight)
        at += columns
    high, low = split(total)
    both = to_natural(jnp.concatenate([high, low], axis=0), spread[...])
    both = jnp.concatenate(both, axis=1)
    grad_normed = both[:tokens] + both[tokens:]
    gain = small[expert_count : expert_count + 1].astype(f32)
    grad_value, grad_gain = normalize_back(hidden[...].astype(f32), gain, grad_normed)
    total = grad_middle[...] + grad_value
    low_ref[...] = total.astype(bf16)
    low_ref.send()
    out_ref[...] = total
    out_ref.send()
    gain_ref[...] = jnp.broadcast_to(grad_gain, gain_ref.shape)


def qkv_weight_kernel(core, normed, grads, small, spread, own_ref, other_ref):
    seq_count, tokens, columns = grads.shape
    chips, rows, wide = own_ref.shape
    shards = 2 * chips
    inputs = normed[...].reshape(seq_count * tokens, normed.shape[2])
    total = tn(inputs, grads[...].reshape(seq_count * tokens, columns))
    extra = column_blocks(small[...].astype(bf16), seq_count)
    extra = to_gathered(extra, spread[...])
    extra = jnp.concatenate([extra, jnp.zeros((HD - extra.shape[0], extra.shape[1]), f32)], axis=0).T
    total = jnp.concatenate([total, extra], axis=1).astype(bf16).reshape(shards, rows, wide)
    keep_shards(own_ref, other_ref, core[0], 0, total)


def expert_grads_kernel(*refs):
    sums, (gate_ref, up_ref, down_ref) = refs[:LAYERS], refs[LAYERS:]
    rows = gate_ref.shape[2]
    half = gate_ref.shape[3]
    for layer in range(LAYERS):
        block = sums[layer][...].astype(f32)
        for e in range(gate_ref.shape[1]):
            at = 3 * rows * e
            gate_ref[layer, e] = block[at : at + rows]
            up_ref[layer, e] = block[at + rows : at + 2 * rows]
            at += 2 * rows
            down_ref[layer, e, :, :half] = block[at : at + rows // 2]
            down_ref[layer, e, :, half:] = block[at + rows // 2 : at + rows]


def arrange_kernel(first, above, out_ref):
    seq_count, blocks, padded, half = out_ref.shape
    parts = blocks // LAYERS
    rows = first.shape[0] // (parts * seq_count)
    below = jnp.zeros((padded - rows, half), f32)
    for layer, ref in enumerate((first, above)):
        total = ref[...].astype(f32)
        for part in range(parts):
            for s in range(seq_count):
                at = (part * seq_count + s) * rows
                block = jnp.concatenate([total[at : at + rows], below], axis=0)
                out_ref[s, layer * parts + part] = block.astype(bf16)


def dense_grads_kernel(
    blocks, query_ref, key_ref, value_ref, out_ref, router_ref, gain_attn_ref, gain_ffn_ref
):
    seq_count, count, _, columns = blocks.shape
    parts = count // LAYERS
    rows, expert_count = query_ref.shape[0], router_ref.shape[1]
    local = columns - 3 * HD
    share = seq_count // KVHEADS
    for layer in range(LAYERS):
        whole = [blocks[s, layer * parts].astype(f32) for s in range(seq_count)]
        for s in range(seq_count):
            query_ref[:, layer, s * local : (s + 1) * local] = whole[s][:rows, :local]
        for c in range(KVHEADS):
            total = functools.reduce(jnp.add, whole[c * share : (c + 1) * share])[:rows]
            key_ref[:, layer, c * HD : (c + 1) * HD] = total[:, local : local + HD]
            value_ref[:, layer, c * HD : (c + 1) * HD] = total[:, local + HD : local + 2 * HD]
        small = functools.reduce(jnp.add, [block[:, local + 2 * HD :] for block in whole]).T
        router_ref[layer] = small[:expert_count, :rows]
        gain_attn_ref[layer : layer + 1] = small[expert_count : expert_count + 1, :rows]
        gain_ffn_ref[layer : layer + 1] = small[expert_count + 1 : expert_count + 2, :rows]
        for side in range(2):
            sides = [blocks[s, layer * parts + 1 + side].astype(f32) for s in range(seq_count)]
            total = functools.reduce(jnp.add, sides)[:rows]
            out_ref[:, layer, side * columns : (side + 1) * columns] = total


def swap_seq(block):
    return lax.all_to_all(block, "seq", split_axis=0, concat_axis=0, tiled=True)


def around_seq(block):
    count = lax.axis_size("seq")
    others = [
        lax.ppermute(block, "seq", [((i + k) % count, i) for i in range(count)])
        for k in range(1, count)
    ]
    return [block] + others


def halves(block):
    cut = block.shape[-1] // 2
    return jnp.concatenate([block[..., :cut], block[..., cut:]], axis=-2)


def per_device(
    tokens_in,
    cotangent,
    routes,
    order,
    segment_ids,
    gain_attn,
    w_query,
    w_key,
    w_value,
    w_out,
    gain_ffn,
    w_router,
    w_gate,
    w_up,
    w_down,
):
    tok_count = tokens_in.shape[1]
    width = tokens_in.shape[2]
    seq_count = lax.axis_size("seq")
    shard_count = lax.axis_size("fsdp")
    seq_index = lax.axis_index("seq")
    core = lax.rem(lax.axis_index("fsdp"), 2)
    place = jnp.full((1,), seq_index, jnp.int32)
    core_place = jnp.full((1,), core, jnp.int32)
    group_tok = seq_count * tok_count
    prompt_len = group_tok - segment_ids.shape[1]
    local_experts = w_gate.shape[1]
    expert_count = local_experts * seq_count
    capacity = 9 * tok_count * TOPK // (8 * expert_count)
    total_slots = expert_count * capacity
    head_local = HEADS // seq_count
    local_width = head_local * HD
    dense_rows = w_query.shape[1]
    shard_rows = dense_rows * seq_count
    gate_rows = w_gate.shape[2]
    down_rows = w_down.shape[2]
    expert_rows = 2 * gate_rows + 2 * down_rows
    qkv_width = (HEADS + 2 * KVHEADS) * HD
    half_width = width // 2
    inner_width = w_gate.shape[3]
    slot_rows = seq_count * capacity

    cos_half, sin_half, labels = group_tables(segment_ids[0], prompt_len)
    cos_all = jnp.concatenate([cos_half, cos_half], axis=1)
    sin_all = jnp.concatenate([-sin_half, sin_half], axis=1)
    cos_own = lax.dynamic_slice_in_dim(cos_all, seq_index * tok_count, tok_count, 0)
    sin_own = lax.dynamic_slice_in_dim(sin_all, seq_index * tok_count, tok_count, 0)
    key_pos = jnp.arange(group_tok, dtype=jnp.int32)
    allowed = jnp.logical_and(
        key_pos[None, :] <= key_pos[:, None],
        jnp.logical_or(key_pos[None, :] < prompt_len, labels[None, :] == labels[:, None]),
    )
    bias = jnp.where(allowed, 0.0, masked_value)

    column = jnp.arange(width // seq_count, dtype=jnp.int32)
    natural = (
        column % shard_rows // dense_rows * (width // seq_count // seq_count)
        + column // shard_rows * dense_rows
        + column % dense_rows
    )
    spread = (column[:, None] == natural[None, :]).astype(bf16)

    def small_rows_of(layer):
        return jnp.concatenate(
            [
                w_router[layer],
                gain_attn[layer][:, None],
                gain_ffn[layer][:, None],
                jnp.zeros((dense_rows, HD - 2 - expert_count), bf16),
            ],
            axis=1,
        )

    def dense_rows_of(layer):
        return jnp.concatenate(
            [w_query[layer], w_key[layer], w_value[layer], small_rows_of(layer), w_out[layer]],
            axis=1,
        )

    def shards_of_core(count):
        rows = count // shard_count
        wanted = jnp.arange(count // 2, dtype=jnp.int32)
        wanted = (wanted // rows * 2 + core) * rows + wanted % rows
        return (jnp.arange(count, dtype=jnp.int32)[:, None] == wanted[None, :]).astype(bf16)

    picks = (shards_of_core(width), shards_of_core(inner_width))

    def spread_seq(dense):
        dense = swap_seq(jnp.broadcast_to(dense[None], (seq_count,) + dense.shape))
        return dense.reshape(shard_rows, dense.shape[2])

    def own_columns(weight):
        pick = seq_index * KVHEADS // seq_count
        starts = (seq_index * local_width, (HEADS + pick) * HD, (HEADS + KVHEADS + pick) * HD)
        parts = [
            lax.dynamic_slice_in_dim(weight, start, size, 1)
            for start, size in zip(starts, (local_width, HD, HD))
        ]
        return jnp.concatenate(parts + [weight[:, qkv_width : qkv_width + HD]], axis=1)

    def expert_part(layer):
        return [
            part
            for e in range(local_experts)
            for part in (w_gate[layer, e], w_up[layer, e], halves(w_down[layer, e]))
        ]

    def out_part(dense):
        return [halves(dense[:, qkv_width + HD :])]

    def qkv_part(dense):
        wide = jnp.concatenate(
            [dense[:, : qkv_width + HD], jnp.zeros((shard_rows, HD), bf16)], axis=1
        )
        return [wide[:, at : at + half_width] for at in range(0, wide.shape[1], half_width)]

    def fetch(parts):
        return lax.all_gather(jnp.concatenate(parts, axis=0), "fsdp", axis=0, tiled=False)

    chips = [[i + c for i in range(0, shard_count, 2)] for c in range(2)]

    def swap_chips(block):
        return lax.all_to_all(
            block, "fsdp", split_axis=0, concat_axis=0, tiled=True, axis_index_groups=chips
        )

    def swap_cores(block):
        return lax.ppermute(block, "fsdp", [(i, i ^ 1) for i in range(shard_count)])

    def both_cores(block):
        other = swap_cores(block)
        first = jnp.where(core == 0, block, other)
        second = jnp.where(core == 0, other, block)
        return jnp.stack([first, second], axis=1).reshape((shard_count,) + block.shape[1:])

    def to_chips(block):
        return swap_chips(jnp.broadcast_to(block[None], (shard_count // 2,) + block.shape))

    weight_parts = [
        (e * expert_rows + k * gate_rows, gate_rows) for e in range(local_experts) for k in range(3)
    ]
    back_parts = [weight_parts[3 * e + k] for e in range(local_experts) for k in (2, 0, 1)]
    out_cut = ((1, local_experts * expert_rows, 2 * shard_rows),)

    slots_shape = shape((seq_count, local_experts, capacity, width), bf16)
    inner_shape = (local_experts, slot_rows, inner_width)
    expert_flops = 6 * total_slots * width * inner_width
    dense_flops = 2 * tok_count * width * width
    records = []
    hidden = tokens_in[0]
    dense = spread_seq(jnp.concatenate([dense_rows_of(0), dense_rows_of(1)], axis=1))
    dense, next_dense = jnp.split(dense, 2, axis=1)
    next_small = next_dense[:, qkv_width : qkv_width + HD]
    columns = jnp.concatenate([own_columns(dense), next_small], axis=1)
    both_rows = jnp.concatenate([hidden, cotangent[0]], axis=0)
    columns, both_rows = lax.optimization_barrier((columns, both_rows))
    both_blocks = around_seq(both_rows)
    packs = [fetch(expert_part(0) + out_part(dense)), None]
    columns = to_chips(columns)
    pairs = jnp.concatenate(
        [array[layer, 0].T for array in (routes, order) for layer in range(LAYERS)], axis=0
    )
    pairs = swap_seq(jnp.broadcast_to(pairs[None], (seq_count,) + pairs.shape))
    pairs = pairs.reshape(seq_count, 2, LAYERS, TOPK, tok_count)
    slots_of = functools.partial(slot_table, expert_count=expert_count, capacity=capacity)
    all_routes = [pairs[:, 0, layer] for layer in range(LAYERS)]
    all_targets = [
        jax.vmap(slots_of)(pairs[:, 0, layer], pairs[:, 1, layer]) for layer in range(LAYERS)
    ]
    targets = [lax.dynamic_index_in_dim(t, seq_index, 0, False) for t in all_targets]
    routes_ts = [lax.dynamic_index_in_dim(t, seq_index, 0, False) for t in all_routes]
    early = (both_blocks, all_targets, all_routes, targets, routes_ts)
    early = early + (cos_all, sin_all, bias, spread, picks)
    columns, early = lax.optimization_barrier((columns, early))
    both_blocks, all_targets, all_routes, targets, routes_ts = early[:5]
    cos_all, sin_all, bias, spread, picks = early[5:]
    first_columns = both_cores(columns).reshape(width, columns.shape[2])
    grad_blocks, grad_cut = both_blocks, ((0, tok_count, tok_count),)
    own_at = local_experts * expert_rows + 2 * shard_rows
    heads_shape = shape((seq_count, tok_count, local_width + 2 * HD), bf16)
    attended_shape = shape((seq_count, tok_count, local_width), bf16)
    normed_shape = shape((seq_count, tok_count, width), bf16)
    small_shape = shape((LAYERS, 2 * expert_count, width), bf16)
    attention_flops = 4 * head_local * group_tok * group_tok * HD + 2 * dense_flops
    for layer in range(LAYERS):
        pack, routes_t, target_t = packs[layer], routes_ts[layer], targets[layer]
        if layer == 0:
            heads, attended, normed_all, smalls = once(
                first_attention_kernel,
                [heads_shape, attended_shape, normed_shape, small_shape],
                place, *both_blocks, first_columns, spread, cos_all, sin_all, bias,
                scalar=True, cut={n: ((0, 0, tok_count),) for n in range(1, 5)}, flops=attention_flops + 4 * dense_flops,
            )
            small = smalls[layer]
        else:
            small = smalls[layer]
            normed_p, hidden = once(
                input_kernel,
                [shape((tok_count, width), bf16), shape((tok_count, width), f32)],
                middle, combined, gates_t, above_target, small, spread, flops=2 * dense_flops,
            )
            heads, attended, normed_all = once(
                next_attention_kernel,
                [heads_shape, attended_shape, normed_shape],
                place, *around_seq(normed_p), pack, cos_all, sin_all, bias,
                scalar=True, cut={5: ((1, own_at, shard_rows),)}, flops=attention_flops,
            )
        if layer == 0:
            back = swap_seq(attended)
            next_parts = expert_part(1) + out_part(next_dense) + [own_columns(next_dense)]
            next_parts = jnp.concatenate(next_parts, axis=0)
            pack, next_parts, back = lax.optimization_barrier((pack, next_parts, back))
            packs = [pack, fetch([next_parts])]
        else:
            back = swap_seq(attended)
            qkv_parts = jnp.concatenate(qkv_part(dense) + qkv_part(next_dense), axis=0)
            qkv_parts, back = lax.optimization_barrier((qkv_parts, back))
            qkv_w = fetch([qkv_parts])
        middle, normed_ffn, gates_t, attended_p = once(
            after_attention_kernel,
            [
                shape((tok_count, width), f32),
                shape((tok_count, width), bf16),
                shape((2 * TOPK, tok_count), f32),
                shape((tok_count, width), bf16),
            ],
            back, spread, hidden, small, pack, routes_t,
            cut={4: out_cut}, flops=3 * dense_flops,
        )
        expert_out, received, gate_val, up_val, all_gates = once(
            expert_kernel,
            [
                slots_shape,
                shape((local_experts, slot_rows, width), bf16),
                shape(inner_shape, bf16),
                shape(inner_shape, bf16),
                shape((seq_count, 2 * TOPK, tok_count), f32),
            ],
            place, *around_seq(normed_ffn), all_targets[layer], all_routes[layer], small,
            *[pack] * len(weight_parts),
            scalar=True,
            cut={n + 8: ((1, *part),) for n, part in enumerate(weight_parts)},
            pieces={n: (1 if n == 0 else 0, local_experts) for n in range(4)},
            flops=expert_flops,
        )
        picked = once(
            pick_kernel,
            [
                shape((local_experts, 2 * slot_rows, width // 2), bf16),
                shape((2 * tok_count, width // 2), bf16),
            ],
            received, swap_cores(received), attended_p, swap_cores(attended_p), picks[0],
            pieces={0: (0, local_experts)}, flops=expert_flops // 3,
        )
        combined, picked = lax.optimization_barrier(
            (swap_seq(expert_out).reshape(total_slots, width), picked)
        )
        above_target = target_t
        records.append(
            (
                (pack, small, routes_t, target_t),
                (hidden, normed_all, heads),
                (middle, normed_ffn, gates_t, combined),
                (picked, gate_val, up_val, all_gates),
            )
        )
    (result,) = once(
        result_kernel, [shape((tok_count, width), bf16)], middle, combined, gates_t, target_t,
        flops=dense_flops,
    )

    grad_hidden = cotangent[0].astype(f32)
    sums = [None] * LAYERS
    waiting = None
    for layer in range(LAYERS - 1, -1, -1):
        weights, attn_saved, mid_saved, expert_saved = records[layer]
        pack, small, routes_t, target_t = weights
        row = layer * 3 * shard_rows
        below, normed_all, heads = attn_saved
        middle, normed_ffn, gates_t, combined = mid_saved
        picked, gate_val, up_val, all_gates = expert_saved
        if waiting is None:
            tied = lax.optimization_barrier((grad_blocks, qkv_w, result, combined))
            grad_blocks, qkv_w, result, combined = tied
        else:
            grad_blocks, waiting = lax.optimization_barrier((grad_blocks, waiting))
        grad_rows, kept = once(
            expert_back_kernel,
            [slots_shape, shape((local_experts, slot_rows, width + 3 * inner_width), bf16)],
            place, *grad_blocks, all_targets[layer], all_gates, pack, gate_val, up_val,
            *[pack] * (len(back_parts) - 1),
            scalar=True,
            cut={n + 9 if n else 7: ((1, *part),) for n, part in enumerate(back_parts)}
            | {n: grad_cut for n in range(1, 5)},
            pieces={0: (1, local_experts), 1: (0, local_experts)},
            flops=expert_flops,
        )
        (logits_grad,) = once(
            logits_grad_kernel,
            [shape((2 * expert_count, tok_count), bf16)],
            grad_hidden, combined, gates_t, routes_t, target_t, flops=3 * dense_flops,
        )
        sent = swap_seq(grad_rows)
        extra = () if layer == LAYERS - 1 else waiting
        pack_rows = local_experts * expert_rows + (3 * shard_rows if extra else 0)
        (packed,) = once(
            expert_weight_kernel,
            [shape((shard_count // 2, pack_rows, half_width), bf16)],
            core_place, picked[0], picks[1], kept, swap_cores(kept), *extra,
            scalar=True, pieces={0: (1, pack_rows // 16)}, flops=2 * expert_flops,
        )
        sent, packed, logits_grad = lax.optimization_barrier((sent, packed, logits_grad))
        if layer < LAYERS - 1:
            packed, sums[layer + 1] = lax.optimization_barrier((packed, sums[layer + 1]))
        summed = lax.psum_scatter(
            packed.reshape(-1, half_width), "fsdp", scatter_dimension=0, tiled=True,
            axis_index_groups=chips,
        )
        grad_middle, branch, send, small_grad = once(
            after_experts_kernel,
            [
                shape((tok_count, width), f32),
                shape((tok_count, width), bf16),
                shape((seq_count, tok_count, local_width), bf16),
                shape((2 * expert_count, width), f32),
            ],
            grad_hidden, sent.reshape(total_slots, width), middle, normed_ffn, logits_grad,
            target_t, small, pack, spread,
            cut={7: out_cut}, flops=4 * dense_flops,
        )
        grad_heads = swap_seq(send)
        (grad_own,) = once(
            attention_back_kernel,
            [shape((seq_count, tok_count, local_width + 2 * HD), bf16)],
            heads, grad_heads, bias, cos_all, sin_all,
            flops=10 * head_local * group_tok * group_tok * HD,
        )
        qkv_block_grad = once(
            qkv_weight_kernel,
            [shape((shard_count // 2, shard_rows, half_width), bf16)] * 2,
            core_place, normed_all, grad_own, small_grad, spread, scalar=True, flops=2 * dense_flops,
        )
        sent, qkv_block_grad = lax.optimization_barrier((swap_seq(grad_own), qkv_block_grad))
        grad_hidden, grad_low, gain_grad = once(
            before_attention_kernel,
            [
                shape((tok_count, width), f32),
                shape((tok_count, width), bf16),
                shape((8, width), f32),
            ],
            sent, qkv_w, qkv_w, qkv_w, spread, small, below, grad_middle,
            cut={
                1: ((1, row, shard_rows),),
                2: ((1, row + shard_rows, shard_rows),),
                3: ((1, row + 2 * shard_rows, shard_rows), (2, 0, 2 * KVHEADS * HD)),
            },
            flops=4 * dense_flops,
        )
        sums[layer] = summed
        dense_sources = (
            qkv_block_grad[0], swap_cores(qkv_block_grad[1]), gain_grad, swap_cores(gain_grad),
            spread, picked[1], branch, swap_cores(branch),
        )
        if layer > 0:
            grad_blocks, grad_cut, waiting = around_seq(grad_low), (), dense_sources
    (dense_pack,) = once(
        dense_kernel,
        [shape((shard_count // 2, 3 * shard_rows, half_width), bf16)],
        core_place, *dense_sources, scalar=True, flops=2 * dense_flops,
    )
    dense_sum = jnp.sum(swap_chips(dense_pack).astype(f32), axis=0).astype(bf16)
    (rows,) = once(
        arrange_kernel,
        [shape((seq_count, 3 * LAYERS, 16, half_width), bf16)],
        dense_sum, sums[0], cut={1: ((0, local_experts * expert_rows, 3 * shard_rows),)},
    )
    rows = swap_seq(rows)
    gate_grads, up_grads, down_grads = once(
        expert_grads_kernel,
        [
            shape((LAYERS,) + w_gate.shape[1:], f32),
            shape((LAYERS,) + w_up.shape[1:], f32),
            shape((LAYERS,) + w_down.shape[1:], f32),
        ],
        *sums,
        cut={0: ((0, 0, local_experts * expert_rows),)},
    )
    query_grads, key_grads, value_grads, out_grads, router_grads, *gain_grads = once(
        dense_grads_kernel,
        [
            shape((dense_rows, LAYERS, HEADS * HD), f32),
            shape((dense_rows, LAYERS, KVHEADS * HD), f32),
            shape((dense_rows, LAYERS, KVHEADS * HD), f32),
            shape((dense_rows, LAYERS, width), f32),
            shape((LAYERS, expert_count, dense_rows), f32),
            shape((LAYERS, dense_rows), f32),
            shape((LAYERS, dense_rows), f32),
        ],
        rows,
    )
    return (
        result[None],
        grad_hidden[None],
        gain_grads[0],
        query_grads.transpose(1, 0, 2),
        key_grads.transpose(1, 0, 2),
        value_grads.transpose(1, 0, 2),
        out_grads.transpose(1, 0, 2),
        gain_grads[1],
        router_grads.transpose(0, 2, 1),
        gate_grads,
        up_grads,
        down_grads,
    )


def solution(mesh):
    in_specs = (
        P("fsdp", "seq", None),
        P("fsdp", "seq", None),
        P(None, "fsdp", "seq", None),
        P(None, "fsdp", "seq", None),
        P("fsdp", None),
        P(None, ("seq", "fsdp")),
        P(None, ("seq", "fsdp"), None),
        P(None, ("seq", "fsdp"), None),
        P(None, ("seq", "fsdp"), None),
        P(None, ("seq", "fsdp"), None),
        P(None, ("seq", "fsdp")),
        P(None, ("seq", "fsdp"), None),
        P(None, "seq", "fsdp", None),
        P(None, "seq", "fsdp", None),
        P(None, "seq", "fsdp", None),
    )
    out_specs = (
        P("fsdp", "seq", None),
        P("fsdp", "seq", None),
        P(None, ("seq", "fsdp")),
        P(None, ("seq", "fsdp"), None),
        P(None, ("seq", "fsdp"), None),
        P(None, ("seq", "fsdp"), None),
        P(None, ("seq", "fsdp"), None),
        P(None, ("seq", "fsdp")),
        P(None, ("seq", "fsdp"), None),
        P(None, "seq", "fsdp", None),
        P(None, "seq", "fsdp", None),
        P(None, "seq", "fsdp", None),
    )
    return jax.shard_map(
        per_device, mesh=mesh, in_specs=in_specs, out_specs=out_specs, check_vma=False
    )
```
